32 devices in a mesh: sub: 4 (over z), coarse: 8 (over y, x, core).
Axes of the slice: x: 2, y: 2, z: 4, core: 2. Of those that a mesh axis runs over, the one named last changes fastest.
Arguments:
- schur_inverse: bfloat16 [64, 1536, 1536], P(('sub', 'coarse')), may hold values from -1 to 2, as said below
- corner_coupling: bfloat16 [64, 24, 1536], P(('sub', 'coarse')), may hold values from -0.21875 to 0.21875
- coarse_inverse: bfloat16 [4, 8, 24, 768], P(None, 'coarse', None, 'sub'), may hold values from -1 to 2, as said below
- load_cases: bfloat16 [64, 16, 1536], P(('sub', 'coarse')), may hold values from -16 to 16
- face_order: int32 [64, 768], P(('sub', 'coarse')), may hold values from 0 to 767, each once within a row
- corner_dofs: int32 [64, 24], P(('sub', 'coarse')), may hold values from 0 to 767, as said below
- scene_loads: int32 [128, 2], replicated, may hold values from 0 to 15
- scene_weights: float32 [128, 2], replicated, may hold values from 0.3 to 3
Outputs:
- multipliers: float32 [64, 128, 768], P(('sub', 'coarse'))
- residual: float32 [64, 128, 768], P(('sub', 'coarse'))
The draws below stay inside these ranges and needn't reach their ends.
Inputs may be any that keep to these rules, and one draw needn't show every extreme that they name: `schur_inverse`: each subdomain's block is symmetric positive definite. `coarse_inverse`: K as defined in the reference program is symmetric positive definite. `corner_dofs`: every entry of row n has the form (a * 8 + c) * 24 + r with c the group of subdomain n, 0 <= a < 4 and 0 <= r < 24; every coarse dof of a group is named by exactly 2 entries of that group's rows.
All inputs are finite; a program needn't handle non-finite values.
Results may differ from the reference program's by a relative error of at most 0.034.
Values may be sent and summed in bfloat16 or wider, within the bound.
No kernel may reach another device: no remote copies, remote signals or barrier semaphores. Data moves between devices by JAX's collectives and lax.ppermute only.
A program may use at most 64 MiB of HBM per device.

```python
import math
import jax
import jax.numpy as jnp
from jax import lax

FACE = 768
CORNERS = 24
LOADS = 16
ITERS = 2
SCENES = 128
SUB_DEV = 2
IFACE = 1536
NSUBS = 64
COARSE = 768
N_SUB = 4
N_COARSE = 8


def dominant_block(key, matrix_order):
    noise_key, diag_key = jax.random.split(key)
    noise_part = jax.random.normal(noise_key, (matrix_order, matrix_order), jnp.float32)
    diagonal = jax.random.uniform(diag_key, (matrix_order,), jnp.float32, 0.8, 1.6)
    symmetric = (noise_part + noise_part.T) * (0.25 / math.sqrt(2.0 * matrix_order))
    return symmetric + jnp.diag(diagonal)


def draw_schur_inverse(key, part):
    all_keys = jax.random.split(jax.random.fold_in(key, 3), NSUBS)
    return lax.map(lambda sub_key: dominant_block(sub_key, IFACE).astype(jnp.bfloat16), all_keys)


def draw_coarse_inverse(key, part):
    matrix = dominant_block(jax.random.fold_in(key, 5), COARSE).astype(jnp.bfloat16)
    return matrix.reshape(N_SUB, N_COARSE, CORNERS, COARSE)


def draw_load_cases(key, part):
    base_key, jitter_key = jax.random.split(jax.random.fold_in(key, 7))
    position = jnp.arange(NSUBS, dtype=jnp.float32) / max(NSUBS - 1, 1)
    jitter = jnp.exp(jax.random.uniform(jitter_key, (NSUBS,), jnp.float32, -0.35, 0.35))
    base_values = jnp.clip(jax.random.normal(base_key, (NSUBS, LOADS, IFACE), jnp.float32), -6.0, 6.0)
    rising = jnp.exp(math.log(3.0) * position) * jitter
    return (base_values * rising[:, None, None] * 0.6).astype(jnp.bfloat16)


def draw_corner_dofs(key, part):
    span_size = N_SUB * CORNERS
    all_keys = jax.random.split(jax.random.fold_in(key, 11), N_COARSE * SUB_DEV)
    shuffled = jax.vmap(lambda one_key: jax.random.permutation(one_key, span_size))(all_keys)
    local_dofs = shuffled.reshape(N_COARSE, N_SUB * SUB_DEV, CORNERS)
    column_ids = jnp.arange(N_COARSE)[:, None, None]
    coarse_dof = (local_dofs // CORNERS * N_COARSE + column_ids) * CORNERS + local_dofs % CORNERS
    grouped = coarse_dof.reshape(N_COARSE, N_SUB, SUB_DEV, CORNERS)
    return jnp.swapaxes(grouped, 0, 1).reshape(N_SUB * N_COARSE * SUB_DEV, CORNERS).astype(jnp.int32)


def set_ends(entries, rng, smallest, top_value):
    spot = [jax.random.randint(jax.random.fold_in(rng, axis), (), 0, length) for axis, length in enumerate(entries.shape)]
    widest = entries.shape.index(max(entries.shape))
    next_to = spot[:widest] + [(spot[widest] + 1) % entries.shape[widest]] + spot[widest + 1:]
    return entries.at[tuple(spot)].set(smallest).at[tuple(next_to)].set(top_value)


def block_scale(rng, shape, cuts, least, high):
    def one(dim, blocks):
        heights = jax.random.uniform(jax.random.fold_in(jax.random.fold_in(rng, 6), dim), (blocks,), jnp.float32, least / len(cuts), high / len(cuts))
        return jnp.repeat(jnp.exp(heights), shape[dim] // blocks).reshape((-1,) + (1,) * (len(shape) - dim - 1))

    gain = one(*cuts[0])
    for cut in cuts[1:]:
        gain = gain * one(*cut)
    return gain


def bell_draw(rng, shape, width, limit, cuts=(), kind=jnp.bfloat16):
    entries = width * jax.random.normal(rng, shape, jnp.float32)
    if cuts:
        entries = entries * block_scale(rng, shape, cuts, -0.22, 0.18)
    return jnp.clip(entries, -limit, limit).astype(kind)


def setup_inputs(seed: int = 0) -> dict:
    seeds = jax.random.split(jax.random.key(seed), 9)
    return {
        "schur_inverse": draw_schur_inverse(jax.random.fold_in(seeds[8], 71), 0),
        "corner_coupling": bell_draw(seeds[1], (NSUBS, CORNERS, IFACE), (IFACE // 2) ** -0.5, 0.21875, ((0, 32),)),
        "coarse_inverse": draw_coarse_inverse(jax.random.fold_in(seeds[8], 71), 0),
        "load_cases": draw_load_cases(jax.random.fold_in(seeds[8], 71), 0),
        "face_order": jax.vmap(lambda own: jax.random.permutation(own, FACE))(jax.random.split(seeds[4], NSUBS)).reshape((NSUBS, FACE)).astype(jnp.int32),
        "corner_dofs": draw_corner_dofs(jax.random.fold_in(seeds[8], 71), 0),
        "scene_loads": set_ends(jax.random.randint(seeds[6], (SCENES, 2), 0, LOADS), jax.random.fold_in(seeds[6], 1), 0, LOADS - 1).astype(jnp.int32),
        "scene_weights": jnp.clip(jnp.exp(jax.random.uniform(seeds[7], (SCENES, 2), jnp.float32, math.log(0.3), math.log(3.0))), 0.3, 3.0),
    }


def chain_order(values):
    tail_shape = values.shape[1:]
    grouped = values.reshape((N_SUB, N_COARSE, SUB_DEV) + tail_shape)
    return jnp.swapaxes(grouped, 0, 1).reshape((N_COARSE, N_SUB * SUB_DEV) + tail_shape)


def block_order(values):
    tail_shape = values.shape[2:]
    grouped = values.reshape((N_COARSE, N_SUB, SUB_DEV) + tail_shape)
    return jnp.swapaxes(grouped, 0, 1).reshape((N_SUB * N_COARSE * SUB_DEV,) + tail_shape)


def permute_faces(values, indices):
    return jax.vmap(lambda one_block, one_order: jnp.take(one_block, one_order, axis=1))(values, indices)


def inverse_order(face_order):
    row_ids = jnp.arange(face_order.shape[0], dtype=jnp.int32)[:, None]
    ranked = jnp.broadcast_to(jnp.arange(face_order.shape[1], dtype=jnp.int32)[None, :], face_order.shape)
    return jnp.zeros_like(face_order).at[row_ids, face_order].set(ranked)


def reference(schur_inverse, corner_coupling, coarse_inverse, load_cases, face_order, corner_dofs, scene_loads, scene_weights):
    inverse_face = inverse_order(face_order)
    position = jnp.arange(N_SUB * SUB_DEV)
    heads = block_order(jnp.broadcast_to(position[None, :] == 0, (N_COARSE, N_SUB * SUB_DEV)))
    kernel = coarse_inverse.reshape(COARSE, COARSE)

    def transposed_jump(values):
        moved = chain_order(permute_faces(values, inverse_face))
        shifted = jnp.concatenate([moved[:, 1:], jnp.zeros_like(moved[:, :1])], axis=1)
        return jnp.concatenate([-values, block_order(shifted)], axis=2)

    def jump(displaced):
        right_faces = chain_order(displaced[:, :, FACE:])
        previous = jnp.concatenate([jnp.zeros_like(right_faces[:, :1]), right_faces[:, :-1]], axis=1)
        raw_jump = permute_faces(block_order(previous), face_order) - displaced[:, :, :FACE]
        return jnp.where(heads[:, None, None], 0.0, raw_jump)

    def primal_solve(loads):
        corner_terms = lax.map(lambda operands: jnp.dot(operands[0], operands[1].T, preferred_element_type=jnp.float32), (corner_coupling, loads))
        assembled = jnp.zeros((COARSE, SCENES), jnp.float32).at[corner_dofs.reshape(-1)].add(corner_terms.reshape(-1, SCENES))
        coarse_values = jnp.dot(kernel, assembled.astype(jnp.bfloat16), preferred_element_type=jnp.float32).astype(jnp.bfloat16)
        corner_values = coarse_values[corner_dofs]

        def one_subdomain(operands):
            local_part = jnp.dot(operands[0], operands[1], preferred_element_type=jnp.float32)
            return local_part + jnp.dot(operands[2].T, operands[3], preferred_element_type=jnp.float32)

        return lax.map(one_subdomain, (loads, schur_inverse, corner_values, corner_coupling))

    selection = (scene_loads[:, :, None] == jnp.arange(LOADS, dtype=jnp.int32)[None, None, :]).astype(jnp.float32)
    mixing = jnp.sum(selection * scene_weights[:, :, None], axis=1)
    external = jnp.einsum("sl,nlb->nsb", mixing, load_cases.astype(jnp.float32), precision=lax.Precision.HIGHEST).astype(jnp.bfloat16)

    residual = jump(primal_solve(external))
    direction = residual
    multipliers = jnp.zeros_like(residual)
    norm_now = jnp.sum(residual * residual, axis=(0, 2))
    for iteration in range(ITERS):
        image_dir = jump(primal_solve(transposed_jump(direction.astype(jnp.bfloat16))))
        step_size = norm_now / jnp.sum(direction * image_dir, axis=(0, 2))
        multipliers = multipliers + step_size[None, :, None] * direction
        residual = residual - step_size[None, :, None] * image_dir
        norm_next = jnp.sum(residual * residual, axis=(0, 2))
        direction = residual + (norm_next / norm_now)[None, :, None] * direction
        norm_now = norm_next
    return multipliers, residual
```

```python
import jax
import jax.numpy as jnp
from jax import lax
from jax.sharding import PartitionSpec as P

ITERS = 2
HIGH = lax.Precision.HIGHEST


def shifted(array, axis, by):
    length = lax.axis_size(axis)
    pairs = [(i, i + by) for i in range(length) if 0 <= i + by < length]
    return lax.ppermute(array, axis, pairs)


def swapped(array, axis, bit):
    return lax.ppermute(array, axis, [(i, i ^ bit) for i in range(lax.axis_size(axis))])


def bits_of(axis):
    length = lax.axis_size(axis)
    return [1 << b for b in range(length.bit_length() - 1)]


def halves(x):
    high = lax.reduce_precision(x, exponent_bits=8, mantissa_bits=7)
    return high.astype(jnp.bfloat16), (x - high).astype(jnp.bfloat16)


def by_narrow(x, narrow):
    rows = x.shape[-2]
    stacked = jnp.concatenate(halves(x), axis=-2)
    out = lax.dot_general(
        stacked, narrow, (((2,), (1,)), ((0,), (0,))), preferred_element_type=jnp.float32
    )
    return out[:, :rows] + out[:, rows:]


def dot(a, b, dims, precision=HIGH):
    return lax.dot_general(
        a, b, (dims, ((), ())), precision=precision, preferred_element_type=jnp.float32
    )


def sum_axis(x, axis):
    for bit in bits_of(axis):
        x = x + swapped(x, axis, bit)
    return x


def gather_axis(x, axis):
    index = lax.axis_index(axis)
    for bit in bits_of(axis):
        other = swapped(x, axis, bit)
        upper = (index & bit) != 0
        x = jnp.where(
            upper, jnp.concatenate([other, x], axis=0), jnp.concatenate([x, other], axis=0)
        )
    return x


def spread_gather(x):
    return gather_axis(sum_axis(x, "sub")[None], "coarse")


def direct_gather(x):
    chain, groups = lax.axis_size("sub"), lax.axis_size("coarse")
    copies = jnp.broadcast_to(x[None], (chain * groups,) + x.shape)
    parts = lax.all_to_all(copies, ("sub", "coarse"), 0, 0)
    return jnp.sum(parts.reshape((chain, groups) + x.shape), axis=0)


def per_device(
    schur_inverse,
    corner_coupling,
    coarse_inverse,
    load_cases,
    face_order,
    corner_dofs,
    scene_loads,
    scene_weights,
):
    local_subs, iface = schur_inverse.shape[0], schur_inverse.shape[1]
    face = face_order.shape[1]
    corners = corner_dofs.shape[1]
    cases = load_cases.shape[1]
    chain, groups = lax.axis_size("sub"), lax.axis_size("coarse")
    column = chain * corners
    position, group = lax.axis_index("sub"), lax.axis_index("coarse")
    at_head, at_tail = position == 0, position == chain - 1

    shard = coarse_inverse.reshape(column, groups * corners)
    kernel_rows = jnp.moveaxis(
        gather_axis(shard[None], "sub").reshape(chain, column, groups * corners), 0, 1
    ).reshape(column, chain * groups * corners)
    ids = jnp.arange(chain * groups * corners, dtype=jnp.int32)
    target = (
        ids // corners % groups * column + ids // (groups * corners) * corners + ids % corners
    )
    regroup = (target[:, None] == ids[None, :]).astype(jnp.bfloat16)
    kernel_rows = dot(kernel_rows, regroup, ((1,), (0,)), None).astype(jnp.bfloat16)
    whole_fits = groups * column * groups * column <= schur_inverse.size
    kernel_whole = None
    if whole_fits:
        kernel_whole = lax.all_gather(kernel_rows, "coarse", axis=0, tiled=True)

    face_ids = jnp.arange(face, dtype=jnp.int32)
    forward_table = (face_order[:, None, :] == face_ids[None, :, None]).astype(jnp.bfloat16)
    backward_table = (face_order[:, :, None] == face_ids[None, None, :]).astype(jnp.bfloat16)
    local_index = corner_dofs // (groups * corners) * corners + corner_dofs % corners
    column_ids = jnp.arange(column, dtype=jnp.int32)
    spread = (local_index[:, :, None] == column_ids[None, None, :]).astype(jnp.bfloat16)
    left_mask = jnp.logical_and(jnp.arange(local_subs) == 0, at_head)[:, None, None]
    right_mask = jnp.logical_and(jnp.arange(local_subs) == local_subs - 1, at_tail)[:, None, None]

    def jump_pair(displaced, from_before, from_after, forward, backward):
        moved = forward(
            jnp.concatenate([from_before[None], displaced[:-1, :, face:]], axis=0)
        )
        back = jnp.concatenate([backward[1:], from_after[None]], axis=0)
        left = jnp.where(left_mask, 0.0, displaced[:, :, :face] - moved)
        right = jnp.where(right_mask, 0.0, displaced[:, :, face:] - back)
        return jnp.concatenate([left, right], axis=2)

    def forward_of(x):
        return by_narrow(x, forward_table)

    def spring(displaced):
        backward = by_narrow(displaced[:, :, :face], backward_table)
        before = shifted(displaced[local_subs - 1, :, face:], "sub", 1)
        after = shifted(backward[0], "sub", -1)
        return jump_pair(displaced, before, after, forward_of, backward)

    coupled = lax.dot_general(
        spread, corner_coupling, (((1,), (1,)), ((0,), (0,))), preferred_element_type=jnp.float32
    )
    cases_f32 = load_cases.astype(jnp.float32)
    loads_at_corners = dot(cases_f32, coupled, ((0, 2), (0, 2)))
    corner_sums = direct_gather(loads_at_corners)

    displaced = lax.dot_general(
        load_cases, schur_inverse, (((2,), (1,)), ((0,), (0,))), preferred_element_type=jnp.float32
    )
    lone = spring(displaced)
    lifts = spring(coupled)

    def solved(sums):
        flat = jnp.moveaxis(sums, 0, 1).reshape(cases, groups * column)
        return dot(flat, kernel_rows.astype(jnp.float32), ((1,), (1,)))

    def lifted(values):
        return jnp.einsum("ij,njk->nik", values, lifts, precision=HIGH)

    def at_corners(pulled):
        return dot(pulled[:, :, :face], lifts[:, :, :face], ((0, 2), (0, 2)))

    def gram(a, b):
        return dot(a, b, ((0, 2), (0, 2)))

    pull0 = lone + lifted(solved(corner_sums))
    sums1 = spread_gather(at_corners(pull0))
    image1 = spring(by_narrow(pull0, schur_inverse))
    pull1 = image1 + lifted(solved(sums1))
    displaced2 = by_narrow(pull1, schur_inverse)
    grams = jnp.concatenate(
        [
            gram(pull0[:, :, :face], pull0[:, :, :face]),
            gram(pull0[:, :, :face], pull1[:, :, :face]),
            gram(pull1[:, :, :face], pull1[:, :, :face]),
            gram(pull1, displaced2),
        ],
        axis=1,
    )
    packed = direct_gather(jnp.concatenate([at_corners(pull1), grams], axis=1))
    sums2 = packed[:, :, :column]
    grams = jnp.sum(packed[:, :, column:], axis=0).reshape(cases, 4, cases)
    image2 = spring(displaced2)
    values2 = solved(sums2)
    pull2 = image2 + lifted(values2)
    if whole_fits:
        flat = jnp.moveaxis(sums2, 0, 1).reshape(cases, groups * column)
        energy = dot(
            dot(flat, kernel_whole.astype(jnp.float32), ((1,), (1,))), flat, ((1,), (1,))
        )
    else:
        own = lax.dynamic_index_in_dim(sums2, group, 0, keepdims=False)
        energy = lax.psum(dot(values2, own, ((1,), (1,))), "coarse")

    selection = (
        scene_loads[:, :, None] == jnp.arange(cases, dtype=jnp.int32)[None, None, :]
    ).astype(jnp.float32)
    mixing = jnp.sum(selection * scene_weights[:, :, None], axis=1)

    def moment(matrix):
        return jnp.sum(dot(mixing, matrix, ((1,), (0,))) * mixing, axis=1)

    moment0, moment1, moment2 = moment(grams[:, 0]), moment(grams[:, 1]), moment(grams[:, 2])
    moment3 = moment(grams[:, 3] + energy)
    step0 = moment0 / moment1
    norm1 = moment0 - 2.0 * step0 * moment1 + step0 * step0 * moment2
    grow = 1.0 + norm1 / moment0
    curvature = grow * grow * moment1 - 2.0 * grow * step0 * moment2 + step0 * step0 * moment3
    step1 = norm1 / curvature
    basis = -jnp.concatenate(
        [pull0[:, :, :face], pull1[:, :, :face], pull2[:, :, :face]], axis=1
    )
    weights_multipliers = jnp.concatenate(
        [(step0 + step1 * grow)[:, None] * mixing, (-step0 * step1)[:, None] * mixing], axis=1
    )
    weights_residual = jnp.concatenate(
        [mixing, (-step0 - step1 * grow)[:, None] * mixing, (step0 * step1)[:, None] * mixing],
        axis=1,
    )
    multipliers = jnp.einsum("sj,njk->nsk", weights_multipliers, basis[:, : 2 * cases], precision=HIGH)
    residual = jnp.einsum("sj,njk->nsk", weights_residual, basis, precision=HIGH)
    return (multipliers, residual)


def solution(mesh):
    return jax.shard_map(
        per_device,
        mesh=mesh,
        in_specs=(
            P(("sub", "coarse"), None, None),
            P(("sub", "coarse"), None, None),
            P(None, "coarse", None, "sub"),
            P(("sub", "coarse"), None, None),
            P(("sub", "coarse"), None),
            P(("sub", "coarse"), None),
            P(),
            P(),
        ),
        out_specs=(P(("sub", "coarse"), None, None), P(("sub", "coarse"), None, None)),
        check_vma=False,
    )
```

```python
import jax
import jax.numpy as jnp
from jax import lax
from jax.sharding import PartitionSpec as P

ITERS = 2
HIGH = lax.Precision.HIGHEST


def halves(x):
    high = lax.reduce_precision(x, exponent_bits=8, mantissa_bits=7)
    return high.astype(jnp.bfloat16), (x - high).astype(jnp.bfloat16)


def by_narrow(x, narrow):
    rows = x.shape[-2]
    stacked = jnp.concatenate(halves(x), axis=-2)
    out = lax.dot_general(
        stacked, narrow, (((2,), (1,)), ((0,), (0,))), preferred_element_type=jnp.float32
    )
    return out[:, :rows] + out[:, rows:]


def dot(a, b, dims, precision=HIGH):
    return lax.dot_general(
        a, b, (dims, ((), ())), precision=precision, preferred_element_type=jnp.float32
    )


def everywhere(x, axes):
    count = lax.axis_size(axes)
    return lax.all_to_all(jnp.broadcast_to(x[None], (count,) + x.shape), axes, 0, 0)


def exchange(to_after, to_before):
    length = lax.axis_size("sub")
    odd = (lax.axis_index("sub") & 1) == 1
    first = lax.ppermute(
        jnp.where(odd, to_before, to_after),
        "sub",
        [(i, i ^ 1) for i in range(length) if i ^ 1 < length],
    )
    second = lax.ppermute(
        jnp.where(odd, to_after, to_before),
        "sub",
        [(i, j) for i in range(length) for j in [i + 1 if i & 1 else i - 1] if 0 <= j < length],
    )
    return jnp.where(odd, first, second), jnp.where(odd, second, first)


def per_device(
    schur_inverse,
    corner_coupling,
    coarse_inverse,
    load_cases,
    face_order,
    corner_dofs,
    scene_loads,
    scene_weights,
):
    local_subs, iface = schur_inverse.shape[0], schur_inverse.shape[1]
    face = face_order.shape[1]
    corners = corner_dofs.shape[1]
    cases = load_cases.shape[1]
    chain, groups = lax.axis_size("sub"), lax.axis_size("coarse")
    column = chain * corners
    position, group = lax.axis_index("sub"), lax.axis_index("coarse")
    at_head, at_tail = position == 0, position == chain - 1

    shard = coarse_inverse.reshape(column, groups * corners)
    kernel_rows = jnp.moveaxis(everywhere(shard, "sub"), 0, 1).reshape(
        column, chain * groups * corners
    )
    ids = jnp.arange(chain * groups * corners, dtype=jnp.int32)
    target = (
        ids // corners % groups * column + ids // (groups * corners) * corners + ids % corners
    )
    regroup = (target[:, None] == ids[None, :]).astype(jnp.bfloat16)
    kernel_rows = dot(kernel_rows, regroup, ((1,), (0,)), None).astype(jnp.bfloat16)
    whole_fits = groups * column * groups * column <= schur_inverse.size
    kernel_whole = None
    if whole_fits:
        kernel_whole = everywhere(kernel_rows, "coarse").reshape(groups * column, groups * column)

    face_ids = jnp.arange(face, dtype=jnp.int32)
    forward_table = (face_order[:, None, :] == face_ids[None, :, None]).astype(jnp.bfloat16)
    backward_table = (face_order[:, :, None] == face_ids[None, None, :]).astype(jnp.bfloat16)
    local_index = corner_dofs // (groups * corners) * corners + corner_dofs % corners
    column_ids = jnp.arange(column, dtype=jnp.int32)
    spread = (local_index[:, :, None] == column_ids[None, None, :]).astype(jnp.bfloat16)
    left_mask = jnp.logical_and(jnp.arange(local_subs) == 0, at_head)[:, None, None]
    right_mask = jnp.logical_and(jnp.arange(local_subs) == local_subs - 1, at_tail)[:, None, None]

    def jump_pair(displaced, from_before, from_after, forward, backward):
        moved = forward(
            jnp.concatenate([from_before[None], displaced[:-1, :, face:]], axis=0)
        )
        back = jnp.concatenate([backward[1:], from_after[None]], axis=0)
        left = jnp.where(left_mask, 0.0, displaced[:, :, :face] - moved)
        right = jnp.where(right_mask, 0.0, displaced[:, :, face:] - back)
        return jnp.concatenate([left, right], axis=2)

    def forward_of(x):
        return by_narrow(x, forward_table)

    def spring(displaced):
        backward = by_narrow(displaced[:, :, :face], backward_table)
        before, after = exchange(displaced[local_subs - 1, :, face:], backward[0])
        return jump_pair(displaced, before, after, forward_of, backward)

    coupled = lax.dot_general(
        spread, corner_coupling, (((1,), (1,)), ((0,), (0,))), preferred_element_type=jnp.float32
    )
    cases_f32 = load_cases.astype(jnp.float32)
    loads_at_corners = dot(cases_f32, coupled, ((0, 2), (0, 2)))

    def gathered(*pieces):
        parts = [pieces[0].astype(jnp.bfloat16)]
        for piece in pieces[1:]:
            parts.extend(halves(piece))
        received = everywhere(jnp.concatenate(parts, axis=1), ("sub", "coarse"))
        received = received.reshape((chain, groups) + received.shape[1:]).astype(jnp.float32)
        sums = jnp.sum(received[..., :column], axis=0)
        totals = []
        at = column
        for piece in pieces[1:]:
            width = piece.shape[1]
            whole = jnp.sum(received[..., at : at + 2 * width], axis=(0, 1))
            totals.append(whole[:, :width] + whole[:, width:])
            at += 2 * width
        return sums, totals

    corner_sums, _ = gathered(loads_at_corners)

    displaced = lax.dot_general(
        load_cases, schur_inverse, (((2,), (1,)), ((0,), (0,))), preferred_element_type=jnp.float32
    )
    lone = spring(displaced)
    hints = jnp.concatenate(
        [
            jnp.concatenate(
                [
                    corner_coupling[local_subs - 1, :, face:],
                    lax.dot_general(
                        corner_coupling[0, :, :face],
                        backward_table[0],
                        (((1,), (0,)), ((), ())),
                        preferred_element_type=jnp.float32,
                    ).astype(jnp.bfloat16),
                ],
                axis=0,
            ),
            jnp.concatenate([spread[local_subs - 1], spread[0]], axis=0),
        ],
        axis=1,
    )
    hint_before, hint_after = exchange(hints[:corners], hints[corners:])

    def spread_hint(hint):
        return lax.dot_general(
            hint[:, face:],
            hint[:, :face],
            (((0,), (0,)), ((), ())),
            preferred_element_type=jnp.float32,
        )

    lifts = jump_pair(
        coupled,
        spread_hint(hint_before),
        spread_hint(hint_after),
        forward_of,
        by_narrow(coupled[:, :, :face], backward_table),
    )

    def solved(sums):
        flat = jnp.moveaxis(sums, 0, 1).reshape(cases, groups * column)
        return dot(flat, kernel_rows.astype(jnp.float32), ((1,), (1,)))

    def lifted(values):
        return jnp.einsum("ij,njk->nik", values, lifts, precision=HIGH)

    def at_corners(pulled):
        return dot(pulled[:, :, :face], lifts[:, :, :face], ((0, 2), (0, 2)))

    def gram(a, b):
        return dot(a, b, ((0, 2), (0, 2)))

    pull0 = lone + lifted(solved(corner_sums))
    sums1, (gram0,) = gathered(
        at_corners(pull0), gram(pull0[:, :, :face], pull0[:, :, :face])
    )
    image1 = spring(by_narrow(pull0, schur_inverse))
    pull1 = image1 + lifted(solved(sums1))
    displaced2 = by_narrow(pull1, schur_inverse)
    sums2, (gram1, gram2, gram3) = gathered(
        at_corners(pull1),
        gram(pull0[:, :, :face], pull1[:, :, :face]),
        gram(pull1[:, :, :face], pull1[:, :, :face]),
        gram(pull1, displaced2),
    )
    image2 = spring(displaced2)
    values2 = solved(sums2)
    pull2 = image2 + lifted(values2)
    if whole_fits:
        flat = jnp.moveaxis(sums2, 0, 1).reshape(cases, groups * column)
        energy = dot(
            dot(flat, kernel_whole.astype(jnp.float32), ((1,), (1,))), flat, ((1,), (1,))
        )
    else:
        own = lax.dynamic_index_in_dim(sums2, group, 0, keepdims=False)
        energy = lax.psum(dot(values2, own, ((1,), (1,))), "coarse")

    selection = (
        scene_loads[:, :, None] == jnp.arange(cases, dtype=jnp.int32)[None, None, :]
    ).astype(jnp.float32)
    mixing = jnp.sum(selection * scene_weights[:, :, None], axis=1)

    def moment(matrix):
        return jnp.sum(dot(mixing, matrix, ((1,), (0,))) * mixing, axis=1)

    moment0, moment1, moment2 = moment(gram0), moment(gram1), moment(gram2)
    moment3 = moment(gram3 + energy)
    step0 = moment0 / moment1
    norm1 = moment0 - 2.0 * step0 * moment1 + step0 * step0 * moment2
    grow = 1.0 + norm1 / moment0
    curvature = grow * grow * moment1 - 2.0 * grow * step0 * moment2 + step0 * step0 * moment3
    step1 = norm1 / curvature
    basis = -jnp.concatenate(
        [pull0[:, :, :face], pull1[:, :, :face], pull2[:, :, :face]], axis=1
    )
    weights_multipliers = jnp.concatenate(
        [(step0 + step1 * grow)[:, None] * mixing, (-step0 * step1)[:, None] * mixing], axis=1
    )
    weights_residual = jnp.concatenate(
        [mixing, (-step0 - step1 * grow)[:, None] * mixing, (step0 * step1)[:, None] * mixing],
        axis=1,
    )
    multipliers = jnp.einsum("sj,njk->nsk", weights_multipliers, basis[:, : 2 * cases], precision=HIGH)
    residual = jnp.einsum("sj,njk->nsk", weights_residual, basis, precision=HIGH)
    return (multipliers, residual)


def solution(mesh):
    return jax.shard_map(
        per_device,
        mesh=mesh,
        in_specs=(
            P(("sub", "coarse"), None, None),
            P(("sub", "coarse"), None, None),
            P(None, "coarse", None, "sub"),
            P(("sub", "coarse"), None, None),
            P(("sub", "coarse"), None),
            P(("sub", "coarse"), None),
            P(),
            P(),
        ),
        out_specs=(P(("sub", "coarse"), None, None), P(("sub", "coarse"), None, None)),
        check_vma=False,
    )
```

```python
import functools

import jax
import jax.numpy as jnp
import numpy as np
from jax import lax
from jax.experimental import pallas as pl
from jax.experimental.pallas import tpu as pltpu
from jax.sharding import PartitionSpec as P

LANES = 128
CHUNK = 256
F32, BF16 = jnp.float32, jnp.bfloat16


def nn(a, b):
    return lax.dot_general(a, b, (((1,), (0,)), ((), ())), preferred_element_type=F32)


def nt(a, b):
    return lax.dot_general(a, b, (((1,), (1,)), ((), ())), preferred_element_type=F32)


def halves(x):
    high = x.astype(BF16)
    return high, (x - high.astype(F32)).astype(BF16)


def stacked(x):
    return jnp.concatenate(halves(x), axis=0)


def folded(x):
    rows = x.shape[0] // 2
    return x[:rows] + x[rows:]


def nn2(x, narrow):
    return folded(nn(stacked(x), narrow))


def nt2(x, narrow):
    return folded(nt(stacked(x), narrow))


def both3(product, x, y):
    high, low = halves(y)
    return folded(product(stacked(x), high)) + product(x.astype(BF16), low)


def equal(a, b):
    return jnp.where(a == b, 1.0, 0.0).astype(BF16)


def iota(shape, dim):
    return lax.broadcasted_iota(jnp.int32, shape, dim)


def rounded_up(value, unit):
    return (value + unit - 1) // unit * unit


def table(order_row):
    size = order_row.shape[1]
    return equal(iota((size, size), 0), order_row)


def spread_of(dofs_row, chain, corners, groups):
    column = chain * corners
    ids = iota((column, 1), 0)
    slot = sum((ids >= t * corners).astype(jnp.int32) for t in range(1, chain))
    target = ids + slot * ((groups - 1) * corners) + lax.axis_index("coarse") * corners
    return equal(target, dofs_row)


def placed(x, width, at):
    rows = x.shape[1]
    return nn(x, equal(iota((rows, width), 0) + at, iota((rows, width), 1)))


def picked(x, at, count):
    width = x.shape[1]
    lane = iota((width, count), 0) - at
    column = iota((width, count), 1)
    hit = jnp.where(lane == column, 1.0, 0.0) + jnp.where(lane == column + count, 1.0, 0.0)
    return nn2(x, hit.astype(BF16))


def by_parity(to_after, to_before):
    odd = (lax.axis_index("sub") & 1) == 1
    return jnp.where(odd, to_before, to_after), jnp.where(odd, to_after, to_before)


def start_fetch(matrix, held, sems):
    subs, size = matrix.shape[0], matrix.shape[1]
    copies = []
    for n in range(subs):
        for k in range(size // CHUNK):
            part = pl.ds(k * CHUNK, CHUNK)
            copy = pltpu.make_async_copy(
                matrix.at[n, part], held.at[n, part], sems.at[n * (size // CHUNK) + k]
            )
            copy.start()
            copies.append(copy)
    return copies


def times_matrix(x, n, held, copies):
    size = held.shape[1]
    count = size // CHUNK
    total = None
    for k in range(count):
        copies[n * count + k].wait()
        part = nn(x[:, k * CHUNK : (k + 1) * CHUNK], held[n, k * CHUNK : (k + 1) * CHUNK])
        total = part if total is None else total + part
    return total


def jumped(displaced, order, from_before, from_after, left_only=False):
    subs = len(displaced)
    face = order.shape[1]
    at_head = lax.axis_index("sub") == 0
    at_tail = lax.axis_index("sub") == lax.axis_size("sub") - 1
    result = []
    for n in range(subs):
        own = table(order[n : n + 1])
        before = nn(from_before, own) if n == 0 else nn2(displaced[n - 1][:, face:], own)
        left = displaced[n][:, :face] - before
        if n == 0:
            left = jnp.where(at_head, 0.0, left)
        if left_only:
            result.append(left)
            continue
        if n == subs - 1:
            right = displaced[n][:, face:] - from_after
            right = jnp.where(at_tail, 0.0, right)
        else:
            following = table(order[n + 1 : n + 2])
            right = displaced[n][:, face:] - nt2(displaced[n + 1][:, :face], following)
        result.append(jnp.concatenate([left, right], axis=1))
    return result


def chain_sums(received, groups, width):
    chain = received.shape[0] // groups
    sums = []
    for c in range(groups):
        total = None
        for z in range(chain):
            part = received[z * groups + c, :, :width].astype(F32)
            total = part if total is None else total + part
        sums.append(total)
    return sums


def copies_of(out, x):
    for i in range(out.shape[0]):
        out[i] = x


def corner_kernel(loads, coupling, dofs, out, *, chain, groups):
    corners = coupling.shape[1]
    total = None
    for n in range(loads.shape[0]):
        terms = nt(loads[n], coupling[n])
        part = nt2(terms, spread_of(dofs[n : n + 1], chain, corners, groups))
        total = part if total is None else total + part
    copies_of(out, placed(total.astype(BF16), out.shape[2], 0).astype(BF16))


def first_kernel(
    matrix, loads, order, coupling, dofs, out, first, second, held, sems, *, chain, groups
):
    copies = start_fetch(matrix, held, sems)
    subs, cases, iface = loads.shape
    corners, face = coupling.shape[1], order.shape[1]
    pad = rounded_up(corners, 16) - corners
    near = table(order[0:1])

    def packet(displaced, coupled, n):
        spread = spread_of(dofs[n : n + 1], chain, corners, groups)
        eye = equal(iota((corners, corners), 0), iota((corners, corners), 1))
        hot = placed(nt(eye, spread).astype(BF16), first.shape[1] - face, 0)
        lower = jnp.concatenate([coupled, hot], axis=1)
        upper = jnp.concatenate([displaced, jnp.zeros((cases, hot.shape[1]), F32)], axis=1)
        return jnp.concatenate([upper, lower, jnp.zeros((pad, lower.shape[1]), F32)], axis=0)

    for n in range(subs):
        out[n] = times_matrix(loads[n], n, held, copies)
    last = subs - 1
    to_after = packet(out[last, :, face:], coupling[last, :, face:].astype(F32), last)
    to_before = packet(
        nt(out[0, :, :face].astype(BF16), near), nt(coupling[0, :, :face], near), 0
    )
    one, two = by_parity(to_after, to_before)
    first[...] = one.astype(BF16)
    second[...] = two.astype(BF16)


def lift_kernel(
    displaced, first, second, received, *refs, chain, groups
):
    shards = refs[:chain]
    coupling, dofs, order, regroup, lifts, kernel, pull, out = refs[chain:]
    subs, cases, _ = displaced.shape
    corners, face = coupling.shape[1], order.shape[1]
    column = chain * corners
    wide = rounded_up(column, LANES)
    position = lax.axis_index("sub")
    depth = groups * corners
    rows = None
    for j in range(chain):
        ids = iota((depth, regroup.shape[1]), 0) + (position ^ j) * depth
        part = nn(shards[j][...], equal(ids, regroup[...]))
        rows = part if rows is None else rows + part
    kernel[...] = rows.astype(BF16)

    from_after, from_before = by_parity(first[...].astype(F32), second[...].astype(F32))
    eye = equal(iota((column, first.shape[1] - face), 0), iota((column, first.shape[1] - face), 1))

    def neighbour(block):
        low = block[cases:].astype(BF16)
        return low[:, :face], nt(eye, low[:, face:]).astype(BF16)

    before_coupling, before_spread = neighbour(from_before)
    after_coupling, after_spread = neighbour(from_after)
    spreads = [spread_of(dofs[n : n + 1], chain, corners, groups) for n in range(subs)]
    at_head, at_tail = position == 0, position == chain - 1
    lifted = []
    for n in range(subs):
        own = table(order[n : n + 1])
        if n == 0:
            moved = nn(before_spread, nn(before_coupling, own).astype(BF16))
        else:
            moved = nn(spreads[n - 1], nn(coupling[n - 1, :, face:], own).astype(BF16))
        left = nn(spreads[n], coupling[n, :, :face]) - moved
        if n == 0:
            left = jnp.where(at_head, 0.0, left)
        if n == subs - 1:
            back = nn(after_spread, after_coupling)
        else:
            following = table(order[n + 1 : n + 2])
            back = nn(spreads[n + 1], nt(coupling[n + 1, :, :face], following).astype(BF16))
        right = nn(spreads[n], coupling[n, :, face:]) - back
        if n == subs - 1:
            right = jnp.where(at_tail, 0.0, right)
        lifted.append(jnp.concatenate([left, right], axis=1).astype(BF16))
        lifts[n] = lifted[n]

    flat = jnp.concatenate(chain_sums(received, groups, wide), axis=1)
    values = nt2(flat, kernel[...])
    bent = jumped(
        [displaced[n] for n in range(subs)],
        order,
        from_before[:cases, :face].astype(BF16),
        from_after[:cases, :face],
    )
    corner, norms = None, None
    for n in range(subs):
        whole = bent[n] + nn2(values, lifted[n])
        pull[n] = whole
        left = whole[:, :face]
        part, norm = nt2(left, lifted[n][:, :face]), both3(nt, left, left)
        corner = part if corner is None else corner + part
        norms = norm if norms is None else norms + norm
    copies_of(out, packed(out.shape[2], corner, norms))


def packed(width, corner, *grams):
    total = placed(corner.astype(BF16), width, 0)
    at = corner.shape[1]
    for gram in grams:
        for half in halves(gram):
            total = total + placed(half, width, at)
            at += gram.shape[1]
    return total.astype(BF16)


def second_kernel(matrix, pull, order, out, first, second, held, sems):
    copies = start_fetch(matrix, held, sems)
    subs = pull.shape[0]
    face = order.shape[1]
    near = table(order[0:1])
    for n in range(subs):
        out[n] = folded(times_matrix(stacked(pull[n]), n, held, copies))
    one, two = by_parity(out[subs - 1, :, face:], nt2(out[0, :, :face], near))
    first[...] = one.astype(BF16)
    second[...] = two.astype(BF16)


def third_kernel(
    matrix, displaced, first, second, received, kernel, lifts, pull0, order,
    pull, out, after, payload, norms0, held, sems, *, groups
):
    copies = start_fetch(matrix, held, sems)
    subs, cases, _ = displaced.shape
    face = order.shape[1]
    column = lifts.shape[1]
    wide = rounded_up(column, LANES)
    from_after, from_before = by_parity(first[...].astype(F32), second[...].astype(F32))
    sums = chain_sums(received, groups, received.shape[2])
    flat = jnp.concatenate([part[:, :wide] for part in sums], axis=1)
    values = nt2(flat, kernel[...])
    norms0[...] = picked(sum(sums), column, cases)
    bent = jumped(
        [displaced[n] for n in range(subs)], order, from_before.astype(BF16), from_after
    )
    totals = None
    for n in range(subs):
        whole = bent[n] + nn2(values, lifts[n])
        pull[n] = whole
        left = whole[:, :face]
        moved = folded(times_matrix(stacked(whole), n, held, copies))
        out[n] = moved
        parts = [
            nt2(left, lifts[n, :, :face]),
            both3(nt, pull0[n, :, :face], left),
            both3(nt, left, left),
            both3(nt, whole, moved),
        ]
        totals = parts if totals is None else [a + b for a, b in zip(totals, parts)]
    after[...] = out[subs - 1, :, face:].astype(BF16)
    copies_of(payload, packed(payload.shape[2], *totals))


def scene_kernel(
    displaced, from_before, received, kernel, lifts, pull0, pull1, order, norms0,
    scene_loads, scene_weights, *refs, groups, pieces
):
    blocks = refs[:pieces]
    multipliers, residual, held = refs[pieces:]
    subs, cases, _ = displaced.shape
    face = order.shape[1]
    column = lifts.shape[1]
    wide = rounded_up(column, LANES)
    group = lax.axis_index("coarse")
    sums = chain_sums(received, groups, received.shape[2])
    for c in range(groups):
        held[c] = sums[c][:, :wide]
    flat = jnp.concatenate([part[:, :wide] for part in sums], axis=1)
    values = nt2(flat, kernel[...])
    if groups_whole(blocks, column, groups):
        energy, index = None, 0
        for block in blocks:
            for i in range(block.shape[0] // column):
                lifted = nt2(flat, block[i * column : (i + 1) * column])
                part = both3(nt, lifted, held[group ^ index][:, :column])
                energy = part if energy is None else energy + part
                index += 1
    else:
        energy = blocks[0][...]
    total = sum(sums)
    norms1 = picked(total, column, cases)
    norms2 = picked(total, column + 2 * cases, cases)
    norms3 = picked(total, column + 4 * cases, cases) + energy

    ids = iota((cases, scene_loads.shape[1]), 0)
    mixing = sum(
        jnp.where(ids == scene_loads[i : i + 1], scene_weights[i : i + 1], 0.0)
        for i in range(scene_loads.shape[0])
    )

    def moment(norms):
        return jnp.sum(both3(nn, norms, mixing) * mixing, axis=0, keepdims=True)

    moment0, moment1 = moment(norms0[...]), moment(norms1)
    moment2, moment3 = moment(norms2), moment(norms3)
    step0 = moment0 / moment1
    norm1 = moment0 - 2.0 * step0 * moment1 + step0 * step0 * moment2
    grow = 1.0 + norm1 / moment0
    curvature = grow * grow * moment1 - 2.0 * grow * step0 * moment2 + step0 * step0 * moment3
    step1 = norm1 / curvature
    zeros = jnp.zeros_like(mixing)

    def transposed(parts):
        weights = -jnp.concatenate(parts, axis=0)
        high = weights.astype(BF16).astype(F32)
        return jnp.concatenate([high, high, weights - high], axis=0).T.astype(BF16)

    for_multipliers = transposed(
        [(step0 + step1 * grow) * mixing, (-step0 * step1) * mixing, zeros]
    )
    for_residual = transposed(
        [mixing, (-step0 - step1 * grow) * mixing, (step0 * step1) * mixing]
    )
    bent = jumped([displaced[n] for n in range(subs)], order, from_before[...], None, True)
    for n in range(subs):
        pull2 = bent[n] + nn2(values, lifts[n, :, :face])
        basis = jnp.concatenate([pull0[n, :, :face], pull1[n, :, :face], pull2], axis=0)
        high, low = halves(basis)
        basis = jnp.concatenate([high, low, high], axis=0)
        multipliers[n] = nn(for_multipliers, basis)
        residual[n] = nn(for_residual, basis)


def groups_whole(blocks, column, groups):
    return sum(block.shape[0] for block in blocks) == column * groups


def everywhere(x, axes):
    return lax.all_to_all(x, axes, 0, 0)


def swapped(x, axis, bit):
    return lax.ppermute(x, axis, [(i, i ^ bit) for i in range(lax.axis_size(axis))])


def pair_swaps(first, second):
    length = lax.axis_size("sub")
    one = lax.ppermute(first, "sub", [(i, i ^ 1) for i in range(length) if i ^ 1 < length])
    two = lax.ppermute(
        second,
        "sub",
        [(i, j) for i in range(length) for j in [i + 1 if i & 1 else i - 1] if 0 <= j < length],
    )
    return one, two


def call(kernel, outs, args, scratch=(), flops=0, moved=0, limit=32, in_place=()):
    specs = [
        pl.BlockSpec(memory_space=pl.ANY if i in in_place else pltpu.VMEM)
        for i in range(len(args))
    ]
    return pl.pallas_call(
        kernel,
        out_shape=[jax.ShapeDtypeStruct(shape, kind) for shape, kind in outs],
        in_specs=specs,
        out_specs=[pl.BlockSpec(memory_space=pltpu.VMEM)] * len(outs),
        scratch_shapes=list(scratch),
        compiler_params=pltpu.CompilerParams(vmem_limit_bytes=limit << 20),
        cost_estimate=pl.CostEstimate(flops=flops, bytes_accessed=moved, transcendentals=0),
    )(*args)


def per_device(
    schur_inverse,
    corner_coupling,
    coarse_inverse,
    load_cases,
    face_order,
    corner_dofs,
    scene_loads,
    scene_weights,
):
    subs, iface = schur_inverse.shape[0], schur_inverse.shape[1]
    face = face_order.shape[1]
    corners = corner_dofs.shape[1]
    cases = load_cases.shape[1]
    scenes = scene_loads.shape[0]
    chain, groups = lax.axis_size("sub"), lax.axis_size("coarse")
    devices = chain * groups
    column = chain * corners
    wide = rounded_up(column, LANES)
    along = groups * wide
    work = dict(flops=4 * cases * schur_inverse.size, moved=2 * schur_inverse.size)
    fetch = [
        pltpu.VMEM(schur_inverse.shape, BF16),
        pltpu.SemaphoreType.DMA((subs * (iface // CHUNK),)),
    ]

    shard = coarse_inverse.reshape(column, groups * corners)
    shards = [shard] + [swapped(shard, "sub", j) for j in range(1, chain)]

    lane = np.arange(along)
    inner = lane % wide
    source = (inner // corners * groups + lane // wide) * corners + inner % corners
    regroup = jnp.asarray(np.where(inner < column, source, -1)[None].astype(np.int32))

    (sent0,) = call(
        functools.partial(corner_kernel, chain=chain, groups=groups),
        [((devices, cases, wide), BF16)],
        [load_cases, corner_coupling, corner_dofs],
    )
    received0 = everywhere(sent0, ("sub", "coarse"))
    packet = (cases + rounded_up(corners, 16), face + wide)
    displaced0, first, second = call(
        functools.partial(first_kernel, chain=chain, groups=groups),
        [((subs, cases, iface), F32), (packet, BF16), (packet, BF16)],
        [schur_inverse, load_cases, face_order, corner_coupling, corner_dofs],
        fetch,
        in_place=(0,),
        **work,
    )
    first, second = pair_swaps(first, second)
    lifts, kernel, pull0, sent1 = call(
        functools.partial(lift_kernel, chain=chain, groups=groups),
        [
            ((subs, column, iface), BF16),
            ((column, along), BF16),
            ((subs, cases, iface), F32),
            ((devices, cases, rounded_up(column + 2 * cases, LANES)), BF16),
        ],
        [displaced0, first, second, received0, *shards]
        + [corner_coupling, corner_dofs, face_order, regroup],
        flops=10**9,
        moved=10**6,
    )
    received1 = everywhere(sent1, ("sub", "coarse"))
    displaced1, first, second = call(
        second_kernel,
        [((subs, cases, iface), F32), ((cases, face), BF16), ((cases, face), BF16)],
        [schur_inverse, pull0, face_order],
        fetch,
        in_place=(0,),
        **work,
    )
    first, second = pair_swaps(first, second)

    blocks = None
    if column * groups * column * groups <= schur_inverse.size:
        blocks = [kernel]
        bit = 1
        while bit < groups:
            block = jnp.concatenate(blocks, axis=0) if len(blocks) > 1 else blocks[0]
            blocks.append(swapped(block, "coarse", bit))
            bit *= 2

    pull1, displaced2, after, sent2, norms0 = call(
        functools.partial(third_kernel, groups=groups),
        [
            ((subs, cases, iface), F32),
            ((subs, cases, iface), F32),
            ((cases, face), BF16),
            ((devices, cases, rounded_up(column + 6 * cases, LANES)), BF16),
            ((cases, cases), F32),
        ],
        [schur_inverse, displaced1, first, second, received1, kernel, lifts, pull0, face_order],
        fetch,
        in_place=(0,),
        **work,
    )
    received2 = everywhere(sent2, ("sub", "coarse"))
    before = lax.ppermute(after, "sub", [(i, i + 1) for i in range(chain - 1)])
    if blocks is None:
        sums = jnp.sum(received2.reshape(chain, groups, cases, -1)[..., :wide].astype(F32), axis=0)
        flat = jnp.moveaxis(sums, 0, 1).reshape(cases, along)
        own = lax.dynamic_index_in_dim(sums, lax.axis_index("coarse"), 0, keepdims=False)
        values = jnp.dot(flat, kernel.astype(F32).T, precision=lax.Precision.HIGHEST)
        energy = jnp.dot(values, own[:, :column].T, precision=lax.Precision.HIGHEST)
        blocks = [lax.psum(energy, "coarse")]
    multipliers, residual = call(
        functools.partial(scene_kernel, groups=groups, pieces=len(blocks)),
        [((subs, scenes, face), F32), ((subs, scenes, face), F32)],
        [displaced2, before, received2, kernel, lifts, pull0, pull1, face_order, norms0]
        + [scene_loads.T, scene_weights.T, *blocks],
        [pltpu.VMEM((groups, cases, wide), F32)],
        flops=10**9,
        moved=4 * 10**6,
    )
    return (multipliers, residual)


def solution(mesh):
    return jax.shard_map(
        per_device,
        mesh=mesh,
        in_specs=(
            P(("sub", "coarse"), None, None),
            P(("sub", "coarse"), None, None),
            P(None, "coarse", None, "sub"),
            P(("sub", "coarse"), None, None),
            P(("sub", "coarse"), None),
            P(("sub", "coarse"), None),
            P(),
            P(),
        ),
        out_specs=(P(("sub", "coarse"), None, None), P(("sub", "coarse"), None, None)),
        check_vma=False,
    )
```

```python
import functools

import jax
import jax.numpy as jnp
import numpy as np
from jax import lax
from jax.experimental import pallas as pl
from jax.experimental.pallas import tpu as pltpu
from jax.sharding import PartitionSpec as P

LANES = 128
CHUNK = 256
F32, BF16 = jnp.float32, jnp.bfloat16


def nn(a, b):
    return lax.dot_general(a, b, (((1,), (0,)), ((), ())), preferred_element_type=F32)


def nt(a, b):
    return lax.dot_general(a, b, (((1,), (1,)), ((), ())), preferred_element_type=F32)


def halves(x):
    high = x.astype(BF16)
    return high, (x - high.astype(F32)).astype(BF16)


def stacked(x):
    return jnp.concatenate(halves(x), axis=0)


def folded(x):
    rows = x.shape[0] // 2
    return x[:rows] + x[rows:]


def nn2(x, narrow):
    return folded(nn(stacked(x), narrow))


def nt2(x, narrow):
    return folded(nt(stacked(x), narrow))


def both3(product, x, y):
    high, low = halves(y)
    return folded(product(stacked(x), high)) + product(x.astype(BF16), low)


def equal(a, b):
    return jnp.where(a == b, 1.0, 0.0).astype(BF16)


def iota(shape, dim):
    return lax.broadcasted_iota(jnp.int32, shape, dim)


def rounded_up(value, unit):
    return (value + unit - 1) // unit * unit


def table(order_row):
    size = order_row.shape[1]
    return equal(iota((size, size), 0), order_row)


def spread_of(dofs_row, chain, corners, groups):
    column = chain * corners
    ids = iota((column, 1), 0)
    slot = sum((ids >= t * corners).astype(jnp.int32) for t in range(1, chain))
    target = ids + slot * ((groups - 1) * corners) + lax.axis_index("coarse") * corners
    return equal(target, dofs_row)


def placed(x, width, at):
    rows = x.shape[1]
    return nn(x, equal(iota((rows, width), 0) + at, iota((rows, width), 1)))


def picked(x, at, count):
    width = x.shape[1]
    lane = iota((width, count), 0) - at
    column = iota((width, count), 1)
    hit = jnp.where(lane == column, 1.0, 0.0) + jnp.where(lane == column + count, 1.0, 0.0)
    return nn2(x, hit.astype(BF16))


def by_parity(to_after, to_before):
    odd = (lax.axis_index("sub") & 1) == 1
    return jnp.where(odd, to_before, to_after), jnp.where(odd, to_after, to_before)


def start_fetch(matrix, held, sems):
    subs, size = matrix.shape[0], matrix.shape[1]
    copies = []
    for n in range(subs):
        for k in range(size // CHUNK):
            part = pl.ds(k * CHUNK, CHUNK)
            copy = pltpu.make_async_copy(
                matrix.at[n, part], held.at[n, part], sems.at[n * (size // CHUNK) + k]
            )
            copy.start()
            copies.append(copy)
    return copies


def times_matrix(x, n, held, copies):
    size = held.shape[1]
    count = size // CHUNK
    total = None
    for k in range(count):
        copies[n * count + k].wait()
        part = nn(x[:, k * CHUNK : (k + 1) * CHUNK], held[n, k * CHUNK : (k + 1) * CHUNK])
        total = part if total is None else total + part
    return total


def jumped(displaced, order, from_before, from_after, left_only=False):
    subs = len(displaced)
    face = order.shape[1]
    at_head = lax.axis_index("sub") == 0
    at_tail = lax.axis_index("sub") == lax.axis_size("sub") - 1
    result = []
    for n in range(subs):
        own = table(order[n : n + 1])
        before = nn(from_before, own) if n == 0 else nn2(displaced[n - 1][:, face:], own)
        left = displaced[n][:, :face] - before
        if n == 0:
            left = jnp.where(at_head, 0.0, left)
        if left_only:
            result.append(left)
            continue
        if n == subs - 1:
            right = displaced[n][:, face:] - from_after
            right = jnp.where(at_tail, 0.0, right)
        else:
            following = table(order[n + 1 : n + 2])
            right = displaced[n][:, face:] - nt2(displaced[n + 1][:, :face], following)
        result.append(jnp.concatenate([left, right], axis=1))
    return result


def chain_sums(received, groups, width):
    chain = received.shape[0] // groups
    sums = []
    for c in range(groups):
        total = None
        for z in range(chain):
            part = received[z * groups + c, :, :width].astype(F32)
            total = part if total is None else total + part
        sums.append(total)
    return sums


def copies_of(out, x):
    for i in range(out.shape[0]):
        out[i] = x


def fetched(pairs, sems):
    copies = [pltpu.make_async_copy(a, b, sems.at[i]) for i, (a, b) in enumerate(pairs)]
    for copy in copies:
        copy.start()
    return copies


def corner_kernel(loads_far, coupling_far, dofs_far, out, loads, coupling, dofs, sems, *, chain, groups):
    pairs = [(dofs_far, dofs), (coupling_far, coupling), (loads_far, loads)]
    for copy in fetched(pairs, sems):
        copy.wait()
    corners = coupling.shape[1]
    total = None
    for n in range(loads.shape[0]):
        terms = nt(loads[n], coupling[n])
        part = nt2(terms, spread_of(dofs[n : n + 1], chain, corners, groups))
        total = part if total is None else total + part
    copies_of(out, placed(total.astype(BF16), out.shape[2], 0).astype(BF16))


def first_kernel(
    matrix, loads_far, order_far, coupling_far, dofs_far, shard_far, *refs, chain, groups
):
    shards = refs[: chain - 1]
    regroup, out, first, second, kernel, held, sems = refs[chain - 1 : chain + 6]
    loads, order, coupling, dofs, shard, small = refs[chain + 6 :]
    pairs = [(loads_far, loads), (dofs_far, dofs), (order_far, order), (shard_far, shard)]
    small_copies = fetched(pairs + [(coupling_far, coupling)], small)
    copies = start_fetch(matrix, held, sems)
    for copy in small_copies:
        copy.wait()
    subs, cases, iface = loads.shape
    corners, face = coupling.shape[1], order.shape[1]
    pad = rounded_up(corners, 16) - corners
    near = table(order[0:1])
    position = lax.axis_index("sub")
    depth = groups * corners
    rows = None
    for j, block in enumerate([shard, *shards]):
        ids = iota((depth, regroup.shape[1]), 0) + (position ^ j) * depth
        part = nn(block[...], equal(ids, regroup[...]))
        rows = part if rows is None else rows + part
    kernel[...] = rows.astype(BF16)

    def packet(displaced, coupled, n):
        spread = spread_of(dofs[n : n + 1], chain, corners, groups)
        eye = equal(iota((corners, corners), 0), iota((corners, corners), 1))
        hot = placed(nt(eye, spread).astype(BF16), first.shape[1] - face, 0)
        lower = jnp.concatenate([coupled, hot], axis=1)
        upper = jnp.concatenate([displaced, jnp.zeros((cases, hot.shape[1]), F32)], axis=1)
        return jnp.concatenate([upper, lower, jnp.zeros((pad, lower.shape[1]), F32)], axis=0)

    for n in range(subs):
        out[n] = times_matrix(loads[n], n, held, copies)
    last = subs - 1
    to_after = packet(out[last, :, face:], coupling[last, :, face:].astype(F32), last)
    to_before = packet(
        nt(out[0, :, :face].astype(BF16), near), nt(coupling[0, :, :face], near), 0
    )
    one, two = by_parity(to_after, to_before)
    first[...] = one.astype(BF16)
    second[...] = two.astype(BF16)


def lift_kernel(
    displaced, first, second, received, kernel, other, coupling, dofs, order,
    lifts, pull, out, *joined, chain, groups
):
    subs, cases, _ = displaced.shape
    corners, face = coupling.shape[1], order.shape[1]
    column = chain * corners
    wide = rounded_up(column, LANES)
    position = lax.axis_index("sub")
    join(joined, kernel, other)

    from_after, from_before = by_parity(first[...].astype(F32), second[...].astype(F32))
    eye = equal(iota((column, first.shape[1] - face), 0), iota((column, first.shape[1] - face), 1))

    def neighbour(block):
        low = block[cases:].astype(BF16)
        return low[:, :face], nt(eye, low[:, face:]).astype(BF16)

    before_coupling, before_spread = neighbour(from_before)
    after_coupling, after_spread = neighbour(from_after)
    spreads = [spread_of(dofs[n : n + 1], chain, corners, groups) for n in range(subs)]
    at_head, at_tail = position == 0, position == chain - 1
    lifted = []
    for n in range(subs):
        own = table(order[n : n + 1])
        if n == 0:
            moved = nn(before_spread, nn(before_coupling, own).astype(BF16))
        else:
            moved = nn(spreads[n - 1], nn(coupling[n - 1, :, face:], own).astype(BF16))
        left = nn(spreads[n], coupling[n, :, :face]) - moved
        if n == 0:
            left = jnp.where(at_head, 0.0, left)
        if n == subs - 1:
            back = nn(after_spread, after_coupling)
        else:
            following = table(order[n + 1 : n + 2])
            back = nn(spreads[n + 1], nt(coupling[n + 1, :, :face], following).astype(BF16))
        right = nn(spreads[n], coupling[n, :, face:]) - back
        if n == subs - 1:
            right = jnp.where(at_tail, 0.0, right)
        lifted.append(jnp.concatenate([left, right], axis=1).astype(BF16))
        lifts[n] = lifted[n]

    flat = jnp.concatenate(chain_sums(received, groups, wide), axis=1)
    values = nt2(flat, kernel[...])
    bent = jumped(
        [displaced[n] for n in range(subs)],
        order,
        from_before[:cases, :face].astype(BF16),
        from_after[:cases, :face],
    )
    corner, norms = None, None
    for n in range(subs):
        whole = bent[n] + nn2(values, lifted[n])
        pull[n] = whole
        left = whole[:, :face]
        part, norm = nt2(left, lifted[n][:, :face]), both3(nt, left, left)
        corner = part if corner is None else corner + part
        norms = norm if norms is None else norms + norm
    copies_of(out, packed(out.shape[2], corner, norms))


def join(out, low, high):
    for ref in out:
        ref[: low.shape[0]] = low[...]
        ref[low.shape[0] :] = high[...]


def packed(width, corner, *grams):
    total = placed(corner.astype(BF16), width, 0)
    at = corner.shape[1]
    for gram in grams:
        for half in halves(gram):
            total = total + placed(half, width, at)
            at += gram.shape[1]
    return total.astype(BF16)


def second_kernel(matrix, pull, order, out, first, second, held, sems):
    copies = start_fetch(matrix, held, sems)
    subs = pull.shape[0]
    face = order.shape[1]
    near = table(order[0:1])
    for n in range(subs):
        out[n] = folded(times_matrix(stacked(pull[n]), n, held, copies))
    one, two = by_parity(out[subs - 1, :, face:], nt2(out[0, :, :face], near))
    first[...] = one.astype(BF16)
    second[...] = two.astype(BF16)


def third_kernel(
    matrix, displaced, first, second, received, kernel, lifts, pull0, order, low, high, *refs, groups
):
    pull, out, after, payload, norms0, *joined, held, sems = refs
    copies = start_fetch(matrix, held, sems)
    join(joined, low, high)
    subs, cases, _ = displaced.shape
    face = order.shape[1]
    column = lifts.shape[1]
    wide = rounded_up(column, LANES)
    from_after, from_before = by_parity(first[...].astype(F32), second[...].astype(F32))
    sums = chain_sums(received, groups, received.shape[2])
    flat = jnp.concatenate([part[:, :wide] for part in sums], axis=1)
    values = nt2(flat, kernel[...])
    norms0[...] = picked(sum(sums), column, cases)
    bent = jumped(
        [displaced[n] for n in range(subs)], order, from_before.astype(BF16), from_after
    )
    totals = None
    for n in range(subs):
        whole = bent[n] + nn2(values, lifts[n])
        pull[n] = whole
        left = whole[:, :face]
        moved = folded(times_matrix(stacked(whole), n, held, copies))
        out[n] = moved
        parts = [
            nt2(left, lifts[n, :, :face]),
            both3(nt, pull0[n, :, :face], left),
            both3(nt, left, left),
            both3(nt, whole, moved),
        ]
        totals = parts if totals is None else [a + b for a, b in zip(totals, parts)]
    after[...] = out[subs - 1, :, face:].astype(BF16)
    copies_of(payload, packed(payload.shape[2], *totals))


def scene_kernel(
    displaced, first, second, received, kernel, lifts, pull0, pull1, order, norms0,
    scene_loads, scene_weights, *refs, groups, pieces, slots
):
    blocks = refs[:pieces]
    multipliers, residual, held = refs[pieces:]
    subs, cases, _ = displaced.shape
    face = order.shape[1]
    column = lifts.shape[1]
    wide = rounded_up(column, LANES)
    group = lax.axis_index("coarse")
    sums = chain_sums(received, groups, received.shape[2])
    for c in range(groups):
        held[c] = sums[c][:, :wide]
    flat = jnp.concatenate([part[:, :wide] for part in sums], axis=1)
    values = nt2(flat, kernel[...])
    if groups_whole(blocks, column, groups):
        energy, index = None, iter(slots)
        for block in blocks:
            for i in range(block.shape[0] // column):
                lifted = nt2(flat, block[i * column : (i + 1) * column])
                part = both3(nt, lifted, held[group ^ next(index)][:, :column])
                energy = part if energy is None else energy + part
    else:
        energy = blocks[0][...]
    total = sum(sums)
    norms1 = picked(total, column, cases)
    norms2 = picked(total, column + 2 * cases, cases)
    norms3 = picked(total, column + 4 * cases, cases) + energy

    ids = iota((cases, scene_loads.shape[1]), 0)
    mixing = sum(
        jnp.where(ids == scene_loads[i : i + 1], scene_weights[i : i + 1], 0.0)
        for i in range(scene_loads.shape[0])
    )

    def moment(norms):
        return jnp.sum(both3(nn, norms, mixing) * mixing, axis=0, keepdims=True)

    moment0, moment1 = moment(norms0[...]), moment(norms1)
    moment2, moment3 = moment(norms2), moment(norms3)
    step0 = moment0 / moment1
    norm1 = moment0 - 2.0 * step0 * moment1 + step0 * step0 * moment2
    grow = 1.0 + norm1 / moment0
    curvature = grow * grow * moment1 - 2.0 * grow * step0 * moment2 + step0 * step0 * moment3
    step1 = norm1 / curvature
    zeros = jnp.zeros_like(mixing)

    def transposed(parts):
        weights = -jnp.concatenate(parts, axis=0)
        high = weights.astype(BF16).astype(F32)
        return jnp.concatenate([high, high, weights - high], axis=0).T.astype(BF16)

    for_multipliers = transposed(
        [(step0 + step1 * grow) * mixing, (-step0 * step1) * mixing, zeros]
    )
    for_residual = transposed(
        [mixing, (-step0 - step1 * grow) * mixing, (step0 * step1) * mixing]
    )
    _, from_before = by_parity(first[...].astype(F32), second[...].astype(F32))
    bent = jumped([displaced[n] for n in range(subs)], order, from_before.astype(BF16), None, True)
    for n in range(subs):
        pull2 = bent[n] + nn2(values, lifts[n, :, :face])
        basis = jnp.concatenate([pull0[n, :, :face], pull1[n, :, :face], pull2], axis=0)
        high, low = halves(basis)
        basis = jnp.concatenate([high, low, high], axis=0)
        multipliers[n] = nn(for_multipliers, basis)
        residual[n] = nn(for_residual, basis)


def groups_whole(blocks, column, groups):
    return sum(block.shape[0] for block in blocks) == column * groups


def everywhere(x, axes):
    return lax.all_to_all(x, axes, 0, 0)


def swapped(x, axis, bit):
    return lax.ppermute(x, axis, [(i, i ^ bit) for i in range(lax.axis_size(axis))])


def pair_swaps(first, second):
    length = lax.axis_size("sub")
    one = lax.ppermute(first, "sub", [(i, i ^ 1) for i in range(length) if i ^ 1 < length])
    two = lax.ppermute(
        second,
        "sub",
        [(i, j) for i in range(length) for j in [i + 1 if i & 1 else i - 1] if 0 <= j < length],
    )
    return one, two


def call(kernel, outs, args, scratch=(), flops=0, moved=0, limit=32, in_place=()):
    specs = [
        pl.BlockSpec(memory_space=pltpu.HBM if i in in_place else pltpu.VMEM)
        for i in range(len(args))
    ]
    return pl.pallas_call(
        kernel,
        out_shape=[jax.ShapeDtypeStruct(shape, kind) for shape, kind in outs],
        in_specs=specs,
        out_specs=[pl.BlockSpec(memory_space=pltpu.VMEM)] * len(outs),
        scratch_shapes=list(scratch),
        compiler_params=pltpu.CompilerParams(vmem_limit_bytes=limit << 20),
        cost_estimate=pl.CostEstimate(flops=flops, bytes_accessed=moved, transcendentals=0),
    )(*args)


def per_device(
    schur_inverse,
    corner_coupling,
    coarse_inverse,
    load_cases,
    face_order,
    corner_dofs,
    scene_loads,
    scene_weights,
):
    subs, iface = schur_inverse.shape[0], schur_inverse.shape[1]
    face = face_order.shape[1]
    corners = corner_dofs.shape[1]
    cases = load_cases.shape[1]
    scenes = scene_loads.shape[0]
    chain, groups = lax.axis_size("sub"), lax.axis_size("coarse")
    devices = chain * groups
    column = chain * corners
    wide = rounded_up(column, LANES)
    along = groups * wide
    work = dict(flops=4 * cases * schur_inverse.size, moved=2 * schur_inverse.size)
    fetch = [
        pltpu.VMEM(schur_inverse.shape, BF16),
        pltpu.SemaphoreType.DMA((subs * (iface // CHUNK),)),
    ]

    shard = coarse_inverse.reshape(column, groups * corners)
    shards = [swapped(shard, "sub", j) for j in range(1, chain)]

    lane = np.arange(along)
    inner = lane % wide
    source = (inner // corners * groups + lane // wide) * corners + inner % corners
    regroup = jnp.asarray(np.where(inner < column, source, -1)[None].astype(np.int32))

    bits = []
    if groups == 1 << 3 and (column * groups) ** 2 <= schur_inverse.size:
        bits = [1 << b for b in reversed(range(groups.bit_length() - 1))]

    small = [
        pltpu.VMEM(x.shape, x.dtype)
        for x in (load_cases, face_order, corner_coupling, corner_dofs, shard)
    ]
    (sent0,) = call(
        functools.partial(corner_kernel, chain=chain, groups=groups),
        [((devices, cases, wide), BF16)],
        [load_cases, corner_coupling, corner_dofs],
        [small[0], small[2], small[3], pltpu.SemaphoreType.DMA((3,))],
        in_place=(0, 1, 2),
    )
    received0 = everywhere(sent0, ("sub", "coarse"))
    packet = (cases + rounded_up(corners, 16), face + wide)
    displaced0, first, second, kernel = call(
        functools.partial(first_kernel, chain=chain, groups=groups),
        [((subs, cases, iface), F32), (packet, BF16), (packet, BF16), ((column, along), BF16)],
        [schur_inverse, load_cases, face_order, corner_coupling, corner_dofs, shard]
        + [*shards, regroup],
        [*fetch, *small, pltpu.SemaphoreType.DMA((5,))],
        in_place=range(6),
        **work,
    )
    first, second = pair_swaps(first, second)
    other = swapped(kernel, "coarse", bits[0]) if bits else kernel
    lifts, pull0, sent1, *joined = call(
        functools.partial(lift_kernel, chain=chain, groups=groups),
        [
            ((subs, column, iface), BF16),
            ((subs, cases, iface), F32),
            ((devices, cases, rounded_up(column + 2 * cases, LANES)), BF16),
        ]
        + [((2 * column, along), BF16)] * bool(bits),
        [displaced0, first, second, received0, kernel, other]
        + [corner_coupling, corner_dofs, face_order],
        flops=10**9,
        moved=10**6,
    )
    received1 = everywhere(sent1, ("sub", "coarse"))
    displaced1, first, second = call(
        second_kernel,
        [((subs, cases, iface), F32), ((cases, face), BF16), ((cases, face), BF16)],
        [schur_inverse, pull0, face_order],
        fetch,
        in_place=(0,),
        **work,
    )
    first, second = pair_swaps(first, second)

    low = joined[0] if bits else kernel
    high = swapped(low, "coarse", bits[1]) if bits else kernel
    pull1, displaced2, after, sent2, norms0, *joined = call(
        functools.partial(third_kernel, groups=groups),
        [
            ((subs, cases, iface), F32),
            ((subs, cases, iface), F32),
            ((cases, face), BF16),
            ((devices, cases, rounded_up(column + 6 * cases, LANES)), BF16),
            ((cases, cases), F32),
        ]
        + [((4 * column, along), BF16)] * bool(bits),
        [schur_inverse, displaced1, first, second, received1, kernel, lifts, pull0, face_order]
        + [low, high],
        fetch,
        in_place=(0,),
        **work,
    )
    received2 = everywhere(sent2, ("sub", "coarse"))
    first, second = pair_swaps(after, after)
    if bits:
        blocks = [joined[0], swapped(joined[0], "coarse", bits[2])]
        slots = [0, bits[0], bits[1], bits[0] ^ bits[1]]
        slots = slots + [slot ^ bits[2] for slot in slots]
    else:
        slots = []
        sums = jnp.sum(received2.reshape(chain, groups, cases, -1)[..., :wide].astype(F32), axis=0)
        flat = jnp.moveaxis(sums, 0, 1).reshape(cases, along)
        own = lax.dynamic_index_in_dim(sums, lax.axis_index("coarse"), 0, keepdims=False)
        values = jnp.dot(flat, kernel.astype(F32).T, precision=lax.Precision.HIGHEST)
        energy = jnp.dot(values, own[:, :column].T, precision=lax.Precision.HIGHEST)
        blocks = [lax.psum(energy, "coarse")]
    multipliers, residual = call(
        functools.partial(scene_kernel, groups=groups, pieces=len(blocks), slots=slots),
        [((subs, scenes, face), F32), ((subs, scenes, face), F32)],
        [displaced2, first, second, received2, kernel, lifts, pull0, pull1, face_order, norms0]
        + [scene_loads.T, scene_weights.T, *blocks],
        [pltpu.VMEM((groups, cases, wide), F32)],
        flops=10**9,
        moved=4 * 10**6,
    )
    return (multipliers, residual)


def solution(mesh):
    return jax.shard_map(
        per_device,
        mesh=mesh,
        in_specs=(
            P(("sub", "coarse"), None, None),
            P(("sub", "coarse"), None, None),
            P(None, "coarse", None, "sub"),
            P(("sub", "coarse"), None, None),
            P(("sub", "coarse"), None),
            P(("sub", "coarse"), None),
            P(),
            P(),
        ),
        out_specs=(P(("sub", "coarse"), None, None), P(("sub", "coarse"), None, None)),
        check_vma=False,
    )
```

```python
import functools

import jax
import jax.numpy as jnp
import numpy as np
from jax import lax
from jax.experimental import pallas as pl
from jax.experimental.pallas import tpu as pltpu
from jax.sharding import PartitionSpec as P

LANES = 128
CHUNK = 256
ALL_VMEM = 56 << 20
MOST_VMEM = 46 << 20
SOME_VMEM = 32 << 20
F32, BF16 = jnp.float32, jnp.bfloat16


def nn(a, b):
    return lax.dot_general(a, b, (((1,), (0,)), ((), ())), preferred_element_type=F32)


def nt(a, b):
    return lax.dot_general(a, b, (((1,), (1,)), ((), ())), preferred_element_type=F32)


def halves(x):
    high = x.astype(BF16)
    return high, (x - high.astype(F32)).astype(BF16)


def stacked(x):
    return jnp.concatenate(halves(x), axis=0)


def folded(x):
    rows = x.shape[0] // 2
    return x[:rows] + x[rows:]


def nn2(x, narrow):
    return folded(nn(stacked(x), narrow))


def nt2(x, narrow):
    return folded(nt(stacked(x), narrow))


def both3(product, x, y):
    high, low = halves(y)
    return folded(product(stacked(x), high)) + product(x.astype(BF16), low)


def equal(a, b):
    return jnp.where(a == b, 1.0, 0.0).astype(BF16)


def iota(shape, dim):
    return lax.broadcasted_iota(jnp.int32, shape, dim)


def rounded_up(value, unit):
    return (value + unit - 1) // unit * unit


def table(order_row):
    size = order_row.shape[1]
    return equal(iota((size, size), 0), order_row)


def spread_of(dofs_row, chain, corners, groups):
    column = chain * corners
    ids = iota((column, 1), 0)
    slot = sum((ids >= t * corners).astype(jnp.int32) for t in range(1, chain))
    target = ids + slot * ((groups - 1) * corners) + lax.axis_index("coarse") * corners
    return equal(target, dofs_row)


def placed(x, width, at):
    rows = x.shape[1]
    return nn(x, equal(iota((rows, width), 0) + at, iota((rows, width), 1)))


def picked(x, at, count):
    width = x.shape[1]
    return nn2(x, equal(iota((width, count), 0) - at, iota((width, count), 1)))


def by_parity(to_after, to_before):
    odd = (lax.axis_index("sub") & 1) == 1
    return jnp.where(odd, to_before, to_after), jnp.where(odd, to_after, to_before)


def start_fetch(matrix, held, sems):
    subs, size = matrix.shape[0], matrix.shape[1]
    copies = []
    for n in range(subs):
        for k in range(size // CHUNK):
            part = pl.ds(k * CHUNK, CHUNK)
            copy = pltpu.make_async_copy(
                matrix.at[n, part], held.at[n, part], sems.at[n * (size // CHUNK) + k]
            )
            copy.start()
            copies.append(copy)
    return copies


def times_matrix(x, n, held, copies):
    size = held.shape[1]
    count = size // CHUNK
    total = None
    for k in range(count):
        copies[n * count + k].wait()
        part = nn(x[:, k * CHUNK : (k + 1) * CHUNK], held[n, k * CHUNK : (k + 1) * CHUNK])
        total = part if total is None else total + part
    return total


def jumped(displaced, tables, from_before, from_after, left_only=False):
    subs = len(displaced)
    face = tables.shape[1]
    at_head = lax.axis_index("sub") == 0
    at_tail = lax.axis_index("sub") == lax.axis_size("sub") - 1
    result = []
    for n in range(subs):
        own = tables[n]
        before = nn(from_before, own) if n == 0 else nn2(displaced[n - 1][:, face:], own)
        left = displaced[n][:, :face] - before
        if n == 0:
            left = jnp.where(at_head, 0.0, left)
        if left_only:
            result.append(left)
            continue
        if n == subs - 1:
            right = displaced[n][:, face:] - from_after
            right = jnp.where(at_tail, 0.0, right)
        else:
            right = displaced[n][:, face:] - nt2(displaced[n + 1][:, :face], tables[n + 1])
        result.append(jnp.concatenate([left, right], axis=1))
    return result


def chain_sums(received, groups, width):
    chain = received.shape[0] // groups
    sums = []
    for c in range(groups):
        total = None
        for z in range(chain):
            part = received[z * groups + c, :, :width].astype(F32)
            total = part if total is None else total + part
        sums.append(total)
    return sums


def copies_of(out, x):
    for i in range(out.shape[0]):
        out[i] = x


def fetched(pairs, sems):
    copies = [pltpu.make_async_copy(a, b, sems.at[i]) for i, (a, b) in enumerate(pairs)]
    for copy in copies:
        copy.start()
    return copies


def corner_kernel(loads_far, coupling_far, dofs_far, out, loads, coupling, dofs, sems, *, chain, groups):
    pairs = [(dofs_far, dofs), (coupling_far, coupling), (loads_far, loads)]
    for copy in fetched(pairs, sems):
        copy.wait()
    corners = coupling.shape[1]
    total = None
    for n in range(loads.shape[0]):
        terms = nt(loads[n], coupling[n])
        part = nt2(terms, spread_of(dofs[n : n + 1], chain, corners, groups))
        total = part if total is None else total + part
    copies_of(out, placed(total.astype(BF16), out.shape[2], 0).astype(BF16))


def first_kernel(matrix, *refs, chain, groups):
    far, (out, first, second, kernel, held, sems) = refs[:6], refs[6:12]
    near_refs, small = refs[12:-1], refs[-1]
    small_copies = fetched(list(zip(far, near_refs)), small)
    copies = start_fetch(matrix, held, sems)
    for copy in small_copies:
        copy.wait()
    loads, order, coupling, dofs, regroup, shards = near_refs
    subs, cases, iface = loads.shape
    corners, face = coupling.shape[1], order.shape[1]
    pad = rounded_up(corners, 16) - corners
    near = table(order[0:1])
    position = lax.axis_index("sub")
    depth = groups * corners
    rows = None
    for j in range(chain):
        ids = iota((depth, regroup.shape[1]), 0) + (position ^ j) * depth
        part = nn(shards[j], equal(ids, regroup[...]))
        rows = part if rows is None else rows + part
    kernel[...] = rows.astype(BF16)

    def packet(displaced, coupled, n):
        spread = spread_of(dofs[n : n + 1], chain, corners, groups)
        eye = equal(iota((corners, corners), 0), iota((corners, corners), 1))
        hot = placed(nt(eye, spread).astype(BF16), first.shape[1] - face, 0)
        lower = jnp.concatenate([coupled, hot], axis=1)
        upper = jnp.concatenate([displaced, jnp.zeros((cases, hot.shape[1]), F32)], axis=1)
        return jnp.concatenate([upper, lower, jnp.zeros((pad, lower.shape[1]), F32)], axis=0)

    for n in range(subs):
        out[n] = times_matrix(loads[n], n, held, copies)
    last = subs - 1
    to_after = packet(out[last, :, face:], coupling[last, :, face:].astype(F32), last)
    to_before = packet(
        nt(out[0, :, :face].astype(BF16), near), nt(coupling[0, :, :face], near), 0
    )
    one, two = by_parity(to_after, to_before)
    first[...] = one.astype(BF16)
    second[...] = two.astype(BF16)


def lift_kernel(
    displaced, first, second, received, kernel, other, coupling, dofs, order,
    lifts, pull, out, tables, *joined, chain, groups
):
    subs, cases, _ = displaced.shape
    for n in range(subs):
        tables[n] = table(order[n : n + 1])
    corners, face = coupling.shape[1], order.shape[1]
    column = chain * corners
    wide = rounded_up(column, LANES)
    position = lax.axis_index("sub")
    join(joined, kernel, other)

    from_after, from_before = by_parity(first[...].astype(F32), second[...].astype(F32))
    eye = equal(iota((column, first.shape[1] - face), 0), iota((column, first.shape[1] - face), 1))

    def neighbour(block):
        low = block[cases:].astype(BF16)
        return low[:, :face], nt(eye, low[:, face:]).astype(BF16)

    before_coupling, before_spread = neighbour(from_before)
    after_coupling, after_spread = neighbour(from_after)
    spreads = [spread_of(dofs[n : n + 1], chain, corners, groups) for n in range(subs)]
    at_head, at_tail = position == 0, position == chain - 1
    lifted = []
    for n in range(subs):
        own = tables[n]
        if n == 0:
            moved = nn(before_spread, nn(before_coupling, own).astype(BF16))
        else:
            moved = nn(spreads[n - 1], nn(coupling[n - 1, :, face:], own).astype(BF16))
        left = nn(spreads[n], coupling[n, :, :face]) - moved
        if n == 0:
            left = jnp.where(at_head, 0.0, left)
        if n == subs - 1:
            back = nn(after_spread, after_coupling)
        else:
            back = nn(
                spreads[n + 1], nt(coupling[n + 1, :, :face], tables[n + 1]).astype(BF16)
            )
        right = nn(spreads[n], coupling[n, :, face:]) - back
        if n == subs - 1:
            right = jnp.where(at_tail, 0.0, right)
        lifted.append(jnp.concatenate([left, right], axis=1).astype(BF16))
        lifts[n] = lifted[n]

    flat = jnp.concatenate(chain_sums(received, groups, wide), axis=1)
    values = nt2(flat, kernel[...])
    bent = jumped(
        [displaced[n] for n in range(subs)],
        tables,
        from_before[:cases, :face].astype(BF16),
        from_after[:cases, :face],
    )
    corner, norms = None, None
    for n in range(subs):
        whole = bent[n] + nn2(values, lifted[n])
        pull[n] = whole
        left = whole[:, :face]
        part, norm = nt2(left, lifted[n][:, :face]), both3(nt, left, left)
        corner = part if corner is None else corner + part
        norms = norm if norms is None else norms + norm
    copies_of(out, packed(out.shape[2], corner, norms))


def join(out, low, high):
    for ref in out:
        ref[: low.shape[0]] = low[...]
        ref[low.shape[0] :] = high[...]


def packed(width, corner, *grams):
    total = placed(corner.astype(BF16), width, 0)
    at = corner.shape[1]
    for gram in grams:
        for half in halves(gram):
            total = total + placed(half, width, at)
            at += gram.shape[1]
    return total.astype(BF16)


def second_kernel(matrix, pull, tables, out, first, second, held, sems):
    copies = start_fetch(matrix, held, sems)
    subs = pull.shape[0]
    face = tables.shape[1]
    for n in range(subs):
        out[n] = folded(times_matrix(stacked(pull[n]), n, held, copies))
    one, two = by_parity(out[subs - 1, :, face:], nt2(out[0, :, :face], tables[0]))
    first[...] = one.astype(BF16)
    second[...] = two.astype(BF16)


def third_kernel(
    matrix, displaced, first, second, received, kernel, lifts, pull0, tables, low, high, *refs, groups
):
    pull, out, after, payload, norms0, *joined, held, sems = refs
    copies = start_fetch(matrix, held, sems)
    join(joined, low, high)
    subs, cases, _ = displaced.shape
    face = tables.shape[1]
    column = lifts.shape[1]
    wide = rounded_up(column, LANES)
    from_after, from_before = by_parity(first[...].astype(F32), second[...].astype(F32))
    sums = chain_sums(received, groups, received.shape[2])
    flat = jnp.concatenate([part[:, :wide] for part in sums], axis=1)
    values = nt2(flat, kernel[...])
    whole = sum(sums)
    norms0[...] = picked(whole, column, cases) + picked(whole, column + cases, cases)
    bent = jumped(
        [displaced[n] for n in range(subs)], tables, from_before.astype(BF16), from_after
    )
    totals = None
    for n in range(subs):
        whole = bent[n] + nn2(values, lifts[n])
        pull[n] = whole
        left = whole[:, :face]
        moved = folded(times_matrix(stacked(whole), n, held, copies))
        out[n] = moved
        parts = [
            nt2(left, lifts[n, :, :face]),
            both3(nt, pull0[n, :, :face], left),
            both3(nt, left, left),
            both3(nt, whole, moved),
        ]
        totals = parts if totals is None else [a + b for a, b in zip(totals, parts)]
    after[...] = out[subs - 1, :, face:].astype(BF16)
    width, at = payload.shape[1], 0
    row = None
    for part in totals:
        for half in halves(part):
            moved = placed(half, width, at)
            row = moved if row is None else row + moved
        at += part.shape[1]
    payload[...] = row


def scene_kernel(
    displaced, first, second, received, other, kernel, lifts, pull0, pull1, tables, norms0,
    scene_loads, scene_weights, *refs, groups, pieces, slots, where
):
    blocks = refs[:pieces]
    multipliers, residual, held = refs[pieces:]
    subs, cases, _ = displaced.shape
    face = tables.shape[1]
    column = lifts.shape[1]
    wide = rounded_up(column, LANES)
    group = lax.axis_index("coarse")
    total = None
    for ref, places in ((received, where), (other, [place ^ 1 for place in where])):
        for i, place in enumerate(places):
            part = ref[i]
            held[group ^ place] = part[:, :wide]
            total = part if total is None else total + part
    flat = jnp.concatenate([held[c] for c in range(groups)], axis=1)
    values = nt2(flat, kernel[...])
    if groups_whole(blocks, column, groups):
        energy, index = None, iter(slots)
        for block in blocks:
            for i in range(block.shape[0] // column):
                lifted = nt2(flat, block[i * column : (i + 1) * column])
                part = both3(nt, lifted, held[group ^ next(index)][:, :column])
                energy = part if energy is None else energy + part
    else:
        energy = blocks[0][...]
    norms1 = picked(total, column, cases)
    norms2 = picked(total, column + cases, cases)
    norms3 = picked(total, column + 2 * cases, cases) + energy

    ids = iota((cases, scene_loads.shape[1]), 0)
    mixing = sum(
        jnp.where(ids == scene_loads[i : i + 1], scene_weights[i : i + 1], 0.0)
        for i in range(scene_loads.shape[0])
    )

    def moment(norms):
        return jnp.sum(both3(nn, norms, mixing) * mixing, axis=0, keepdims=True)

    moment0, moment1 = moment(norms0[...]), moment(norms1)
    moment2, moment3 = moment(norms2), moment(norms3)
    step0 = moment0 / moment1
    norm1 = moment0 - 2.0 * step0 * moment1 + step0 * step0 * moment2
    grow = 1.0 + norm1 / moment0
    curvature = grow * grow * moment1 - 2.0 * grow * step0 * moment2 + step0 * step0 * moment3
    step1 = norm1 / curvature
    zeros = jnp.zeros_like(mixing)

    def transposed(parts):
        weights = -jnp.concatenate(parts, axis=0)
        high = weights.astype(BF16).astype(F32)
        return jnp.concatenate([high, high, weights - high], axis=0).T.astype(BF16)

    for_multipliers = transposed(
        [(step0 + step1 * grow) * mixing, (-step0 * step1) * mixing, zeros]
    )
    for_residual = transposed(
        [mixing, (-step0 - step1 * grow) * mixing, (step0 * step1) * mixing]
    )
    _, from_before = by_parity(first[...].astype(F32), second[...].astype(F32))
    bent = jumped([displaced[n] for n in range(subs)], tables, from_before.astype(BF16), None, True)
    for n in range(subs):
        pull2 = bent[n] + nn2(values, lifts[n, :, :face])
        basis = jnp.concatenate([pull0[n, :, :face], pull1[n, :, :face], pull2], axis=0)
        high, low = halves(basis)
        basis = jnp.concatenate([high, low, high], axis=0)
        multipliers[n] = nn(for_multipliers, basis)
        residual[n] = nn(for_residual, basis)


def groups_whole(blocks, column, groups):
    return sum(block.shape[0] for block in blocks) == column * groups


def everywhere(x, axes):
    return lax.all_to_all(x, axes, 0, 0)


def swapped(x, axis, bit):
    return lax.ppermute(x, axis, [(i, i ^ bit) for i in range(lax.axis_size(axis))])


def pair_swaps(first, second):
    length = lax.axis_size("sub")
    one = lax.ppermute(first, "sub", [(i, i ^ 1) for i in range(length) if i ^ 1 < length])
    two = lax.ppermute(
        second,
        "sub",
        [(i, j) for i in range(length) for j in [i + 1 if i & 1 else i - 1] if 0 <= j < length],
    )
    return one, two


def call(kernel, outs, args, scratch=(), flops=0, moved=0, limit=SOME_VMEM, in_place=()):
    specs = [
        pl.BlockSpec(memory_space=pltpu.HBM if i in in_place else pltpu.VMEM)
        for i in range(len(args))
    ]
    return pl.pallas_call(
        kernel,
        out_shape=[jax.ShapeDtypeStruct(shape, kind) for shape, kind in outs],
        in_specs=specs,
        out_specs=[pl.BlockSpec(memory_space=pltpu.VMEM)] * len(outs),
        scratch_shapes=list(scratch),
        compiler_params=pltpu.CompilerParams(vmem_limit_bytes=limit),
        cost_estimate=pl.CostEstimate(flops=flops, bytes_accessed=moved, transcendentals=0),
    )(*args)


def per_device(
    schur_inverse,
    corner_coupling,
    coarse_inverse,
    load_cases,
    face_order,
    corner_dofs,
    scene_loads,
    scene_weights,
):
    subs, iface = schur_inverse.shape[0], schur_inverse.shape[1]
    face = face_order.shape[1]
    corners = corner_dofs.shape[1]
    cases = load_cases.shape[1]
    scenes = scene_loads.shape[0]
    chain, groups = lax.axis_size("sub"), lax.axis_size("coarse")
    devices = chain * groups
    column = chain * corners
    wide = rounded_up(column, LANES)
    along = groups * wide
    work = dict(flops=4 * cases * schur_inverse.size, moved=2 * schur_inverse.size)
    fetch = [
        pltpu.VMEM(schur_inverse.shape, BF16),
        pltpu.SemaphoreType.DMA((subs * (iface // CHUNK),)),
    ]

    shard = coarse_inverse.reshape(column, groups * corners)
    shards = jnp.stack([shard] + [swapped(shard, "sub", j) for j in range(1, chain)])

    lane = np.arange(along)
    inner = lane % wide
    source = (inner // corners * groups + lane // wide) * corners + inner % corners
    regroup = jnp.asarray(np.where(inner < column, source, -1)[None].astype(np.int32))

    bits = []
    if groups == 1 << 3 and (column * groups) ** 2 <= schur_inverse.size:
        bits = [1 << b for b in reversed(range(groups.bit_length() - 1))]

    small = [load_cases, face_order, corner_coupling, corner_dofs, regroup, shards]
    near = [pltpu.VMEM(x.shape, x.dtype) for x in small]
    (sent0,) = call(
        functools.partial(corner_kernel, chain=chain, groups=groups),
        [((devices, cases, wide), BF16)],
        [load_cases, corner_coupling, corner_dofs],
        [near[0], near[2], near[3], pltpu.SemaphoreType.DMA((3,))],
        in_place=(0, 1, 2),
        limit=ALL_VMEM,
    )
    received0 = everywhere(sent0, ("sub", "coarse"))
    packet = (cases + rounded_up(corners, 16), face + wide)
    displaced0, first, second, kernel = call(
        functools.partial(first_kernel, chain=chain, groups=groups),
        [((subs, cases, iface), F32), (packet, BF16), (packet, BF16), ((column, along), BF16)],
        [schur_inverse, *small],
        [*fetch, *near, pltpu.SemaphoreType.DMA((len(small),))],
        in_place=range(1 + len(small)),
        limit=ALL_VMEM,
        **work,
    )
    first, second = pair_swaps(first, second)
    other = swapped(kernel, "coarse", bits[0]) if bits else kernel
    lifts, pull0, sent1, tables, *joined = call(
        functools.partial(lift_kernel, chain=chain, groups=groups),
        [
            ((subs, column, iface), BF16),
            ((subs, cases, iface), F32),
            ((devices, cases, rounded_up(column + 2 * cases, LANES)), BF16),
            ((subs, face, face), BF16),
        ]
        + [((2 * column, along), BF16)] * bool(bits),
        [displaced0, first, second, received0, kernel, other]
        + [corner_coupling, corner_dofs, face_order],
        flops=10**9,
        moved=10**6,
    )
    received1 = everywhere(sent1, ("sub", "coarse"))
    displaced1, first, second = call(
        second_kernel,
        [((subs, cases, iface), F32), ((cases, face), BF16), ((cases, face), BF16)],
        [schur_inverse, pull0, tables],
        fetch,
        in_place=(0,),
        limit=MOST_VMEM,
        **work,
    )
    first, second = pair_swaps(first, second)

    low = joined[0] if bits else kernel
    high = swapped(low, "coarse", bits[1]) if bits else kernel
    pull1, displaced2, after, sent2, norms0, *joined = call(
        functools.partial(third_kernel, groups=groups),
        [
            ((subs, cases, iface), F32),
            ((subs, cases, iface), F32),
            ((cases, face), BF16),
            ((cases, rounded_up(column + 3 * cases, LANES)), F32),
            ((cases, cases), F32),
        ]
        + [((4 * column, along), BF16)] * bool(bits),
        [schur_inverse, displaced1, first, second, received1, kernel, lifts, pull0, tables]
        + [low, high],
        fetch,
        in_place=(0,),
        limit=MOST_VMEM,
        **work,
    )
    first, second = pair_swaps(after, after)
    received2 = sum([swapped(sent2, "sub", j) for j in range(1, chain)], sent2)[None]
    where, step = [0], groups
    while step > 2:
        unit = max(step // 4, 2)
        moves = range(unit, step, unit)
        received2 = jnp.concatenate(
            [received2] + [swapped(received2, "coarse", j) for j in moves], axis=0
        )
        where = where + [place ^ j for j in moves for place in where]
        step = unit
    other2 = swapped(received2, "coarse", 1)
    if bits:
        blocks = [joined[0], swapped(joined[0], "coarse", bits[2])]
        slots = [0, bits[0], bits[1], bits[0] ^ bits[1]]
        slots = slots + [slot ^ bits[2] for slot in slots]
    else:
        slots = []
        index = lax.axis_index("coarse")
        places = np.array(where + [place ^ 1 for place in where])
        sums = jnp.zeros((groups, cases, wide), F32)
        sums = sums.at[index ^ places].set(jnp.concatenate([received2, other2])[..., :wide])
        flat = jnp.moveaxis(sums, 0, 1).reshape(cases, along)
        own = lax.dynamic_index_in_dim(sums, index, 0, keepdims=False)
        values = jnp.dot(flat, kernel.astype(F32).T, precision=lax.Precision.HIGHEST)
        energy = jnp.dot(values, own[:, :column].T, precision=lax.Precision.HIGHEST)
        blocks = [lax.psum(energy, "coarse")]
    multipliers, residual = call(
        functools.partial(scene_kernel, groups=groups, pieces=len(blocks), slots=slots, where=where),
        [((subs, scenes, face), F32), ((subs, scenes, face), F32)],
        [displaced2, first, second, received2, other2, kernel, lifts, pull0, pull1, tables, norms0]
        + [scene_loads.T, scene_weights.T, *blocks],
        [pltpu.VMEM((groups, cases, wide), F32)],
        flops=10**9,
        moved=4 * 10**6,
    )
    return (multipliers, residual)


def solution(mesh):
    return jax.shard_map(
        per_device,
        mesh=mesh,
        in_specs=(
            P(("sub", "coarse"), None, None),
            P(("sub", "coarse"), None, None),
            P(None, "coarse", None, "sub"),
            P(("sub", "coarse"), None, None),
            P(("sub", "coarse"), None),
            P(("sub", "coarse"), None),
            P(),
            P(),
        ),
        out_specs=(P(("sub", "coarse"), None, None), P(("sub", "coarse"), None, None)),
        check_vma=False,
    )
```

```python
import functools

import jax
import jax.numpy as jnp
import numpy as np
from jax import lax
from jax.experimental import pallas as pl
from jax.experimental.pallas import tpu as pltpu
from jax.sharding import PartitionSpec as P

LANES = 128
CHUNK = 256
F32, BF16 = jnp.float32, jnp.bfloat16


def nn(a, b):
    return lax.dot_general(a, b, (((1,), (0,)), ((), ())), preferred_element_type=F32)


def nt(a, b):
    return lax.dot_general(a, b, (((1,), (1,)), ((), ())), preferred_element_type=F32)


def halves(x):
    high = x.astype(BF16)
    return high, (x - high.astype(F32)).astype(BF16)


def stacked(x):
    return jnp.concatenate(halves(x), axis=0)


def folded(x):
    rows = x.shape[0] // 2
    return x[:rows] + x[rows:]


def nn2(x, narrow):
    return folded(nn(stacked(x), narrow))


def nt2(x, narrow):
    return folded(nt(stacked(x), narrow))


def both3(product, x, y):
    high, low = halves(y)
    return folded(product(stacked(x), high)) + product(x.astype(BF16), low)


def equal(a, b):
    return jnp.where(a == b, 1.0, 0.0).astype(BF16)


def iota(shape, dim):
    return lax.broadcasted_iota(jnp.int32, shape, dim)


def rounded_up(value, unit):
    return (value + unit - 1) // unit * unit


def table(order_row):
    size = order_row.shape[1]
    return equal(iota((size, size), 0), order_row)


def spread_of(dofs_row, chain, corners, groups):
    column = chain * corners
    ids = iota((column, 1), 0)
    slot = sum((ids >= t * corners).astype(jnp.int32) for t in range(1, chain))
    target = ids + slot * ((groups - 1) * corners) + lax.axis_index("coarse") * corners
    return equal(target, dofs_row)


def placed(x, width, at):
    rows = x.shape[1]
    return nn(x, equal(iota((rows, width), 0) + at, iota((rows, width), 1)))


def picked(x, at, count):
    width = x.shape[1]
    return nn2(x, equal(iota((width, count), 0) - at, iota((width, count), 1)))


def by_parity(to_after, to_before):
    odd = (lax.axis_index("sub") & 1) == 1
    return jnp.where(odd, to_before, to_after), jnp.where(odd, to_after, to_before)


def start_fetch(matrix, held, sems):
    subs, size = matrix.shape[0], matrix.shape[1]
    copies = []
    for n in range(subs):
        for k in range(size // CHUNK):
            part = pl.ds(k * CHUNK, CHUNK)
            copy = pltpu.make_async_copy(
                matrix.at[n, part], held.at[n, part], sems.at[n * (size // CHUNK) + k]
            )
            copy.start()
            copies.append(copy)
    return copies


def times_matrix(x, n, held, copies=None):
    if copies is None:
        return nn(x, held[n])
    size = held.shape[1]
    count = size // CHUNK
    total = None
    for k in range(count):
        copies[n * count + k].wait()
        part = nn(x[:, k * CHUNK : (k + 1) * CHUNK], held[n, k * CHUNK : (k + 1) * CHUNK])
        total = part if total is None else total + part
    return total


def jumped(displaced, tables, from_before, from_after, left_only=False):
    subs = len(displaced)
    face = tables.shape[1]
    at_head = lax.axis_index("sub") == 0
    at_tail = lax.axis_index("sub") == lax.axis_size("sub") - 1
    result = []
    for n in range(subs):
        own = tables[n]
        before = nn(from_before, own) if n == 0 else nn2(displaced[n - 1][:, face:], own)
        left = displaced[n][:, :face] - before
        if n == 0:
            left = jnp.where(at_head, 0.0, left)
        if left_only:
            result.append(left)
            continue
        if n == subs - 1:
            right = displaced[n][:, face:] - from_after
            right = jnp.where(at_tail, 0.0, right)
        else:
            right = displaced[n][:, face:] - nt2(displaced[n + 1][:, :face], tables[n + 1])
        result.append(jnp.concatenate([left, right], axis=1))
    return result


def chain_sums(received, groups, width):
    chain = received.shape[0] // groups
    sums = []
    for c in range(groups):
        total = None
        for z in range(chain):
            part = received[z * groups + c, :, :width].astype(F32)
            total = part if total is None else total + part
        sums.append(total)
    return sums


def copies_of(out, x):
    for i in range(out.shape[0]):
        out[i] = x


def fetched(pairs, sems):
    copies = [pltpu.make_async_copy(a, b, sems.at[i]) for i, (a, b) in enumerate(pairs)]
    for copy in copies:
        copy.start()
    return copies


def corner_kernel(loads_far, coupling_far, dofs_far, out, loads, coupling, dofs, sems, *, chain, groups):
    pairs = [(dofs_far, dofs), (coupling_far, coupling), (loads_far, loads)]
    for copy in fetched(pairs, sems):
        copy.wait()
    corners = coupling.shape[1]
    total = None
    for n in range(loads.shape[0]):
        terms = nt(loads[n], coupling[n])
        part = nt2(terms, spread_of(dofs[n : n + 1], chain, corners, groups))
        total = part if total is None else total + part
    copies_of(out, placed(total.astype(BF16), out.shape[2], 0).astype(BF16))


def first_kernel(matrix, *refs, chain, groups):
    far, shards, refs = refs[:6], refs[6 : 5 + chain], refs[5 + chain :]
    out, first, second, kernel, tables, held, sems, *near_refs, small = refs
    small_copies = fetched(list(zip(far, near_refs)), small)
    copies = start_fetch(matrix, held, sems)
    for copy in small_copies:
        copy.wait()
    order, regroup, shard, coupling, dofs, loads = near_refs
    subs, cases, iface = loads.shape
    corners, face = coupling.shape[1], order.shape[1]
    pad = rounded_up(corners, 16) - corners
    for n in range(subs):
        tables[n] = table(order[n : n + 1])
    near = tables[0]
    position = lax.axis_index("sub")
    depth = groups * corners
    rows = None
    for j, block in enumerate([shard, *shards]):
        ids = iota((depth, regroup.shape[1]), 0) + (position ^ j) * depth
        part = nn(block[...], equal(ids, regroup[...]))
        rows = part if rows is None else rows + part
    kernel[...] = rows.astype(BF16)

    def packet(displaced, coupled, n):
        spread = spread_of(dofs[n : n + 1], chain, corners, groups)
        eye = equal(iota((corners, corners), 0), iota((corners, corners), 1))
        hot = placed(nt(eye, spread).astype(BF16), first.shape[1] - face, 0)
        lower = jnp.concatenate([coupled, hot], axis=1)
        upper = jnp.concatenate([displaced, jnp.zeros((cases, hot.shape[1]), F32)], axis=1)
        return jnp.concatenate([upper, lower, jnp.zeros((pad, lower.shape[1]), F32)], axis=0)

    for n in range(subs):
        out[n] = times_matrix(loads[n], n, held, copies)
    last = subs - 1
    to_after = packet(out[last, :, face:], coupling[last, :, face:].astype(F32), last)
    to_before = packet(
        nt(out[0, :, :face].astype(BF16), near), nt(coupling[0, :, :face], near), 0
    )
    one, two = by_parity(to_after, to_before)
    first[...] = one.astype(BF16)
    second[...] = two.astype(BF16)


def lift_kernel(
    displaced, first, second, received, kernel, other, coupling, dofs, tables,
    lifts, pull, out, *joined, chain, groups
):
    subs, cases, _ = displaced.shape
    corners, face = coupling.shape[1], tables.shape[1]
    column = chain * corners
    wide = rounded_up(column, LANES)
    position = lax.axis_index("sub")
    join(joined, kernel, other)

    from_after, from_before = by_parity(first[...].astype(F32), second[...].astype(F32))
    eye = equal(iota((column, first.shape[1] - face), 0), iota((column, first.shape[1] - face), 1))

    def neighbour(block):
        low = block[cases:].astype(BF16)
        return low[:, :face], nt(eye, low[:, face:]).astype(BF16)

    before_coupling, before_spread = neighbour(from_before)
    after_coupling, after_spread = neighbour(from_after)
    spreads = [spread_of(dofs[n : n + 1], chain, corners, groups) for n in range(subs)]
    at_head, at_tail = position == 0, position == chain - 1
    lifted = []
    for n in range(subs):
        own = tables[n]
        if n == 0:
            moved = nn(before_spread, nn(before_coupling, own).astype(BF16))
        else:
            moved = nn(spreads[n - 1], nn(coupling[n - 1, :, face:], own).astype(BF16))
        left = nn(spreads[n], coupling[n, :, :face]) - moved
        if n == 0:
            left = jnp.where(at_head, 0.0, left)
        if n == subs - 1:
            back = nn(after_spread, after_coupling)
        else:
            back = nn(
                spreads[n + 1], nt(coupling[n + 1, :, :face], tables[n + 1]).astype(BF16)
            )
        right = nn(spreads[n], coupling[n, :, face:]) - back
        if n == subs - 1:
            right = jnp.where(at_tail, 0.0, right)
        lifted.append(jnp.concatenate([left, right], axis=1).astype(BF16))
        lifts[n] = lifted[n]

    flat = jnp.concatenate(chain_sums(received, groups, wide), axis=1)
    values = nt2(flat, kernel[...])
    bent = jumped(
        [displaced[n] for n in range(subs)],
        tables,
        from_before[:cases, :face].astype(BF16),
        from_after[:cases, :face],
    )
    corner, norms = None, None
    for n in range(subs):
        whole = bent[n] + nn2(values, lifted[n])
        pull[n] = whole
        left = whole[:, :face]
        part, norm = nt2(left, lifted[n][:, :face]), both3(nt, left, left)
        corner = part if corner is None else corner + part
        norms = norm if norms is None else norms + norm
    copies_of(out, packed(out.shape[2], corner, norms))


def join(out, low, high):
    for ref in out:
        ref[: low.shape[0]] = low[...]
        ref[low.shape[0] :] = high[...]


def packed(width, corner, *grams):
    total = placed(corner.astype(BF16), width, 0)
    at = corner.shape[1]
    for gram in grams:
        for half in halves(gram):
            total = total + placed(half, width, at)
            at += gram.shape[1]
    return total.astype(BF16)


def second_kernel(matrix, pull, tables, out, first, second):
    subs = pull.shape[0]
    face = tables.shape[1]
    for n in range(subs):
        out[n] = folded(times_matrix(stacked(pull[n]), n, matrix))
    one, two = by_parity(out[subs - 1, :, face:], nt2(out[0, :, :face], tables[0]))
    first[...] = one.astype(BF16)
    second[...] = two.astype(BF16)


def third_kernel(
    matrix, displaced, first, second, received, kernel, lifts, pull0, tables, low, high, *refs, groups
):
    pull, out, after, payload, norms0, *joined = refs
    join(joined, low, high)
    subs, cases, _ = displaced.shape
    face = tables.shape[1]
    column = lifts.shape[1]
    wide = rounded_up(column, LANES)
    from_after, from_before = by_parity(first[...].astype(F32), second[...].astype(F32))
    sums = chain_sums(received, groups, received.shape[2])
    flat = jnp.concatenate([part[:, :wide] for part in sums], axis=1)
    values = nt2(flat, kernel[...])
    whole = sum(sums)
    norms0[...] = picked(whole, column, cases) + picked(whole, column + cases, cases)
    bent = jumped(
        [displaced[n] for n in range(subs)], tables, from_before.astype(BF16), from_after
    )
    totals = None
    for n in range(subs):
        whole = bent[n] + nn2(values, lifts[n])
        pull[n] = whole
        left = whole[:, :face]
        moved = folded(times_matrix(stacked(whole), n, matrix))
        out[n] = moved
        parts = [
            nt2(left, lifts[n, :, :face]),
            both3(nt, pull0[n, :, :face], left),
            both3(nt, left, left),
            both3(nt, whole, moved),
        ]
        totals = parts if totals is None else [a + b for a, b in zip(totals, parts)]
    after[...] = out[subs - 1, :, face:].astype(BF16)
    corner, gram1, gram2, gram3 = totals
    width = payload.shape[2]
    upper = placed(corner.astype(BF16), width, 0)
    for i, half in enumerate(halves(gram1)):
        upper = upper + placed(half, width, column + i * cases)
    lower, step = None, cases // 2
    for i, half in enumerate(halves(gram2) + halves(gram3)):
        for j in range(2):
            part = half.astype(F32)[j * step : (j + 1) * step].astype(BF16)
            moved = placed(part, width, (4 * j + i) * cases)
            lower = moved if lower is None else lower + moved
    copies_of(payload, jnp.concatenate([upper, lower], axis=0).astype(BF16))


def scene_kernel(
    displaced, first, second, received, kernel, lifts, pull0, pull1, tables, norms0,
    scene_loads, scene_weights, *refs, groups, pieces, slots
):
    blocks = refs[:pieces]
    multipliers, residual, held = refs[pieces:]
    subs, cases, _ = displaced.shape
    face = tables.shape[1]
    column = lifts.shape[1]
    wide = rounded_up(column, LANES)
    group = lax.axis_index("coarse")
    sums = chain_sums(received, groups, received.shape[2])
    for c in range(groups):
        held[c] = sums[c][:cases, :wide]
    flat = jnp.concatenate([held[c] for c in range(groups)], axis=1)
    values = nt2(flat, kernel[...])
    if groups_whole(blocks, column, groups):
        energy, index = None, iter(slots)
        for block in blocks:
            for i in range(block.shape[0] // column):
                lifted = nt2(flat, block[i * column : (i + 1) * column])
                part = both3(nt, lifted, held[group ^ next(index)][:, :column])
                energy = part if energy is None else energy + part
    else:
        energy = blocks[0][...]
    total = sum(sums)
    norms1 = picked(total[:cases], column, cases) + picked(total[:cases], column + cases, cases)
    lower = total[cases:]
    others = [picked(lower, i * cases, cases) for i in range(8)]
    norms2 = jnp.concatenate([others[0] + others[1], others[4] + others[5]], axis=0)
    norms3 = jnp.concatenate([others[2] + others[3], others[6] + others[7]], axis=0) + energy

    ids = iota((cases, scene_loads.shape[1]), 0)
    mixing = sum(
        jnp.where(ids == scene_loads[i : i + 1], scene_weights[i : i + 1], 0.0)
        for i in range(scene_loads.shape[0])
    )

    def moment(norms):
        return jnp.sum(both3(nn, norms, mixing) * mixing, axis=0, keepdims=True)

    moment0, moment1 = moment(norms0[...]), moment(norms1)
    moment2, moment3 = moment(norms2), moment(norms3)
    step0 = moment0 / moment1
    norm1 = moment0 - 2.0 * step0 * moment1 + step0 * step0 * moment2
    grow = 1.0 + norm1 / moment0
    curvature = grow * grow * moment1 - 2.0 * grow * step0 * moment2 + step0 * step0 * moment3
    step1 = norm1 / curvature
    zeros = jnp.zeros_like(mixing)

    def transposed(parts):
        weights = -jnp.concatenate(parts, axis=0)
        high = weights.astype(BF16).astype(F32)
        return jnp.concatenate([high, high, weights - high], axis=0).T.astype(BF16)

    for_multipliers = transposed(
        [(step0 + step1 * grow) * mixing, (-step0 * step1) * mixing, zeros]
    )
    for_residual = transposed(
        [mixing, (-step0 - step1 * grow) * mixing, (step0 * step1) * mixing]
    )
    _, from_before = by_parity(first[...].astype(F32), second[...].astype(F32))
    bent = jumped([displaced[n] for n in range(subs)], tables, from_before.astype(BF16), None, True)
    for n in range(subs):
        pull2 = bent[n] + nn2(values, lifts[n, :, :face])
        basis = jnp.concatenate([pull0[n, :, :face], pull1[n, :, :face], pull2], axis=0)
        high, low = halves(basis)
        basis = jnp.concatenate([high, low, high], axis=0)
        multipliers[n] = nn(for_multipliers, basis)
        residual[n] = nn(for_residual, basis)


def groups_whole(blocks, column, groups):
    return sum(block.shape[0] for block in blocks) == column * groups


def everywhere(x, axes):
    return lax.all_to_all(x, axes, 0, 0)


def swapped(x, axis, bit):
    return lax.ppermute(x, axis, [(i, i ^ bit) for i in range(lax.axis_size(axis))])


def pair_swaps(first, second):
    length = lax.axis_size("sub")
    one = lax.ppermute(first, "sub", [(i, i ^ 1) for i in range(length) if i ^ 1 < length])
    two = lax.ppermute(
        second,
        "sub",
        [(i, j) for i in range(length) for j in [i + 1 if i & 1 else i - 1] if 0 <= j < length],
    )
    return one, two


def call(kernel, outs, args, scratch=(), flops=0, moved=0, far=0, kept=0):
    specs = [pl.BlockSpec(memory_space=pltpu.HBM)] * far
    specs += [pl.BlockSpec(memory_space=pltpu.VMEM)] * (len(args) - far)
    pinned = [pltpu.with_memory_space_constraint(x, pltpu.HBM) for x in args[:far]]
    shapes = [jax.ShapeDtypeStruct(shape, kind) for shape, kind in outs]
    for i in range(len(outs) - kept, len(outs)):
        shapes[i] = pltpu.VMEM(*outs[i])
    return pl.pallas_call(
        kernel,
        out_shape=shapes,
        in_specs=specs,
        out_specs=[pl.BlockSpec(memory_space=pltpu.VMEM)] * len(outs),
        scratch_shapes=list(scratch),
        compiler_params=pltpu.CompilerParams(vmem_limit_bytes=32 << 20),
        cost_estimate=pl.CostEstimate(flops=flops, bytes_accessed=moved, transcendentals=0),
    )(*pinned, *args[far:])


def per_device(
    schur_inverse,
    corner_coupling,
    coarse_inverse,
    load_cases,
    face_order,
    corner_dofs,
    scene_loads,
    scene_weights,
):
    subs, iface = schur_inverse.shape[0], schur_inverse.shape[1]
    face = face_order.shape[1]
    corners = corner_dofs.shape[1]
    cases = load_cases.shape[1]
    scenes = scene_loads.shape[0]
    chain, groups = lax.axis_size("sub"), lax.axis_size("coarse")
    devices = chain * groups
    column = chain * corners
    wide = rounded_up(column, LANES)
    along = groups * wide
    work = dict(flops=4 * cases * schur_inverse.size, moved=2 * schur_inverse.size)

    shard = coarse_inverse.reshape(column, groups * corners)
    shards = [swapped(shard, "sub", j) for j in range(1, chain)]

    lane = np.arange(along)
    inner = lane % wide
    source = (inner // corners * groups + lane // wide) * corners + inner % corners
    regroup = jnp.asarray(np.where(inner < column, source, -1)[None].astype(np.int32))

    bits = []
    if groups == 1 << 3 and (column * groups) ** 2 <= schur_inverse.size:
        bits = [1 << b for b in reversed(range(groups.bit_length() - 1))]

    small = [face_order, regroup, shard, corner_coupling, corner_dofs, load_cases]
    near = [pltpu.VMEM(x.shape, x.dtype) for x in small]
    (sent0,) = call(
        functools.partial(corner_kernel, chain=chain, groups=groups),
        [((devices, cases, wide), BF16)],
        [load_cases, corner_coupling, corner_dofs],
        [near[5], near[3], near[4], pltpu.SemaphoreType.DMA((3,))],
        far=3,
    )
    received0 = everywhere(sent0, ("sub", "coarse"))
    packet = (cases + rounded_up(corners, 16), face + wide)
    displaced0, first, second, kernel, tables, matrix = call(
        functools.partial(first_kernel, chain=chain, groups=groups),
        [
            ((subs, cases, iface), F32),
            (packet, BF16),
            (packet, BF16),
            ((column, along), BF16),
            ((subs, face, face), BF16),
            (schur_inverse.shape, BF16),
        ],
        [schur_inverse, *small, *shards],
        [pltpu.SemaphoreType.DMA((subs * (iface // CHUNK),)), *near]
        + [pltpu.SemaphoreType.DMA((len(small),))],
        far=1 + len(small),
        kept=2,
        **work,
    )
    first, second = pair_swaps(first, second)
    other = swapped(kernel, "coarse", bits[0]) if bits else kernel
    lifts, pull0, sent1, *joined = call(
        functools.partial(lift_kernel, chain=chain, groups=groups),
        [
            ((subs, column, iface), BF16),
            ((subs, cases, iface), F32),
            ((devices, cases, rounded_up(column + 2 * cases, LANES)), BF16),
        ]
        + [((2 * column, along), BF16)] * bool(bits),
        [displaced0, first, second, received0, kernel, other]
        + [corner_coupling, corner_dofs, tables],
        flops=10**9,
        moved=10**6,
    )
    received1 = everywhere(sent1, ("sub", "coarse"))
    displaced1, first, second = call(
        second_kernel,
        [((subs, cases, iface), F32), ((cases, face), BF16), ((cases, face), BF16)],
        [matrix, pull0, tables],
        **work,
    )
    first, second = pair_swaps(first, second)

    low = joined[0] if bits else kernel
    high = swapped(low, "coarse", bits[1]) if bits else kernel
    pull1, displaced2, after, sent2, norms0, *joined = call(
        functools.partial(third_kernel, groups=groups),
        [
            ((subs, cases, iface), F32),
            ((subs, cases, iface), F32),
            ((cases, face), BF16),
            ((devices, cases + cases // 2, rounded_up(column + 2 * cases, LANES)), BF16),
            ((cases, cases), F32),
        ]
        + [((4 * column, along), BF16)] * bool(bits),
        [matrix, displaced1, first, second, received1, kernel, lifts, pull0, tables]
        + [low, high],
        **work,
    )
    received2 = everywhere(sent2, ("sub", "coarse"))
    first, second = pair_swaps(after, after)
    if bits:
        blocks = [joined[0], swapped(joined[0], "coarse", bits[2])]
        slots = [0, bits[0], bits[1], bits[0] ^ bits[1]]
        slots = slots + [slot ^ bits[2] for slot in slots]
    else:
        slots = []
        sums = received2.reshape((chain, groups) + received2.shape[1:])[..., :cases, :wide]
        sums = jnp.sum(sums.astype(F32), axis=0)
        flat = jnp.moveaxis(sums, 0, 1).reshape(cases, along)
        own = lax.dynamic_index_in_dim(sums, lax.axis_index("coarse"), 0, keepdims=False)
        values = jnp.dot(flat, kernel.astype(F32).T, precision=lax.Precision.HIGHEST)
        energy = jnp.dot(values, own[:, :column].T, precision=lax.Precision.HIGHEST)
        blocks = [lax.psum(energy, "coarse")]
    multipliers, residual = call(
        functools.partial(scene_kernel, groups=groups, pieces=len(blocks), slots=slots),
        [((subs, scenes, face), F32), ((subs, scenes, face), F32)],
        [displaced2, first, second, received2, kernel, lifts, pull0, pull1, tables, norms0]
        + [scene_loads.T, scene_weights.T, *blocks],
        [pltpu.VMEM((groups, cases, wide), F32)],
        flops=10**9,
        moved=4 * 10**6,
    )
    return (multipliers, residual)


def solution(mesh):
    return jax.shard_map(
        per_device,
        mesh=mesh,
        in_specs=(
            P(("sub", "coarse"), None, None),
            P(("sub", "coarse"), None, None),
            P(None, "coarse", None, "sub"),
            P(("sub", "coarse"), None, None),
            P(("sub", "coarse"), None),
            P(("sub", "coarse"), None),
            P(),
            P(),
        ),
        out_specs=(P(("sub", "coarse"), None, None), P(("sub", "coarse"), None, None)),
        check_vma=False,
    )
```

```python
import functools

import jax
import jax.numpy as jnp
import numpy as np
from jax import lax
from jax.experimental import pallas as pl
from jax.experimental.pallas import tpu as pltpu
from jax.sharding import PartitionSpec as P

LANES = 128
CHUNK = 256
F32, BF16 = jnp.float32, jnp.bfloat16


def nn(a, b):
    return lax.dot_general(a, b, (((1,), (0,)), ((), ())), preferred_element_type=F32)


def nt(a, b):
    return lax.dot_general(a, b, (((1,), (1,)), ((), ())), preferred_element_type=F32)


def halves(x):
    high = x.astype(BF16)
    return high, (x - high.astype(F32)).astype(BF16)


def stacked(x):
    return jnp.concatenate(halves(x), axis=0)


def folded(x):
    rows = x.shape[0] // 2
    return x[:rows] + x[rows:]


def nn2(x, narrow):
    return folded(nn(stacked(x), narrow))


def nt2(x, narrow):
    return folded(nt(stacked(x), narrow))


def both3(product, x, y):
    high, low = halves(y)
    return folded(product(stacked(x), high)) + product(x.astype(BF16), low)


def equal(a, b):
    return jnp.where(a == b, 1.0, 0.0).astype(BF16)


def iota(shape, dim):
    return lax.broadcasted_iota(jnp.int32, shape, dim)


def rounded_up(value, unit):
    return (value + unit - 1) // unit * unit


def table(order_row):
    size = order_row.shape[1]
    return equal(iota((size, size), 0), order_row)


def fill_tables(tables, order):
    for n in range(tables.shape[0]):
        tables[n] = table(order[n : n + 1])


def spread_of(dofs_row, chain, corners, groups):
    column = chain * corners
    ids = iota((column, 1), 0)
    slot = sum((ids >= t * corners).astype(jnp.int32) for t in range(1, chain))
    target = ids + slot * ((groups - 1) * corners) + lax.axis_index("coarse") * corners
    return equal(target, dofs_row)


def placed(x, width, at):
    rows = x.shape[1]
    return nn(x, equal(iota((rows, width), 0) + at, iota((rows, width), 1)))


def picked(x, at, count):
    width = x.shape[1]
    return nn2(x, equal(iota((width, count), 0) - at, iota((width, count), 1)))


def by_parity(to_after, to_before):
    odd = (lax.axis_index("sub") & 1) == 1
    return jnp.where(odd, to_before, to_after), jnp.where(odd, to_after, to_before)


def start_fetch(matrix, held, sems):
    subs, size = matrix.shape[0], matrix.shape[1]
    copies = []
    for n in range(subs):
        for k in range(size // CHUNK):
            rows, columns = pl.ds(k * CHUNK, CHUNK), pl.ds(k * CHUNK, size - k * CHUNK)
            copy = pltpu.make_async_copy(
                matrix.at[n, rows, columns],
                held.at[n, rows, columns],
                sems.at[n * (size // CHUNK) + k],
            )
            copy.start()
            copies.append(copy)
    return copies


def times_matrix(x, n, held, copies):
    size = held.shape[1]
    count = size // CHUNK
    sums = [None] * count

    def add(j, part):
        sums[j] = part if sums[j] is None else sums[j] + part

    for i in range(count):
        copies[n * count + i].wait()
        at, after = i * CHUNK, (i + 1) * CHUNK
        here = nn(x[:, at:after], held[n, at:after, at:])
        for j in range(i, count):
            add(j, here[:, (j - i) * CHUNK : (j - i + 1) * CHUNK])
        if after < size:
            add(i, nt(x[:, after:], held[n, at:after, after:]))
    return jnp.concatenate(sums, axis=1)


def jumped(displaced, tables, from_before, from_after):
    subs = len(displaced)
    face = tables.shape[1]
    at_head = lax.axis_index("sub") == 0
    at_tail = lax.axis_index("sub") == lax.axis_size("sub") - 1
    result = []
    for n in range(subs):
        own = tables[n]
        before = nn(from_before, own) if n == 0 else nn2(displaced[n - 1][:, face:], own)
        left = displaced[n][:, :face] - before
        if n == 0:
            left = jnp.where(at_head, 0.0, left)
        if n == subs - 1:
            right = displaced[n][:, face:] - from_after
            right = jnp.where(at_tail, 0.0, right)
        else:
            right = displaced[n][:, face:] - nt2(displaced[n + 1][:, :face], tables[n + 1])
        result.append(jnp.concatenate([left, right], axis=1))
    return result


def chain_sums(received, groups, width):
    chain = received.shape[0] // groups
    sums = []
    for c in range(groups):
        total = None
        for z in range(chain):
            part = received[z * groups + c, :, :width].astype(F32)
            total = part if total is None else total + part
        sums.append(total)
    return sums


def copies_of(out, x):
    for i in range(out.shape[0]):
        out[i] = x


def fetched(pairs, sems):
    copies = [pltpu.make_async_copy(a, b, sems.at[i]) for i, (a, b) in enumerate(pairs)]
    for copy in copies:
        copy.start()
    return copies


def corner_kernel(loads_far, coupling_far, dofs_far, out, loads, coupling, dofs, sems, *, chain, groups):
    pairs = [(dofs_far, dofs), (coupling_far, coupling), (loads_far, loads)]
    for copy in fetched(pairs, sems):
        copy.wait()
    corners = coupling.shape[1]
    total = None
    for n in range(loads.shape[0]):
        terms = nt(loads[n], coupling[n])
        part = nt2(terms, spread_of(dofs[n : n + 1], chain, corners, groups))
        total = part if total is None else total + part
    copies_of(out, placed(total.astype(BF16), out.shape[2], 0).astype(BF16))


def first_kernel(matrix, *refs, chain, groups):
    far, shards, refs = refs[:6], refs[6 : 5 + chain], refs[5 + chain :]
    out, first, second, kernel, held, sems, *near_refs, small = refs
    small_copies = fetched(list(zip(far, near_refs)), small)
    copies = start_fetch(matrix, held, sems)
    for copy in small_copies:
        copy.wait()
    order, regroup, shard, coupling, dofs, loads = near_refs
    subs, cases, iface = loads.shape
    corners, face = coupling.shape[1], order.shape[1]
    pad = rounded_up(corners, 16) - corners

    def packet(displaced, coupled, n):
        spread = spread_of(dofs[n : n + 1], chain, corners, groups)
        eye = equal(iota((corners, corners), 0), iota((corners, corners), 1))
        hot = placed(nt(eye, spread).astype(BF16), first.shape[1] - face, 0)
        lower = jnp.concatenate([coupled, hot], axis=1)
        upper = jnp.concatenate([displaced, jnp.zeros((cases, hot.shape[1]), F32)], axis=1)
        return jnp.concatenate([upper, lower, jnp.zeros((pad, lower.shape[1]), F32)], axis=0)

    for n in range(subs):
        out[n] = times_matrix(loads[n], n, held, copies)
        if n == 0:
            near = table(order[0:1])
            to_before = packet(
                nt(out[0, :, :face].astype(BF16), near), nt(coupling[0, :, :face], near), 0
            )
            position = lax.axis_index("sub")
            depth = groups * corners
            rows = None
            for j, block in enumerate([shard, *shards]):
                ids = iota((depth, regroup.shape[1]), 0) + (position ^ j) * depth
                part = nn(block[...], equal(ids, regroup[...]))
                rows = part if rows is None else rows + part
            kernel[...] = rows.astype(BF16)
    last = subs - 1
    to_after = packet(out[last, :, face:], coupling[last, :, face:].astype(F32), last)
    one, two = by_parity(to_after, to_before)
    first[...] = one.astype(BF16)
    second[...] = two.astype(BF16)


def lift_kernel(
    displaced, first, second, received, kernel, other, coupling, dofs, order,
    lifts, lifts_left, pull, pull_left, out, *joined, chain, groups
):
    *joined, tables = joined
    fill_tables(tables, order)
    subs, cases, _ = displaced.shape
    corners, face = coupling.shape[1], tables.shape[1]
    column = chain * corners
    wide = rounded_up(column, LANES)
    position = lax.axis_index("sub")
    join(joined, kernel, other)

    from_after, from_before = by_parity(first[...].astype(F32), second[...].astype(F32))
    eye = equal(iota((column, first.shape[1] - face), 0), iota((column, first.shape[1] - face), 1))

    def neighbour(block):
        low = block[cases:].astype(BF16)
        return low[:, :face], nt(eye, low[:, face:]).astype(BF16)

    before_coupling, before_spread = neighbour(from_before)
    after_coupling, after_spread = neighbour(from_after)
    spreads = [spread_of(dofs[n : n + 1], chain, corners, groups) for n in range(subs)]
    at_head, at_tail = position == 0, position == chain - 1
    lifted = []
    for n in range(subs):
        own = tables[n]
        if n == 0:
            moved = nn(before_spread, nn(before_coupling, own).astype(BF16))
        else:
            moved = nn(spreads[n - 1], nn(coupling[n - 1, :, face:], own).astype(BF16))
        left = nn(spreads[n], coupling[n, :, :face]) - moved
        if n == 0:
            left = jnp.where(at_head, 0.0, left)
        if n == subs - 1:
            back = nn(after_spread, after_coupling)
        else:
            back = nn(
                spreads[n + 1], nt(coupling[n + 1, :, :face], tables[n + 1]).astype(BF16)
            )
        right = nn(spreads[n], coupling[n, :, face:]) - back
        if n == subs - 1:
            right = jnp.where(at_tail, 0.0, right)
        lifted.append(jnp.concatenate([left, right], axis=1).astype(BF16))
        lifts[n] = lifted[n]
        lifts_left[n] = lifted[n][:, :face]

    flat = jnp.concatenate(chain_sums(received, groups, wide), axis=1)
    values = nt2(flat, kernel[...])
    bent = jumped(
        [displaced[n] for n in range(subs)],
        tables,
        from_before[:cases, :face].astype(BF16),
        from_after[:cases, :face],
    )
    corner, norms = None, None
    for n in range(subs):
        whole = bent[n] + nn2(values, lifted[n])
        pull[n] = whole
        left = whole[:, :face]
        pull_left[n] = left
        part, norm = nt2(left, lifted[n][:, :face]), both3(nt, left, left)
        corner = part if corner is None else corner + part
        norms = norm if norms is None else norms + norm
    copies_of(out, packed(out.shape[2], corner, norms))


def join(out, low, high):
    for ref in out:
        ref[: low.shape[0]] = low[...]
        ref[low.shape[0] :] = high[...]


def packed(width, corner, *grams):
    total = placed(corner.astype(BF16), width, 0)
    at = corner.shape[1]
    for gram in grams:
        for half in halves(gram):
            total = total + placed(half, width, at)
            at += gram.shape[1]
    return total.astype(BF16)


def second_kernel(matrix, pull, order, out, first, second, held, sems):
    copies = start_fetch(matrix, held, sems)
    subs = pull.shape[0]
    face = order.shape[1]
    near = table(order[0:1])
    for n in range(subs):
        out[n] = folded(times_matrix(stacked(pull[n]), n, held, copies))
    one, two = by_parity(out[subs - 1, :, face:], nt2(out[0, :, :face], near))
    first[...] = one.astype(BF16)
    second[...] = two.astype(BF16)


def third_kernel(
    matrix, displaced, first, second, received, kernel, lifts, pull0, order, low, high, *refs, groups
):
    pull, bent2, after, payload, norms0, *joined, held, sems, tables = refs
    copies = start_fetch(matrix, held, sems)
    fill_tables(tables, order)
    join(joined, low, high)
    subs, cases, _ = displaced.shape
    face = tables.shape[1]
    column = lifts.shape[1]
    wide = rounded_up(column, LANES)
    from_after, from_before = by_parity(first[...].astype(F32), second[...].astype(F32))
    sums = chain_sums(received, groups, received.shape[2])
    flat = jnp.concatenate([part[:, :wide] for part in sums], axis=1)
    values = nt2(flat, kernel[...])
    whole = sum(sums)
    norms0[...] = picked(whole, column, cases) + picked(whole, column + cases, cases)
    bent = jumped(
        [displaced[n] for n in range(subs)], tables, from_before.astype(BF16), from_after
    )
    totals = None
    for n in range(subs):
        whole = bent[n] + nn2(values, lifts[n])
        left = whole[:, :face]
        pull[n] = left
        moved = folded(times_matrix(stacked(whole), n, held, copies))
        bent2[n] = moved[:, :face]
        if n > 0:
            bent2[n] = moved[:, :face] - nn2(previous, tables[n])
        previous = moved[:, face:]
        parts = [
            nt2(left, lifts[n, :, :face]),
            both3(nt, pull0[n], left),
            both3(nt, left, left),
            both3(nt, whole, moved),
        ]
        totals = parts if totals is None else [a + b for a, b in zip(totals, parts)]
    after[...] = previous.astype(BF16)
    corner, gram1, gram2, gram3 = totals
    width = payload.shape[2]
    upper = placed(corner.astype(BF16), width, 0)
    for i, half in enumerate(halves(gram1)):
        upper = upper + placed(half, width, column + i * cases)
    lower, step = None, cases // 2
    for i, half in enumerate(halves(gram2) + halves(gram3)):
        for j in range(2):
            part = half.astype(F32)[j * step : (j + 1) * step].astype(BF16)
            moved = placed(part, width, (4 * j + i) * cases)
            lower = moved if lower is None else lower + moved
    copies_of(payload, jnp.concatenate([upper, lower], axis=0).astype(BF16))


def scene_kernel(
    bent, first, second, received, kernel, lifts, pull0, pull1, order, norms0,
    scene_loads, scene_weights, *refs, groups, pieces, slots
):
    blocks = refs[:pieces]
    multipliers, residual, held, turned = refs[pieces:]
    subs, cases, _ = bent.shape
    column = lifts.shape[1]
    wide = rounded_up(column, LANES)
    group = lax.axis_index("coarse")
    sums = chain_sums(received, groups, received.shape[2])
    for c in range(groups):
        held[c] = sums[c][:cases, :wide]
    flat = jnp.concatenate([held[c] for c in range(groups)], axis=1)
    values = nt2(flat, kernel[:column])
    if groups_whole(blocks, column, groups):
        index = 0
        turned[...] = jnp.zeros(turned.shape, F32)
        for block in blocks:
            for i in range(block.shape[0] // column):
                lifted = nt2(flat, block[i * column : (i + 1) * column])
                turned[:, index * wide : index * wide + column] = lifted
                index += 1
        met = jnp.concatenate([held[group ^ slot] for slot in slots], axis=1)
        energy = both3(nt, turned[...], met)
    else:
        energy = blocks[0][...]
    total = sum(sums)
    norms1 = picked(total[:cases], column, cases) + picked(total[:cases], column + cases, cases)
    lower = total[cases:]
    others = [picked(lower, i * cases, cases) for i in range(8)]
    norms2 = jnp.concatenate([others[0] + others[1], others[4] + others[5]], axis=0)
    norms3 = jnp.concatenate([others[2] + others[3], others[6] + others[7]], axis=0) + energy

    ids = iota((cases, scene_loads.shape[1]), 0)
    mixing = sum(
        jnp.where(ids == scene_loads[i : i + 1], scene_weights[i : i + 1], 0.0)
        for i in range(scene_loads.shape[0])
    )

    def moment(norms):
        return jnp.sum(both3(nn, norms, mixing) * mixing, axis=0, keepdims=True)

    moment0, moment1 = moment(norms0[...]), moment(norms1)
    moment2, moment3 = moment(norms2), moment(norms3)
    step0 = moment0 / moment1
    norm1 = moment0 - 2.0 * step0 * moment1 + step0 * step0 * moment2
    grow = 1.0 + norm1 / moment0
    curvature = grow * grow * moment1 - 2.0 * grow * step0 * moment2 + step0 * step0 * moment3
    step1 = norm1 / curvature
    zeros = jnp.zeros_like(mixing)

    def transposed(parts):
        weights = -jnp.concatenate(parts, axis=0)
        high = weights.astype(BF16).astype(F32)
        return jnp.concatenate([high, high, weights - high], axis=0).T.astype(BF16)

    for_multipliers = transposed(
        [(step0 + step1 * grow) * mixing, (-step0 * step1) * mixing, zeros]
    )
    for_residual = transposed(
        [mixing, (-step0 - step1 * grow) * mixing, (step0 * step1) * mixing]
    )
    _, from_before = by_parity(first[...].astype(F32), second[...].astype(F32))
    for n in range(subs):
        pull2 = bent[n]
        if n == 0:
            pull2 = pull2 - nn(from_before.astype(BF16), table(order[0:1]))
            pull2 = jnp.where(lax.axis_index("sub") == 0, 0.0, pull2)
        pull2 = pull2 + nn2(values, lifts[n])
        basis = jnp.concatenate([pull0[n], pull1[n], pull2], axis=0)
        high, low = halves(basis)
        basis = jnp.concatenate([high, low, high], axis=0)
        multipliers[n] = nn(for_multipliers, basis)
        residual[n] = nn(for_residual, basis)


def groups_whole(blocks, column, groups):
    return sum(block.shape[0] for block in blocks) == column * groups


def everywhere(x, axes):
    return lax.all_to_all(x, axes, 0, 0)


def swapped(x, axis, bit):
    return lax.ppermute(x, axis, [(i, i ^ bit) for i in range(lax.axis_size(axis))])


def pair_swaps(first, second):
    length = lax.axis_size("sub")

    def partner(i, j):
        return (i, j if 0 <= j < length else i)

    one = lax.ppermute(first, "sub", [partner(i, i ^ 1) for i in range(length)])
    two = lax.ppermute(
        second, "sub", [partner(i, i + 1 if i & 1 else i - 1) for i in range(length)]
    )
    return one, two


def call(kernel, outs, args, scratch=(), flops=0, moved=0, far=0):
    specs = [pl.BlockSpec(memory_space=pltpu.HBM)] * far
    specs += [pl.BlockSpec(memory_space=pltpu.VMEM)] * (len(args) - far)
    pinned = [pltpu.with_memory_space_constraint(x, pltpu.HBM) for x in args[:far]]
    shapes = [jax.ShapeDtypeStruct(shape, kind) for shape, kind in outs]
    return pl.pallas_call(
        kernel,
        out_shape=shapes,
        in_specs=specs,
        out_specs=[pl.BlockSpec(memory_space=pltpu.VMEM)] * len(outs),
        scratch_shapes=list(scratch),
        compiler_params=pltpu.CompilerParams(vmem_limit_bytes=32 << 20),
        cost_estimate=pl.CostEstimate(flops=flops, bytes_accessed=moved, transcendentals=0),
    )(*pinned, *args[far:])


def per_device(
    schur_inverse,
    corner_coupling,
    coarse_inverse,
    load_cases,
    face_order,
    corner_dofs,
    scene_loads,
    scene_weights,
):
    subs, iface = schur_inverse.shape[0], schur_inverse.shape[1]
    face = face_order.shape[1]
    corners = corner_dofs.shape[1]
    cases = load_cases.shape[1]
    scenes = scene_loads.shape[0]
    chain, groups = lax.axis_size("sub"), lax.axis_size("coarse")
    devices = chain * groups
    column = chain * corners
    wide = rounded_up(column, LANES)
    along = groups * wide
    work = dict(flops=4 * cases * schur_inverse.size, moved=2 * schur_inverse.size)

    fetch = [
        pltpu.VMEM(schur_inverse.shape, BF16),
        pltpu.SemaphoreType.DMA((subs * (iface // CHUNK),)),
    ]
    tables = pltpu.VMEM((subs, face, face), BF16)

    shard = coarse_inverse.reshape(column, groups * corners)
    shards = [swapped(shard, "sub", j) for j in range(1, chain)]

    lane = np.arange(along)
    inner = lane % wide
    source = (inner // corners * groups + lane // wide) * corners + inner % corners
    regroup = jnp.asarray(np.where(inner < column, source, -1)[None].astype(np.int32))

    bits = []
    if groups == 1 << 3 and (column * groups) ** 2 <= schur_inverse.size:
        bits = [1 << b for b in reversed(range(groups.bit_length() - 1))]

    small = [face_order, regroup, shard, corner_coupling, corner_dofs, load_cases]
    near = [pltpu.VMEM(x.shape, x.dtype) for x in small]
    (sent0,) = call(
        functools.partial(corner_kernel, chain=chain, groups=groups),
        [((devices, cases, wide), BF16)],
        [load_cases, corner_coupling, corner_dofs],
        [near[5], near[3], near[4], pltpu.SemaphoreType.DMA((3,))],
        far=3,
    )
    received0 = everywhere(sent0, ("sub", "coarse"))
    packet = (cases + rounded_up(corners, 16), face + wide)
    displaced0, first, second, kernel = call(
        functools.partial(first_kernel, chain=chain, groups=groups),
        [
            ((subs, cases, iface), F32),
            (packet, BF16),
            (packet, BF16),
            ((column, along), BF16),
        ],
        [schur_inverse, *small, *shards],
        [*fetch, *near, pltpu.SemaphoreType.DMA((len(small),))],
        far=1 + len(small),
        **work,
    )
    first, second = pair_swaps(first, second)
    other = swapped(kernel, "coarse", bits[0]) if bits else kernel
    lifts, lifts_left, pull0, pull0_left, sent1, *joined = call(
        functools.partial(lift_kernel, chain=chain, groups=groups),
        [
            ((subs, column, iface), BF16),
            ((subs, column, face), BF16),
            ((subs, cases, iface), F32),
            ((subs, cases, face), F32),
            ((devices, cases, rounded_up(column + 2 * cases, LANES)), BF16),
        ]
        + [((2 * column, along), BF16)] * bool(bits),
        [displaced0, first, second, received0, kernel, other]
        + [corner_coupling, corner_dofs, face_order],
        [tables],
        flops=10**9,
        moved=10**6,
    )
    received1 = everywhere(sent1, ("sub", "coarse"))
    displaced1, first, second = call(
        second_kernel,
        [((subs, cases, iface), F32), ((cases, face), BF16), ((cases, face), BF16)],
        [schur_inverse, pull0, face_order],
        fetch,
        far=1,
        **work,
    )
    first, second = pair_swaps(first, second)

    low = joined[0] if bits else kernel
    high = swapped(low, "coarse", bits[1]) if bits else kernel
    pull1, bent2, after, sent2, norms0, *joined = call(
        functools.partial(third_kernel, groups=groups),
        [
            ((subs, cases, face), F32),
            ((subs, cases, face), F32),
            ((cases, face), BF16),
            ((devices, cases + cases // 2, rounded_up(column + 2 * cases, LANES)), BF16),
            ((cases, cases), F32),
        ]
        + [((4 * column, along), BF16)] * bool(bits),
        [schur_inverse, displaced1, first, second, received1, kernel, lifts, pull0_left]
        + [face_order, low, high],
        [*fetch, tables],
        far=1,
        **work,
    )
    received2 = everywhere(sent2, ("sub", "coarse"))
    first, second = pair_swaps(after, after)
    if bits:
        blocks = [joined[0], swapped(joined[0], "coarse", bits[2])]
        slots = [0, bits[0], bits[1], bits[0] ^ bits[1]]
        slots = slots + [slot ^ bits[2] for slot in slots]
    else:
        slots = []
        sums = received2.reshape((chain, groups) + received2.shape[1:])[..., :cases, :wide]
        sums = jnp.sum(sums.astype(F32), axis=0)
        flat = jnp.moveaxis(sums, 0, 1).reshape(cases, along)
        own = lax.dynamic_index_in_dim(sums, lax.axis_index("coarse"), 0, keepdims=False)
        values = jnp.dot(flat, kernel.astype(F32).T, precision=lax.Precision.HIGHEST)
        energy = jnp.dot(values, own[:, :column].T, precision=lax.Precision.HIGHEST)
        blocks = [lax.psum(energy, "coarse")]
    multipliers, residual = call(
        functools.partial(scene_kernel, groups=groups, pieces=len(blocks), slots=slots),
        [((subs, scenes, face), F32), ((subs, scenes, face), F32)],
        [bent2, first, second, received2, joined[0] if bits else kernel, lifts_left, pull0_left]
        + [pull1, face_order, norms0]
        + [scene_loads.T, scene_weights.T, *blocks],
        [pltpu.VMEM((groups, cases, wide), F32), pltpu.VMEM((cases, along), F32)],
        flops=10**9,
        moved=4 * 10**6,
    )
    return (multipliers, residual)


def solution(mesh):
    return jax.shard_map(
        per_device,
        mesh=mesh,
        in_specs=(
            P(("sub", "coarse"), None, None),
            P(("sub", "coarse"), None, None),
            P(None, "coarse", None, "sub"),
            P(("sub", "coarse"), None, None),
            P(("sub", "coarse"), None),
            P(("sub", "coarse"), None),
            P(),
            P(),
        ),
        out_specs=(P(("sub", "coarse"), None, None), P(("sub", "coarse"), None, None)),
        check_vma=False,
    )
```

```python
import functools

import jax
import jax.numpy as jnp
import numpy as np
from jax import lax
from jax.experimental import pallas as pl
from jax.experimental.pallas import tpu as pltpu
from jax.sharding import PartitionSpec as P

LANES = 128
CHUNK = 256
F32, BF16 = jnp.float32, jnp.bfloat16


def nn(a, b):
    return lax.dot_general(a, b, (((1,), (0,)), ((), ())), preferred_element_type=F32)


def nt(a, b):
    return lax.dot_general(a, b, (((1,), (1,)), ((), ())), preferred_element_type=F32)


def halves(x):
    high = x.astype(BF16)
    return high, (x - high.astype(F32)).astype(BF16)


def stacked(x):
    return jnp.concatenate(halves(x), axis=0)


def folded(x):
    rows = x.shape[0] // 2
    return x[:rows] + x[rows:]


def nn2(x, narrow):
    return folded(nn(stacked(x), narrow))


def nt2(x, narrow):
    return folded(nt(stacked(x), narrow))


def both3(product, x, y):
    high, low = halves(y)
    return folded(product(stacked(x), high)) + product(x.astype(BF16), low)


def equal(a, b):
    return jnp.where(a == b, 1.0, 0.0).astype(BF16)


def iota(shape, dim):
    return lax.broadcasted_iota(jnp.int32, shape, dim)


def rounded_up(value, unit):
    return (value + unit - 1) // unit * unit


def table(order_row):
    size = order_row.shape[1]
    return equal(iota((size, size), 0), order_row)


def fill_tables(tables, order):
    for n in range(tables.shape[0]):
        tables[n] = table(order[n : n + 1])


def spread_of(dofs_row, chain, corners, groups):
    column = chain * corners
    ids = iota((column, 1), 0)
    slot = sum((ids >= t * corners).astype(jnp.int32) for t in range(1, chain))
    target = ids + slot * ((groups - 1) * corners) + lax.axis_index("coarse") * corners
    return equal(target, dofs_row)


def placed(x, width, at):
    rows = x.shape[1]
    return nn(x, equal(iota((rows, width), 0) + at, iota((rows, width), 1)))


def by_parity(to_after, to_before):
    odd = (lax.axis_index("sub") & 1) == 1
    return jnp.where(odd, to_before, to_after), jnp.where(odd, to_after, to_before)


def start_fetch(matrix, held, sems):
    subs, size = matrix.shape[0], matrix.shape[1]
    copies = []
    for n in range(subs):
        for k in range(size // CHUNK):
            part = pl.ds(k * CHUNK, CHUNK)
            copy = pltpu.make_async_copy(
                matrix.at[n, part], held.at[n, part], sems.at[n * (size // CHUNK) + k]
            )
            copy.start()
            copies.append(copy)
    return copies


def times_matrix(x, n, held, copies):
    size = held.shape[1]
    count = size // CHUNK
    total = None
    for k in range(count):
        copies[n * count + k].wait()
        part = nn(x[:, k * CHUNK : (k + 1) * CHUNK], held[n, k * CHUNK : (k + 1) * CHUNK])
        total = part if total is None else total + part
    return total


def jumped(displaced, tables, from_before, from_after):
    subs = len(displaced)
    face = tables.shape[1]
    at_head = lax.axis_index("sub") == 0
    at_tail = lax.axis_index("sub") == lax.axis_size("sub") - 1
    result = []
    for n in range(subs):
        own = tables[n]
        before = nn(from_before, own) if n == 0 else nn2(displaced[n - 1][:, face:], own)
        left = displaced[n][:, :face] - before
        if n == 0:
            left = jnp.where(at_head, 0.0, left)
        if n == subs - 1:
            right = displaced[n][:, face:] - from_after
            right = jnp.where(at_tail, 0.0, right)
        else:
            right = displaced[n][:, face:] - nt2(displaced[n + 1][:, :face], tables[n + 1])
        result.append(jnp.concatenate([left, right], axis=1))
    return result


def chain_sums(received, groups, width):
    chain = received.shape[0] // groups
    sums = []
    for c in range(groups):
        total = None
        for z in range(chain):
            part = received[z * groups + c, :, :width].astype(F32)
            total = part if total is None else total + part
        sums.append(total)
    return sums


def copies_of(out, x):
    for i in range(out.shape[0]):
        out[i] = x


def fetched(pairs, sems):
    copies = [pltpu.make_async_copy(a, b, sems.at[i]) for i, (a, b) in enumerate(pairs)]
    for copy in copies:
        copy.start()
    return copies


def corner_kernel(loads_far, coupling_far, dofs_far, out, loads, coupling, dofs, sems, *, chain, groups):
    pairs = [(dofs_far, dofs), (coupling_far, coupling), (loads_far, loads)]
    for copy in fetched(pairs, sems):
        copy.wait()
    corners = coupling.shape[1]
    total = None
    for n in range(loads.shape[0]):
        terms = nt(loads[n], coupling[n])
        part = nt2(terms, spread_of(dofs[n : n + 1], chain, corners, groups))
        total = part if total is None else total + part
    copies_of(out, placed(total.astype(BF16), out.shape[2], 0).astype(BF16))


def first_kernel(matrix, *refs, chain, groups):
    far, shards, refs = refs[:6], refs[6 : 5 + chain], refs[5 + chain :]
    out, first, second, kernel, held, sems, *near_refs, small = refs
    small_copies = fetched(list(zip(far, near_refs)), small)
    copies = start_fetch(matrix, held, sems)
    for copy in small_copies:
        copy.wait()
    order, regroup, shard, coupling, dofs, loads = near_refs
    subs, cases, iface = loads.shape
    corners, face = coupling.shape[1], order.shape[1]
    pad = rounded_up(corners, 16) - corners

    def packet(displaced, coupled, n):
        spread = spread_of(dofs[n : n + 1], chain, corners, groups)
        eye = equal(iota((corners, corners), 0), iota((corners, corners), 1))
        hot = placed(nt(eye, spread).astype(BF16), first.shape[1] - face, 0)
        lower = jnp.concatenate([coupled, hot], axis=1)
        upper = jnp.concatenate([displaced, jnp.zeros((cases, hot.shape[1]), F32)], axis=1)
        return jnp.concatenate([upper, lower, jnp.zeros((pad, lower.shape[1]), F32)], axis=0)

    for n in range(subs):
        out[n] = times_matrix(loads[n], n, held, copies)
        if n == 0:
            near = table(order[0:1])
            to_before = packet(
                nt(out[0, :, :face].astype(BF16), near), nt(coupling[0, :, :face], near), 0
            )
            position = lax.axis_index("sub")
            depth = groups * corners
            rows = None
            for j, block in enumerate([shard, *shards]):
                ids = iota((depth, regroup.shape[1]), 0) + (position ^ j) * depth
                part = nn(block[...], equal(ids, regroup[...]))
                rows = part if rows is None else rows + part
            kernel[...] = rows.astype(BF16)
    last = subs - 1
    to_after = packet(out[last, :, face:], coupling[last, :, face:].astype(F32), last)
    one, two = by_parity(to_after, to_before)
    first[...] = one.astype(BF16)
    second[...] = two.astype(BF16)


def lift_kernel(
    displaced, first, second, received, kernel, other, coupling, dofs, order,
    lifts, lifts_left, pull, pull_left, out, *joined, chain, groups
):
    *joined, tables, row = joined
    fill_tables(tables, order)
    subs, cases, _ = displaced.shape
    corners, face = coupling.shape[1], tables.shape[1]
    column = chain * corners
    wide = rounded_up(column, LANES)
    position = lax.axis_index("sub")
    join(joined, kernel, other)

    from_after, from_before = by_parity(first[...].astype(F32), second[...].astype(F32))
    eye = equal(iota((column, first.shape[1] - face), 0), iota((column, first.shape[1] - face), 1))

    def neighbour(block):
        low = block[cases:].astype(BF16)
        return low[:, :face], nt(eye, low[:, face:]).astype(BF16)

    before_coupling, before_spread = neighbour(from_before)
    after_coupling, after_spread = neighbour(from_after)
    spreads = [spread_of(dofs[n : n + 1], chain, corners, groups) for n in range(subs)]
    at_head, at_tail = position == 0, position == chain - 1
    lifted = []
    for n in range(subs):
        own = tables[n]
        if n == 0:
            moved = nn(before_spread, nn(before_coupling, own).astype(BF16))
        else:
            moved = nn(spreads[n - 1], nn(coupling[n - 1, :, face:], own).astype(BF16))
        left = nn(spreads[n], coupling[n, :, :face]) - moved
        if n == 0:
            left = jnp.where(at_head, 0.0, left)
        if n == subs - 1:
            back = nn(after_spread, after_coupling)
        else:
            back = nn(
                spreads[n + 1], nt(coupling[n + 1, :, :face], tables[n + 1]).astype(BF16)
            )
        right = nn(spreads[n], coupling[n, :, face:]) - back
        if n == subs - 1:
            right = jnp.where(at_tail, 0.0, right)
        lifted.append(jnp.concatenate([left, right], axis=1).astype(BF16))
        lifts[n] = lifted[n]
        lifts_left[n] = lifted[n][:, :face]

    flat = jnp.concatenate(chain_sums(received, groups, wide), axis=1)
    values = nt2(flat, kernel[...])
    bent = jumped(
        [displaced[n] for n in range(subs)],
        tables,
        from_before[:cases, :face].astype(BF16),
        from_after[:cases, :face],
    )
    corner, norms = None, None
    for n in range(subs):
        whole = bent[n] + nn2(values, lifted[n])
        pull[n] = whole
        left = whole[:, :face]
        pull_left[n] = left
        part, norm = nt2(left, lifted[n][:, :face]), both3(nt, left, left)
        corner = part if corner is None else corner + part
        norms = norm if norms is None else norms + norm
    row[...] = jnp.zeros(row.shape, F32)
    row[:, :column] = corner
    store_halves(row, norms, slice(0, cases), column)
    copies_of(out, row[...].astype(BF16))


def join(out, low, high):
    for ref in out:
        ref[: low.shape[0]] = low[...]
        ref[low.shape[0] :] = high[...]


def store_halves(row, gram, rows, at):
    for half in halves(gram):
        row[rows, at : at + gram.shape[1]] = half.astype(F32)
        at += gram.shape[1]


def sum_halves(row, rows, at, count):
    return row[rows, at : at + count] + row[rows, at + count : at + 2 * count]


def second_kernel(matrix, pull, order, out, first, second, held, sems):
    copies = start_fetch(matrix, held, sems)
    subs = pull.shape[0]
    face = order.shape[1]
    near = table(order[0:1])
    for n in range(subs):
        out[n] = folded(times_matrix(stacked(pull[n]), n, held, copies))
    one, two = by_parity(out[subs - 1, :, face:], nt2(out[0, :, :face], near))
    first[...] = one.astype(BF16)
    second[...] = two.astype(BF16)


def third_kernel(
    matrix, displaced, first, second, received, kernel, lifts, pull0, order, low, high, *refs, groups
):
    pull, bent2, after, payload, norms0, *joined, held, sems, tables, row = refs
    copies = start_fetch(matrix, held, sems)
    fill_tables(tables, order)
    join(joined, low, high)
    subs, cases, _ = displaced.shape
    face = tables.shape[1]
    column = lifts.shape[1]
    wide = rounded_up(column, LANES)
    from_after, from_before = by_parity(first[...].astype(F32), second[...].astype(F32))
    sums = chain_sums(received, groups, received.shape[2])
    flat = jnp.concatenate([part[:, :wide] for part in sums], axis=1)
    values = nt2(flat, kernel[...])
    row[:cases] = sum(sums)
    norms0[...] = sum_halves(row, slice(0, cases), column, cases)
    bent = jumped(
        [displaced[n] for n in range(subs)], tables, from_before.astype(BF16), from_after
    )
    totals = None
    for n in range(subs):
        whole = bent[n] + nn2(values, lifts[n])
        left = whole[:, :face]
        pull[n] = left
        moved = folded(times_matrix(stacked(whole), n, held, copies))
        bent2[n] = moved[:, :face]
        if n > 0:
            bent2[n] = moved[:, :face] - nn2(previous, tables[n])
        previous = moved[:, face:]
        parts = [
            nt2(left, lifts[n, :, :face]),
            both3(nt, pull0[n], left),
            both3(nt, left, left),
            both3(nt, whole, moved),
        ]
        totals = parts if totals is None else [a + b for a, b in zip(totals, parts)]
    after[...] = previous.astype(BF16)
    corner, gram1, gram2, gram3 = totals
    row[...] = jnp.zeros(row.shape, F32)
    row[:cases, :column] = corner
    store_halves(row, gram1, slice(0, cases), column)
    step = cases // 2
    for j in range(2):
        for i, gram in enumerate((gram2, gram3)):
            part = gram[j * step : (j + 1) * step]
            store_halves(row, part, slice(cases, cases + step), (4 * j + 2 * i) * cases)
    copies_of(payload, row[...].astype(BF16))


def scene_kernel(
    bent, first, second, received, kernel, lifts, pull0, pull1, order, norms0,
    scene_loads, scene_weights, *refs, groups, pieces, slots
):
    blocks = refs[:pieces]
    multipliers, residual, held, turned, row = refs[pieces:]
    subs, cases, _ = bent.shape
    column = lifts.shape[1]
    wide = rounded_up(column, LANES)
    group = lax.axis_index("coarse")
    sums = chain_sums(received, groups, received.shape[2])
    for c in range(groups):
        held[c] = sums[c][:cases, :wide]
    flat = jnp.concatenate([held[c] for c in range(groups)], axis=1)
    values = nt2(flat, kernel[:column])
    if groups_whole(blocks, column, groups):
        index = 0
        turned[...] = jnp.zeros(turned.shape, F32)
        for block in blocks:
            for i in range(block.shape[0] // column):
                lifted = nt2(flat, block[i * column : (i + 1) * column])
                turned[:, index * wide : index * wide + column] = lifted
                index += 1
        met = jnp.concatenate([held[group ^ slot] for slot in slots], axis=1)
        energy = both3(nt, turned[...], met)
    else:
        energy = blocks[0][...]
    row[...] = sum(sums)
    norms1 = sum_halves(row, slice(0, cases), column, cases)
    lower = slice(cases, cases + cases // 2)
    norms2, norms3 = (
        jnp.concatenate(
            [sum_halves(row, lower, (4 * j + 2 * i) * cases, cases) for j in range(2)], axis=0
        )
        for i in range(2)
    )
    norms3 = norms3 + energy

    ids = iota((cases, scene_loads.shape[1]), 0)
    mixing = sum(
        jnp.where(ids == scene_loads[i : i + 1], scene_weights[i : i + 1], 0.0)
        for i in range(scene_loads.shape[0])
    )

    def moment(norms):
        return jnp.sum(both3(nn, norms, mixing) * mixing, axis=0, keepdims=True)

    moment0, moment1 = moment(norms0[...]), moment(norms1)
    moment2, moment3 = moment(norms2), moment(norms3)
    step0 = moment0 / moment1
    norm1 = moment0 - 2.0 * step0 * moment1 + step0 * step0 * moment2
    grow = 1.0 + norm1 / moment0
    curvature = grow * grow * moment1 - 2.0 * grow * step0 * moment2 + step0 * step0 * moment3
    step1 = norm1 / curvature
    zeros = jnp.zeros_like(mixing)

    def transposed(parts):
        weights = -jnp.concatenate(parts, axis=0)
        high = weights.astype(BF16).astype(F32)
        return jnp.concatenate([high, high, weights - high], axis=0).T.astype(BF16)

    for_multipliers = transposed(
        [(step0 + step1 * grow) * mixing, (-step0 * step1) * mixing, zeros]
    )
    for_residual = transposed(
        [mixing, (-step0 - step1 * grow) * mixing, (step0 * step1) * mixing]
    )
    _, from_before = by_parity(first[...].astype(F32), second[...].astype(F32))
    for n in range(subs):
        pull2 = bent[n]
        if n == 0:
            pull2 = pull2 - nn(from_before.astype(BF16), table(order[0:1]))
            pull2 = jnp.where(lax.axis_index("sub") == 0, 0.0, pull2)
        pull2 = pull2 + nn2(values, lifts[n])
        basis = jnp.concatenate([pull0[n], pull1[n], pull2], axis=0)
        high, low = halves(basis)
        basis = jnp.concatenate([high, low, high], axis=0)
        multipliers[n] = nn(for_multipliers, basis)
        residual[n] = nn(for_residual, basis)


def groups_whole(blocks, column, groups):
    return sum(block.shape[0] for block in blocks) == column * groups


def everywhere(x, axes):
    return lax.all_to_all(x, axes, 0, 0)


def swapped(x, axis, bit):
    return lax.ppermute(x, axis, [(i, i ^ bit) for i in range(lax.axis_size(axis))])


def pair_swaps(first, second):
    length = lax.axis_size("sub")
    one = lax.ppermute(first, "sub", [(i, i ^ 1) for i in range(length)])
    two = lax.ppermute(
        second, "sub", [(i, (i + 1 if i & 1 else i - 1) % length) for i in range(length)]
    )
    return one, two


def call(kernel, outs, args, scratch=(), flops=0, moved=0, far=0):
    specs = [pl.BlockSpec(memory_space=pltpu.HBM)] * far
    specs += [pl.BlockSpec(memory_space=pltpu.VMEM)] * (len(args) - far)
    pinned = [pltpu.with_memory_space_constraint(x, pltpu.HBM) for x in args[:far]]
    shapes = [jax.ShapeDtypeStruct(shape, kind) for shape, kind in outs]
    return pl.pallas_call(
        kernel,
        out_shape=shapes,
        in_specs=specs,
        out_specs=[pl.BlockSpec(memory_space=pltpu.VMEM)] * len(outs),
        scratch_shapes=list(scratch),
        compiler_params=pltpu.CompilerParams(vmem_limit_bytes=32 << 20),
        cost_estimate=pl.CostEstimate(flops=flops, bytes_accessed=moved, transcendentals=0),
    )(*pinned, *args[far:])


def per_device(
    schur_inverse,
    corner_coupling,
    coarse_inverse,
    load_cases,
    face_order,
    corner_dofs,
    scene_loads,
    scene_weights,
):
    subs, iface = schur_inverse.shape[0], schur_inverse.shape[1]
    face = face_order.shape[1]
    corners = corner_dofs.shape[1]
    cases = load_cases.shape[1]
    scenes = scene_loads.shape[0]
    chain, groups = lax.axis_size("sub"), lax.axis_size("coarse")
    devices = chain * groups
    column = chain * corners
    wide = rounded_up(column, LANES)
    along = groups * wide
    work = dict(flops=4 * cases * schur_inverse.size, moved=2 * schur_inverse.size)

    fetch = [
        pltpu.VMEM(schur_inverse.shape, BF16),
        pltpu.SemaphoreType.DMA((subs * (iface // CHUNK),)),
    ]
    tables = pltpu.VMEM((subs, face, face), BF16)
    row = pltpu.VMEM((cases + cases // 2, rounded_up(column + 2 * cases, LANES)), F32)

    shard = coarse_inverse.reshape(column, groups * corners)
    shards = [swapped(shard, "sub", j) for j in range(1, chain)]

    lane = np.arange(along)
    inner = lane % wide
    source = (inner // corners * groups + lane // wide) * corners + inner % corners
    regroup = jnp.asarray(np.where(inner < column, source, -1)[None].astype(np.int32))

    bits = []
    if groups == 1 << 3 and (column * groups) ** 2 <= schur_inverse.size:
        bits = [1 << b for b in reversed(range(groups.bit_length() - 1))]

    small = [face_order, regroup, shard, corner_coupling, corner_dofs, load_cases]
    near = [pltpu.VMEM(x.shape, x.dtype) for x in small]
    (sent0,) = call(
        functools.partial(corner_kernel, chain=chain, groups=groups),
        [((devices, cases, wide), BF16)],
        [load_cases, corner_coupling, corner_dofs],
        [near[5], near[3], near[4], pltpu.SemaphoreType.DMA((3,))],
        far=3,
    )
    received0 = everywhere(sent0, ("sub", "coarse"))
    packet = (cases + rounded_up(corners, 16), face + wide)
    displaced0, first, second, kernel = call(
        functools.partial(first_kernel, chain=chain, groups=groups),
        [
            ((subs, cases, iface), F32),
            (packet, BF16),
            (packet, BF16),
            ((column, along), BF16),
        ],
        [schur_inverse, *small, *shards],
        [*fetch, *near, pltpu.SemaphoreType.DMA((len(small),))],
        far=1 + len(small),
        **work,
    )
    first, second = pair_swaps(first, second)
    other = swapped(kernel, "coarse", bits[0]) if bits else kernel
    lifts, lifts_left, pull0, pull0_left, sent1, *joined = call(
        functools.partial(lift_kernel, chain=chain, groups=groups),
        [
            ((subs, column, iface), BF16),
            ((subs, column, face), BF16),
            ((subs, cases, iface), F32),
            ((subs, cases, face), F32),
            ((devices, cases, rounded_up(column + 2 * cases, LANES)), BF16),
        ]
        + [((2 * column, along), BF16)] * bool(bits),
        [displaced0, first, second, received0, kernel, other]
        + [corner_coupling, corner_dofs, face_order],
        [tables, pltpu.VMEM((cases, rounded_up(column + 2 * cases, LANES)), F32)],
        flops=10**9,
        moved=10**6,
    )
    received1 = everywhere(sent1, ("sub", "coarse"))
    displaced1, first, second = call(
        second_kernel,
        [((subs, cases, iface), F32), ((cases, face), BF16), ((cases, face), BF16)],
        [schur_inverse, pull0, face_order],
        fetch,
        far=1,
        **work,
    )
    first, second = pair_swaps(first, second)

    low = joined[0] if bits else kernel
    high = swapped(low, "coarse", bits[1]) if bits else kernel
    pull1, bent2, after, sent2, norms0, *joined = call(
        functools.partial(third_kernel, groups=groups),
        [
            ((subs, cases, face), F32),
            ((subs, cases, face), F32),
            ((cases, face), BF16),
            ((devices, cases + cases // 2, rounded_up(column + 2 * cases, LANES)), BF16),
            ((cases, cases), F32),
        ]
        + [((4 * column, along), BF16)] * bool(bits),
        [schur_inverse, displaced1, first, second, received1, kernel, lifts, pull0_left]
        + [face_order, low, high],
        [*fetch, tables, row],
        far=1,
        **work,
    )
    received2 = everywhere(sent2, ("sub", "coarse"))
    first, second = pair_swaps(after, after)
    if bits:
        blocks = [joined[0], swapped(joined[0], "coarse", bits[2])]
        slots = [0, bits[0], bits[1], bits[0] ^ bits[1]]
        slots = slots + [slot ^ bits[2] for slot in slots]
    else:
        slots = []
        sums = received2.reshape((chain, groups) + received2.shape[1:])[..., :cases, :wide]
        sums = jnp.sum(sums.astype(F32), axis=0)
        flat = jnp.moveaxis(sums, 0, 1).reshape(cases, along)
        own = lax.dynamic_index_in_dim(sums, lax.axis_index("coarse"), 0, keepdims=False)
        values = jnp.dot(flat, kernel.astype(F32).T, precision=lax.Precision.HIGHEST)
        energy = jnp.dot(values, own[:, :column].T, precision=lax.Precision.HIGHEST)
        blocks = [lax.psum(energy, "coarse")]
    multipliers, residual = call(
        functools.partial(scene_kernel, groups=groups, pieces=len(blocks), slots=slots),
        [((subs, scenes, face), F32), ((subs, scenes, face), F32)],
        [bent2, first, second, received2, joined[0] if bits else kernel, lifts_left, pull0_left]
        + [pull1, face_order, norms0]
        + [scene_loads.T, scene_weights.T, *blocks],
        [pltpu.VMEM((groups, cases, wide), F32), pltpu.VMEM((cases, along), F32), row],
        flops=10**9,
        moved=4 * 10**6,
    )
    return (multipliers, residual)


def solution(mesh):
    return jax.shard_map(
        per_device,
        mesh=mesh,
        in_specs=(
            P(("sub", "coarse"), None, None),
            P(("sub", "coarse"), None, None),
            P(None, "coarse", None, "sub"),
            P(("sub", "coarse"), None, None),
            P(("sub", "coarse"), None),
            P(("sub", "coarse"), None),
            P(),
            P(),
        ),
        out_specs=(P(("sub", "coarse"), None, None), P(("sub", "coarse"), None, None)),
        check_vma=False,
    )
```

```python
import functools

import jax
import jax.numpy as jnp
import numpy as np
from jax import lax
from jax.experimental import pallas as pl
from jax.experimental.pallas import tpu as pltpu
from jax.sharding import PartitionSpec as P

LANES = 128
CHUNK = 256
F32, BF16 = jnp.float32, jnp.bfloat16


def nn(a, b):
    return lax.dot_general(a, b, (((1,), (0,)), ((), ())), preferred_element_type=F32)


def nt(a, b):
    return lax.dot_general(a, b, (((1,), (1,)), ((), ())), preferred_element_type=F32)


def halves(x):
    high = x.astype(BF16)
    return high, (x - high.astype(F32)).astype(BF16)


def stacked(x):
    return jnp.concatenate(halves(x), axis=0)


def folded(x):
    rows = x.shape[0] // 2
    return x[:rows] + x[rows:]


def nn2(x, narrow):
    return folded(nn(stacked(x), narrow))


def nt2(x, narrow):
    return folded(nt(stacked(x), narrow))


def both3(product, x, y):
    high, low = halves(y)
    return folded(product(stacked(x), high)) + product(x.astype(BF16), low)


def equal(a, b):
    return jnp.where(a == b, 1.0, 0.0).astype(BF16)


def iota(shape, dim):
    return lax.broadcasted_iota(jnp.int32, shape, dim)


def rounded_up(value, unit):
    return (value + unit - 1) // unit * unit


def table(order_row):
    size = order_row.shape[1]
    return equal(iota((size, size), 0), order_row)


def back_table(order, n):
    subs, size = order.shape
    rows = jnp.concatenate(
        [order[...].astype(F32), jnp.zeros((rounded_up(subs, 8) - subs, size), F32)], axis=0
    )
    return equal(rows.T[:, n : n + 1].astype(jnp.int32), iota((size, size), 1))


def fill_tables(tables, backs, order):
    for n in range(tables.shape[0]):
        tables[n] = table(order[n : n + 1])
        if n > 0:
            backs[n - 1] = back_table(order, n)


def spread_of(dofs_row, chain, corners, groups):
    column = chain * corners
    ids = iota((column, 1), 0)
    slot = sum((ids >= t * corners).astype(jnp.int32) for t in range(1, chain))
    target = ids + slot * ((groups - 1) * corners) + lax.axis_index("coarse") * corners
    return equal(target, dofs_row)


def placed(x, width, at):
    rows = x.shape[1]
    return nn(x, equal(iota((rows, width), 0) + at, iota((rows, width), 1)))


def by_parity(to_after, to_before):
    odd = (lax.axis_index("sub") & 1) == 1
    return jnp.where(odd, to_before, to_after), jnp.where(odd, to_after, to_before)


def start_fetch(matrix, held, sems):
    subs, size = matrix.shape[0], matrix.shape[1]
    copies = []
    for n in range(subs):
        for k in range(size // CHUNK):
            part = pl.ds(k * CHUNK, CHUNK)
            copy = pltpu.make_async_copy(
                matrix.at[n, part], held.at[n, part], sems.at[n * (size // CHUNK) + k]
            )
            copy.start()
            copies.append(copy)
    return copies


def times_matrix(x, n, held, copies):
    size = held.shape[1]
    count = size // CHUNK
    total = None
    for k in range(count):
        copies[n * count + k].wait()
        part = nn(x[:, k * CHUNK : (k + 1) * CHUNK], held[n, k * CHUNK : (k + 1) * CHUNK])
        total = part if total is None else total + part
    return total


def jumped(displaced, tables, backs, from_before, from_after):
    subs = len(displaced)
    face = tables.shape[1]
    at_head = lax.axis_index("sub") == 0
    at_tail = lax.axis_index("sub") == lax.axis_size("sub") - 1
    result = []
    for n in range(subs):
        own = tables[n]
        before = nn(from_before, own) if n == 0 else nn2(displaced[n - 1][:, face:], own)
        left = displaced[n][:, :face] - before
        if n == 0:
            left = jnp.where(at_head, 0.0, left)
        if n == subs - 1:
            right = displaced[n][:, face:] - from_after
            right = jnp.where(at_tail, 0.0, right)
        else:
            right = displaced[n][:, face:] - nn2(displaced[n + 1][:, :face], backs[n])
        result.append(jnp.concatenate([left, right], axis=1))
    return result


def chain_sums(received, groups, width):
    chain = received.shape[0] // groups
    sums = []
    for c in range(groups):
        total = None
        for z in range(chain):
            part = received[z * groups + c, :, :width].astype(F32)
            total = part if total is None else total + part
        sums.append(total)
    return sums


def copies_of(out, x):
    for i in range(out.shape[0]):
        out[i] = x


def fetched(pairs, sems):
    copies = [pltpu.make_async_copy(a, b, sems.at[i]) for i, (a, b) in enumerate(pairs)]
    for copy in copies:
        copy.start()
    return copies


def corner_kernel(loads_far, coupling_far, dofs_far, out, loads, coupling, dofs, sems, *, chain, groups):
    pairs = [(dofs_far, dofs), (coupling_far, coupling), (loads_far, loads)]
    for copy in fetched(pairs, sems):
        copy.wait()
    corners = coupling.shape[1]
    total = None
    for n in range(loads.shape[0]):
        terms = nt(loads[n], coupling[n])
        part = nt2(terms, spread_of(dofs[n : n + 1], chain, corners, groups))
        total = part if total is None else total + part
    copies_of(out, placed(total.astype(BF16), out.shape[2], 0).astype(BF16))


def first_kernel(matrix, *refs, chain, groups):
    far, shards, refs = refs[:6], refs[6 : 5 + chain], refs[5 + chain :]
    out, first, second, kernel, held, sems, *near_refs, small = refs
    small_copies = fetched(list(zip(far, near_refs)), small)
    copies = start_fetch(matrix, held, sems)
    for copy in small_copies:
        copy.wait()
    order, regroup, shard, coupling, dofs, loads = near_refs
    subs, cases, iface = loads.shape
    corners, face = coupling.shape[1], order.shape[1]
    pad = rounded_up(corners, 16) - corners

    def packet(displaced, coupled, n):
        spread = spread_of(dofs[n : n + 1], chain, corners, groups)
        eye = equal(iota((corners, corners), 0), iota((corners, corners), 1))
        hot = placed(nt(eye, spread).astype(BF16), first.shape[1] - face, 0)
        lower = jnp.concatenate([coupled, hot], axis=1)
        upper = jnp.concatenate([displaced, jnp.zeros((cases, hot.shape[1]), F32)], axis=1)
        return jnp.concatenate([upper, lower, jnp.zeros((pad, lower.shape[1]), F32)], axis=0)

    for n in range(subs):
        out[n] = times_matrix(loads[n], n, held, copies)
        if n == 0:
            both = jnp.concatenate(
                [out[0, :, :face], coupling[0, :, :face].astype(F32)], axis=0
            ).astype(BF16)
            both = nn(both, back_table(order, 0))
            to_before = packet(both[:cases], both[cases:], 0)
            position = lax.axis_index("sub")
            depth = groups * corners
            rows = None
            for j, block in enumerate([shard, *shards]):
                ids = iota((depth, regroup.shape[1]), 0) + (position ^ j) * depth
                part = nn(block[...], equal(ids, regroup[...]))
                rows = part if rows is None else rows + part
            kernel[...] = rows.astype(BF16)
    last = subs - 1
    to_after = packet(out[last, :, face:], coupling[last, :, face:].astype(F32), last)
    one, two = by_parity(to_after, to_before)
    first[...] = one.astype(BF16)
    second[...] = two.astype(BF16)


def lift_kernel(
    displaced, first, second, received, kernel, other, coupling, dofs, order,
    lifts, lifts_left, pull, pull_left, out, *joined, chain, groups
):
    *joined, tables, backs, row = joined
    fill_tables(tables, backs, order)
    subs, cases, _ = displaced.shape
    corners, face = coupling.shape[1], tables.shape[1]
    column = chain * corners
    wide = rounded_up(column, LANES)
    position = lax.axis_index("sub")
    join(joined, kernel, other)

    from_after, from_before = by_parity(first[...].astype(F32), second[...].astype(F32))
    eye = equal(iota((column, first.shape[1] - face), 0), iota((column, first.shape[1] - face), 1))

    def neighbour(block):
        low = block[cases:].astype(BF16)
        return low[:, :face], nt(eye, low[:, face:]).astype(BF16)

    before_coupling, before_spread = neighbour(from_before)
    after_coupling, after_spread = neighbour(from_after)
    spreads = [spread_of(dofs[n : n + 1], chain, corners, groups) for n in range(subs)]
    at_head, at_tail = position == 0, position == chain - 1
    lifted = []
    for n in range(subs):
        own = tables[n]
        if n == 0:
            moved = nn(before_spread, nn(before_coupling, own).astype(BF16))
        else:
            moved = nn(spreads[n - 1], nn(coupling[n - 1, :, face:], own).astype(BF16))
        left = nn(spreads[n], coupling[n, :, :face]) - moved
        if n == 0:
            left = jnp.where(at_head, 0.0, left)
        if n == subs - 1:
            back = nn(after_spread, after_coupling)
        else:
            back = nn(
                spreads[n + 1], nn(coupling[n + 1, :, :face], backs[n]).astype(BF16)
            )
        right = nn(spreads[n], coupling[n, :, face:]) - back
        if n == subs - 1:
            right = jnp.where(at_tail, 0.0, right)
        lifted.append(jnp.concatenate([left, right], axis=1).astype(BF16))
        lifts[n] = lifted[n]
        lifts_left[n] = lifted[n][:, :face]

    flat = jnp.concatenate(chain_sums(received, groups, wide), axis=1)
    values = nt2(flat, kernel[...])
    bent = jumped(
        [displaced[n] for n in range(subs)],
        tables,
        backs,
        from_before[:cases, :face].astype(BF16),
        from_after[:cases, :face],
    )
    corner, norms = None, None
    for n in range(subs):
        whole = bent[n] + nn2(values, lifted[n])
        pull[n] = whole
        left = whole[:, :face]
        pull_left[n] = left
        part, norm = nt2(left, lifted[n][:, :face]), both3(nt, left, left)
        corner = part if corner is None else corner + part
        norms = norm if norms is None else norms + norm
    row[...] = jnp.zeros(row.shape, F32)
    row[:, :column] = corner
    store_halves(row, norms, slice(0, cases), column)
    copies_of(out, row[...].astype(BF16))


def join(out, low, high):
    for ref in out:
        ref[: low.shape[0]] = low[...]
        ref[low.shape[0] :] = high[...]


def store_halves(row, gram, rows, at):
    for half in halves(gram):
        row[rows, at : at + gram.shape[1]] = half.astype(F32)
        at += gram.shape[1]


def sum_halves(row, rows, at, count):
    return row[rows, at : at + count] + row[rows, at + count : at + 2 * count]


def second_kernel(matrix, pull, order, out, first, second, held, sems):
    copies = start_fetch(matrix, held, sems)
    subs = pull.shape[0]
    face = order.shape[1]
    near = back_table(order, 0)
    for n in range(subs):
        out[n] = folded(times_matrix(stacked(pull[n]), n, held, copies))
    one, two = by_parity(out[subs - 1, :, face:], nn2(out[0, :, :face], near))
    first[...] = one.astype(BF16)
    second[...] = two.astype(BF16)


def third_kernel(
    matrix, displaced, first, second, received, kernel, lifts, pull0, order, low, high, *refs, groups
):
    pull, bent2, after, payload, norms0, *joined, held, sems, tables, backs, row = refs
    copies = start_fetch(matrix, held, sems)
    fill_tables(tables, backs, order)
    join(joined, low, high)
    subs, cases, _ = displaced.shape
    face = tables.shape[1]
    column = lifts.shape[1]
    wide = rounded_up(column, LANES)
    from_after, from_before = by_parity(first[...].astype(F32), second[...].astype(F32))
    sums = chain_sums(received, groups, received.shape[2])
    flat = jnp.concatenate([part[:, :wide] for part in sums], axis=1)
    values = nt2(flat, kernel[...])
    row[:cases] = sum(sums)
    norms0[...] = sum_halves(row, slice(0, cases), column, cases)
    bent = jumped(
        [displaced[n] for n in range(subs)], tables, backs, from_before.astype(BF16), from_after
    )
    totals = None
    for n in range(subs):
        whole = bent[n] + nn2(values, lifts[n])
        left = whole[:, :face]
        pull[n] = left
        moved = folded(times_matrix(stacked(whole), n, held, copies))
        bent2[n] = moved[:, :face]
        if n > 0:
            bent2[n] = moved[:, :face] - nn2(previous, tables[n])
        previous = moved[:, face:]
        parts = [
            nt2(left, lifts[n, :, :face]),
            both3(nt, pull0[n], left),
            both3(nt, left, left),
            both3(nt, whole, moved),
        ]
        totals = parts if totals is None else [a + b for a, b in zip(totals, parts)]
    after[...] = previous.astype(BF16)
    corner, gram1, gram2, gram3 = totals
    row[...] = jnp.zeros(row.shape, F32)
    row[:cases, :column] = corner
    store_halves(row, gram1, slice(0, cases), column)
    step = cases // 2
    for j in range(2):
        for i, gram in enumerate((gram2, gram3)):
            part = gram[j * step : (j + 1) * step]
            store_halves(row, part, slice(cases, cases + step), (4 * j + 2 * i) * cases)
    copies_of(payload, row[...].astype(BF16))


def scene_kernel(
    bent, first, second, received, kernel, lifts, pull0, pull1, order, norms0,
    scene_loads, scene_weights, *refs, groups, pieces, slots
):
    blocks = refs[:pieces]
    multipliers, residual, held, row = refs[pieces:]
    subs, cases, _ = bent.shape
    column = lifts.shape[1]
    wide = rounded_up(column, LANES)
    group = lax.axis_index("coarse")
    sums = chain_sums(received, groups, received.shape[2])
    for c in range(groups):
        held[c] = sums[c][:cases, :wide]
    flat = jnp.concatenate([held[c] for c in range(groups)], axis=1)
    values = nt2(flat, kernel[:column])
    if groups_whole(blocks, column, groups):
        lifted, index = None, iter(slots)
        for block in blocks:
            for i in range(block.shape[0] // column):
                sums_here = held[group ^ next(index)][:, :column]
                part = nn2(sums_here, block[i * column : (i + 1) * column])
                lifted = part if lifted is None else lifted + part
        energy = both3(nt, lifted, flat)
    else:
        energy = blocks[0][...]
    row[...] = sum(sums)
    norms1 = sum_halves(row, slice(0, cases), column, cases)
    lower = slice(cases, cases + cases // 2)
    norms2, norms3 = (
        jnp.concatenate(
            [sum_halves(row, lower, (4 * j + 2 * i) * cases, cases) for j in range(2)], axis=0
        )
        for i in range(2)
    )
    norms3 = norms3 + energy

    ids = iota((cases, scene_loads.shape[1]), 0)
    mixing = sum(
        jnp.where(ids == scene_loads[i : i + 1], scene_weights[i : i + 1], 0.0)
        for i in range(scene_loads.shape[0])
    )

    def moment(norms):
        return jnp.sum(both3(nn, norms, mixing) * mixing, axis=0, keepdims=True)

    moment0, moment1 = moment(norms0[...]), moment(norms1)
    moment2, moment3 = moment(norms2), moment(norms3)
    step0 = moment0 / moment1
    norm1 = moment0 - 2.0 * step0 * moment1 + step0 * step0 * moment2
    grow = 1.0 + norm1 / moment0
    curvature = grow * grow * moment1 - 2.0 * grow * step0 * moment2 + step0 * step0 * moment3
    step1 = norm1 / curvature
    zeros = jnp.zeros_like(mixing)

    def transposed(parts):
        weights = -jnp.concatenate(parts, axis=0)
        high = weights.astype(BF16).astype(F32)
        return jnp.concatenate([high, high, weights - high], axis=0).T.astype(BF16)

    for_multipliers = transposed(
        [(step0 + step1 * grow) * mixing, (-step0 * step1) * mixing, zeros]
    )
    for_residual = transposed(
        [mixing, (-step0 - step1 * grow) * mixing, (step0 * step1) * mixing]
    )
    _, from_before = by_parity(first[...].astype(F32), second[...].astype(F32))
    for n in range(subs):
        pull2 = bent[n]
        if n == 0:
            pull2 = pull2 - nn(from_before.astype(BF16), table(order[0:1]))
            pull2 = jnp.where(lax.axis_index("sub") == 0, 0.0, pull2)
        pull2 = pull2 + nn2(values, lifts[n])
        basis = jnp.concatenate([pull0[n], pull1[n], pull2], axis=0)
        high, low = halves(basis)
        basis = jnp.concatenate([high, low, high], axis=0)
        multipliers[n] = nn(for_multipliers, basis)
        residual[n] = nn(for_residual, basis)


def groups_whole(blocks, column, groups):
    return sum(block.shape[0] for block in blocks) == column * groups


def everywhere(x, axes):
    return lax.all_to_all(x, axes, 0, 0)


def swapped(x, axis, bit):
    return lax.ppermute(x, axis, [(i, i ^ bit) for i in range(lax.axis_size(axis))])


def pair_swaps(first, second):
    length = lax.axis_size("sub")
    one = lax.ppermute(first, "sub", [(i, i ^ 1) for i in range(length)])
    two = lax.ppermute(
        second, "sub", [(i, (i + 1 if i & 1 else i - 1) % length) for i in range(length)]
    )
    return one, two


def call(kernel, outs, args, scratch=(), flops=0, moved=0, far=0):
    specs = [pl.BlockSpec(memory_space=pltpu.HBM)] * far
    specs += [pl.BlockSpec(memory_space=pltpu.VMEM)] * (len(args) - far)
    pinned = [pltpu.with_memory_space_constraint(x, pltpu.HBM) for x in args[:far]]
    shapes = [jax.ShapeDtypeStruct(shape, kind) for shape, kind in outs]
    return pl.pallas_call(
        kernel,
        out_shape=shapes,
        in_specs=specs,
        out_specs=[pl.BlockSpec(memory_space=pltpu.VMEM)] * len(outs),
        scratch_shapes=list(scratch),
        compiler_params=pltpu.CompilerParams(vmem_limit_bytes=32 << 20),
        cost_estimate=pl.CostEstimate(flops=flops, bytes_accessed=moved, transcendentals=0),
    )(*pinned, *args[far:])


def per_device(
    schur_inverse,
    corner_coupling,
    coarse_inverse,
    load_cases,
    face_order,
    corner_dofs,
    scene_loads,
    scene_weights,
):
    subs, iface = schur_inverse.shape[0], schur_inverse.shape[1]
    face = face_order.shape[1]
    corners = corner_dofs.shape[1]
    cases = load_cases.shape[1]
    scenes = scene_loads.shape[0]
    chain, groups = lax.axis_size("sub"), lax.axis_size("coarse")
    devices = chain * groups
    column = chain * corners
    wide = rounded_up(column, LANES)
    along = groups * wide
    work = dict(flops=4 * cases * schur_inverse.size, moved=2 * schur_inverse.size)

    fetch = [
        pltpu.VMEM(schur_inverse.shape, BF16),
        pltpu.SemaphoreType.DMA((subs * (iface // CHUNK),)),
    ]
    tables = [
        pltpu.VMEM((subs, face, face), BF16), pltpu.VMEM((max(subs - 1, 1), face, face), BF16)
    ]
    row = pltpu.VMEM((cases + cases // 2, rounded_up(column + 2 * cases, LANES)), F32)

    shard = coarse_inverse.reshape(column, groups * corners)
    shards = [swapped(shard, "sub", j) for j in range(1, chain)]

    lane = np.arange(along)
    inner = lane % wide
    source = (inner // corners * groups + lane // wide) * corners + inner % corners
    regroup = jnp.asarray(np.where(inner < column, source, -1)[None].astype(np.int32))

    bits = []
    if groups == 1 << 3 and (column * groups) ** 2 <= schur_inverse.size:
        bits = [1 << b for b in reversed(range(groups.bit_length() - 1))]

    small = [face_order, regroup, shard, corner_coupling, corner_dofs, load_cases]
    near = [pltpu.VMEM(x.shape, x.dtype) for x in small]
    (sent0,) = call(
        functools.partial(corner_kernel, chain=chain, groups=groups),
        [((devices, cases, wide), BF16)],
        [load_cases, corner_coupling, corner_dofs],
        [near[5], near[3], near[4], pltpu.SemaphoreType.DMA((3,))],
        far=3,
    )
    received0 = everywhere(sent0, ("sub", "coarse"))
    packet = (cases + rounded_up(corners, 16), face + wide)
    displaced0, first, second, kernel = call(
        functools.partial(first_kernel, chain=chain, groups=groups),
        [
            ((subs, cases, iface), F32),
            (packet, BF16),
            (packet, BF16),
            ((column, along), BF16),
        ],
        [schur_inverse, *small, *shards],
        [*fetch, *near, pltpu.SemaphoreType.DMA((len(small),))],
        far=1 + len(small),
        **work,
    )
    first, second = pair_swaps(first, second)
    other = swapped(kernel, "coarse", bits[0]) if bits else kernel
    lifts, lifts_left, pull0, pull0_left, sent1, *joined = call(
        functools.partial(lift_kernel, chain=chain, groups=groups),
        [
            ((subs, column, iface), BF16),
            ((subs, column, face), BF16),
            ((subs, cases, iface), F32),
            ((subs, cases, face), F32),
            ((devices, cases, rounded_up(column + 2 * cases, LANES)), BF16),
        ]
        + [((2 * column, along), BF16)] * bool(bits),
        [displaced0, first, second, received0, kernel, other]
        + [corner_coupling, corner_dofs, face_order],
        [*tables, pltpu.VMEM((cases, rounded_up(column + 2 * cases, LANES)), F32)],
        flops=10**9,
        moved=10**6,
    )
    received1 = everywhere(sent1, ("sub", "coarse"))
    displaced1, first, second = call(
        second_kernel,
        [((subs, cases, iface), F32), ((cases, face), BF16), ((cases, face), BF16)],
        [schur_inverse, pull0, face_order],
        fetch,
        far=1,
        **work,
    )
    first, second = pair_swaps(first, second)

    low = joined[0] if bits else kernel
    high = swapped(low, "coarse", bits[1]) if bits else kernel
    pull1, bent2, after, sent2, norms0, *joined = call(
        functools.partial(third_kernel, groups=groups),
        [
            ((subs, cases, face), F32),
            ((subs, cases, face), F32),
            ((cases, face), BF16),
            ((devices, cases + cases // 2, rounded_up(column + 2 * cases, LANES)), BF16),
            ((cases, cases), F32),
        ]
        + [((4 * column, along), BF16)] * bool(bits),
        [schur_inverse, displaced1, first, second, received1, kernel, lifts, pull0_left]
        + [face_order, low, high],
        [*fetch, *tables, row],
        far=1,
        **work,
    )
    received2 = everywhere(sent2, ("sub", "coarse"))
    first, second = pair_swaps(after, after)
    if bits:
        blocks = [joined[0], swapped(joined[0], "coarse", bits[2])]
        slots = [0, bits[0], bits[1], bits[0] ^ bits[1]]
        slots = slots + [slot ^ bits[2] for slot in slots]
    else:
        slots = []
        sums = received2.reshape((chain, groups) + received2.shape[1:])[..., :cases, :wide]
        sums = jnp.sum(sums.astype(F32), axis=0)
        flat = jnp.moveaxis(sums, 0, 1).reshape(cases, along)
        own = lax.dynamic_index_in_dim(sums, lax.axis_index("coarse"), 0, keepdims=False)
        values = jnp.dot(flat, kernel.astype(F32).T, precision=lax.Precision.HIGHEST)
        energy = jnp.dot(values, own[:, :column].T, precision=lax.Precision.HIGHEST)
        blocks = [lax.psum(energy, "coarse")]
    multipliers, residual = call(
        functools.partial(scene_kernel, groups=groups, pieces=len(blocks), slots=slots),
        [((subs, scenes, face), F32), ((subs, scenes, face), F32)],
        [bent2, first, second, received2, joined[0] if bits else kernel, lifts_left, pull0_left]
        + [pull1, face_order, norms0]
        + [scene_loads.T, scene_weights.T, *blocks],
        [pltpu.VMEM((groups, cases, wide), F32), row],
        flops=10**9,
        moved=4 * 10**6,
    )
    return (multipliers, residual)


def solution(mesh):
    return jax.shard_map(
        per_device,
        mesh=mesh,
        in_specs=(
            P(("sub", "coarse"), None, None),
            P(("sub", "coarse"), None, None),
            P(None, "coarse", None, "sub"),
            P(("sub", "coarse"), None, None),
            P(("sub", "coarse"), None),
            P(("sub", "coarse"), None),
            P(),
            P(),
        ),
        out_specs=(P(("sub", "coarse"), None, None), P(("sub", "coarse"), None, None)),
        check_vma=False,
    )
```

```python
import functools

import jax
import jax.numpy as jnp
import numpy as np
from jax import lax
from jax.experimental import pallas as pl
from jax.experimental.pallas import tpu as pltpu
from jax.sharding import PartitionSpec as P

LANES = 128
CHUNK = 256
F32, BF16 = jnp.float32, jnp.bfloat16


def nn(a, b):
    return lax.dot_general(a, b, (((1,), (0,)), ((), ())), preferred_element_type=F32)


def nt(a, b):
    return lax.dot_general(a, b, (((1,), (1,)), ((), ())), preferred_element_type=F32)


def halves(x):
    high = x.astype(BF16)
    return high, (x - high.astype(F32)).astype(BF16)


def stacked(x):
    return jnp.concatenate(halves(x), axis=0)


def folded(x):
    rows = x.shape[0] // 2
    return x[:rows] + x[rows:]


def nn2(x, narrow):
    return folded(nn(stacked(x), narrow))


def nt2(x, narrow):
    return folded(nt(stacked(x), narrow))


def both3(product, x, y):
    high, low = halves(y)
    return folded(product(stacked(x), high)) + product(x.astype(BF16), low)


def equal(a, b):
    return jnp.where(a == b, 1.0, 0.0).astype(BF16)


def iota(shape, dim):
    return lax.broadcasted_iota(jnp.int32, shape, dim)


def rounded_up(value, unit):
    return (value + unit - 1) // unit * unit


def table(order_row):
    size = order_row.shape[1]
    return equal(iota((size, size), 0), order_row)


def back_table(order, n):
    subs, size = order.shape
    rows = jnp.concatenate(
        [order[...].astype(F32), jnp.zeros((rounded_up(subs, 8) - subs, size), F32)], axis=0
    )
    return equal(rows.T[:, n : n + 1].astype(jnp.int32), iota((size, size), 1))


def fill_tables(tables, backs, order):
    for n in range(tables.shape[0]):
        tables[n] = table(order[n : n + 1])
        if n > 0:
            backs[n - 1] = back_table(order, n)


def spread_of(dofs_row, chain, corners, groups):
    column = chain * corners
    ids = iota((column, 1), 0)
    slot = sum((ids >= t * corners).astype(jnp.int32) for t in range(1, chain))
    target = ids + slot * ((groups - 1) * corners) + lax.axis_index("coarse") * corners
    return equal(target, dofs_row)


def placed(x, width, at):
    rows = x.shape[1]
    return nn(x, equal(iota((rows, width), 0) + at, iota((rows, width), 1)))


def by_parity(to_after, to_before):
    odd = (lax.axis_index("sub") & 1) == 1
    return jnp.where(odd, to_before, to_after), jnp.where(odd, to_after, to_before)


def start_fetch(matrix, held, sems):
    subs, size = matrix.shape[0], matrix.shape[1]
    copies = []
    for n in range(subs):
        for k in range(size // CHUNK):
            part = pl.ds(k * CHUNK, CHUNK)
            copy = pltpu.make_async_copy(
                matrix.at[n, part], held.at[n, part], sems.at[n * (size // CHUNK) + k]
            )
            copy.start()
            copies.append(copy)
    return copies


def times_matrix(x, n, held, copies):
    size = held.shape[1]
    count = size // CHUNK
    total = None
    for k in range(count):
        copies[n * count + k].wait()
        part = nn(x[:, k * CHUNK : (k + 1) * CHUNK], held[n, k * CHUNK : (k + 1) * CHUNK])
        total = part if total is None else total + part
    return total


def inner_jump(displaced, tables, backs):
    subs = len(displaced)
    face = tables.shape[1]
    lefts = [part[:, :face] for part in displaced]
    rights = [part[:, face:] for part in displaced]
    for n in range(1, subs):
        lefts[n] = lefts[n] - nn2(displaced[n - 1][:, face:], tables[n])
        rights[n - 1] = rights[n - 1] - nn2(displaced[n][:, :face], backs[n - 1])
    return lefts, rights


def outer_jump(lefts, rights, before, after):
    at_head = lax.axis_index("sub") == 0
    at_tail = lax.axis_index("sub") == lax.axis_size("sub") - 1
    lefts = [jnp.where(at_head, 0.0, lefts[0] - before), *lefts[1:]]
    rights = [*rights[:-1], jnp.where(at_tail, 0.0, rights[-1] - after)]
    return [jnp.concatenate(pair, axis=1) for pair in zip(lefts, rights)]


def chain_sums(received, groups, width):
    chain = received.shape[0] // groups
    sums = []
    for c in range(groups):
        total = None
        for z in range(chain):
            part = received[z * groups + c, :, :width].astype(F32)
            total = part if total is None else total + part
        sums.append(total)
    return sums


def copies_of(out, x):
    for i in range(out.shape[0]):
        out[i] = x


def fetched(pairs, sems):
    copies = [pltpu.make_async_copy(a, b, sems.at[i]) for i, (a, b) in enumerate(pairs)]
    for copy in copies:
        copy.start()
    return copies


def corner_kernel(loads_far, coupling_far, dofs_far, out, loads, coupling, dofs, sems, *, chain, groups):
    pairs = [(dofs_far, dofs), (coupling_far, coupling), (loads_far, loads)]
    for copy in fetched(pairs, sems):
        copy.wait()
    corners = coupling.shape[1]
    total = None
    for n in range(loads.shape[0]):
        terms = nt(loads[n], coupling[n])
        part = nt2(terms, spread_of(dofs[n : n + 1], chain, corners, groups))
        total = part if total is None else total + part
    copies_of(out, placed(total.astype(BF16), out.shape[2], 0).astype(BF16))


def first_kernel(matrix, *refs, chain, groups):
    far, (out, first, second, held, sems, *near_refs, small) = refs[:4], refs[4:]
    small_copies = fetched(list(zip(far, near_refs)), small)
    copies = start_fetch(matrix, held, sems)
    for copy in small_copies:
        copy.wait()
    order, coupling, dofs, loads = near_refs
    subs, cases, iface = loads.shape
    corners, face = coupling.shape[1], order.shape[1]
    pad = rounded_up(corners, 16) - corners

    def packet(displaced, coupled, n):
        spread = spread_of(dofs[n : n + 1], chain, corners, groups)
        eye = equal(iota((corners, corners), 0), iota((corners, corners), 1))
        hot = placed(nt(eye, spread).astype(BF16), first.shape[1] - face, 0)
        lower = jnp.concatenate([coupled, hot], axis=1)
        upper = jnp.concatenate([displaced, jnp.zeros((cases, hot.shape[1]), F32)], axis=1)
        return jnp.concatenate([upper, lower, jnp.zeros((pad, lower.shape[1]), F32)], axis=0)

    for n in range(subs):
        out[n] = times_matrix(loads[n], n, held, copies)
        if n == 0:
            near = table(order[0:1])
            to_before = packet(
                nt(out[0, :, :face].astype(BF16), near), nt(coupling[0, :, :face], near), 0
            )
    last = subs - 1
    to_after = packet(out[last, :, face:], coupling[last, :, face:].astype(F32), last)
    one, two = by_parity(to_after, to_before)
    first[...] = one.astype(BF16)
    second[...] = two.astype(BF16)


def inner_kernel(
    displaced, coupling, dofs, order, regroup, *refs, chain, groups
):
    shards, (kernel, lifts, bent, tables, backs) = refs[:chain], refs[chain:]
    subs, cases, _ = displaced.shape
    corners, face = coupling.shape[1], order.shape[1]
    position = lax.axis_index("sub")
    depth = groups * corners
    rows = None
    for j, block in enumerate(shards):
        ids = iota((depth, regroup.shape[1]), 0) + (position ^ j) * depth
        part = nn(block[...], equal(ids, regroup[...]))
        rows = part if rows is None else rows + part
    kernel[...] = rows.astype(BF16)
    fill_tables(tables, backs, order)
    spreads = [spread_of(dofs[n : n + 1], chain, corners, groups) for n in range(subs)]
    for n in range(subs):
        left, right = nn(spreads[n], coupling[n, :, :face]), nn(spreads[n], coupling[n, :, face:])
        if n > 0:
            moved = nn(coupling[n - 1, :, face:], tables[n]).astype(BF16)
            left = left - nn(spreads[n - 1], moved)
        if n < subs - 1:
            moved = nn(coupling[n + 1, :, :face], backs[n]).astype(BF16)
            right = right - nn(spreads[n + 1], moved)
        lifts[n, :, :face] = left
        lifts[n, :, face:] = right
    lefts, rights = inner_jump([displaced[n] for n in range(subs)], tables, backs)
    for n in range(subs):
        bent[n, :, :face] = lefts[n]
        bent[n, :, face:] = rights[n]


def lift_kernel(
    bent, own_lifts, first, second, received, kernel, other, order,
    lifts, lifts_left, pull, pull_left, out, *refs, groups
):
    *joined, row = refs
    subs, cases, _ = bent.shape
    column, face = own_lifts.shape[1], order.shape[1]
    wide = rounded_up(column, LANES)
    join(joined, kernel, other)
    near = table(order[0:1])
    from_after, from_before = by_parity(first[...].astype(F32), second[...].astype(F32))
    eye = equal(iota((column, first.shape[1] - face), 0), iota((column, first.shape[1] - face), 1))

    def neighbour(block):
        low = block[cases:].astype(BF16)
        return low[:, :face], nt(eye, low[:, face:]).astype(BF16)

    before = nn(from_before[:, :face].astype(BF16), near)
    _, before_spread = neighbour(from_before)
    after_coupling, after_spread = neighbour(from_after)
    lifted = outer_jump(
        [own_lifts[n, :, :face] for n in range(subs)],
        [own_lifts[n, :, face:] for n in range(subs)],
        nn(before_spread, before[cases:].astype(BF16)),
        nn(after_spread, after_coupling),
    )
    bent = outer_jump(
        [bent[n, :, :face] for n in range(subs)],
        [bent[n, :, face:] for n in range(subs)],
        before[:cases],
        from_after[:cases, :face],
    )
    for n in range(subs):
        lifted[n] = lifted[n].astype(BF16)
        lifts[n] = lifted[n]
        lifts_left[n] = lifted[n][:, :face]
    flat = jnp.concatenate(chain_sums(received, groups, wide), axis=1)
    values = nt2(flat, kernel[...])
    corner, norms = None, None
    for n in range(subs):
        whole = bent[n] + nn2(values, lifted[n])
        pull[n] = whole
        left = whole[:, :face]
        pull_left[n] = left
        part, norm = nt2(left, lifted[n][:, :face]), both3(nt, left, left)
        corner = part if corner is None else corner + part
        norms = norm if norms is None else norms + norm
    row[...] = jnp.zeros(row.shape, F32)
    row[:, :column] = corner
    store_halves(row, norms, slice(0, cases), column)
    copies_of(out, row[...].astype(BF16))


def join(out, low, high):
    for ref in out:
        ref[: low.shape[0]] = low[...]
        ref[low.shape[0] :] = high[...]


def store_halves(row, gram, rows, at):
    for half in halves(gram):
        row[rows, at : at + gram.shape[1]] = half.astype(F32)
        at += gram.shape[1]


def sum_halves(row, rows, at, count):
    return row[rows, at : at + count] + row[rows, at + count : at + 2 * count]


def second_kernel(matrix, pull, order, out, first, second, held, sems):
    copies = start_fetch(matrix, held, sems)
    subs = pull.shape[0]
    face = order.shape[1]
    near = back_table(order, 0)
    for n in range(subs):
        out[n] = folded(times_matrix(stacked(pull[n]), n, held, copies))
    one, two = by_parity(out[subs - 1, :, face:], nn2(out[0, :, :face], near))
    first[...] = one.astype(BF16)
    second[...] = two.astype(BF16)


def third_kernel(
    matrix, displaced, first, second, received, kernel, lifts, pull0, order, low, high, *refs, groups
):
    pull, bent2, after, payload, norms0, *joined, held, sems, tables, backs, row = refs
    copies = start_fetch(matrix, held, sems)
    fill_tables(tables, backs, order)
    join(joined, low, high)
    subs, cases, _ = displaced.shape
    face = tables.shape[1]
    column = lifts.shape[1]
    wide = rounded_up(column, LANES)
    from_after, from_before = by_parity(first[...].astype(F32), second[...].astype(F32))
    sums = chain_sums(received, groups, received.shape[2])
    flat = jnp.concatenate([part[:, :wide] for part in sums], axis=1)
    values = nt2(flat, kernel[...])
    row[:cases] = sum(sums)
    norms0[...] = sum_halves(row, slice(0, cases), column, cases)
    lefts, rights = inner_jump([displaced[n] for n in range(subs)], tables, backs)
    bent = outer_jump(lefts, rights, nn(from_before.astype(BF16), tables[0]), from_after)
    totals = None
    for n in range(subs):
        whole = bent[n] + nn2(values, lifts[n])
        left = whole[:, :face]
        pull[n] = left
        moved = folded(times_matrix(stacked(whole), n, held, copies))
        bent2[n] = moved[:, :face]
        if n > 0:
            bent2[n] = moved[:, :face] - nn2(previous, tables[n])
        previous = moved[:, face:]
        parts = [
            nt2(left, lifts[n, :, :face]),
            both3(nt, pull0[n], left),
            both3(nt, left, left),
            both3(nt, whole, moved),
        ]
        totals = parts if totals is None else [a + b for a, b in zip(totals, parts)]
    after[...] = previous.astype(BF16)
    corner, gram1, gram2, gram3 = totals
    row[...] = jnp.zeros(row.shape, F32)
    row[:cases, :column] = corner
    store_halves(row, gram1, slice(0, cases), column)
    step = cases // 2
    for j in range(2):
        for i, gram in enumerate((gram2, gram3)):
            part = gram[j * step : (j + 1) * step]
            store_halves(row, part, slice(cases, cases + step), (4 * j + 2 * i) * cases)
    copies_of(payload, row[...].astype(BF16))


def scene_kernel(
    bent, first, second, received, kernel, lifts, pull0, pull1, order, norms0,
    scene_loads, scene_weights, *refs, groups, pieces, slots
):
    blocks = refs[:pieces]
    multipliers, residual, held, row = refs[pieces:]
    subs, cases, _ = bent.shape
    column = lifts.shape[1]
    wide = rounded_up(column, LANES)
    group = lax.axis_index("coarse")
    sums = chain_sums(received, groups, received.shape[2])
    for c in range(groups):
        held[c] = sums[c][:cases, :wide]
    flat = jnp.concatenate([held[c] for c in range(groups)], axis=1)
    values = nt2(flat, kernel[:column])
    if groups_whole(blocks, column, groups):
        lifted, index = None, iter(slots)
        for block in blocks:
            for i in range(block.shape[0] // column):
                sums_here = held[group ^ next(index)][:, :column]
                part = nn2(sums_here, block[i * column : (i + 1) * column])
                lifted = part if lifted is None else lifted + part
        energy = both3(nt, lifted, flat)
    else:
        energy = blocks[0][...]
    row[...] = sum(sums)
    norms1 = sum_halves(row, slice(0, cases), column, cases)
    lower = slice(cases, cases + cases // 2)
    norms2, norms3 = (
        jnp.concatenate(
            [sum_halves(row, lower, (4 * j + 2 * i) * cases, cases) for j in range(2)], axis=0
        )
        for i in range(2)
    )
    norms3 = norms3 + energy

    ids = iota((cases, scene_loads.shape[1]), 0)
    mixing = sum(
        jnp.where(ids == scene_loads[i : i + 1], scene_weights[i : i + 1], 0.0)
        for i in range(scene_loads.shape[0])
    )

    def moment(norms):
        return jnp.sum(both3(nn, norms, mixing) * mixing, axis=0, keepdims=True)

    moment0, moment1 = moment(norms0[...]), moment(norms1)
    moment2, moment3 = moment(norms2), moment(norms3)
    step0 = moment0 / moment1
    norm1 = moment0 - 2.0 * step0 * moment1 + step0 * step0 * moment2
    grow = 1.0 + norm1 / moment0
    curvature = grow * grow * moment1 - 2.0 * grow * step0 * moment2 + step0 * step0 * moment3
    step1 = norm1 / curvature
    zeros = jnp.zeros_like(mixing)

    def transposed(parts):
        weights = -jnp.concatenate(parts, axis=0)
        high = weights.astype(BF16).astype(F32)
        return jnp.concatenate([high, high, weights - high], axis=0).T.astype(BF16)

    for_multipliers = transposed(
        [(step0 + step1 * grow) * mixing, (-step0 * step1) * mixing, zeros]
    )
    for_residual = transposed(
        [mixing, (-step0 - step1 * grow) * mixing, (step0 * step1) * mixing]
    )
    _, from_before = by_parity(first[...].astype(F32), second[...].astype(F32))
    for n in range(subs):
        pull2 = bent[n]
        if n == 0:
            pull2 = pull2 - nn(from_before.astype(BF16), table(order[0:1]))
            pull2 = jnp.where(lax.axis_index("sub") == 0, 0.0, pull2)
        pull2 = pull2 + nn2(values, lifts[n])
        basis = jnp.concatenate([pull0[n], pull1[n], pull2], axis=0)
        high, low = halves(basis)
        basis = jnp.concatenate([high, low, high], axis=0)
        multipliers[n] = nn(for_multipliers, basis)
        residual[n] = nn(for_residual, basis)


def groups_whole(blocks, column, groups):
    return sum(block.shape[0] for block in blocks) == column * groups


def everywhere(x, axes):
    return lax.all_to_all(x, axes, 0, 0)


def swapped(x, axis, bit):
    return lax.ppermute(x, axis, [(i, i ^ bit) for i in range(lax.axis_size(axis))])


def pair_swaps(first, second, wrap=True):
    length = lax.axis_size("sub")

    def partner(i, j):
        return (i, j % length if wrap or 0 <= j < length else i)

    one = lax.ppermute(first, "sub", [partner(i, i ^ 1) for i in range(length)])
    two = lax.ppermute(
        second, "sub", [partner(i, i + 1 if i & 1 else i - 1) for i in range(length)]
    )
    return one, two


def call(kernel, outs, args, scratch=(), flops=0, moved=0, far=0):
    specs = [pl.BlockSpec(memory_space=pltpu.HBM)] * far
    specs += [pl.BlockSpec(memory_space=pltpu.VMEM)] * (len(args) - far)
    pinned = [pltpu.with_memory_space_constraint(x, pltpu.HBM) for x in args[:far]]
    shapes = [jax.ShapeDtypeStruct(shape, kind) for shape, kind in outs]
    return pl.pallas_call(
        kernel,
        out_shape=shapes,
        in_specs=specs,
        out_specs=[pl.BlockSpec(memory_space=pltpu.VMEM)] * len(outs),
        scratch_shapes=list(scratch),
        compiler_params=pltpu.CompilerParams(vmem_limit_bytes=32 << 20),
        cost_estimate=pl.CostEstimate(flops=flops, bytes_accessed=moved, transcendentals=0),
    )(*pinned, *args[far:])


def per_device(
    schur_inverse,
    corner_coupling,
    coarse_inverse,
    load_cases,
    face_order,
    corner_dofs,
    scene_loads,
    scene_weights,
):
    subs, iface = schur_inverse.shape[0], schur_inverse.shape[1]
    face = face_order.shape[1]
    corners = corner_dofs.shape[1]
    cases = load_cases.shape[1]
    scenes = scene_loads.shape[0]
    chain, groups = lax.axis_size("sub"), lax.axis_size("coarse")
    devices = chain * groups
    column = chain * corners
    wide = rounded_up(column, LANES)
    along = groups * wide
    work = dict(flops=4 * cases * schur_inverse.size, moved=2 * schur_inverse.size)

    fetch = [
        pltpu.VMEM(schur_inverse.shape, BF16),
        pltpu.SemaphoreType.DMA((subs * (iface // CHUNK),)),
    ]
    tables = [
        pltpu.VMEM((subs, face, face), BF16), pltpu.VMEM((max(subs - 1, 1), face, face), BF16)
    ]
    row = pltpu.VMEM((cases + cases // 2, rounded_up(column + 2 * cases, LANES)), F32)

    shard = coarse_inverse.reshape(column, groups * corners)
    shards = [swapped(shard, "sub", j) for j in range(1, chain)]

    lane = np.arange(along)
    inner = lane % wide
    source = (inner // corners * groups + lane // wide) * corners + inner % corners
    regroup = jnp.asarray(np.where(inner < column, source, -1)[None].astype(np.int32))

    bits = []
    if groups == 1 << 3 and (column * groups) ** 2 <= schur_inverse.size:
        bits = [1 << b for b in reversed(range(groups.bit_length() - 1))]

    small = [face_order, corner_coupling, corner_dofs, load_cases]
    near = [pltpu.VMEM(x.shape, x.dtype) for x in small]
    (sent0,) = call(
        functools.partial(corner_kernel, chain=chain, groups=groups),
        [((devices, cases, wide), BF16)],
        [load_cases, corner_coupling, corner_dofs],
        [near[3], near[1], near[2], pltpu.SemaphoreType.DMA((3,))],
        far=3,
    )
    received0 = everywhere(sent0, ("sub", "coarse"))
    packet = (cases + rounded_up(corners, 16), face + wide)
    displaced0, first, second = call(
        functools.partial(first_kernel, chain=chain, groups=groups),
        [((subs, cases, iface), F32), (packet, BF16), (packet, BF16)],
        [schur_inverse, *small],
        [*fetch, *near, pltpu.SemaphoreType.DMA((len(small),))],
        far=1 + len(small),
        **work,
    )
    first, second = pair_swaps(first, second)
    kernel, own_lifts, bent0 = call(
        functools.partial(inner_kernel, chain=chain, groups=groups),
        [((column, along), BF16), ((subs, column, iface), F32), ((subs, cases, iface), F32)],
        [displaced0, corner_coupling, corner_dofs, face_order, regroup, shard, *shards],
        tables,
        flops=10**9,
        moved=2 * 10**6,
    )
    other = swapped(kernel, "coarse", bits[0]) if bits else kernel
    lifts, lifts_left, pull0, pull0_left, sent1, *joined = call(
        functools.partial(lift_kernel, groups=groups),
        [
            ((subs, column, iface), BF16),
            ((subs, column, face), BF16),
            ((subs, cases, iface), F32),
            ((subs, cases, face), F32),
            ((devices, cases, rounded_up(column + 2 * cases, LANES)), BF16),
        ]
        + [((2 * column, along), BF16)] * bool(bits),
        [bent0, own_lifts, first, second, received0, kernel, other, face_order],
        [pltpu.VMEM((cases, rounded_up(column + 2 * cases, LANES)), F32)],
        flops=10**9,
        moved=10**6,
    )
    received1 = everywhere(sent1, ("sub", "coarse"))
    displaced1, first, second = call(
        second_kernel,
        [((subs, cases, iface), F32), ((cases, face), BF16), ((cases, face), BF16)],
        [schur_inverse, pull0, face_order],
        fetch,
        far=1,
        **work,
    )
    first, second = pair_swaps(first, second)

    low = joined[0] if bits else kernel
    high = swapped(low, "coarse", bits[1]) if bits else kernel
    pull1, bent2, after, sent2, norms0, *joined = call(
        functools.partial(third_kernel, groups=groups),
        [
            ((subs, cases, face), F32),
            ((subs, cases, face), F32),
            ((cases, face), BF16),
            ((devices, cases + cases // 2, rounded_up(column + 2 * cases, LANES)), BF16),
            ((cases, cases), F32),
        ]
        + [((4 * column, along), BF16)] * bool(bits),
        [schur_inverse, displaced1, first, second, received1, kernel, lifts, pull0_left]
        + [face_order, low, high],
        [*fetch, *tables, row],
        far=1,
        **work,
    )
    received2 = everywhere(sent2, ("sub", "coarse"))
    first, second = pair_swaps(after, after, wrap=False)
    if bits:
        blocks = [joined[0], swapped(joined[0], "coarse", bits[2])]
        slots = [0, bits[0], bits[1], bits[0] ^ bits[1]]
        slots = slots + [slot ^ bits[2] for slot in slots]
    else:
        slots = []
        sums = received2.reshape((chain, groups) + received2.shape[1:])[..., :cases, :wide]
        sums = jnp.sum(sums.astype(F32), axis=0)
        flat = jnp.moveaxis(sums, 0, 1).reshape(cases, along)
        own = lax.dynamic_index_in_dim(sums, lax.axis_index("coarse"), 0, keepdims=False)
        values = jnp.dot(flat, kernel.astype(F32).T, precision=lax.Precision.HIGHEST)
        energy = jnp.dot(values, own[:, :column].T, precision=lax.Precision.HIGHEST)
        blocks = [lax.psum(energy, "coarse")]
    multipliers, residual = call(
        functools.partial(scene_kernel, groups=groups, pieces=len(blocks), slots=slots),
        [((subs, scenes, face), F32), ((subs, scenes, face), F32)],
        [bent2, first, second, received2, joined[0] if bits else kernel, lifts_left, pull0_left]
        + [pull1, face_order, norms0]
        + [scene_loads.T, scene_weights.T, *blocks],
        [pltpu.VMEM((groups, cases, wide), F32), row],
        flops=10**9,
        moved=4 * 10**6,
    )
    return (multipliers, residual)


def solution(mesh):
    return jax.shard_map(
        per_device,
        mesh=mesh,
        in_specs=(
            P(("sub", "coarse"), None, None),
            P(("sub", "coarse"), None, None),
            P(None, "coarse", None, "sub"),
            P(("sub", "coarse"), None, None),
            P(("sub", "coarse"), None),
            P(("sub", "coarse"), None),
            P(),
            P(),
        ),
        out_specs=(P(("sub", "coarse"), None, None), P(("sub", "coarse"), None, None)),
        check_vma=False,
    )
```

```python
import functools

import jax
import jax.numpy as jnp
import numpy as np
from jax import lax
from jax.experimental import pallas as pl
from jax.experimental.pallas import tpu as pltpu
from jax.sharding import PartitionSpec as P

LANES = 128
CHUNK = 256
F32, BF16 = jnp.float32, jnp.bfloat16


def nn(a, b):
    return lax.dot_general(a, b, (((1,), (0,)), ((), ())), preferred_element_type=F32)


def nt(a, b):
    return lax.dot_general(a, b, (((1,), (1,)), ((), ())), preferred_element_type=F32)


def halves(x):
    high = x.astype(BF16)
    return high, (x - high.astype(F32)).astype(BF16)


def stacked(x):
    return jnp.concatenate(halves(x), axis=0)


def folded(x):
    rows = x.shape[0] // 2
    return x[:rows] + x[rows:]


def nn2(x, narrow):
    return folded(nn(stacked(x), narrow))


def nt2(x, narrow):
    return folded(nt(stacked(x), narrow))


def both3(product, x, y):
    high, low = halves(y)
    return folded(product(stacked(x), high)) + product(x.astype(BF16), low)


def equal(a, b):
    return jnp.where(a == b, 1.0, 0.0).astype(BF16)


def iota(shape, dim):
    return lax.broadcasted_iota(jnp.int32, shape, dim)


def rounded_up(value, unit):
    return (value + unit - 1) // unit * unit


def table(order_row):
    size = order_row.shape[1]
    return equal(iota((size, size), 0), order_row)


def back_table(order, n):
    subs, size = order.shape
    rows = jnp.concatenate(
        [order[...].astype(F32), jnp.zeros((rounded_up(subs, 8) - subs, size), F32)], axis=0
    )
    return equal(rows.T[:, n : n + 1].astype(jnp.int32), iota((size, size), 1))


def fill_tables(tables, backs, order):
    for n in range(tables.shape[0]):
        tables[n] = table(order[n : n + 1])
        if n > 0:
            backs[n - 1] = back_table(order, n)


def spread_of(dofs_row, chain, corners, groups):
    column = chain * corners
    ids = iota((column, 1), 0)
    slot = sum((ids >= t * corners).astype(jnp.int32) for t in range(1, chain))
    target = ids + slot * ((groups - 1) * corners) + lax.axis_index("coarse") * corners
    return equal(target, dofs_row)


def placed(x, width, at):
    rows = x.shape[1]
    return nn(x, equal(iota((rows, width), 0) + at, iota((rows, width), 1)))


def by_parity(to_after, to_before):
    odd = (lax.axis_index("sub") & 1) == 1
    return jnp.where(odd, to_before, to_after), jnp.where(odd, to_after, to_before)


def start_fetch(matrix, held, sems):
    subs, size = matrix.shape[0], matrix.shape[1]
    copies = []
    for n in range(subs):
        for k in range(size // CHUNK):
            part = pl.ds(k * CHUNK, CHUNK)
            copy = pltpu.make_async_copy(
                matrix.at[n, part], held.at[n, part], sems.at[n * (size // CHUNK) + k]
            )
            copy.start()
            copies.append(copy)
    return copies


def times_matrix(x, n, held, copies):
    size = held.shape[1]
    count = size // CHUNK
    total = None
    for k in range(count):
        copies[n * count + k].wait()
        part = nn(x[:, k * CHUNK : (k + 1) * CHUNK], held[n, k * CHUNK : (k + 1) * CHUNK])
        total = part if total is None else total + part
    return total


def inner_jump(displaced, tables, backs):
    subs = len(displaced)
    face = tables.shape[1]
    lefts = [part[:, :face] for part in displaced]
    rights = [part[:, face:] for part in displaced]
    for n in range(1, subs):
        lefts[n] = lefts[n] - nn2(displaced[n - 1][:, face:], tables[n])
        rights[n - 1] = rights[n - 1] - nn2(displaced[n][:, :face], backs[n - 1])
    return lefts, rights


def outer_jump(lefts, rights, before, after):
    at_head = lax.axis_index("sub") == 0
    at_tail = lax.axis_index("sub") == lax.axis_size("sub") - 1
    lefts = [jnp.where(at_head, 0.0, lefts[0] - before), *lefts[1:]]
    rights = [*rights[:-1], jnp.where(at_tail, 0.0, rights[-1] - after)]
    return [jnp.concatenate(pair, axis=1) for pair in zip(lefts, rights)]


def chain_sums(received, groups, width):
    chain = received.shape[0] // groups
    sums = []
    for c in range(groups):
        total = None
        for z in range(chain):
            part = received[z * groups + c, :, :width].astype(F32)
            total = part if total is None else total + part
        sums.append(total)
    return sums


def copies_of(out, x):
    for i in range(out.shape[0]):
        out[i] = x


def fetched(pairs, sems):
    copies = [pltpu.make_async_copy(a, b, sems.at[i]) for i, (a, b) in enumerate(pairs)]
    for copy in copies:
        copy.start()
    return copies


def corner_kernel(*refs, chain, groups):
    far, out, (order, coupling, dofs, loads), sems = refs[:4], refs[4], refs[5:9], refs[9]
    for copy in fetched(list(zip(far, refs[5:9])), sems):
        copy.wait()
    corners = coupling.shape[1]
    total = None
    for n in range(loads.shape[0]):
        terms = nt(loads[n], coupling[n])
        part = nt2(terms, spread_of(dofs[n : n + 1], chain, corners, groups))
        total = part if total is None else total + part
    copies_of(out, placed(total.astype(BF16), out.shape[2], 0).astype(BF16))


def first_kernel(
    matrix, shard_far, regroup_far, order, coupling, dofs, loads, *refs, chain, groups
):
    shards, refs = refs[: chain - 1], refs[chain - 1 :]
    out, first, second, kernel, held, sems, shard, regroup, small = refs
    copies = start_fetch(matrix, held, sems)
    small_copies = fetched([(shard_far, shard), (regroup_far, regroup)], small)
    subs, cases, iface = loads.shape
    corners, face = coupling.shape[1], order.shape[1]
    pad = rounded_up(corners, 16) - corners

    def packet(displaced, coupled, n):
        spread = spread_of(dofs[n : n + 1], chain, corners, groups)
        eye = equal(iota((corners, corners), 0), iota((corners, corners), 1))
        hot = placed(nt(eye, spread).astype(BF16), first.shape[1] - face, 0)
        lower = jnp.concatenate([coupled, hot], axis=1)
        upper = jnp.concatenate([displaced, jnp.zeros((cases, hot.shape[1]), F32)], axis=1)
        return jnp.concatenate([upper, lower, jnp.zeros((pad, lower.shape[1]), F32)], axis=0)

    for n in range(subs):
        out[n] = times_matrix(loads[n], n, held, copies)
        if n == 0:
            near = table(order[0:1])
            to_before = packet(
                nt(out[0, :, :face].astype(BF16), near), nt(coupling[0, :, :face], near), 0
            )
            for copy in small_copies:
                copy.wait()
            position = lax.axis_index("sub")
            depth = groups * corners
            rows = None
            for j, block in enumerate([shard, *shards]):
                ids = iota((depth, regroup.shape[1]), 0) + (position ^ j) * depth
                part = nn(block[...], equal(ids, regroup[...]))
                rows = part if rows is None else rows + part
            kernel[...] = rows.astype(BF16)
    last = subs - 1
    to_after = packet(out[last, :, face:], coupling[last, :, face:].astype(F32), last)
    one, two = by_parity(to_after, to_before)
    first[...] = one.astype(BF16)
    second[...] = two.astype(BF16)


def inner_kernel(
    displaced, coupling, dofs, order, lifts, bent, tables, backs, *, chain, groups
):
    subs, cases, _ = displaced.shape
    corners, face = coupling.shape[1], order.shape[1]
    fill_tables(tables, backs, order)
    spreads = [spread_of(dofs[n : n + 1], chain, corners, groups) for n in range(subs)]
    for n in range(subs):
        left, right = nn(spreads[n], coupling[n, :, :face]), nn(spreads[n], coupling[n, :, face:])
        if n > 0:
            moved = nn(coupling[n - 1, :, face:], tables[n]).astype(BF16)
            left = left - nn(spreads[n - 1], moved)
        if n < subs - 1:
            moved = nn(coupling[n + 1, :, :face], backs[n]).astype(BF16)
            right = right - nn(spreads[n + 1], moved)
        lifts[n, :, :face] = left.astype(BF16)
        lifts[n, :, face:] = right.astype(BF16)
    lefts, rights = inner_jump([displaced[n] for n in range(subs)], tables, backs)
    for n in range(subs):
        bent[n, :, :face] = lefts[n]
        bent[n, :, face:] = rights[n]


def lift_kernel(
    bent, own_lifts, first, second, received, kernel, other, order,
    lifts, lifts_left, pull, pull_left, out, *refs, groups
):
    *joined, row = refs
    subs, cases, _ = bent.shape
    column, face = own_lifts.shape[1], order.shape[1]
    wide = rounded_up(column, LANES)
    join(joined, kernel, other)
    near = table(order[0:1])
    from_after, from_before = by_parity(first[...].astype(F32), second[...].astype(F32))
    eye = equal(iota((column, first.shape[1] - face), 0), iota((column, first.shape[1] - face), 1))

    def neighbour(block):
        low = block[cases:].astype(BF16)
        return low[:, :face], nt(eye, low[:, face:]).astype(BF16)

    before = nn(from_before[:, :face].astype(BF16), near)
    _, before_spread = neighbour(from_before)
    after_coupling, after_spread = neighbour(from_after)
    lifted = outer_jump(
        [own_lifts[n, :, :face].astype(F32) for n in range(subs)],
        [own_lifts[n, :, face:].astype(F32) for n in range(subs)],
        nn(before_spread, before[cases:].astype(BF16)).astype(BF16).astype(F32),
        nn(after_spread, after_coupling).astype(BF16).astype(F32),
    )
    bent = outer_jump(
        [bent[n, :, :face] for n in range(subs)],
        [bent[n, :, face:] for n in range(subs)],
        before[:cases],
        from_after[:cases, :face],
    )
    for n in range(subs):
        lifted[n] = lifted[n].astype(BF16)
        lifts[n] = lifted[n]
        lifts_left[n] = lifted[n][:, :face]
    flat = jnp.concatenate(chain_sums(received, groups, wide), axis=1)
    values = nt2(flat, kernel[...])
    corner, norms = None, None
    for n in range(subs):
        whole = bent[n] + nn2(values, lifted[n])
        pull[n] = whole
        left = whole[:, :face]
        pull_left[n] = left
        part, norm = nt2(left, lifted[n][:, :face]), both3(nt, left, left)
        corner = part if corner is None else corner + part
        norms = norm if norms is None else norms + norm
    row[...] = jnp.zeros(row.shape, F32)
    row[:, :column] = corner
    store_halves(row, norms, slice(0, cases), column)
    copies_of(out, row[...].astype(BF16))


def join(out, low, high):
    for ref in out:
        ref[: low.shape[0]] = low[...]
        ref[low.shape[0] :] = high[...]


def store_halves(row, gram, rows, at):
    for half in halves(gram):
        row[rows, at : at + gram.shape[1]] = half.astype(F32)
        at += gram.shape[1]


def sum_halves(row, rows, at, count):
    return row[rows, at : at + count] + row[rows, at + count : at + 2 * count]


def second_kernel(matrix, pull, order, out, first, second, held, sems):
    copies = start_fetch(matrix, held, sems)
    subs = pull.shape[0]
    face = order.shape[1]
    near = back_table(order, 0)
    for n in range(subs):
        out[n] = folded(times_matrix(stacked(pull[n]), n, held, copies))
    one, two = by_parity(out[subs - 1, :, face:], nn2(out[0, :, :face], near))
    first[...] = one.astype(BF16)
    second[...] = two.astype(BF16)


def middle_kernel(displaced, received, kernel, lifts, order, base, norms0, row, tables, backs):
    subs, cases, _ = displaced.shape
    column, face = lifts.shape[1], order.shape[1]
    wide = rounded_up(column, LANES)
    groups = kernel.shape[1] // wide
    fill_tables(tables, backs, order)
    sums = chain_sums(received, groups, received.shape[2])
    flat = jnp.concatenate([part[:, :wide] for part in sums], axis=1)
    values = nt2(flat, kernel[...])
    row[:cases] = sum(sums)
    norms0[...] = sum_halves(row, slice(0, cases), column, cases)
    lefts, rights = inner_jump([displaced[n] for n in range(subs)], tables, backs)
    for n in range(subs):
        base[n] = jnp.concatenate([lefts[n], rights[n]], axis=1) + nn2(values, lifts[n])


def third_kernel(matrix, base, first, second, lifts, pull0, order, low, high, *refs):
    pull, bent2, after, payload, *joined, held, sems, tables, _, row = refs
    copies = start_fetch(matrix, held, sems)
    subs, cases, _ = base.shape
    face = order.shape[1]
    column = lifts.shape[1]
    for n in range(subs):
        tables[n] = table(order[n : n + 1])
    join(joined, low, high)
    from_after, from_before = by_parity(first[...].astype(F32), second[...].astype(F32))
    bent = outer_jump(
        [base[n, :, :face] for n in range(subs)],
        [base[n, :, face:] for n in range(subs)],
        nn(from_before.astype(BF16), tables[0]),
        from_after,
    )
    totals = None
    for n in range(subs):
        whole = bent[n]
        left = whole[:, :face]
        pull[n] = left
        moved = folded(times_matrix(stacked(whole), n, held, copies))
        bent2[n] = moved[:, :face]
        if n > 0:
            bent2[n] = moved[:, :face] - nn2(previous, tables[n])
        previous = moved[:, face:]
        parts = [
            nt2(left, lifts[n]),
            both3(nt, pull0[n], left),
            both3(nt, left, left),
            both3(nt, whole, moved),
        ]
        totals = parts if totals is None else [a + b for a, b in zip(totals, parts)]
    after[...] = previous.astype(BF16)
    corner, gram1, gram2, gram3 = totals
    row[...] = jnp.zeros(row.shape, F32)
    row[:cases, :column] = corner
    store_halves(row, gram1, slice(0, cases), column)
    step = cases // 2
    for j in range(2):
        for i, gram in enumerate((gram2, gram3)):
            part = gram[j * step : (j + 1) * step]
            store_halves(row, part, slice(cases, cases + step), (4 * j + 2 * i) * cases)
    copies_of(payload, row[...].astype(BF16))


def scene_kernel(
    bent, first, second, received, kernel, lifts, pull0, pull1, order, norms0,
    scene_loads, scene_weights, *refs, groups, pieces, slots
):
    blocks = refs[:pieces]
    multipliers, residual, held, row = refs[pieces:]
    subs, cases, _ = bent.shape
    column = lifts.shape[1]
    wide = rounded_up(column, LANES)
    group = lax.axis_index("coarse")
    sums = chain_sums(received, groups, received.shape[2])
    for c in range(groups):
        held[c] = sums[c][:cases, :wide]
    flat = jnp.concatenate([held[c] for c in range(groups)], axis=1)
    values = nt2(flat, kernel[:column])
    if groups_whole(blocks, column, groups):
        lifted, index = None, iter(slots)
        for block in blocks:
            for i in range(block.shape[0] // column):
                sums_here = held[group ^ next(index)][:, :column]
                part = nn2(sums_here, block[i * column : (i + 1) * column])
                lifted = part if lifted is None else lifted + part
        energy = both3(nt, lifted, flat)
    else:
        energy = blocks[0][...]
    row[...] = sum(sums)
    norms1 = sum_halves(row, slice(0, cases), column, cases)
    lower = slice(cases, cases + cases // 2)
    norms2, norms3 = (
        jnp.concatenate(
            [sum_halves(row, lower, (4 * j + 2 * i) * cases, cases) for j in range(2)], axis=0
        )
        for i in range(2)
    )
    norms3 = norms3 + energy

    ids = iota((cases, scene_loads.shape[1]), 0)
    mixing = sum(
        jnp.where(ids == scene_loads[i : i + 1], scene_weights[i : i + 1], 0.0)
        for i in range(scene_loads.shape[0])
    )

    def moment(norms):
        return jnp.sum(both3(nn, norms, mixing) * mixing, axis=0, keepdims=True)

    moment0, moment1 = moment(norms0[...]), moment(norms1)
    moment2, moment3 = moment(norms2), moment(norms3)
    step0 = moment0 / moment1
    norm1 = moment0 - 2.0 * step0 * moment1 + step0 * step0 * moment2
    grow = 1.0 + norm1 / moment0
    curvature = grow * grow * moment1 - 2.0 * grow * step0 * moment2 + step0 * step0 * moment3
    step1 = norm1 / curvature
    zeros = jnp.zeros_like(mixing)

    def transposed(parts):
        weights = -jnp.concatenate(parts, axis=0)
        high = weights.astype(BF16).astype(F32)
        return jnp.concatenate([high, high, weights - high], axis=0).T.astype(BF16)

    for_multipliers = transposed(
        [(step0 + step1 * grow) * mixing, (-step0 * step1) * mixing, zeros]
    )
    for_residual = transposed(
        [mixing, (-step0 - step1 * grow) * mixing, (step0 * step1) * mixing]
    )
    _, from_before = by_parity(first[...].astype(F32), second[...].astype(F32))
    for n in range(subs):
        pull2 = bent[n]
        if n == 0:
            pull2 = pull2 - nn(from_before.astype(BF16), table(order[0:1]))
            pull2 = jnp.where(lax.axis_index("sub") == 0, 0.0, pull2)
        pull2 = pull2 + nn2(values, lifts[n])
        basis = jnp.concatenate([pull0[n], pull1[n], pull2], axis=0)
        high, low = halves(basis)
        basis = jnp.concatenate([high, low, high], axis=0)
        multipliers[n] = nn(for_multipliers, basis)
        residual[n] = nn(for_residual, basis)


def groups_whole(blocks, column, groups):
    return sum(block.shape[0] for block in blocks) == column * groups


def everywhere(x, axes):
    return lax.all_to_all(x, axes, 0, 0)


def swapped(x, axis, bit):
    return lax.ppermute(x, axis, [(i, i ^ bit) for i in range(lax.axis_size(axis))])


def pair_swaps(first, second, wrap=True):
    length = lax.axis_size("sub")

    def partner(i, j):
        return (i, j % length if wrap or 0 <= j < length else i)

    one = lax.ppermute(first, "sub", [partner(i, i ^ 1) for i in range(length)])
    two = lax.ppermute(
        second, "sub", [partner(i, i + 1 if i & 1 else i - 1) for i in range(length)]
    )
    return one, two


def call(kernel, outs, args, scratch=(), flops=0, moved=0, far=0):
    specs = [pl.BlockSpec(memory_space=pltpu.HBM)] * far
    specs += [pl.BlockSpec(memory_space=pltpu.VMEM)] * (len(args) - far)
    pinned = [pltpu.with_memory_space_constraint(x, pltpu.HBM) for x in args[:far]]
    shapes = [jax.ShapeDtypeStruct(shape, kind) for shape, kind in outs]
    return pl.pallas_call(
        kernel,
        out_shape=shapes,
        in_specs=specs,
        out_specs=[pl.BlockSpec(memory_space=pltpu.VMEM)] * len(outs),
        scratch_shapes=list(scratch),
        compiler_params=pltpu.CompilerParams(vmem_limit_bytes=32 << 20),
        cost_estimate=pl.CostEstimate(flops=flops, bytes_accessed=moved, transcendentals=0),
    )(*pinned, *args[far:])


def per_device(
    schur_inverse,
    corner_coupling,
    coarse_inverse,
    load_cases,
    face_order,
    corner_dofs,
    scene_loads,
    scene_weights,
):
    subs, iface = schur_inverse.shape[0], schur_inverse.shape[1]
    face = face_order.shape[1]
    corners = corner_dofs.shape[1]
    cases = load_cases.shape[1]
    scenes = scene_loads.shape[0]
    chain, groups = lax.axis_size("sub"), lax.axis_size("coarse")
    devices = chain * groups
    column = chain * corners
    wide = rounded_up(column, LANES)
    along = groups * wide
    work = dict(flops=4 * cases * schur_inverse.size, moved=2 * schur_inverse.size)

    fetch = [
        pltpu.VMEM(schur_inverse.shape, BF16),
        pltpu.SemaphoreType.DMA((subs * (iface // CHUNK),)),
    ]
    tables = [
        pltpu.VMEM((subs, face, face), BF16), pltpu.VMEM((max(subs - 1, 1), face, face), BF16)
    ]
    row = pltpu.VMEM((cases + cases // 2, rounded_up(column + 2 * cases, LANES)), F32)

    shard = coarse_inverse.reshape(column, groups * corners)
    shards = [swapped(shard, "sub", j) for j in range(1, chain)]

    lane = np.arange(along)
    inner = lane % wide
    source = (inner // corners * groups + lane // wide) * corners + inner % corners
    regroup = jnp.asarray(np.where(inner < column, source, -1)[None].astype(np.int32))

    bits = []
    if groups == 1 << 3 and (column * groups) ** 2 <= schur_inverse.size:
        bits = [1 << b for b in reversed(range(groups.bit_length() - 1))]

    small = [face_order, corner_coupling, corner_dofs, load_cases]
    sent0, *small = call(
        functools.partial(corner_kernel, chain=chain, groups=groups),
        [((devices, cases, wide), BF16)] + [(x.shape, x.dtype) for x in small],
        small,
        [pltpu.SemaphoreType.DMA((len(small),))],
        far=len(small),
    )
    face_order, corner_coupling, corner_dofs, load_cases = small
    received0 = everywhere(sent0, ("sub", "coarse"))
    packet = (cases + rounded_up(corners, 16), face + wide)
    displaced0, first, second, kernel = call(
        functools.partial(first_kernel, chain=chain, groups=groups),
        [
            ((subs, cases, iface), F32),
            (packet, BF16),
            (packet, BF16),
            ((column, along), BF16),
        ],
        [schur_inverse, shard, regroup, *small, *shards],
        fetch
        + [pltpu.VMEM(x.shape, x.dtype) for x in (shard, regroup)]
        + [pltpu.SemaphoreType.DMA((2,))],
        far=3,
        **work,
    )
    first, second = pair_swaps(first, second)
    own_lifts, bent0 = call(
        functools.partial(inner_kernel, chain=chain, groups=groups),
        [((subs, column, iface), BF16), ((subs, cases, iface), F32)],
        [displaced0, corner_coupling, corner_dofs, face_order],
        tables,
        flops=10**9,
        moved=2 * 10**6,
    )
    other = swapped(kernel, "coarse", bits[0]) if bits else kernel
    lifts, lifts_left, pull0, pull0_left, sent1, *joined = call(
        functools.partial(lift_kernel, groups=groups),
        [
            ((subs, column, iface), BF16),
            ((subs, column, face), BF16),
            ((subs, cases, iface), F32),
            ((subs, cases, face), F32),
            ((devices, cases, rounded_up(column + 2 * cases, LANES)), BF16),
        ]
        + [((2 * column, along), BF16)] * bool(bits),
        [bent0, own_lifts, first, second, received0, kernel, other, face_order],
        [pltpu.VMEM((cases, rounded_up(column + 2 * cases, LANES)), F32)],
        flops=10**9,
        moved=10**6,
    )
    received1 = everywhere(sent1, ("sub", "coarse"))
    displaced1, first, second = call(
        second_kernel,
        [((subs, cases, iface), F32), ((cases, face), BF16), ((cases, face), BF16)],
        [schur_inverse, pull0, face_order],
        fetch,
        far=1,
        **work,
    )
    first, second = pair_swaps(first, second)

    low = joined[0] if bits else kernel
    high = swapped(low, "coarse", bits[1]) if bits else kernel
    base, norms0 = call(
        middle_kernel,
        [((subs, cases, iface), F32), ((cases, cases), F32)],
        [displaced1, received1, kernel, lifts, face_order],
        [row, *tables],
        flops=10**9,
        moved=2 * 10**6,
    )
    pull1, bent2, after, sent2, *joined = call(
        third_kernel,
        [
            ((subs, cases, face), F32),
            ((subs, cases, face), F32),
            ((cases, face), BF16),
            ((devices, cases + cases // 2, rounded_up(column + 2 * cases, LANES)), BF16),
        ]
        + [((4 * column, along), BF16)] * bool(bits),
        [schur_inverse, base, first, second, lifts_left, pull0_left, face_order, low, high],
        [*fetch, *tables, row],
        far=1,
        **work,
    )
    received2 = everywhere(sent2, ("sub", "coarse"))
    first, second = pair_swaps(after, after, wrap=False)
    if bits:
        blocks = [joined[0], swapped(joined[0], "coarse", bits[2])]
        slots = [0, bits[0], bits[1], bits[0] ^ bits[1]]
        slots = slots + [slot ^ bits[2] for slot in slots]
    else:
        slots = []
        sums = received2.reshape((chain, groups) + received2.shape[1:])[..., :cases, :wide]
        sums = jnp.sum(sums.astype(F32), axis=0)
        flat = jnp.moveaxis(sums, 0, 1).reshape(cases, along)
        own = lax.dynamic_index_in_dim(sums, lax.axis_index("coarse"), 0, keepdims=False)
        values = jnp.dot(flat, kernel.astype(F32).T, precision=lax.Precision.HIGHEST)
        energy = jnp.dot(values, own[:, :column].T, precision=lax.Precision.HIGHEST)
        blocks = [lax.psum(energy, "coarse")]
    multipliers, residual = call(
        functools.partial(scene_kernel, groups=groups, pieces=len(blocks), slots=slots),
        [((subs, scenes, face), F32), ((subs, scenes, face), F32)],
        [bent2, first, second, received2, joined[0] if bits else kernel, lifts_left, pull0_left]
        + [pull1, face_order, norms0]
        + [scene_loads.T, scene_weights.T, *blocks],
        [pltpu.VMEM((groups, cases, wide), F32), row],
        flops=10**9,
        moved=4 * 10**6,
    )
    return (multipliers, residual)


def solution(mesh):
    return jax.shard_map(
        per_device,
        mesh=mesh,
        in_specs=(
            P(("sub", "coarse"), None, None),
            P(("sub", "coarse"), None, None),
            P(None, "coarse", None, "sub"),
            P(("sub", "coarse"), None, None),
            P(("sub", "coarse"), None),
            P(("sub", "coarse"), None),
            P(),
            P(),
        ),
        out_specs=(P(("sub", "coarse"), None, None), P(("sub", "coarse"), None, None)),
        check_vma=False,
    )
```

```python
import functools

import jax
import jax.numpy as jnp
import numpy as np
from jax import lax
from jax.experimental import pallas as pl
from jax.experimental.pallas import tpu as pltpu
from jax.sharding import PartitionSpec as P

LANES = 128
CHUNK = 256
AHEAD = (2, 3)
F32, BF16 = jnp.float32, jnp.bfloat16


def nn(a, b):
    return lax.dot_general(a, b, (((1,), (0,)), ((), ())), preferred_element_type=F32)


def nt(a, b):
    return lax.dot_general(a, b, (((1,), (1,)), ((), ())), preferred_element_type=F32)


def halves(x):
    high = x.astype(BF16)
    return high, (x - high.astype(F32)).astype(BF16)


def stacked(x):
    return jnp.concatenate(halves(x), axis=0)


def folded(x):
    rows = x.shape[0] // 2
    return x[:rows] + x[rows:]


def nn2(x, narrow):
    return folded(nn(stacked(x), narrow))


def nt2(x, narrow):
    return folded(nt(stacked(x), narrow))


def both3(product, x, y):
    high, low = halves(y)
    return folded(product(stacked(x), high)) + product(x.astype(BF16), low)


def equal(a, b):
    return jnp.where(a == b, 1.0, 0.0).astype(BF16)


def iota(shape, dim):
    return lax.broadcasted_iota(jnp.int32, shape, dim)


def rounded_up(value, unit):
    return (value + unit - 1) // unit * unit


def table(order_row):
    size = order_row.shape[1]
    return equal(iota((size, size), 0), order_row)


def back_table(order, n):
    subs, size = order.shape
    rows = jnp.concatenate(
        [order[...].astype(F32), jnp.zeros((rounded_up(subs, 8) - subs, size), F32)], axis=0
    )
    return equal(rows.T[:, n : n + 1].astype(jnp.int32), iota((size, size), 1))


def fill_tables(tables, backs, order):
    for n in range(tables.shape[0]):
        tables[n] = table(order[n : n + 1])
        if n > 0:
            backs[n - 1] = back_table(order, n)


def spread_of(dofs_row, chain, corners, groups):
    column = chain * corners
    ids = iota((column, 1), 0)
    slot = sum((ids >= t * corners).astype(jnp.int32) for t in range(1, chain))
    target = ids + slot * ((groups - 1) * corners) + lax.axis_index("coarse") * corners
    return equal(target, dofs_row)


def placed(x, width, at):
    rows = x.shape[1]
    return nn(x, equal(iota((rows, width), 0) + at, iota((rows, width), 1)))


def by_parity(to_after, to_before):
    odd = (lax.axis_index("sub") & 1) == 1
    return jnp.where(odd, to_before, to_after), jnp.where(odd, to_after, to_before)


def start_fetch(matrix, held, sems, ready=0):
    subs, size = matrix.shape[0], matrix.shape[1]
    copies = []
    for n in range(subs):
        for k in range(size // CHUNK):
            copies.append(None)
            if len(copies) > ready:
                part = pl.ds(k * CHUNK, CHUNK)
                copies[-1] = pltpu.make_async_copy(
                    matrix.at[n, part], held.at[n, part], sems.at[n * (size // CHUNK) + k]
                )
                copies[-1].start()
    return copies


def start_ahead(matrix, ahead, sems):
    copies = []
    for k in range(ahead.shape[0] // CHUNK):
        part = pl.ds(k * CHUNK, CHUNK)
        copies.append(pltpu.make_async_copy(matrix.at[0, part], ahead.at[part], sems.at[k]))
        copies[-1].start()
    return copies


def times_matrix(x, n, held, copies, ahead=None):
    size = held.shape[1]
    count = size // CHUNK
    total = None
    for k in range(count):
        part = slice(k * CHUNK, (k + 1) * CHUNK)
        if copies[n * count + k] is None:
            chunk = ahead[part]
        else:
            copies[n * count + k].wait()
            chunk = held[n, part]
        part = nn(x[:, part], chunk)
        total = part if total is None else total + part
    return total


def inner_jump(displaced, tables, backs):
    subs = len(displaced)
    face = tables.shape[1]
    lefts = [part[:, :face] for part in displaced]
    rights = [part[:, face:] for part in displaced]
    for n in range(1, subs):
        lefts[n] = lefts[n] - nn2(displaced[n - 1][:, face:], tables[n])
        rights[n - 1] = rights[n - 1] - nn2(displaced[n][:, :face], backs[n - 1])
    return lefts, rights


def outer_jump(lefts, rights, before, after):
    at_head = lax.axis_index("sub") == 0
    at_tail = lax.axis_index("sub") == lax.axis_size("sub") - 1
    lefts = [jnp.where(at_head, 0.0, lefts[0] - before), *lefts[1:]]
    rights = [*rights[:-1], jnp.where(at_tail, 0.0, rights[-1] - after)]
    return [jnp.concatenate(pair, axis=1) for pair in zip(lefts, rights)]


def chain_sums(received, groups, width):
    chain = received.shape[0] // groups
    sums = []
    for c in range(groups):
        total = None
        for z in range(chain):
            part = received[z * groups + c, :, :width].astype(F32)
            total = part if total is None else total + part
        sums.append(total)
    return sums


def copies_of(out, x):
    for i in range(out.shape[0]):
        out[i] = x


def fetched(pairs, sems):
    copies = [pltpu.make_async_copy(a, b, sems.at[i]) for i, (a, b) in enumerate(pairs)]
    for copy in copies:
        copy.start()
    return copies


def corner_kernel(*refs, chain, groups):
    matrix, far, out, (order, coupling, dofs, loads) = refs[0], refs[1:5], refs[5], refs[6:10]
    ahead, sems, ahead_sems = refs[10:]
    small_copies = fetched(list(zip(far, refs[6:10])), sems)
    copies = start_ahead(matrix, ahead, ahead_sems)
    for copy in small_copies:
        copy.wait()
    corners = coupling.shape[1]
    total = None
    for n in range(loads.shape[0]):
        terms = nt(loads[n], coupling[n])
        part = nt2(terms, spread_of(dofs[n : n + 1], chain, corners, groups))
        total = part if total is None else total + part
    copies_of(out, placed(total.astype(BF16), out.shape[2], 0).astype(BF16))
    for copy in copies:
        copy.wait()


def first_kernel(
    matrix, shard_far, regroup_far, order, coupling, dofs, loads, ahead, *refs, chain, groups
):
    shards, refs = refs[: chain - 1], refs[chain - 1 :]
    out, first, second, kernel, held, sems, shard, regroup, small = refs
    copies = start_fetch(matrix, held, sems, ahead.shape[0] // CHUNK)
    small_copies = fetched([(shard_far, shard), (regroup_far, regroup)], small)
    subs, cases, iface = loads.shape
    corners, face = coupling.shape[1], order.shape[1]
    pad = rounded_up(corners, 16) - corners

    def packet(displaced, coupled, n):
        spread = spread_of(dofs[n : n + 1], chain, corners, groups)
        eye = equal(iota((corners, corners), 0), iota((corners, corners), 1))
        hot = placed(nt(eye, spread).astype(BF16), first.shape[1] - face, 0)
        lower = jnp.concatenate([coupled, hot], axis=1)
        upper = jnp.concatenate([displaced, jnp.zeros((cases, hot.shape[1]), F32)], axis=1)
        return jnp.concatenate([upper, lower, jnp.zeros((pad, lower.shape[1]), F32)], axis=0)

    for n in range(subs):
        out[n] = times_matrix(loads[n], n, held, copies, ahead)
        if n == 0:
            near = table(order[0:1])
            to_before = packet(
                nt(out[0, :, :face].astype(BF16), near), nt(coupling[0, :, :face], near), 0
            )
            for copy in small_copies:
                copy.wait()
            position = lax.axis_index("sub")
            depth = groups * corners
            rows = None
            for j, block in enumerate([shard, *shards]):
                ids = iota((depth, regroup.shape[1]), 0) + (position ^ j) * depth
                part = nn(block[...], equal(ids, regroup[...]))
                rows = part if rows is None else rows + part
            kernel[...] = rows.astype(BF16)
    last = subs - 1
    to_after = packet(out[last, :, face:], coupling[last, :, face:].astype(F32), last)
    one, two = by_parity(to_after, to_before)
    first[...] = one.astype(BF16)
    second[...] = two.astype(BF16)


def inner_kernel(
    displaced, coupling, dofs, order, lifts, bent, tables, backs, *, chain, groups
):
    subs, cases, _ = displaced.shape
    corners, face = coupling.shape[1], order.shape[1]
    fill_tables(tables, backs, order)
    spreads = [spread_of(dofs[n : n + 1], chain, corners, groups) for n in range(subs)]
    for n in range(subs):
        left, right = nn(spreads[n], coupling[n, :, :face]), nn(spreads[n], coupling[n, :, face:])
        if n > 0:
            moved = nn(coupling[n - 1, :, face:], tables[n]).astype(BF16)
            left = left - nn(spreads[n - 1], moved)
        if n < subs - 1:
            moved = nn(coupling[n + 1, :, :face], backs[n]).astype(BF16)
            right = right - nn(spreads[n + 1], moved)
        lifts[n, :, :face] = left.astype(BF16)
        lifts[n, :, face:] = right.astype(BF16)
    lefts, rights = inner_jump([displaced[n] for n in range(subs)], tables, backs)
    for n in range(subs):
        bent[n, :, :face] = lefts[n]
        bent[n, :, face:] = rights[n]


def lift_kernel(
    bent, own_lifts, first, second, received, kernel, other, order,
    lifts, lifts_left, pull, pull_left, out, *refs, groups
):
    *joined, row = refs
    subs, cases, _ = bent.shape
    column, face = own_lifts.shape[1], order.shape[1]
    wide = rounded_up(column, LANES)
    join(joined, kernel, other)
    near = table(order[0:1])
    from_after, from_before = by_parity(first[...].astype(F32), second[...].astype(F32))
    eye = equal(iota((column, first.shape[1] - face), 0), iota((column, first.shape[1] - face), 1))

    def neighbour(block):
        low = block[cases:].astype(BF16)
        return low[:, :face], nt(eye, low[:, face:]).astype(BF16)

    before = nn(from_before[:, :face].astype(BF16), near)
    _, before_spread = neighbour(from_before)
    after_coupling, after_spread = neighbour(from_after)
    lifted = outer_jump(
        [own_lifts[n, :, :face].astype(F32) for n in range(subs)],
        [own_lifts[n, :, face:].astype(F32) for n in range(subs)],
        nn(before_spread, before[cases:].astype(BF16)).astype(BF16).astype(F32),
        nn(after_spread, after_coupling).astype(BF16).astype(F32),
    )
    bent = outer_jump(
        [bent[n, :, :face] for n in range(subs)],
        [bent[n, :, face:] for n in range(subs)],
        before[:cases],
        from_after[:cases, :face],
    )
    for n in range(subs):
        lifted[n] = lifted[n].astype(BF16)
        lifts[n] = lifted[n]
        lifts_left[n] = lifted[n][:, :face]
    flat = jnp.concatenate(chain_sums(received, groups, wide), axis=1)
    values = nt2(flat, kernel[...])
    corner, norms = None, None
    for n in range(subs):
        whole = bent[n] + nn2(values, lifted[n])
        pull[n] = whole
        left = whole[:, :face]
        pull_left[n] = left
        part, norm = nt2(left, lifted[n][:, :face]), both3(nt, left, left)
        corner = part if corner is None else corner + part
        norms = norm if norms is None else norms + norm
    row[...] = jnp.zeros(row.shape, F32)
    row[:, :column] = corner
    store_halves(row, norms, slice(0, cases), column)
    copies_of(out, row[...].astype(BF16))


def join(out, low, high):
    for ref in out:
        ref[: low.shape[0]] = low[...]
        ref[low.shape[0] :] = high[...]


def store_halves(row, gram, rows, at):
    for half in halves(gram):
        row[rows, at : at + gram.shape[1]] = half.astype(F32)
        at += gram.shape[1]


def sum_halves(row, rows, at, count):
    return row[rows, at : at + count] + row[rows, at + count : at + 2 * count]


def second_kernel(matrix, pull, order, out, first, second, held, sems):
    copies = start_fetch(matrix, held, sems)
    subs = pull.shape[0]
    face = order.shape[1]
    near = back_table(order, 0)
    for n in range(subs):
        out[n] = folded(times_matrix(stacked(pull[n]), n, held, copies))
    one, two = by_parity(out[subs - 1, :, face:], nn2(out[0, :, :face], near))
    first[...] = one.astype(BF16)
    second[...] = two.astype(BF16)


def middle_kernel(matrix, displaced, received, kernel, lifts, order, low, high, _, *refs):
    base, norms0, ahead, *joined, row, tables, backs, ahead_sems = refs
    copies = start_ahead(matrix, ahead, ahead_sems)
    join(joined, low, high)
    subs, cases, _ = displaced.shape
    column, face = lifts.shape[1], order.shape[1]
    wide = rounded_up(column, LANES)
    groups = kernel.shape[1] // wide
    fill_tables(tables, backs, order)
    sums = chain_sums(received, groups, received.shape[2])
    flat = jnp.concatenate([part[:, :wide] for part in sums], axis=1)
    values = nt2(flat, kernel[...])
    row[:cases] = sum(sums)
    norms0[...] = sum_halves(row, slice(0, cases), column, cases)
    lefts, rights = inner_jump([displaced[n] for n in range(subs)], tables, backs)
    for n in range(subs):
        base[n] = jnp.concatenate([lefts[n], rights[n]], axis=1) + nn2(values, lifts[n])
    for copy in copies:
        copy.wait()


def third_kernel(matrix, base, first, second, lifts, pull0, order, ahead, *refs):
    pull, bent2, after, payload, held, sems, tables, row = refs
    copies = start_fetch(matrix, held, sems, ahead.shape[0] // CHUNK)
    subs, cases, _ = base.shape
    face = order.shape[1]
    column = lifts.shape[1]
    for n in range(subs):
        tables[n] = table(order[n : n + 1])
    from_after, from_before = by_parity(first[...].astype(F32), second[...].astype(F32))
    bent = outer_jump(
        [base[n, :, :face] for n in range(subs)],
        [base[n, :, face:] for n in range(subs)],
        nn(from_before.astype(BF16), tables[0]),
        from_after,
    )
    corner, gram1, gram2, gram3 = None, None, None, None

    def plus(total, part):
        return part if total is None else total + part

    for n in range(subs):
        left = bent[n][:, :face]
        pull[n] = left
        corner = plus(corner, nt2(left, lifts[n]))
        gram1 = plus(gram1, both3(nt, pull0[n], left))
        gram2 = plus(gram2, both3(nt, left, left))
    row[...] = jnp.zeros(row.shape, F32)
    row[:cases, :column] = corner
    store_halves(row, gram1, slice(0, cases), column)
    for n in range(subs):
        moved = folded(times_matrix(stacked(bent[n]), n, held, copies, ahead))
        bent2[n] = moved[:, :face]
        if n > 0:
            bent2[n] = moved[:, :face] - nn2(previous, tables[n])
        previous = moved[:, face:]
        gram3 = plus(gram3, both3(nt, bent[n], moved))
    after[...] = previous.astype(BF16)
    step = cases // 2
    for j in range(2):
        for i, gram in enumerate((gram2, gram3)):
            part = gram[j * step : (j + 1) * step]
            store_halves(row, part, slice(cases, cases + step), (4 * j + 2 * i) * cases)
    copies_of(payload, row[...].astype(BF16))


def scene_kernel(
    bent, first, second, received, kernel, lifts, pull0, pull1, order, norms0,
    scene_loads, scene_weights, *refs, groups, pieces, slots
):
    blocks = refs[:pieces]
    multipliers_far, residual_far, held, row, multipliers, residual, sems = refs[pieces:]
    subs, cases, _ = bent.shape
    column = lifts.shape[1]
    wide = rounded_up(column, LANES)
    group = lax.axis_index("coarse")
    sums = chain_sums(received, groups, received.shape[2])
    for c in range(groups):
        held[c] = sums[c][:cases, :wide]
    flat = jnp.concatenate([held[c] for c in range(groups)], axis=1)
    values = nt2(flat, kernel[:column])
    if groups_whole(blocks, column, groups):
        lifted, index = None, iter(slots)
        for block in blocks:
            for i in range(block.shape[0] // column):
                sums_here = held[group ^ next(index)][:, :column]
                part = nn2(sums_here, block[i * column : (i + 1) * column])
                lifted = part if lifted is None else lifted + part
        energy = both3(nt, lifted, flat)
    else:
        energy = blocks[0][...]
    row[...] = sum(sums)
    norms1 = sum_halves(row, slice(0, cases), column, cases)
    lower = slice(cases, cases + cases // 2)
    norms2, norms3 = (
        jnp.concatenate(
            [sum_halves(row, lower, (4 * j + 2 * i) * cases, cases) for j in range(2)], axis=0
        )
        for i in range(2)
    )
    norms3 = norms3 + energy

    ids = iota((cases, scene_loads.shape[1]), 0)
    mixing = sum(
        jnp.where(ids == scene_loads[i : i + 1], scene_weights[i : i + 1], 0.0)
        for i in range(scene_loads.shape[0])
    )

    def moment(norms):
        return jnp.sum(both3(nn, norms, mixing) * mixing, axis=0, keepdims=True)

    moment0, moment1 = moment(norms0[...]), moment(norms1)
    moment2, moment3 = moment(norms2), moment(norms3)
    step0 = moment0 / moment1
    norm1 = moment0 - 2.0 * step0 * moment1 + step0 * step0 * moment2
    grow = 1.0 + norm1 / moment0
    curvature = grow * grow * moment1 - 2.0 * grow * step0 * moment2 + step0 * step0 * moment3
    step1 = norm1 / curvature
    zeros = jnp.zeros_like(mixing)

    def transposed(parts):
        weights = -jnp.concatenate(parts, axis=0)
        high = weights.astype(BF16).astype(F32)
        return jnp.concatenate([high, high, weights - high], axis=0).T.astype(BF16)

    for_multipliers = transposed(
        [(step0 + step1 * grow) * mixing, (-step0 * step1) * mixing, zeros]
    )
    for_residual = transposed(
        [mixing, (-step0 - step1 * grow) * mixing, (step0 * step1) * mixing]
    )
    _, from_before = by_parity(first[...].astype(F32), second[...].astype(F32))
    copies = []
    for n in range(subs):
        pull2 = bent[n]
        if n == 0:
            pull2 = pull2 - nn(from_before.astype(BF16), table(order[0:1]))
            pull2 = jnp.where(lax.axis_index("sub") == 0, 0.0, pull2)
        pull2 = pull2 + nn2(values, lifts[n])
        basis = jnp.concatenate([pull0[n], pull1[n], pull2], axis=0)
        high, low = halves(basis)
        basis = jnp.concatenate([high, low, high], axis=0)
        multipliers[n] = nn(for_multipliers, basis)
        copies += fetched([(multipliers.at[n], multipliers_far.at[n])], sems.at[pl.ds(2 * n, 1)])
        residual[n] = nn(for_residual, basis)
        copies += fetched([(residual.at[n], residual_far.at[n])], sems.at[pl.ds(2 * n + 1, 1)])
    for copy in copies:
        copy.wait()


def groups_whole(blocks, column, groups):
    return sum(block.shape[0] for block in blocks) == column * groups


def everywhere(x, axes):
    return lax.all_to_all(x, axes, 0, 0)


def swapped(x, axis, bit):
    return lax.ppermute(x, axis, [(i, i ^ bit) for i in range(lax.axis_size(axis))])


def pair_swaps(first, second, wrap=True):
    length = lax.axis_size("sub")

    def partner(i, j):
        return (i, j % length if wrap or 0 <= j < length else i)

    one = lax.ppermute(first, "sub", [partner(i, i ^ 1) for i in range(length)])
    two = lax.ppermute(
        second, "sub", [partner(i, i + 1 if i & 1 else i - 1) for i in range(length)]
    )
    return one, two


def call(kernel, outs, args, scratch=(), flops=0, moved=0, far=0, ends=pltpu.VMEM):
    specs = [pl.BlockSpec(memory_space=pltpu.HBM)] * far
    specs += [pl.BlockSpec(memory_space=pltpu.VMEM)] * (len(args) - far)
    pinned = [pltpu.with_memory_space_constraint(x, pltpu.HBM) for x in args[:far]]
    shapes = [jax.ShapeDtypeStruct(shape, kind) for shape, kind in outs]
    return pl.pallas_call(
        kernel,
        out_shape=shapes,
        in_specs=specs,
        out_specs=[pl.BlockSpec(memory_space=ends)] * len(outs),
        scratch_shapes=list(scratch),
        compiler_params=pltpu.CompilerParams(vmem_limit_bytes=32 << 20),
        cost_estimate=pl.CostEstimate(flops=flops, bytes_accessed=moved, transcendentals=0),
    )(*pinned, *args[far:])


def per_device(
    schur_inverse,
    corner_coupling,
    coarse_inverse,
    load_cases,
    face_order,
    corner_dofs,
    scene_loads,
    scene_weights,
):
    subs, iface = schur_inverse.shape[0], schur_inverse.shape[1]
    face = face_order.shape[1]
    corners = corner_dofs.shape[1]
    cases = load_cases.shape[1]
    scenes = scene_loads.shape[0]
    chain, groups = lax.axis_size("sub"), lax.axis_size("coarse")
    devices = chain * groups
    column = chain * corners
    wide = rounded_up(column, LANES)
    along = groups * wide
    work = dict(flops=4 * cases * schur_inverse.size, moved=2 * schur_inverse.size)

    fetch = [
        pltpu.VMEM(schur_inverse.shape, BF16),
        pltpu.SemaphoreType.DMA((subs * (iface // CHUNK),)),
    ]
    tables = [
        pltpu.VMEM((subs, face, face), BF16), pltpu.VMEM((max(subs - 1, 1), face, face), BF16)
    ]
    row = pltpu.VMEM((cases + cases // 2, rounded_up(column + 2 * cases, LANES)), F32)

    shard = coarse_inverse.reshape(column, groups * corners)
    shards = [swapped(shard, "sub", j) for j in range(1, chain)]

    lane = np.arange(along)
    inner = lane % wide
    source = (inner // corners * groups + lane // wide) * corners + inner % corners
    regroup = jnp.asarray(np.where(inner < column, source, -1)[None].astype(np.int32))

    bits = []
    if groups == 1 << 3 and (column * groups) ** 2 <= schur_inverse.size:
        bits = [1 << b for b in reversed(range(groups.bit_length() - 1))]

    small = [face_order, corner_coupling, corner_dofs, load_cases]
    ahead = [((chunks * CHUNK, iface), BF16) for chunks in AHEAD]
    sent0, *small, ahead0 = call(
        functools.partial(corner_kernel, chain=chain, groups=groups),
        [((devices, cases, wide), BF16)] + [(x.shape, x.dtype) for x in small] + ahead[:1],
        [schur_inverse, *small],
        [pltpu.SemaphoreType.DMA((len(small),)), pltpu.SemaphoreType.DMA((AHEAD[0],))],
        far=1 + len(small),
    )
    face_order, corner_coupling, corner_dofs, load_cases = small
    received0 = everywhere(sent0, ("sub", "coarse"))
    packet = (cases + rounded_up(corners, 16), face + wide)
    displaced0, first, second, kernel = call(
        functools.partial(first_kernel, chain=chain, groups=groups),
        [
            ((subs, cases, iface), F32),
            (packet, BF16),
            (packet, BF16),
            ((column, along), BF16),
        ],
        [schur_inverse, shard, regroup, *small, ahead0, *shards],
        fetch
        + [pltpu.VMEM(x.shape, x.dtype) for x in (shard, regroup)]
        + [pltpu.SemaphoreType.DMA((2,))],
        far=3,
        **work,
    )
    first, second = pair_swaps(first, second)
    own_lifts, bent0 = call(
        functools.partial(inner_kernel, chain=chain, groups=groups),
        [((subs, column, iface), BF16), ((subs, cases, iface), F32)],
        [displaced0, corner_coupling, corner_dofs, face_order],
        tables,
        flops=10**9,
        moved=2 * 10**6,
    )
    other = swapped(kernel, "coarse", bits[0]) if bits else kernel
    lifts, lifts_left, pull0, pull0_left, sent1, *joined = call(
        functools.partial(lift_kernel, groups=groups),
        [
            ((subs, column, iface), BF16),
            ((subs, column, face), BF16),
            ((subs, cases, iface), F32),
            ((subs, cases, face), F32),
            ((devices, cases, rounded_up(column + 2 * cases, LANES)), BF16),
        ]
        + [((2 * column, along), BF16)] * bool(bits),
        [bent0, own_lifts, first, second, received0, kernel, other, face_order],
        [pltpu.VMEM((cases, rounded_up(column + 2 * cases, LANES)), F32)],
        flops=10**9,
        moved=10**6,
    )
    received1 = everywhere(sent1, ("sub", "coarse"))
    displaced1, first, second = call(
        second_kernel,
        [((subs, cases, iface), F32), ((cases, face), BF16), ((cases, face), BF16)],
        [schur_inverse, pull0, face_order],
        fetch,
        far=1,
        **work,
    )
    first, second = pair_swaps(first, second)

    low = joined[0] if bits else kernel
    high = swapped(low, "coarse", bits[1]) if bits else kernel
    base, norms0, ahead1, *joined = call(
        middle_kernel,
        [((subs, cases, iface), F32), ((cases, cases), F32), ahead[1]]
        + [((4 * column, along), BF16)] * bool(bits),
        [schur_inverse, displaced1, received1, kernel, lifts, face_order, low, high, first],
        [row, *tables, pltpu.SemaphoreType.DMA((AHEAD[1],))],
        flops=10**9,
        moved=2 * 10**6,
        far=1,
    )
    pull1, bent2, after, sent2 = call(
        third_kernel,
        [
            ((subs, cases, face), F32),
            ((subs, cases, face), F32),
            ((cases, face), BF16),
            ((devices, cases + cases // 2, rounded_up(column + 2 * cases, LANES)), BF16),
        ],
        [schur_inverse, base, first, second, lifts_left, pull0_left, face_order, ahead1],
        [*fetch, tables[0], row],
        far=1,
        **work,
    )
    received2 = everywhere(sent2, ("sub", "coarse"))
    first, second = pair_swaps(after, after, wrap=False)
    if bits:
        blocks = [joined[0], swapped(joined[0], "coarse", bits[2])]
        slots = [0, bits[0], bits[1], bits[0] ^ bits[1]]
        slots = slots + [slot ^ bits[2] for slot in slots]
    else:
        slots = []
        sums = received2.reshape((chain, groups) + received2.shape[1:])[..., :cases, :wide]
        sums = jnp.sum(sums.astype(F32), axis=0)
        flat = jnp.moveaxis(sums, 0, 1).reshape(cases, along)
        own = lax.dynamic_index_in_dim(sums, lax.axis_index("coarse"), 0, keepdims=False)
        values = jnp.dot(flat, kernel.astype(F32).T, precision=lax.Precision.HIGHEST)
        energy = jnp.dot(values, own[:, :column].T, precision=lax.Precision.HIGHEST)
        blocks = [lax.psum(energy, "coarse")]
    multipliers, residual = call(
        functools.partial(scene_kernel, groups=groups, pieces=len(blocks), slots=slots),
        [((subs, scenes, face), F32), ((subs, scenes, face), F32)],
        [bent2, first, second, received2, joined[0] if bits else kernel, lifts_left, pull0_left]
        + [pull1, face_order, norms0]
        + [scene_loads.T, scene_weights.T, *blocks],
        [pltpu.VMEM((groups, cases, wide), F32), row]
        + [pltpu.VMEM((subs, scenes, face), F32)] * 2
        + [pltpu.SemaphoreType.DMA((2 * subs,))],
        flops=10**9,
        moved=4 * 10**6,
        ends=pltpu.HBM,
    )
    return (multipliers, residual)


def solution(mesh):
    return jax.shard_map(
        per_device,
        mesh=mesh,
        in_specs=(
            P(("sub", "coarse"), None, None),
            P(("sub", "coarse"), None, None),
            P(None, "coarse", None, "sub"),
            P(("sub", "coarse"), None, None),
            P(("sub", "coarse"), None),
            P(("sub", "coarse"), None),
            P(),
            P(),
        ),
        out_specs=(P(("sub", "coarse"), None, None), P(("sub", "coarse"), None, None)),
        check_vma=False,
    )
```

```python
import functools

import jax
import jax.numpy as jnp
import numpy as np
from jax import lax
from jax.experimental import pallas as pl
from jax.experimental.pallas import tpu as pltpu
from jax.sharding import PartitionSpec as P

LANES = 128
CHUNK = 256
F32, BF16 = jnp.float32, jnp.bfloat16


def nn(a, b):
    return lax.dot_general(a, b, (((1,), (0,)), ((), ())), preferred_element_type=F32)


def nt(a, b):
    return lax.dot_general(a, b, (((1,), (1,)), ((), ())), preferred_element_type=F32)


def halves(x):
    high = x.astype(BF16)
    return high, (x - high.astype(F32)).astype(BF16)


def stacked(x):
    return jnp.concatenate(halves(x), axis=0)


def folded(x):
    rows = x.shape[0] // 2
    return x[:rows] + x[rows:]


def nn2(x, narrow):
    return folded(nn(stacked(x), narrow))


def nt2(x, narrow):
    return folded(nt(stacked(x), narrow))


def both3(product, x, y):
    high, low = halves(y)
    return folded(product(stacked(x), high)) + product(x.astype(BF16), low)


def equal(a, b):
    return jnp.where(a == b, 1.0, 0.0).astype(BF16)


def iota(shape, dim):
    return lax.broadcasted_iota(jnp.int32, shape, dim)


def rounded_up(value, unit):
    return (value + unit - 1) // unit * unit


def table(order_row):
    size = order_row.shape[1]
    return equal(iota((size, size), 0), order_row)


def back_table(order, n):
    subs, size = order.shape
    rows = jnp.concatenate(
        [order[...].astype(F32), jnp.zeros((rounded_up(subs, 8) - subs, size), F32)], axis=0
    )
    return equal(rows.T[:, n : n + 1].astype(jnp.int32), iota((size, size), 1))


def fill_tables(tables, backs, order):
    for n in range(tables.shape[0]):
        tables[n] = table(order[n : n + 1])
        if n > 0:
            backs[n - 1] = back_table(order, n)


def spread_of(dofs_row, chain, corners, groups):
    column = chain * corners
    ids = iota((column, 1), 0)
    slot = sum((ids >= t * corners).astype(jnp.int32) for t in range(1, chain))
    target = ids + slot * ((groups - 1) * corners) + lax.axis_index("coarse") * corners
    return equal(target, dofs_row)


def placed(x, width, at):
    rows = x.shape[1]
    return nn(x, equal(iota((rows, width), 0) + at, iota((rows, width), 1)))


def by_parity(to_after, to_before):
    odd = (lax.axis_index("sub") & 1) == 1
    return jnp.where(odd, to_before, to_after), jnp.where(odd, to_after, to_before)


def start_fetch(matrix, held, sems):
    subs, size = matrix.shape[0], matrix.shape[1]
    copies = []
    for n in range(subs):
        for k in range(size // CHUNK):
            part = pl.ds(k * CHUNK, CHUNK)
            copy = pltpu.make_async_copy(
                matrix.at[n, part], held.at[n, part], sems.at[n * (size // CHUNK) + k]
            )
            copy.start()
            copies.append(copy)
    return copies


def times_matrix(x, n, held, copies):
    size = held.shape[1]
    count = size // CHUNK
    total = None
    for k in range(count):
        copies[n * count + k].wait()
        part = nn(x[:, k * CHUNK : (k + 1) * CHUNK], held[n, k * CHUNK : (k + 1) * CHUNK])
        total = part if total is None else total + part
    return total


def inner_jump(displaced, tables, backs):
    subs = len(displaced)
    face = tables.shape[1]
    lefts = [part[:, :face] for part in displaced]
    rights = [part[:, face:] for part in displaced]
    for n in range(1, subs):
        lefts[n] = lefts[n] - nn2(displaced[n - 1][:, face:], tables[n])
        rights[n - 1] = rights[n - 1] - nn2(displaced[n][:, :face], backs[n - 1])
    return lefts, rights


def outer_jump(lefts, rights, before, after):
    at_head = lax.axis_index("sub") == 0
    at_tail = lax.axis_index("sub") == lax.axis_size("sub") - 1
    lefts = [jnp.where(at_head, 0.0, lefts[0] - before), *lefts[1:]]
    rights = [*rights[:-1], jnp.where(at_tail, 0.0, rights[-1] - after)]
    return [jnp.concatenate(pair, axis=1) for pair in zip(lefts, rights)]


def chain_sums(received, groups, width):
    chain = received.shape[0] // groups
    sums = []
    for c in range(groups):
        total = None
        for z in range(chain):
            part = received[z * groups + c, :, :width].astype(F32)
            total = part if total is None else total + part
        sums.append(total)
    return sums


def copies_of(out, x):
    for i in range(out.shape[0]):
        out[i] = x


def fetched(pairs, sems):
    copies = [pltpu.make_async_copy(a, b, sems.at[i]) for i, (a, b) in enumerate(pairs)]
    for copy in copies:
        copy.start()
    return copies


def first_kernel(matrix, *refs, chain, groups):
    far, shards, refs = refs[:6], refs[6 : 5 + chain], refs[5 + chain :]
    out, first, second, kernel, sums, order, coupling, dofs, loads, *refs = refs
    shard, regroup, held, sems, small = refs
    near = (order, coupling, dofs, loads, shard, regroup)
    small_copies = fetched(list(zip(far, near)), small)
    copies = start_fetch(matrix, held, sems)
    for copy in small_copies:
        copy.wait()
    subs, cases, iface = loads.shape
    corners, face = coupling.shape[1], order.shape[1]
    pad = rounded_up(corners, 16) - corners
    total = None
    for n in range(subs):
        terms = nt(loads[n], coupling[n])
        part = nt2(terms, spread_of(dofs[n : n + 1], chain, corners, groups))
        total = part if total is None else total + part
    copies_of(sums, placed(total.astype(BF16), sums.shape[2], 0).astype(BF16))

    def packet(displaced, coupled, n):
        spread = spread_of(dofs[n : n + 1], chain, corners, groups)
        eye = equal(iota((corners, corners), 0), iota((corners, corners), 1))
        hot = placed(nt(eye, spread).astype(BF16), first.shape[1] - face, 0)
        lower = jnp.concatenate([coupled, hot], axis=1)
        upper = jnp.concatenate([displaced, jnp.zeros((cases, hot.shape[1]), F32)], axis=1)
        return jnp.concatenate([upper, lower, jnp.zeros((pad, lower.shape[1]), F32)], axis=0)

    for n in range(subs):
        out[n] = times_matrix(loads[n], n, held, copies)
        if n == 0:
            near = table(order[0:1])
            to_before = packet(
                nt(out[0, :, :face].astype(BF16), near), nt(coupling[0, :, :face], near), 0
            )
            position = lax.axis_index("sub")
            depth = groups * corners
            rows = None
            for j, block in enumerate([shard, *shards]):
                ids = iota((depth, regroup.shape[1]), 0) + (position ^ j) * depth
                part = nn(block[...], equal(ids, regroup[...]))
                rows = part if rows is None else rows + part
            kernel[...] = rows.astype(BF16)
    last = subs - 1
    to_after = packet(out[last, :, face:], coupling[last, :, face:].astype(F32), last)
    one, two = by_parity(to_after, to_before)
    first[...] = one.astype(BF16)
    second[...] = two.astype(BF16)


def inner_kernel(
    displaced, coupling, dofs, order, lifts, bent, tables, backs, *, chain, groups
):
    subs, cases, _ = displaced.shape
    corners, face = coupling.shape[1], order.shape[1]
    fill_tables(tables, backs, order)
    spreads = [spread_of(dofs[n : n + 1], chain, corners, groups) for n in range(subs)]
    for n in range(subs):
        left, right = nn(spreads[n], coupling[n, :, :face]), nn(spreads[n], coupling[n, :, face:])
        if n > 0:
            moved = nn(coupling[n - 1, :, face:], tables[n]).astype(BF16)
            left = left - nn(spreads[n - 1], moved)
        if n < subs - 1:
            moved = nn(coupling[n + 1, :, :face], backs[n]).astype(BF16)
            right = right - nn(spreads[n + 1], moved)
        lifts[n, :, :face] = left.astype(BF16)
        lifts[n, :, face:] = right.astype(BF16)
    lefts, rights = inner_jump([displaced[n] for n in range(subs)], tables, backs)
    for n in range(subs):
        bent[n, :, :face] = lefts[n]
        bent[n, :, face:] = rights[n]


def lift_kernel(
    bent, own_lifts, first, second, received, kernel, other, order,
    lifts, lifts_left, pull, pull_left, out, *refs, groups
):
    *joined, row = refs
    subs, cases, _ = bent.shape
    column, face = own_lifts.shape[1], order.shape[1]
    wide = rounded_up(column, LANES)
    join(joined, kernel, other)
    near = table(order[0:1])
    from_after, from_before = by_parity(first[...].astype(F32), second[...].astype(F32))
    eye = equal(iota((column, first.shape[1] - face), 0), iota((column, first.shape[1] - face), 1))

    def neighbour(block):
        low = block[cases:].astype(BF16)
        return low[:, :face], nt(eye, low[:, face:]).astype(BF16)

    before = nn(from_before[:, :face].astype(BF16), near)
    _, before_spread = neighbour(from_before)
    after_coupling, after_spread = neighbour(from_after)
    lifted = outer_jump(
        [own_lifts[n, :, :face].astype(F32) for n in range(subs)],
        [own_lifts[n, :, face:].astype(F32) for n in range(subs)],
        nn(before_spread, before[cases:].astype(BF16)).astype(BF16).astype(F32),
        nn(after_spread, after_coupling).astype(BF16).astype(F32),
    )
    bent = outer_jump(
        [bent[n, :, :face] for n in range(subs)],
        [bent[n, :, face:] for n in range(subs)],
        before[:cases],
        from_after[:cases, :face],
    )
    for n in range(subs):
        lifted[n] = lifted[n].astype(BF16)
        lifts[n] = lifted[n]
        lifts_left[n] = lifted[n][:, :face]
    flat = jnp.concatenate(chain_sums(received, groups, wide), axis=1)
    values = nt2(flat, kernel[...])
    corner, norms = None, None
    for n in range(subs):
        whole = bent[n] + nn2(values, lifted[n])
        pull[n] = whole
        left = whole[:, :face]
        pull_left[n] = left
        part, norm = nt2(left, lifted[n][:, :face]), both3(nt, left, left)
        corner = part if corner is None else corner + part
        norms = norm if norms is None else norms + norm
    row[...] = jnp.zeros(row.shape, F32)
    row[:, :column] = corner
    store_halves(row, norms, slice(0, cases), column)
    copies_of(out, row[...].astype(BF16))


def join(out, low, high):
    for ref in out:
        ref[: low.shape[0]] = low[...]
        ref[low.shape[0] :] = high[...]


def store_halves(row, gram, rows, at):
    for half in halves(gram):
        row[rows, at : at + gram.shape[1]] = half.astype(F32)
        at += gram.shape[1]


def sum_halves(row, rows, at, count):
    return row[rows, at : at + count] + row[rows, at + count : at + 2 * count]


def second_kernel(matrix, pull, order, out, first, second, held, sems):
    copies = start_fetch(matrix, held, sems)
    subs = pull.shape[0]
    face = order.shape[1]
    near = back_table(order, 0)
    for n in range(subs):
        out[n] = folded(times_matrix(stacked(pull[n]), n, held, copies))
    one, two = by_parity(out[subs - 1, :, face:], nn2(out[0, :, :face], near))
    first[...] = one.astype(BF16)
    second[...] = two.astype(BF16)


def middle_kernel(displaced, received, kernel, lifts, order, base, norms0, row, tables, backs):
    subs, cases, _ = displaced.shape
    column, face = lifts.shape[1], order.shape[1]
    wide = rounded_up(column, LANES)
    groups = kernel.shape[1] // wide
    fill_tables(tables, backs, order)
    sums = chain_sums(received, groups, received.shape[2])
    flat = jnp.concatenate([part[:, :wide] for part in sums], axis=1)
    values = nt2(flat, kernel[...])
    row[:cases] = sum(sums)
    norms0[...] = sum_halves(row, slice(0, cases), column, cases)
    lefts, rights = inner_jump([displaced[n] for n in range(subs)], tables, backs)
    for n in range(subs):
        base[n] = jnp.concatenate([lefts[n], rights[n]], axis=1) + nn2(values, lifts[n])


def third_kernel(matrix, base, first, second, lifts, pull0, order, low, high, *refs):
    pull, bent2, after, payload, *joined, held, sems, tables, _, row = refs
    copies = start_fetch(matrix, held, sems)
    subs, cases, _ = base.shape
    face = order.shape[1]
    column = lifts.shape[1]
    for n in range(subs):
        tables[n] = table(order[n : n + 1])
    join(joined, low, high)
    from_after, from_before = by_parity(first[...].astype(F32), second[...].astype(F32))
    bent = outer_jump(
        [base[n, :, :face] for n in range(subs)],
        [base[n, :, face:] for n in range(subs)],
        nn(from_before.astype(BF16), tables[0]),
        from_after,
    )
    corner, gram1, gram2, gram3 = None, None, None, None

    def plus(total, part):
        return part if total is None else total + part

    for n in range(subs):
        left = bent[n][:, :face]
        pull[n] = left
        corner = plus(corner, nt2(left, lifts[n]))
        gram1 = plus(gram1, both3(nt, pull0[n], left))
        gram2 = plus(gram2, both3(nt, left, left))
    row[...] = jnp.zeros(row.shape, F32)
    row[:cases, :column] = corner
    store_halves(row, gram1, slice(0, cases), column)
    for n in range(subs):
        moved = folded(times_matrix(stacked(bent[n]), n, held, copies))
        bent2[n] = moved[:, :face]
        if n > 0:
            bent2[n] = moved[:, :face] - nn2(previous, tables[n])
        previous = moved[:, face:]
        gram3 = plus(gram3, both3(nt, bent[n], moved))
    after[...] = previous.astype(BF16)
    step = cases // 2
    for j in range(2):
        for i, gram in enumerate((gram2, gram3)):
            part = gram[j * step : (j + 1) * step]
            store_halves(row, part, slice(cases, cases + step), (4 * j + 2 * i) * cases)
    copies_of(payload, row[...].astype(BF16))


def scene_kernel(
    bent, first, second, received, kernel, lifts, pull0, pull1, order, norms0,
    scene_loads, scene_weights, *refs, groups, pieces, slots
):
    blocks = refs[:pieces]
    multipliers_far, residual_far, held, row, multipliers, residual, sems = refs[pieces:]
    subs, cases, _ = bent.shape
    column = lifts.shape[1]
    wide = rounded_up(column, LANES)
    group = lax.axis_index("coarse")
    sums = chain_sums(received, groups, received.shape[2])
    for c in range(groups):
        held[c] = sums[c][:cases, :wide]
    flat = jnp.concatenate([held[c] for c in range(groups)], axis=1)
    values = nt2(flat, kernel[:column])
    if groups_whole(blocks, column, groups):
        lifted, index = None, iter(slots)
        for block in blocks:
            for i in range(block.shape[0] // column):
                sums_here = held[group ^ next(index)][:, :column]
                part = nn2(sums_here, block[i * column : (i + 1) * column])
                lifted = part if lifted is None else lifted + part
        energy = both3(nt, lifted, flat)
    else:
        energy = blocks[0][...]
    row[...] = sum(sums)
    norms1 = sum_halves(row, slice(0, cases), column, cases)
    lower = slice(cases, cases + cases // 2)
    norms2, norms3 = (
        jnp.concatenate(
            [sum_halves(row, lower, (4 * j + 2 * i) * cases, cases) for j in range(2)], axis=0
        )
        for i in range(2)
    )
    norms3 = norms3 + energy

    ids = iota((cases, scene_loads.shape[1]), 0)
    mixing = sum(
        jnp.where(ids == scene_loads[i : i + 1], scene_weights[i : i + 1], 0.0)
        for i in range(scene_loads.shape[0])
    )

    def moment(norms):
        return jnp.sum(both3(nn, norms, mixing) * mixing, axis=0, keepdims=True)

    moment0, moment1 = moment(norms0[...]), moment(norms1)
    moment2, moment3 = moment(norms2), moment(norms3)
    step0 = moment0 / moment1
    norm1 = moment0 - 2.0 * step0 * moment1 + step0 * step0 * moment2
    grow = 1.0 + norm1 / moment0
    curvature = grow * grow * moment1 - 2.0 * grow * step0 * moment2 + step0 * step0 * moment3
    step1 = norm1 / curvature
    zeros = jnp.zeros_like(mixing)

    def transposed(parts):
        weights = -jnp.concatenate(parts, axis=0)
        high = weights.astype(BF16).astype(F32)
        return jnp.concatenate([high, high, weights - high], axis=0).T.astype(BF16)

    for_multipliers = transposed(
        [(step0 + step1 * grow) * mixing, (-step0 * step1) * mixing, zeros]
    )
    for_residual = transposed(
        [mixing, (-step0 - step1 * grow) * mixing, (step0 * step1) * mixing]
    )
    _, from_before = by_parity(first[...].astype(F32), second[...].astype(F32))
    copies = []
    for n in range(subs):
        pull2 = bent[n]
        if n == 0:
            pull2 = pull2 - nn(from_before.astype(BF16), table(order[0:1]))
            pull2 = jnp.where(lax.axis_index("sub") == 0, 0.0, pull2)
        pull2 = pull2 + nn2(values, lifts[n])
        basis = jnp.concatenate([pull0[n], pull1[n], pull2], axis=0)
        high, low = halves(basis)
        basis = jnp.concatenate([high, low, high], axis=0)
        multipliers[n] = nn(for_multipliers, basis)
        copies += fetched([(multipliers.at[n], multipliers_far.at[n])], sems.at[pl.ds(2 * n, 1)])
        residual[n] = nn(for_residual, basis)
        copies += fetched([(residual.at[n], residual_far.at[n])], sems.at[pl.ds(2 * n + 1, 1)])
    for copy in copies:
        copy.wait()


def groups_whole(blocks, column, groups):
    return sum(block.shape[0] for block in blocks) == column * groups


def everywhere(x, axes):
    return lax.all_to_all(x, axes, 0, 0)


def swapped(x, axis, bit):
    return lax.ppermute(x, axis, [(i, i ^ bit) for i in range(lax.axis_size(axis))])


def pair_swaps(first, second, wrap=True):
    length = lax.axis_size("sub")

    def partner(i, j):
        return (i, j % length if wrap or 0 <= j < length else i)

    one = lax.ppermute(first, "sub", [partner(i, i ^ 1) for i in range(length)])
    two = lax.ppermute(
        second, "sub", [partner(i, i + 1 if i & 1 else i - 1) for i in range(length)]
    )
    return one, two


def call(kernel, outs, args, scratch=(), flops=0, moved=0, far=0, ends=pltpu.VMEM):
    specs = [pl.BlockSpec(memory_space=pltpu.HBM)] * far
    specs += [pl.BlockSpec(memory_space=pltpu.VMEM)] * (len(args) - far)
    pinned = [pltpu.with_memory_space_constraint(x, pltpu.HBM) for x in args[:far]]
    shapes = [jax.ShapeDtypeStruct(shape, kind) for shape, kind in outs]
    return pl.pallas_call(
        kernel,
        out_shape=shapes,
        in_specs=specs,
        out_specs=[pl.BlockSpec(memory_space=ends)] * len(outs),
        scratch_shapes=list(scratch),
        compiler_params=pltpu.CompilerParams(vmem_limit_bytes=32 << 20),
        cost_estimate=pl.CostEstimate(flops=flops, bytes_accessed=moved, transcendentals=0),
    )(*pinned, *args[far:])


def per_device(
    schur_inverse,
    corner_coupling,
    coarse_inverse,
    load_cases,
    face_order,
    corner_dofs,
    scene_loads,
    scene_weights,
):
    subs, iface = schur_inverse.shape[0], schur_inverse.shape[1]
    face = face_order.shape[1]
    corners = corner_dofs.shape[1]
    cases = load_cases.shape[1]
    scenes = scene_loads.shape[0]
    chain, groups = lax.axis_size("sub"), lax.axis_size("coarse")
    devices = chain * groups
    column = chain * corners
    wide = rounded_up(column, LANES)
    along = groups * wide
    work = dict(flops=4 * cases * schur_inverse.size, moved=2 * schur_inverse.size)

    fetch = [
        pltpu.VMEM(schur_inverse.shape, BF16),
        pltpu.SemaphoreType.DMA((subs * (iface // CHUNK),)),
    ]
    tables = [
        pltpu.VMEM((subs, face, face), BF16), pltpu.VMEM((max(subs - 1, 1), face, face), BF16)
    ]
    row = pltpu.VMEM((cases + cases // 2, rounded_up(column + 2 * cases, LANES)), F32)

    shard = coarse_inverse.reshape(column, groups * corners)
    shards = [swapped(shard, "sub", j) for j in range(1, chain)]

    lane = np.arange(along)
    inner = lane % wide
    source = (inner // corners * groups + lane // wide) * corners + inner % corners
    regroup = jnp.asarray(np.where(inner < column, source, -1)[None].astype(np.int32))

    bits = []
    if groups == 1 << 3 and (column * groups) ** 2 <= schur_inverse.size:
        bits = [1 << b for b in reversed(range(groups.bit_length() - 1))]

    packet = (cases + rounded_up(corners, 16), face + wide)
    small = [face_order, corner_coupling, corner_dofs, load_cases]
    displaced0, first, second, kernel, sent0, *small = call(
        functools.partial(first_kernel, chain=chain, groups=groups),
        [
            ((subs, cases, iface), F32),
            (packet, BF16),
            (packet, BF16),
            ((column, along), BF16),
            ((devices, cases, wide), BF16),
        ]
        + [(x.shape, x.dtype) for x in small],
        [schur_inverse, *small, shard, regroup, *shards],
        [pltpu.VMEM(x.shape, x.dtype) for x in (shard, regroup)]
        + [*fetch, pltpu.SemaphoreType.DMA((6,))],
        far=7,
        **work,
    )
    face_order, corner_coupling, corner_dofs, _ = small
    received0 = everywhere(sent0, ("sub", "coarse"))
    first, second = pair_swaps(first, second)
    own_lifts, bent0 = call(
        functools.partial(inner_kernel, chain=chain, groups=groups),
        [((subs, column, iface), BF16), ((subs, cases, iface), F32)],
        [displaced0, corner_coupling, corner_dofs, face_order],
        tables,
        flops=10**9,
        moved=2 * 10**6,
    )
    other = swapped(kernel, "coarse", bits[0]) if bits else kernel
    lifts, lifts_left, pull0, pull0_left, sent1, *joined = call(
        functools.partial(lift_kernel, groups=groups),
        [
            ((subs, column, iface), BF16),
            ((subs, column, face), BF16),
            ((subs, cases, iface), F32),
            ((subs, cases, face), F32),
            ((devices, cases, rounded_up(column + 2 * cases, LANES)), BF16),
        ]
        + [((2 * column, along), BF16)] * bool(bits),
        [bent0, own_lifts, first, second, received0, kernel, other, face_order],
        [pltpu.VMEM((cases, rounded_up(column + 2 * cases, LANES)), F32)],
        flops=10**9,
        moved=10**6,
    )
    received1 = everywhere(sent1, ("sub", "coarse"))
    displaced1, first, second = call(
        second_kernel,
        [((subs, cases, iface), F32), ((cases, face), BF16), ((cases, face), BF16)],
        [schur_inverse, pull0, face_order],
        fetch,
        far=1,
        **work,
    )
    first, second = pair_swaps(first, second)

    low = joined[0] if bits else kernel
    high = swapped(low, "coarse", bits[1]) if bits else kernel
    base, norms0 = call(
        middle_kernel,
        [((subs, cases, iface), F32), ((cases, cases), F32)],
        [displaced1, received1, kernel, lifts, face_order],
        [row, *tables],
        flops=10**9,
        moved=2 * 10**6,
    )
    pull1, bent2, after, sent2, *joined = call(
        third_kernel,
        [
            ((subs, cases, face), F32),
            ((subs, cases, face), F32),
            ((cases, face), BF16),
            ((devices, cases + cases // 2, rounded_up(column + 2 * cases, LANES)), BF16),
        ]
        + [((4 * column, along), BF16)] * bool(bits),
        [schur_inverse, base, first, second, lifts_left, pull0_left, face_order, low, high],
        [*fetch, *tables, row],
        far=1,
        **work,
    )
    received2 = everywhere(sent2, ("sub", "coarse"))
    first, second = pair_swaps(after, after, wrap=False)
    if bits:
        blocks = [joined[0], swapped(joined[0], "coarse", bits[2])]
        slots = [0, bits[0], bits[1], bits[0] ^ bits[1]]
        slots = slots + [slot ^ bits[2] for slot in slots]
    else:
        slots = []
        sums = received2.reshape((chain, groups) + received2.shape[1:])[..., :cases, :wide]
        sums = jnp.sum(sums.astype(F32), axis=0)
        flat = jnp.moveaxis(sums, 0, 1).reshape(cases, along)
        own = lax.dynamic_index_in_dim(sums, lax.axis_index("coarse"), 0, keepdims=False)
        values = jnp.dot(flat, kernel.astype(F32).T, precision=lax.Precision.HIGHEST)
        energy = jnp.dot(values, own[:, :column].T, precision=lax.Precision.HIGHEST)
        blocks = [lax.psum(energy, "coarse")]
    multipliers, residual = call(
        functools.partial(scene_kernel, groups=groups, pieces=len(blocks), slots=slots),
        [((subs, scenes, face), F32), ((subs, scenes, face), F32)],
        [bent2, first, second, received2, joined[0] if bits else kernel, lifts_left, pull0_left]
        + [pull1, face_order, norms0]
        + [scene_loads.T, scene_weights.T, *blocks],
        [pltpu.VMEM((groups, cases, wide), F32), row]
        + [pltpu.VMEM((subs, scenes, face), F32)] * 2
        + [pltpu.SemaphoreType.DMA((2 * subs,))],
        flops=10**9,
        moved=4 * 10**6,
        ends=pltpu.HBM,
    )
    return (multipliers, residual)


def solution(mesh):
    return jax.shard_map(
        per_device,
        mesh=mesh,
        in_specs=(
            P(("sub", "coarse"), None, None),
            P(("sub", "coarse"), None, None),
            P(None, "coarse", None, "sub"),
            P(("sub", "coarse"), None, None),
            P(("sub", "coarse"), None),
            P(("sub", "coarse"), None),
            P(),
            P(),
        ),
        out_specs=(P(("sub", "coarse"), None, None), P(("sub", "coarse"), None, None)),
        check_vma=False,
    )
```

```python
import functools

import jax
import jax.numpy as jnp
import numpy as np
from jax import lax
from jax.experimental import pallas as pl
from jax.experimental.pallas import tpu as pltpu
from jax.sharding import PartitionSpec as P

LANES = 128
CHUNK = 256
AHEAD = 3
F32, BF16 = jnp.float32, jnp.bfloat16


def nn(a, b):
    return lax.dot_general(a, b, (((1,), (0,)), ((), ())), preferred_element_type=F32)


def nt(a, b):
    return lax.dot_general(a, b, (((1,), (1,)), ((), ())), preferred_element_type=F32)


def halves(x):
    high = x.astype(BF16)
    return high, (x - high.astype(F32)).astype(BF16)


def stacked(x):
    return jnp.concatenate(halves(x), axis=0)


def folded(x):
    rows = x.shape[0] // 2
    return x[:rows] + x[rows:]


def nn2(x, narrow):
    return folded(nn(stacked(x), narrow))


def nt2(x, narrow):
    return folded(nt(stacked(x), narrow))


def both3(product, x, y):
    high, low = halves(y)
    return folded(product(stacked(x), high)) + product(x.astype(BF16), low)


def equal(a, b):
    return jnp.where(a == b, 1.0, 0.0).astype(BF16)


def iota(shape, dim):
    return lax.broadcasted_iota(jnp.int32, shape, dim)


def rounded_up(value, unit):
    return (value + unit - 1) // unit * unit


def table(order_row):
    size = order_row.shape[1]
    return equal(iota((size, size), 0), order_row)


def back_table(order, n):
    subs, size = order.shape
    rows = jnp.concatenate(
        [order[...].astype(F32), jnp.zeros((rounded_up(subs, 8) - subs, size), F32)], axis=0
    )
    return equal(rows.T[:, n : n + 1].astype(jnp.int32), iota((size, size), 1))


def fill_tables(tables, backs, order):
    for n in range(tables.shape[0]):
        tables[n] = table(order[n : n + 1])
        if n > 0:
            backs[n - 1] = back_table(order, n)


def spread_of(dofs_row, chain, corners, groups):
    column = chain * corners
    ids = iota((column, 1), 0)
    slot = sum((ids >= t * corners).astype(jnp.int32) for t in range(1, chain))
    target = ids + slot * ((groups - 1) * corners) + lax.axis_index("coarse") * corners
    return equal(target, dofs_row)


def placed(x, width, at):
    rows = x.shape[1]
    return nn(x, equal(iota((rows, width), 0) + at, iota((rows, width), 1)))


def by_parity(to_after, to_before):
    odd = (lax.axis_index("sub") & 1) == 1
    return jnp.where(odd, to_before, to_after), jnp.where(odd, to_after, to_before)


def start_fetch(matrix, held, sems, ready=0):
    subs, size = matrix.shape[0], matrix.shape[1]
    copies = []
    for n in range(subs):
        for k in range(size // CHUNK):
            copies.append(None)
            if len(copies) > ready:
                rows = pl.ds(k * CHUNK, CHUNK)
                half = size // 2
                columns = pl.ds(0, size) if k * CHUNK < half else pl.ds(half, half)
                copies[-1] = pltpu.make_async_copy(
                    matrix.at[n, rows, columns],
                    held.at[n, rows, columns],
                    sems.at[n * (size // CHUNK) + k],
                )
                copies[-1].start()
    return copies


def start_ahead(matrix, ahead, sems):
    copies = []
    for k in range(ahead.shape[0] // CHUNK):
        part = pl.ds(k * CHUNK, CHUNK)
        copies.append(pltpu.make_async_copy(matrix.at[0, part], ahead.at[part], sems.at[k]))
        copies[-1].start()
    return copies


def times_matrix(x, n, held, copies, ahead=None):
    size = held.shape[1]
    count, half = size // CHUNK, size // 2
    left, right, turned = None, None, []

    def plus(total, part):
        return part if total is None else total + part

    for k in range(count):
        rows = slice(k * CHUNK, (k + 1) * CHUNK)
        if copies[n * count + k] is not None:
            copies[n * count + k].wait()
        if k * CHUNK < half:
            chunk = ahead[rows] if copies[n * count + k] is None else held[n, rows]
            part = nn(x[:, rows], chunk)
            left = plus(left, part[:, :half])
            right = plus(right, part[:, half:])
            turned.append(nt(x[:, half:], chunk[:, half:]))
        else:
            right = plus(right, nn(x[:, rows], held[n, rows, half:]))
    return jnp.concatenate([left + jnp.concatenate(turned, axis=1), right], axis=1)


def inner_jump(displaced, tables, backs):
    subs = len(displaced)
    face = tables.shape[1]
    lefts = [part[:, :face] for part in displaced]
    rights = [part[:, face:] for part in displaced]
    for n in range(1, subs):
        lefts[n] = lefts[n] - nn2(displaced[n - 1][:, face:], tables[n])
        rights[n - 1] = rights[n - 1] - nn2(displaced[n][:, :face], backs[n - 1])
    return lefts, rights


def outer_jump(lefts, rights, before, after):
    at_head = lax.axis_index("sub") == 0
    at_tail = lax.axis_index("sub") == lax.axis_size("sub") - 1
    lefts = [jnp.where(at_head, 0.0, lefts[0] - before), *lefts[1:]]
    rights = [*rights[:-1], jnp.where(at_tail, 0.0, rights[-1] - after)]
    return [jnp.concatenate(pair, axis=1) for pair in zip(lefts, rights)]


def chain_sums(received, groups, width):
    chain = received.shape[0] // groups
    sums = []
    for c in range(groups):
        total = None
        for z in range(chain):
            part = received[z * groups + c, :, :width].astype(F32)
            total = part if total is None else total + part
        sums.append(total)
    return sums


def copies_of(out, x):
    for i in range(out.shape[0]):
        out[i] = x


def fetched(pairs, sems):
    copies = [pltpu.make_async_copy(a, b, sems.at[i]) for i, (a, b) in enumerate(pairs)]
    for copy in copies:
        copy.start()
    return copies


def corner_kernel(*refs, chain, groups):
    far, out, (order, coupling, dofs, loads), sems = refs[:4], refs[4], refs[5:9], refs[9]
    for copy in fetched(list(zip(far, refs[5:9])), sems):
        copy.wait()
    corners = coupling.shape[1]
    total = None
    for n in range(loads.shape[0]):
        terms = nt(loads[n], coupling[n])
        part = nt2(terms, spread_of(dofs[n : n + 1], chain, corners, groups))
        total = part if total is None else total + part
    copies_of(out, placed(total.astype(BF16), out.shape[2], 0).astype(BF16))


def first_kernel(
    matrix, shard_far, regroup_far, order, coupling, dofs, loads, *refs, chain, groups
):
    shards, refs = refs[: chain - 1], refs[chain - 1 :]
    out, first, second, kernel, held, sems, shard, regroup, small = refs
    copies = start_fetch(matrix, held, sems)
    small_copies = fetched([(shard_far, shard), (regroup_far, regroup)], small)
    subs, cases, iface = loads.shape
    corners, face = coupling.shape[1], order.shape[1]
    pad = rounded_up(corners, 16) - corners

    def packet(displaced, coupled, n):
        spread = spread_of(dofs[n : n + 1], chain, corners, groups)
        eye = equal(iota((corners, corners), 0), iota((corners, corners), 1))
        hot = placed(nt(eye, spread).astype(BF16), first.shape[1] - face, 0)
        lower = jnp.concatenate([coupled, hot], axis=1)
        upper = jnp.concatenate([displaced, jnp.zeros((cases, hot.shape[1]), F32)], axis=1)
        return jnp.concatenate([upper, lower, jnp.zeros((pad, lower.shape[1]), F32)], axis=0)

    for n in range(subs):
        out[n] = times_matrix(loads[n], n, held, copies)
        if n == 0:
            near = table(order[0:1])
            to_before = packet(
                nt(out[0, :, :face].astype(BF16), near), nt(coupling[0, :, :face], near), 0
            )
            for copy in small_copies:
                copy.wait()
            position = lax.axis_index("sub")
            depth = groups * corners
            rows = None
            for j, block in enumerate([shard, *shards]):
                ids = iota((depth, regroup.shape[1]), 0) + (position ^ j) * depth
                part = nn(block[...], equal(ids, regroup[...]))
                rows = part if rows is None else rows + part
            kernel[...] = rows.astype(BF16)
    last = subs - 1
    to_after = packet(out[last, :, face:], coupling[last, :, face:].astype(F32), last)
    one, two = by_parity(to_after, to_before)
    first[...] = one.astype(BF16)
    second[...] = two.astype(BF16)


def inner_kernel(
    displaced, coupling, dofs, order, lifts, bent, tables, backs, *, chain, groups
):
    subs, cases, _ = displaced.shape
    corners, face = coupling.shape[1], order.shape[1]
    fill_tables(tables, backs, order)
    spreads = [spread_of(dofs[n : n + 1], chain, corners, groups) for n in range(subs)]
    for n in range(subs):
        left, right = nn(spreads[n], coupling[n, :, :face]), nn(spreads[n], coupling[n, :, face:])
        if n > 0:
            moved = nn(coupling[n - 1, :, face:], tables[n]).astype(BF16)
            left = left - nn(spreads[n - 1], moved)
        if n < subs - 1:
            moved = nn(coupling[n + 1, :, :face], backs[n]).astype(BF16)
            right = right - nn(spreads[n + 1], moved)
        lifts[n, :, :face] = left.astype(BF16)
        lifts[n, :, face:] = right.astype(BF16)
    lefts, rights = inner_jump([displaced[n] for n in range(subs)], tables, backs)
    for n in range(subs):
        bent[n, :, :face] = lefts[n]
        bent[n, :, face:] = rights[n]


def lift_kernel(
    bent, own_lifts, first, second, received, kernel, other, order,
    lifts, lifts_left, pull, pull_left, out, *refs, groups
):
    *joined, row = refs
    subs, cases, _ = bent.shape
    column, face = own_lifts.shape[1], order.shape[1]
    wide = rounded_up(column, LANES)
    join(joined, kernel, other)
    near = table(order[0:1])
    from_after, from_before = by_parity(first[...].astype(F32), second[...].astype(F32))
    eye = equal(iota((column, first.shape[1] - face), 0), iota((column, first.shape[1] - face), 1))

    def neighbour(block):
        low = block[cases:].astype(BF16)
        return low[:, :face], nt(eye, low[:, face:]).astype(BF16)

    before = nn(from_before[:, :face].astype(BF16), near)
    _, before_spread = neighbour(from_before)
    after_coupling, after_spread = neighbour(from_after)
    lifted = outer_jump(
        [own_lifts[n, :, :face].astype(F32) for n in range(subs)],
        [own_lifts[n, :, face:].astype(F32) for n in range(subs)],
        nn(before_spread, before[cases:].astype(BF16)).astype(BF16).astype(F32),
        nn(after_spread, after_coupling).astype(BF16).astype(F32),
    )
    bent = outer_jump(
        [bent[n, :, :face] for n in range(subs)],
        [bent[n, :, face:] for n in range(subs)],
        before[:cases],
        from_after[:cases, :face],
    )
    for n in range(subs):
        lifted[n] = lifted[n].astype(BF16)
        lifts[n] = lifted[n]
        lifts_left[n] = lifted[n][:, :face]
    flat = jnp.concatenate(chain_sums(received, groups, wide), axis=1)
    values = nt2(flat, kernel[...])
    corner, norms = None, None
    for n in range(subs):
        whole = bent[n] + nn2(values, lifted[n])
        pull[n] = whole
        left = whole[:, :face]
        pull_left[n] = left
        part, norm = nt2(left, lifted[n][:, :face]), both3(nt, left, left)
        corner = part if corner is None else corner + part
        norms = norm if norms is None else norms + norm
    row[...] = jnp.zeros(row.shape, F32)
    row[:, :column] = corner
    store_halves(row, norms, slice(0, cases), column)
    copies_of(out, row[...].astype(BF16))


def join(out, low, high):
    for ref in out:
        ref[: low.shape[0]] = low[...]
        ref[low.shape[0] :] = high[...]


def store_halves(row, gram, rows, at):
    for half in halves(gram):
        row[rows, at : at + gram.shape[1]] = half.astype(F32)
        at += gram.shape[1]


def sum_halves(row, rows, at, count):
    return row[rows, at : at + count] + row[rows, at + count : at + 2 * count]


def second_kernel(matrix, pull, order, out, first, second, held, sems):
    copies = start_fetch(matrix, held, sems)
    subs = pull.shape[0]
    face = order.shape[1]
    near = back_table(order, 0)
    for n in range(subs):
        out[n] = folded(times_matrix(stacked(pull[n]), n, held, copies))
    one, two = by_parity(out[subs - 1, :, face:], nn2(out[0, :, :face], near))
    first[...] = one.astype(BF16)
    second[...] = two.astype(BF16)


def middle_kernel(matrix, displaced, received, kernel, lifts, order, *refs):
    base, norms0, ahead, row, tables, backs, ahead_sems = refs
    copies = start_ahead(matrix, ahead, ahead_sems)
    subs, cases, _ = displaced.shape
    column, face = lifts.shape[1], order.shape[1]
    wide = rounded_up(column, LANES)
    groups = kernel.shape[1] // wide
    fill_tables(tables, backs, order)
    sums = chain_sums(received, groups, received.shape[2])
    flat = jnp.concatenate([part[:, :wide] for part in sums], axis=1)
    values = nt2(flat, kernel[...])
    row[:cases] = sum(sums)
    norms0[...] = sum_halves(row, slice(0, cases), column, cases)
    lefts, rights = inner_jump([displaced[n] for n in range(subs)], tables, backs)
    for n in range(subs):
        base[n] = jnp.concatenate([lefts[n], rights[n]], axis=1) + nn2(values, lifts[n])
    for copy in copies:
        copy.wait()


def third_kernel(matrix, base, first, second, lifts, pull0, order, ahead, low, high, *refs):
    pull, bent2, after, payload, *joined, held, sems, tables, _, row = refs
    copies = start_fetch(matrix, held, sems, ahead.shape[0] // CHUNK)
    subs, cases, _ = base.shape
    face = order.shape[1]
    column = lifts.shape[1]
    for n in range(subs):
        tables[n] = table(order[n : n + 1])
    join(joined, low, high)
    from_after, from_before = by_parity(first[...].astype(F32), second[...].astype(F32))
    bent = outer_jump(
        [base[n, :, :face] for n in range(subs)],
        [base[n, :, face:] for n in range(subs)],
        nn(from_before.astype(BF16), tables[0]),
        from_after,
    )
    totals = None
    for n in range(subs):
        whole = bent[n]
        left = whole[:, :face]
        pull[n] = left
        moved = folded(times_matrix(stacked(whole), n, held, copies, ahead))
        bent2[n] = moved[:, :face]
        if n > 0:
            bent2[n] = moved[:, :face] - nn2(previous, tables[n])
        previous = moved[:, face:]
        parts = [
            nt2(left, lifts[n]),
            both3(nt, pull0[n], left),
            both3(nt, left, left),
            both3(nt, whole, moved),
        ]
        totals = parts if totals is None else [a + b for a, b in zip(totals, parts)]
    after[...] = previous.astype(BF16)
    corner, gram1, gram2, gram3 = totals
    row[...] = jnp.zeros(row.shape, F32)
    row[:cases, :column] = corner
    store_halves(row, gram1, slice(0, cases), column)
    step = cases // 2
    for j in range(2):
        for i, gram in enumerate((gram2, gram3)):
            part = gram[j * step : (j + 1) * step]
            store_halves(row, part, slice(cases, cases + step), (4 * j + 2 * i) * cases)
    copies_of(payload, row[...].astype(BF16))


def scene_kernel(
    bent, first, second, received, kernel, lifts, pull0, pull1, order, norms0,
    scene_loads, scene_weights, *refs, groups, pieces, slots
):
    blocks = refs[:pieces]
    multipliers_far, residual_far, held, row, multipliers, residual, sems = refs[pieces:]
    subs, cases, _ = bent.shape
    column = lifts.shape[1]
    wide = rounded_up(column, LANES)
    group = lax.axis_index("coarse")
    sums = chain_sums(received, groups, received.shape[2])
    for c in range(groups):
        held[c] = sums[c][:cases, :wide]
    flat = jnp.concatenate([held[c] for c in range(groups)], axis=1)
    values = nt2(flat, kernel[:column])
    if groups_whole(blocks, column, groups):
        lifted, index = None, iter(slots)
        for block in blocks:
            for i in range(block.shape[0] // column):
                sums_here = held[group ^ next(index)][:, :column]
                part = nn2(sums_here, block[i * column : (i + 1) * column])
                lifted = part if lifted is None else lifted + part
        energy = both3(nt, lifted, flat)
    else:
        energy = blocks[0][...]
    row[...] = sum(sums)
    norms1 = sum_halves(row, slice(0, cases), column, cases)
    lower = slice(cases, cases + cases // 2)
    norms2, norms3 = (
        jnp.concatenate(
            [sum_halves(row, lower, (4 * j + 2 * i) * cases, cases) for j in range(2)], axis=0
        )
        for i in range(2)
    )
    norms3 = norms3 + energy

    ids = iota((cases, scene_loads.shape[1]), 0)
    mixing = sum(
        jnp.where(ids == scene_loads[i : i + 1], scene_weights[i : i + 1], 0.0)
        for i in range(scene_loads.shape[0])
    )

    def moment(norms):
        return jnp.sum(both3(nn, norms, mixing) * mixing, axis=0, keepdims=True)

    moment0, moment1 = moment(norms0[...]), moment(norms1)
    moment2, moment3 = moment(norms2), moment(norms3)
    step0 = moment0 / moment1
    norm1 = moment0 - 2.0 * step0 * moment1 + step0 * step0 * moment2
    grow = 1.0 + norm1 / moment0
    curvature = grow * grow * moment1 - 2.0 * grow * step0 * moment2 + step0 * step0 * moment3
    step1 = norm1 / curvature
    zeros = jnp.zeros_like(mixing)

    def transposed(parts):
        weights = -jnp.concatenate(parts, axis=0)
        high = weights.astype(BF16).astype(F32)
        return jnp.concatenate([high, high, weights - high], axis=0).T.astype(BF16)

    for_multipliers = transposed(
        [(step0 + step1 * grow) * mixing, (-step0 * step1) * mixing, zeros]
    )
    for_residual = transposed(
        [mixing, (-step0 - step1 * grow) * mixing, (step0 * step1) * mixing]
    )
    _, from_before = by_parity(first[...].astype(F32), second[...].astype(F32))
    copies = []
    for n in range(subs):
        pull2 = bent[n]
        if n == 0:
            pull2 = pull2 - nn(from_before.astype(BF16), table(order[0:1]))
            pull2 = jnp.where(lax.axis_index("sub") == 0, 0.0, pull2)
        pull2 = pull2 + nn2(values, lifts[n])
        basis = jnp.concatenate([pull0[n], pull1[n], pull2], axis=0)
        high, low = halves(basis)
        basis = jnp.concatenate([high, low, high], axis=0)
        multipliers[n] = nn(for_multipliers, basis)
        copies += fetched([(multipliers.at[n], multipliers_far.at[n])], sems.at[pl.ds(2 * n, 1)])
        residual[n] = nn(for_residual, basis)
        copies += fetched([(residual.at[n], residual_far.at[n])], sems.at[pl.ds(2 * n + 1, 1)])
    for copy in copies:
        copy.wait()


def groups_whole(blocks, column, groups):
    return sum(block.shape[0] for block in blocks) == column * groups


def everywhere(x, axes):
    return lax.all_to_all(x, axes, 0, 0)


def swapped(x, axis, bit):
    return lax.ppermute(x, axis, [(i, i ^ bit) for i in range(lax.axis_size(axis))])


def pair_swaps(first, second, wrap=True):
    length = lax.axis_size("sub")

    def partner(i, j):
        return (i, j % length if wrap or 0 <= j < length else i)

    one = lax.ppermute(first, "sub", [partner(i, i ^ 1) for i in range(length)])
    two = lax.ppermute(
        second, "sub", [partner(i, i + 1 if i & 1 else i - 1) for i in range(length)]
    )
    return one, two


def call(kernel, outs, args, scratch=(), flops=0, moved=0, far=0, ends=pltpu.VMEM):
    specs = [pl.BlockSpec(memory_space=pltpu.HBM)] * far
    specs += [pl.BlockSpec(memory_space=pltpu.VMEM)] * (len(args) - far)
    pinned = [pltpu.with_memory_space_constraint(x, pltpu.HBM) for x in args[:far]]
    shapes = [jax.ShapeDtypeStruct(shape, kind) for shape, kind in outs]
    return pl.pallas_call(
        kernel,
        out_shape=shapes,
        in_specs=specs,
        out_specs=[pl.BlockSpec(memory_space=ends)] * len(outs),
        scratch_shapes=list(scratch),
        compiler_params=pltpu.CompilerParams(vmem_limit_bytes=32 << 20),
        cost_estimate=pl.CostEstimate(flops=flops, bytes_accessed=moved, transcendentals=0),
    )(*pinned, *args[far:])


def per_device(
    schur_inverse,
    corner_coupling,
    coarse_inverse,
    load_cases,
    face_order,
    corner_dofs,
    scene_loads,
    scene_weights,
):
    subs, iface = schur_inverse.shape[0], schur_inverse.shape[1]
    face = face_order.shape[1]
    corners = corner_dofs.shape[1]
    cases = load_cases.shape[1]
    scenes = scene_loads.shape[0]
    chain, groups = lax.axis_size("sub"), lax.axis_size("coarse")
    devices = chain * groups
    column = chain * corners
    wide = rounded_up(column, LANES)
    along = groups * wide
    work = dict(flops=4 * cases * schur_inverse.size, moved=2 * schur_inverse.size)

    fetch = [
        pltpu.VMEM(schur_inverse.shape, BF16),
        pltpu.SemaphoreType.DMA((subs * (iface // CHUNK),)),
    ]
    tables = [
        pltpu.VMEM((subs, face, face), BF16), pltpu.VMEM((max(subs - 1, 1), face, face), BF16)
    ]
    row = pltpu.VMEM((cases + cases // 2, rounded_up(column + 2 * cases, LANES)), F32)

    shard = coarse_inverse.reshape(column, groups * corners)
    shards = [swapped(shard, "sub", j) for j in range(1, chain)]

    lane = np.arange(along)
    inner = lane % wide
    source = (inner // corners * groups + lane // wide) * corners + inner % corners
    regroup = jnp.asarray(np.where(inner < column, source, -1)[None].astype(np.int32))

    bits = []
    if groups == 1 << 3 and (column * groups) ** 2 <= schur_inverse.size:
        bits = [1 << b for b in reversed(range(groups.bit_length() - 1))]

    small = [face_order, corner_coupling, corner_dofs, load_cases]
    sent0, *small = call(
        functools.partial(corner_kernel, chain=chain, groups=groups),
        [((devices, cases, wide), BF16)] + [(x.shape, x.dtype) for x in small],
        small,
        [pltpu.SemaphoreType.DMA((len(small),))],
        far=len(small),
    )
    face_order, corner_coupling, corner_dofs, load_cases = small
    received0 = everywhere(sent0, ("sub", "coarse"))
    packet = (cases + rounded_up(corners, 16), face + wide)
    displaced0, first, second, kernel = call(
        functools.partial(first_kernel, chain=chain, groups=groups),
        [
            ((subs, cases, iface), F32),
            (packet, BF16),
            (packet, BF16),
            ((column, along), BF16),
        ],
        [schur_inverse, shard, regroup, *small, *shards],
        fetch
        + [pltpu.VMEM(x.shape, x.dtype) for x in (shard, regroup)]
        + [pltpu.SemaphoreType.DMA((2,))],
        far=3,
        **work,
    )
    first, second = pair_swaps(first, second)
    own_lifts, bent0 = call(
        functools.partial(inner_kernel, chain=chain, groups=groups),
        [((subs, column, iface), BF16), ((subs, cases, iface), F32)],
        [displaced0, corner_coupling, corner_dofs, face_order],
        tables,
        flops=10**9,
        moved=2 * 10**6,
    )
    other = swapped(kernel, "coarse", bits[0]) if bits else kernel
    lifts, lifts_left, pull0, pull0_left, sent1, *joined = call(
        functools.partial(lift_kernel, groups=groups),
        [
            ((subs, column, iface), BF16),
            ((subs, column, face), BF16),
            ((subs, cases, iface), F32),
            ((subs, cases, face), F32),
            ((devices, cases, rounded_up(column + 2 * cases, LANES)), BF16),
        ]
        + [((2 * column, along), BF16)] * bool(bits),
        [bent0, own_lifts, first, second, received0, kernel, other, face_order],
        [pltpu.VMEM((cases, rounded_up(column + 2 * cases, LANES)), F32)],
        flops=10**9,
        moved=10**6,
    )
    received1 = everywhere(sent1, ("sub", "coarse"))
    displaced1, first, second = call(
        second_kernel,
        [((subs, cases, iface), F32), ((cases, face), BF16), ((cases, face), BF16)],
        [schur_inverse, pull0, face_order],
        fetch,
        far=1,
        **work,
    )
    first, second = pair_swaps(first, second)

    low = joined[0] if bits else kernel
    high = swapped(low, "coarse", bits[1]) if bits else kernel
    base, norms0, ahead = call(
        middle_kernel,
        [
            ((subs, cases, iface), F32),
            ((cases, cases), F32),
            ((AHEAD * CHUNK, iface), BF16),
        ],
        [schur_inverse, displaced1, received1, kernel, lifts, face_order],
        [row, *tables, pltpu.SemaphoreType.DMA((AHEAD,))],
        far=1,
        flops=10**9,
        moved=2 * 10**6,
    )
    pull1, bent2, after, sent2, *joined = call(
        third_kernel,
        [
            ((subs, cases, face), F32),
            ((subs, cases, face), F32),
            ((cases, face), BF16),
            ((devices, cases + cases // 2, rounded_up(column + 2 * cases, LANES)), BF16),
        ]
        + [((4 * column, along), BF16)] * bool(bits),
        [schur_inverse, base, first, second, lifts_left, pull0_left, face_order]
        + [ahead, low, high],
        [*fetch, *tables, row],
        far=1,
        **work,
    )
    received2 = everywhere(sent2, ("sub", "coarse"))
    first, second = pair_swaps(after, after, wrap=False)
    if bits:
        blocks = [joined[0], swapped(joined[0], "coarse", bits[2])]
        slots = [0, bits[0], bits[1], bits[0] ^ bits[1]]
        slots = slots + [slot ^ bits[2] for slot in slots]
    else:
        slots = []
        sums = received2.reshape((chain, groups) + received2.shape[1:])[..., :cases, :wide]
        sums = jnp.sum(sums.astype(F32), axis=0)
        flat = jnp.moveaxis(sums, 0, 1).reshape(cases, along)
        own = lax.dynamic_index_in_dim(sums, lax.axis_index("coarse"), 0, keepdims=False)
        values = jnp.dot(flat, kernel.astype(F32).T, precision=lax.Precision.HIGHEST)
        energy = jnp.dot(values, own[:, :column].T, precision=lax.Precision.HIGHEST)
        blocks = [lax.psum(energy, "coarse")]
    multipliers, residual = call(
        functools.partial(scene_kernel, groups=groups, pieces=len(blocks), slots=slots),
        [((subs, scenes, face), F32), ((subs, scenes, face), F32)],
        [bent2, first, second, received2, joined[0] if bits else kernel, lifts_left, pull0_left]
        + [pull1, face_order, norms0]
        + [scene_loads.T, scene_weights.T, *blocks],
        [pltpu.VMEM((groups, cases, wide), F32), row]
        + [pltpu.VMEM((subs, scenes, face), F32)] * 2
        + [pltpu.SemaphoreType.DMA((2 * subs,))],
        flops=10**9,
        moved=4 * 10**6,
        ends=pltpu.HBM,
    )
    return (multipliers, residual)


def solution(mesh):
    return jax.shard_map(
        per_device,
        mesh=mesh,
        in_specs=(
            P(("sub", "coarse"), None, None),
            P(("sub", "coarse"), None, None),
            P(None, "coarse", None, "sub"),
            P(("sub", "coarse"), None, None),
            P(("sub", "coarse"), None),
            P(("sub", "coarse"), None),
            P(),
            P(),
        ),
        out_specs=(P(("sub", "coarse"), None, None), P(("sub", "coarse"), None, None)),
        check_vma=False,
    )
```

```python
import functools

import jax
import jax.numpy as jnp
import numpy as np
from jax import lax
from jax.experimental import pallas as pl
from jax.experimental.pallas import tpu as pltpu
from jax.sharding import PartitionSpec as P

LANES = 128
CHUNK = 256
AHEAD = 2
F32, BF16 = jnp.float32, jnp.bfloat16


def nn(a, b):
    return lax.dot_general(a, b, (((1,), (0,)), ((), ())), preferred_element_type=F32)


def nt(a, b):
    return lax.dot_general(a, b, (((1,), (1,)), ((), ())), preferred_element_type=F32)


def halves(x):
    high = x.astype(BF16)
    return high, (x - high.astype(F32)).astype(BF16)


def stacked(x):
    return jnp.concatenate(halves(x), axis=0)


def folded(x):
    rows = x.shape[0] // 2
    return x[:rows] + x[rows:]


def nn2(x, narrow):
    return folded(nn(stacked(x), narrow))


def nt2(x, narrow):
    return folded(nt(stacked(x), narrow))


def both3(product, x, y):
    high, low = halves(y)
    return folded(product(stacked(x), high)) + product(x.astype(BF16), low)


def equal(a, b):
    return jnp.where(a == b, 1.0, 0.0).astype(BF16)


def iota(shape, dim):
    return lax.broadcasted_iota(jnp.int32, shape, dim)


def rounded_up(value, unit):
    return (value + unit - 1) // unit * unit


def table(order_row):
    size = order_row.shape[1]
    return equal(iota((size, size), 0), order_row)


def back_table(order, n):
    subs, size = order.shape
    rows = jnp.concatenate(
        [order[...].astype(F32), jnp.zeros((rounded_up(subs, 8) - subs, size), F32)], axis=0
    )
    return equal(rows.T[:, n : n + 1].astype(jnp.int32), iota((size, size), 1))


def fill_tables(tables, backs, order):
    for n in range(1, tables.shape[0]):
        tables[n] = table(order[n : n + 1])
        backs[n - 1] = back_table(order, n)


def spread_of(dofs_row, chain, corners, groups):
    column = chain * corners
    ids = iota((column, 1), 0)
    slot = sum((ids >= t * corners).astype(jnp.int32) for t in range(1, chain))
    target = ids + slot * ((groups - 1) * corners) + lax.axis_index("coarse") * corners
    return equal(target, dofs_row)


def placed(x, width, at):
    rows = x.shape[1]
    return nn(x, equal(iota((rows, width), 0) + at, iota((rows, width), 1)))


def by_parity(to_after, to_before):
    odd = (lax.axis_index("sub") & 1) == 1
    return jnp.where(odd, to_before, to_after), jnp.where(odd, to_after, to_before)


def start_fetch(matrix, held, sems, ready=0):
    subs, size = matrix.shape[0], matrix.shape[1]
    copies = []
    for n in range(subs):
        for k in range(size // CHUNK):
            copies.append(None)
            if len(copies) > ready:
                part = pl.ds(k * CHUNK, CHUNK)
                copies[-1] = pltpu.make_async_copy(
                    matrix.at[n, part], held.at[n, part], sems.at[n * (size // CHUNK) + k]
                )
                copies[-1].start()
    return copies


def start_ahead(matrix, ahead, sems):
    copies = []
    for k in range(ahead.shape[0] // CHUNK):
        part = pl.ds(k * CHUNK, CHUNK)
        copies.append(pltpu.make_async_copy(matrix.at[0, part], ahead.at[part], sems.at[k]))
        copies[-1].start()
    return copies


def times_matrix(x, n, held, copies, ahead=None):
    size = held.shape[1]
    count = size // CHUNK
    total = None
    for k in range(count):
        rows = slice(k * CHUNK, (k + 1) * CHUNK)
        if copies[n * count + k] is None:
            chunk = ahead[rows]
        else:
            copies[n * count + k].wait()
            chunk = held[n, rows]
        part = nn(x[:, rows], chunk)
        total = part if total is None else total + part
    return total


def inner_jump(displaced, tables, backs):
    subs = len(displaced)
    face = tables.shape[1]
    lefts = [part[:, :face] for part in displaced]
    rights = [part[:, face:] for part in displaced]
    for n in range(1, subs):
        lefts[n] = lefts[n] - nn2(displaced[n - 1][:, face:], tables[n])
        rights[n - 1] = rights[n - 1] - nn2(displaced[n][:, :face], backs[n - 1])
    return lefts, rights


def outer_jump(lefts, rights, before, after):
    at_head = lax.axis_index("sub") == 0
    at_tail = lax.axis_index("sub") == lax.axis_size("sub") - 1
    lefts = [jnp.where(at_head, 0.0, lefts[0] - before), *lefts[1:]]
    rights = [*rights[:-1], jnp.where(at_tail, 0.0, rights[-1] - after)]
    return [jnp.concatenate(pair, axis=1) for pair in zip(lefts, rights)]


def chain_sums(received, groups, width):
    chain = received.shape[0] // groups
    sums = []
    for c in range(groups):
        total = None
        for z in range(chain):
            part = received[z * groups + c, :, :width].astype(F32)
            total = part if total is None else total + part
        sums.append(total)
    return sums


def copies_of(out, x):
    for i in range(out.shape[0]):
        out[i] = x


def fetched(pairs, sems):
    copies = [pltpu.make_async_copy(a, b, sems.at[i]) for i, (a, b) in enumerate(pairs)]
    for copy in copies:
        copy.start()
    return copies


def corner_kernel(*refs, chain, groups):
    far, out, (order, coupling, dofs, loads), sems = refs[:4], refs[4], refs[5:9], refs[9]
    for copy in fetched(list(zip(far, refs[5:9])), sems):
        copy.wait()
    corners = coupling.shape[1]
    total = None
    for n in range(loads.shape[0]):
        terms = nt(loads[n], coupling[n])
        part = nt2(terms, spread_of(dofs[n : n + 1], chain, corners, groups))
        total = part if total is None else total + part
    copies_of(out, placed(total.astype(BF16), out.shape[2], 0).astype(BF16))


def first_kernel(
    matrix, shard_far, regroup_far, order, coupling, dofs, loads, *refs, chain, groups
):
    shards, refs = refs[: chain - 1], refs[chain - 1 :]
    out, first, second, kernel, held, sems, shard, regroup, small = refs
    copies = start_fetch(matrix, held, sems)
    small_copies = fetched([(shard_far, shard), (regroup_far, regroup)], small)
    subs, cases, iface = loads.shape
    corners, face = coupling.shape[1], order.shape[1]
    pad = rounded_up(corners, 16) - corners

    def packet(displaced, coupled, n):
        spread = spread_of(dofs[n : n + 1], chain, corners, groups)
        eye = equal(iota((corners, corners), 0), iota((corners, corners), 1))
        hot = placed(nt(eye, spread).astype(BF16), first.shape[1] - face, 0)
        lower = jnp.concatenate([coupled, hot], axis=1)
        upper = jnp.concatenate([displaced, jnp.zeros((cases, hot.shape[1]), F32)], axis=1)
        return jnp.concatenate([upper, lower, jnp.zeros((pad, lower.shape[1]), F32)], axis=0)

    for n in range(subs):
        out[n] = times_matrix(loads[n], n, held, copies)
        if n == 0:
            near = table(order[0:1])
            to_before = packet(
                nt(out[0, :, :face].astype(BF16), near), nt(coupling[0, :, :face], near), 0
            )
            for copy in small_copies:
                copy.wait()
            position = lax.axis_index("sub")
            depth = groups * corners
            rows = None
            for j, block in enumerate([shard, *shards]):
                ids = iota((depth, regroup.shape[1]), 0) + (position ^ j) * depth
                part = nn(block[...], equal(ids, regroup[...]))
                rows = part if rows is None else rows + part
            kernel[...] = rows.astype(BF16)
    last = subs - 1
    to_after = packet(out[last, :, face:], coupling[last, :, face:].astype(F32), last)
    one, two = by_parity(to_after, to_before)
    first[...] = one.astype(BF16)
    second[...] = two.astype(BF16)


def inner_kernel(
    displaced, coupling, dofs, order, lifts, bent, tables, backs, *, chain, groups
):
    subs, cases, _ = displaced.shape
    corners, face = coupling.shape[1], order.shape[1]
    fill_tables(tables, backs, order)
    spreads = [spread_of(dofs[n : n + 1], chain, corners, groups) for n in range(subs)]
    for n in range(subs):
        left, right = nn(spreads[n], coupling[n, :, :face]), nn(spreads[n], coupling[n, :, face:])
        if n > 0:
            moved = nn(coupling[n - 1, :, face:], tables[n]).astype(BF16)
            left = left - nn(spreads[n - 1], moved)
        if n < subs - 1:
            moved = nn(coupling[n + 1, :, :face], backs[n]).astype(BF16)
            right = right - nn(spreads[n + 1], moved)
        lifts[n, :, :face] = left.astype(BF16)
        lifts[n, :, face:] = right.astype(BF16)
    lefts, rights = inner_jump([displaced[n] for n in range(subs)], tables, backs)
    for n in range(subs):
        bent[n, :, :face] = lefts[n]
        bent[n, :, face:] = rights[n]


def lift_kernel(
    bent, own_lifts, first, second, received, kernel, other, order,
    lifts, lifts_left, pull, pull_left, out, *refs, groups
):
    *joined, row = refs
    subs, cases, _ = bent.shape
    column, face = own_lifts.shape[1], order.shape[1]
    wide = rounded_up(column, LANES)
    join(joined, kernel, other)
    near = table(order[0:1])
    from_after, from_before = by_parity(first[...].astype(F32), second[...].astype(F32))
    eye = equal(iota((column, first.shape[1] - face), 0), iota((column, first.shape[1] - face), 1))

    def neighbour(block):
        low = block[cases:].astype(BF16)
        return low[:, :face], nt(eye, low[:, face:]).astype(BF16)

    before = nn(from_before[:, :face].astype(BF16), near)
    _, before_spread = neighbour(from_before)
    after_coupling, after_spread = neighbour(from_after)
    lifted = outer_jump(
        [own_lifts[n, :, :face].astype(F32) for n in range(subs)],
        [own_lifts[n, :, face:].astype(F32) for n in range(subs)],
        nn(before_spread, before[cases:].astype(BF16)).astype(BF16).astype(F32),
        nn(after_spread, after_coupling).astype(BF16).astype(F32),
    )
    bent = outer_jump(
        [bent[n, :, :face] for n in range(subs)],
        [bent[n, :, face:] for n in range(subs)],
        before[:cases],
        from_after[:cases, :face],
    )
    for n in range(subs):
        lifted[n] = lifted[n].astype(BF16)
        lifts[n] = lifted[n]
        lifts_left[n] = lifted[n][:, :face]
    flat = jnp.concatenate(chain_sums(received, groups, wide), axis=1)
    values = nt2(flat, kernel[...])
    corner, norms = None, None
    for n in range(subs):
        whole = bent[n] + nn2(values, lifted[n])
        pull[n] = whole
        left = whole[:, :face]
        pull_left[n] = left
        part, norm = nt2(left, lifted[n][:, :face]), both3(nt, left, left)
        corner = part if corner is None else corner + part
        norms = norm if norms is None else norms + norm
    row[...] = jnp.zeros(row.shape, F32)
    row[:, :column] = corner
    store_halves(row, norms, slice(0, cases), column)
    copies_of(out, row[...].astype(BF16))


def join(out, low, high):
    for ref in out:
        ref[: low.shape[0]] = low[...]
        ref[low.shape[0] :] = high[...]


def store_halves(row, gram, rows, at):
    for half in halves(gram):
        row[rows, at : at + gram.shape[1]] = half.astype(F32)
        at += gram.shape[1]


def sum_halves(row, rows, at, count):
    return row[rows, at : at + count] + row[rows, at + count : at + 2 * count]


def second_kernel(matrix, pull, order, out, first, second, held, sems):
    copies = start_fetch(matrix, held, sems)
    subs = pull.shape[0]
    face = order.shape[1]
    near = back_table(order, 0)
    for n in range(subs):
        out[n] = folded(times_matrix(stacked(pull[n]), n, held, copies))
    one, two = by_parity(out[subs - 1, :, face:], nn2(out[0, :, :face], near))
    first[...] = one.astype(BF16)
    second[...] = two.astype(BF16)


def middle_kernel(matrix, displaced, received, kernel, lifts, order, *refs):
    base, norms0, ahead, row, tables, backs, ahead_sems = refs
    copies = start_ahead(matrix, ahead, ahead_sems)
    subs, cases, _ = displaced.shape
    column, face = lifts.shape[1], order.shape[1]
    wide = rounded_up(column, LANES)
    groups = kernel.shape[1] // wide
    fill_tables(tables, backs, order)
    sums = chain_sums(received, groups, received.shape[2])
    flat = jnp.concatenate([part[:, :wide] for part in sums], axis=1)
    values = nt2(flat, kernel[...])
    row[:cases] = sum(sums)
    norms0[...] = sum_halves(row, slice(0, cases), column, cases)
    lefts, rights = inner_jump([displaced[n] for n in range(subs)], tables, backs)
    for n in range(subs):
        base[n] = jnp.concatenate([lefts[n], rights[n]], axis=1) + nn2(values, lifts[n])
    for copy in copies:
        copy.wait()


def third_kernel(matrix, base, first, second, lifts, pull0, order, ahead, low, high, *refs):
    pull, bent2, after, payload, *joined, held, sems, tables, _, row = refs
    copies = start_fetch(matrix, held, sems, ahead.shape[0] // CHUNK)
    subs, cases, _ = base.shape
    face = order.shape[1]
    column = lifts.shape[1]
    for n in range(subs):
        tables[n] = table(order[n : n + 1])
    join(joined, low, high)
    from_after, from_before = by_parity(first[...].astype(F32), second[...].astype(F32))
    bent = outer_jump(
        [base[n, :, :face] for n in range(subs)],
        [base[n, :, face:] for n in range(subs)],
        nn(from_before.astype(BF16), tables[0]),
        from_after,
    )
    totals = None
    for n in range(subs):
        whole = bent[n]
        left = whole[:, :face]
        pull[n] = left
        moved = folded(times_matrix(stacked(whole), n, held, copies, ahead))
        bent2[n] = moved[:, :face]
        if n > 0:
            bent2[n] = moved[:, :face] - nn2(previous, tables[n])
        previous = moved[:, face:]
        parts = [
            nt2(left, lifts[n]),
            both3(nt, pull0[n], left),
            both3(nt, left, left),
            both3(nt, whole, moved),
        ]
        totals = parts if totals is None else [a + b for a, b in zip(totals, parts)]
    after[...] = previous.astype(BF16)
    corner, gram1, gram2, gram3 = totals
    row[...] = jnp.zeros(row.shape, F32)
    row[:cases, :column] = corner
    store_halves(row, gram1, slice(0, cases), column)
    step = cases // 2
    for j in range(2):
        for i, gram in enumerate((gram2, gram3)):
            part = gram[j * step : (j + 1) * step]
            store_halves(row, part, slice(cases, cases + step), (4 * j + 2 * i) * cases)
    copies_of(payload, row[...].astype(BF16))


def scene_kernel(
    bent, first, second, received, kernel, lifts, pull0, pull1, order, norms0,
    scene_loads, scene_weights, *refs, groups, pieces, slots
):
    blocks = refs[:pieces]
    multipliers_far, residual_far, held, row, multipliers, residual, sems = refs[pieces:]
    subs, cases, _ = bent.shape
    column = lifts.shape[1]
    wide = rounded_up(column, LANES)
    group = lax.axis_index("coarse")
    sums = chain_sums(received, groups, received.shape[2])
    for c in range(groups):
        held[c] = sums[c][:cases, :wide]
    flat = jnp.concatenate([held[c] for c in range(groups)], axis=1)
    values = nt2(flat, kernel[:column])
    if groups_whole(blocks, column, groups):
        lifted, index = None, iter(slots)
        for block in blocks:
            for i in range(block.shape[0] // column):
                sums_here = held[group ^ next(index)][:, :column]
                part = nn2(sums_here, block[i * column : (i + 1) * column])
                lifted = part if lifted is None else lifted + part
        energy = both3(nt, lifted, flat)
    else:
        energy = blocks[0][...]
    row[...] = sum(sums)
    norms1 = sum_halves(row, slice(0, cases), column, cases)
    lower = slice(cases, cases + cases // 2)
    norms2, norms3 = (
        jnp.concatenate(
            [sum_halves(row, lower, (4 * j + 2 * i) * cases, cases) for j in range(2)], axis=0
        )
        for i in range(2)
    )
    norms3 = norms3 + energy

    ids = iota((cases, scene_loads.shape[1]), 0)
    mixing = sum(
        jnp.where(ids == scene_loads[i : i + 1], scene_weights[i : i + 1], 0.0)
        for i in range(scene_loads.shape[0])
    )

    def moment(norms):
        return jnp.sum(both3(nn, norms, mixing) * mixing, axis=0, keepdims=True)

    moment0, moment1 = moment(norms0[...]), moment(norms1)
    moment2, moment3 = moment(norms2), moment(norms3)
    step0 = moment0 / moment1
    norm1 = moment0 - 2.0 * step0 * moment1 + step0 * step0 * moment2
    grow = 1.0 + norm1 / moment0
    curvature = grow * grow * moment1 - 2.0 * grow * step0 * moment2 + step0 * step0 * moment3
    step1 = norm1 / curvature
    zeros = jnp.zeros_like(mixing)

    def transposed(parts):
        weights = -jnp.concatenate(parts, axis=0)
        high = weights.astype(BF16).astype(F32)
        return jnp.concatenate([high, high, weights - high], axis=0).T.astype(BF16)

    for_multipliers = transposed(
        [(step0 + step1 * grow) * mixing, (-step0 * step1) * mixing, zeros]
    )
    for_residual = transposed(
        [mixing, (-step0 - step1 * grow) * mixing, (step0 * step1) * mixing]
    )
    _, from_before = by_parity(first[...].astype(F32), second[...].astype(F32))
    copies = []
    for n in range(subs):
        pull2 = bent[n]
        if n == 0:
            pull2 = pull2 - nn(from_before.astype(BF16), table(order[0:1]))
            pull2 = jnp.where(lax.axis_index("sub") == 0, 0.0, pull2)
        pull2 = pull2 + nn2(values, lifts[n])
        basis = jnp.concatenate([pull0[n], pull1[n], pull2], axis=0)
        high, low = halves(basis)
        basis = jnp.concatenate([high, low, high], axis=0)
        multipliers[n] = nn(for_multipliers, basis)
        copies += fetched([(multipliers.at[n], multipliers_far.at[n])], sems.at[pl.ds(2 * n, 1)])
        residual[n] = nn(for_residual, basis)
        copies += fetched([(residual.at[n], residual_far.at[n])], sems.at[pl.ds(2 * n + 1, 1)])
    for copy in copies:
        copy.wait()


def groups_whole(blocks, column, groups):
    return sum(block.shape[0] for block in blocks) == column * groups


def everywhere(x, axes):
    return lax.all_to_all(x, axes, 0, 0)


def swapped(x, axis, bit):
    return lax.ppermute(x, axis, [(i, i ^ bit) for i in range(lax.axis_size(axis))])


def pair_swaps(first, second, wrap=True):
    length = lax.axis_size("sub")

    def partner(i, j):
        return (i, j % length if wrap or 0 <= j < length else i)

    one = lax.ppermute(first, "sub", [partner(i, i ^ 1) for i in range(length)])
    two = lax.ppermute(
        second, "sub", [partner(i, i + 1 if i & 1 else i - 1) for i in range(length)]
    )
    return one, two


def call(kernel, outs, args, scratch=(), flops=0, moved=0, far=0, ends=pltpu.VMEM):
    specs = [pl.BlockSpec(memory_space=pltpu.HBM)] * far
    specs += [pl.BlockSpec(memory_space=pltpu.VMEM)] * (len(args) - far)
    pinned = [pltpu.with_memory_space_constraint(x, pltpu.HBM) for x in args[:far]]
    shapes = [jax.ShapeDtypeStruct(shape, kind) for shape, kind in outs]
    return pl.pallas_call(
        kernel,
        out_shape=shapes,
        in_specs=specs,
        out_specs=[pl.BlockSpec(memory_space=ends)] * len(outs),
        scratch_shapes=list(scratch),
        compiler_params=pltpu.CompilerParams(vmem_limit_bytes=32 << 20),
        cost_estimate=pl.CostEstimate(flops=flops, bytes_accessed=moved, transcendentals=0),
    )(*pinned, *args[far:])


def per_device(
    schur_inverse,
    corner_coupling,
    coarse_inverse,
    load_cases,
    face_order,
    corner_dofs,
    scene_loads,
    scene_weights,
):
    subs, iface = schur_inverse.shape[0], schur_inverse.shape[1]
    face = face_order.shape[1]
    corners = corner_dofs.shape[1]
    cases = load_cases.shape[1]
    scenes = scene_loads.shape[0]
    chain, groups = lax.axis_size("sub"), lax.axis_size("coarse")
    devices = chain * groups
    column = chain * corners
    wide = rounded_up(column, LANES)
    along = groups * wide
    work = dict(flops=4 * cases * schur_inverse.size, moved=2 * schur_inverse.size)

    fetch = [
        pltpu.VMEM(schur_inverse.shape, BF16),
        pltpu.SemaphoreType.DMA((subs * (iface // CHUNK),)),
    ]
    tables = [
        pltpu.VMEM((subs, face, face), BF16), pltpu.VMEM((max(subs - 1, 1), face, face), BF16)
    ]
    row = pltpu.VMEM((cases + cases // 2, rounded_up(column + 2 * cases, LANES)), F32)

    shard = coarse_inverse.reshape(column, groups * corners)
    shards = [swapped(shard, "sub", j) for j in range(1, chain)]

    lane = np.arange(along)
    inner = lane % wide
    source = (inner // corners * groups + lane // wide) * corners + inner % corners
    regroup = jnp.asarray(np.where(inner < column, source, -1)[None].astype(np.int32))

    bits = []
    if groups == 1 << 3 and (column * groups) ** 2 <= schur_inverse.size:
        bits = [1 << b for b in reversed(range(groups.bit_length() - 1))]

    small = [face_order, corner_coupling, corner_dofs, load_cases]
    sent0, *small = call(
        functools.partial(corner_kernel, chain=chain, groups=groups),
        [((devices, cases, wide), BF16)] + [(x.shape, x.dtype) for x in small],
        small,
        [pltpu.SemaphoreType.DMA((len(small),))],
        far=len(small),
    )
    face_order, corner_coupling, corner_dofs, load_cases = small
    received0 = everywhere(sent0, ("sub", "coarse"))
    packet = (cases + rounded_up(corners, 16), face + wide)
    displaced0, first, second, kernel = call(
        functools.partial(first_kernel, chain=chain, groups=groups),
        [
            ((subs, cases, iface), F32),
            (packet, BF16),
            (packet, BF16),
            ((column, along), BF16),
        ],
        [schur_inverse, shard, regroup, *small, *shards],
        fetch
        + [pltpu.VMEM(x.shape, x.dtype) for x in (shard, regroup)]
        + [pltpu.SemaphoreType.DMA((2,))],
        far=3,
        **work,
    )
    first, second = pair_swaps(first, second)
    own_lifts, bent0 = call(
        functools.partial(inner_kernel, chain=chain, groups=groups),
        [((subs, column, iface), BF16), ((subs, cases, iface), F32)],
        [displaced0, corner_coupling, corner_dofs, face_order],
        tables,
        flops=10**9,
        moved=2 * 10**6,
    )
    other = swapped(kernel, "coarse", bits[0]) if bits else kernel
    lifts, lifts_left, pull0, pull0_left, sent1, *joined = call(
        functools.partial(lift_kernel, groups=groups),
        [
            ((subs, column, iface), BF16),
            ((subs, column, face), BF16),
            ((subs, cases, iface), F32),
            ((subs, cases, face), F32),
            ((devices, cases, rounded_up(column + 2 * cases, LANES)), BF16),
        ]
        + [((2 * column, along), BF16)] * bool(bits),
        [bent0, own_lifts, first, second, received0, kernel, other, face_order],
        [pltpu.VMEM((cases, rounded_up(column + 2 * cases, LANES)), F32)],
        flops=10**9,
        moved=10**6,
    )
    received1 = everywhere(sent1, ("sub", "coarse"))
    displaced1, first, second = call(
        second_kernel,
        [((subs, cases, iface), F32), ((cases, face), BF16), ((cases, face), BF16)],
        [schur_inverse, pull0, face_order],
        fetch,
        far=1,
        **work,
    )
    first, second = pair_swaps(first, second)

    low = joined[0] if bits else kernel
    high = swapped(low, "coarse", bits[1]) if bits else kernel
    base, norms0, ahead = call(
        middle_kernel,
        [
            ((subs, cases, iface), F32),
            ((cases, cases), F32),
            ((AHEAD * CHUNK, iface), BF16),
        ],
        [schur_inverse, displaced1, received1, kernel, lifts, face_order],
        [row, *tables, pltpu.SemaphoreType.DMA((AHEAD,))],
        far=1,
        flops=10**9,
        moved=2 * 10**6,
    )
    pull1, bent2, after, sent2, *joined = call(
        third_kernel,
        [
            ((subs, cases, face), F32),
            ((subs, cases, face), F32),
            ((cases, face), BF16),
            ((devices, cases + cases // 2, rounded_up(column + 2 * cases, LANES)), BF16),
        ]
        + [((4 * column, along), BF16)] * bool(bits),
        [schur_inverse, base, first, second, lifts_left, pull0_left, face_order]
        + [ahead, low, high],
        [*fetch, *tables, row],
        far=1,
        **work,
    )
    received2 = everywhere(sent2, ("sub", "coarse"))
    first, second = pair_swaps(after, after, wrap=False)
    if bits:
        blocks = [joined[0], swapped(joined[0], "coarse", bits[2])]
        slots = [0, bits[0], bits[1], bits[0] ^ bits[1]]
        slots = slots + [slot ^ bits[2] for slot in slots]
    else:
        slots = []
        sums = received2.reshape((chain, groups) + received2.shape[1:])[..., :cases, :wide]
        sums = jnp.sum(sums.astype(F32), axis=0)
        flat = jnp.moveaxis(sums, 0, 1).reshape(cases, along)
        own = lax.dynamic_index_in_dim(sums, lax.axis_index("coarse"), 0, keepdims=False)
        values = jnp.dot(flat, kernel.astype(F32).T, precision=lax.Precision.HIGHEST)
        energy = jnp.dot(values, own[:, :column].T, precision=lax.Precision.HIGHEST)
        blocks = [lax.psum(energy, "coarse")]
    multipliers, residual = call(
        functools.partial(scene_kernel, groups=groups, pieces=len(blocks), slots=slots),
        [((subs, scenes, face), F32), ((subs, scenes, face), F32)],
        [bent2, first, second, received2, joined[0] if bits else kernel, lifts_left, pull0_left]
        + [pull1, face_order, norms0]
        + [scene_loads.T, scene_weights.T, *blocks],
        [pltpu.VMEM((groups, cases, wide), F32), row]
        + [pltpu.VMEM((subs, scenes, face), F32)] * 2
        + [pltpu.SemaphoreType.DMA((2 * subs,))],
        flops=10**9,
        moved=4 * 10**6,
        ends=pltpu.HBM,
    )
    return (multipliers, residual)


def solution(mesh):
    return jax.shard_map(
        per_device,
        mesh=mesh,
        in_specs=(
            P(("sub", "coarse"), None, None),
            P(("sub", "coarse"), None, None),
            P(None, "coarse", None, "sub"),
            P(("sub", "coarse"), None, None),
            P(("sub", "coarse"), None),
            P(("sub", "coarse"), None),
            P(),
            P(),
        ),
        out_specs=(P(("sub", "coarse"), None, None), P(("sub", "coarse"), None, None)),
        check_vma=False,
    )
```

```python
import functools

import jax
import jax.numpy as jnp
import numpy as np
from jax import lax
from jax.experimental import pallas as pl
from jax.experimental.pallas import tpu as pltpu
from jax.sharding import PartitionSpec as P

LANES = 128
CHUNK = 256
AHEAD = 2
F32, BF16 = jnp.float32, jnp.bfloat16


def nn(a, b):
    return lax.dot_general(a, b, (((1,), (0,)), ((), ())), preferred_element_type=F32)


def nt(a, b):
    return lax.dot_general(a, b, (((1,), (1,)), ((), ())), preferred_element_type=F32)


def halves(x):
    high = x.astype(BF16)
    return high, (x - high.astype(F32)).astype(BF16)


def stacked(x):
    return jnp.concatenate(halves(x), axis=0)


def folded(x):
    rows = x.shape[0] // 2
    return x[:rows] + x[rows:]


def nn2(x, narrow):
    return folded(nn(stacked(x), narrow))


def nt2(x, narrow):
    return folded(nt(stacked(x), narrow))


def both3(product, x, y):
    high, low = halves(y)
    return folded(product(stacked(x), high)) + product(x.astype(BF16), low)


def equal(a, b):
    return jnp.where(a == b, 1.0, 0.0).astype(BF16)


def iota(shape, dim):
    return lax.broadcasted_iota(jnp.int32, shape, dim)


def rounded_up(value, unit):
    return (value + unit - 1) // unit * unit


def table(order_row):
    size = order_row.shape[1]
    return equal(iota((size, size), 0), order_row)


def back_table(order, n):
    subs, size = order.shape
    rows = jnp.concatenate(
        [order[...].astype(F32), jnp.zeros((rounded_up(subs, 8) - subs, size), F32)], axis=0
    )
    return equal(rows.T[:, n : n + 1].astype(jnp.int32), iota((size, size), 1))


def fill_tables(tables, backs, order):
    for n in range(1, tables.shape[0]):
        tables[n] = table(order[n : n + 1])
        backs[n - 1] = back_table(order, n)


def spread_of(dofs_row, chain, corners, groups):
    column = chain * corners
    ids = iota((column, 1), 0)
    slot = sum((ids >= t * corners).astype(jnp.int32) for t in range(1, chain))
    target = ids + slot * ((groups - 1) * corners) + lax.axis_index("coarse") * corners
    return equal(target, dofs_row)


def placed(x, width, at):
    rows = x.shape[1]
    return nn(x, equal(iota((rows, width), 0) + at, iota((rows, width), 1)))


def by_parity(to_after, to_before):
    odd = (lax.axis_index("sub") & 1) == 1
    return jnp.where(odd, to_before, to_after), jnp.where(odd, to_after, to_before)


def start_fetch(matrix, held, sems, ready=0):
    subs, size = matrix.shape[0], matrix.shape[1]
    copies = []
    for n in range(subs):
        for k in range(size // CHUNK):
            copies.append(None)
            if len(copies) > ready:
                part = pl.ds(k * CHUNK, CHUNK)
                copies[-1] = pltpu.make_async_copy(
                    matrix.at[n, part], held.at[n, part], sems.at[n * (size // CHUNK) + k]
                )
                copies[-1].start(priority=k % 2)
    return copies


def start_ahead(matrix, ahead, sems):
    copies = []
    for k in range(ahead.shape[0] // CHUNK):
        part = pl.ds(k * CHUNK, CHUNK)
        copies.append(pltpu.make_async_copy(matrix.at[0, part], ahead.at[part], sems.at[k]))
        copies[-1].start()
    return copies


def times_matrix(x, n, held, copies, ahead=None):
    size = held.shape[1]
    count = size // CHUNK
    total = None
    for k in range(count):
        rows = slice(k * CHUNK, (k + 1) * CHUNK)
        if copies[n * count + k] is None:
            chunk = ahead[rows]
        else:
            copies[n * count + k].wait()
            chunk = held[n, rows]
        part = nn(x[:, rows], chunk)
        total = part if total is None else total + part
    return total


def inner_jump(displaced, tables, backs):
    subs = len(displaced)
    face = tables.shape[1]
    lefts = [part[:, :face] for part in displaced]
    rights = [part[:, face:] for part in displaced]
    for n in range(1, subs):
        lefts[n] = lefts[n] - nn2(displaced[n - 1][:, face:], tables[n])
        rights[n - 1] = rights[n - 1] - nn2(displaced[n][:, :face], backs[n - 1])
    return lefts, rights


def outer_jump(lefts, rights, before, after):
    at_head = lax.axis_index("sub") == 0
    at_tail = lax.axis_index("sub") == lax.axis_size("sub") - 1
    lefts = [jnp.where(at_head, 0.0, lefts[0] - before), *lefts[1:]]
    rights = [*rights[:-1], jnp.where(at_tail, 0.0, rights[-1] - after)]
    return [jnp.concatenate(pair, axis=1) for pair in zip(lefts, rights)]


def chain_sums(received, groups, width):
    chain = received.shape[0] // groups
    sums = []
    for c in range(groups):
        total = None
        for z in range(chain):
            part = received[z * groups + c, :, :width].astype(F32)
            total = part if total is None else total + part
        sums.append(total)
    return sums


def copies_of(out, x):
    for i in range(out.shape[0]):
        out[i] = x


def fetched(pairs, sems):
    copies = [pltpu.make_async_copy(a, b, sems.at[i]) for i, (a, b) in enumerate(pairs)]
    for copy in copies:
        copy.start()
    return copies


def corner_kernel(*refs, chain, groups):
    far, out, (order, coupling, dofs, loads), sems = refs[:4], refs[4], refs[5:9], refs[9]
    for copy in fetched(list(zip(far, refs[5:9])), sems):
        copy.wait()
    corners = coupling.shape[1]
    total = None
    for n in range(loads.shape[0]):
        terms = nt(loads[n], coupling[n])
        part = nt2(terms, spread_of(dofs[n : n + 1], chain, corners, groups))
        total = part if total is None else total + part
    copies_of(out, placed(total.astype(BF16), out.shape[2], 0).astype(BF16))


def first_kernel(
    matrix, shard_far, regroup_far, order, coupling, dofs, loads, *refs, chain, groups
):
    shards, refs = refs[: chain - 1], refs[chain - 1 :]
    out, first, second, kernel, held, sems, shard, regroup, small = refs
    copies = start_fetch(matrix, held, sems)
    small_copies = fetched([(shard_far, shard), (regroup_far, regroup)], small)
    subs, cases, iface = loads.shape
    corners, face = coupling.shape[1], order.shape[1]
    pad = rounded_up(corners, 16) - corners

    def packet(displaced, coupled, n):
        spread = spread_of(dofs[n : n + 1], chain, corners, groups)
        eye = equal(iota((corners, corners), 0), iota((corners, corners), 1))
        hot = placed(nt(eye, spread).astype(BF16), first.shape[1] - face, 0)
        lower = jnp.concatenate([coupled, hot], axis=1)
        upper = jnp.concatenate([displaced, jnp.zeros((cases, hot.shape[1]), F32)], axis=1)
        return jnp.concatenate([upper, lower, jnp.zeros((pad, lower.shape[1]), F32)], axis=0)

    for n in range(subs):
        out[n] = times_matrix(loads[n], n, held, copies)
        if n == 0:
            near = table(order[0:1])
            to_before = packet(
                nt(out[0, :, :face].astype(BF16), near), nt(coupling[0, :, :face], near), 0
            )
            for copy in small_copies:
                copy.wait()
            position = lax.axis_index("sub")
            depth = groups * corners
            rows = None
            for j, block in enumerate([shard, *shards]):
                ids = iota((depth, regroup.shape[1]), 0) + (position ^ j) * depth
                part = nn(block[...], equal(ids, regroup[...]))
                rows = part if rows is None else rows + part
            kernel[...] = rows.astype(BF16)
    last = subs - 1
    to_after = packet(out[last, :, face:], coupling[last, :, face:].astype(F32), last)
    one, two = by_parity(to_after, to_before)
    first[...] = one.astype(BF16)
    second[...] = two.astype(BF16)


def inner_kernel(
    displaced, coupling, dofs, order, lifts, bent, tables, backs, *, chain, groups
):
    subs, cases, _ = displaced.shape
    corners, face = coupling.shape[1], order.shape[1]
    fill_tables(tables, backs, order)
    spreads = [spread_of(dofs[n : n + 1], chain, corners, groups) for n in range(subs)]
    for n in range(subs):
        left, right = nn(spreads[n], coupling[n, :, :face]), nn(spreads[n], coupling[n, :, face:])
        if n > 0:
            moved = nn(coupling[n - 1, :, face:], tables[n]).astype(BF16)
            left = left - nn(spreads[n - 1], moved)
        if n < subs - 1:
            moved = nn(coupling[n + 1, :, :face], backs[n]).astype(BF16)
            right = right - nn(spreads[n + 1], moved)
        lifts[n, :, :face] = left.astype(BF16)
        lifts[n, :, face:] = right.astype(BF16)
    lefts, rights = inner_jump([displaced[n] for n in range(subs)], tables, backs)
    for n in range(subs):
        bent[n, :, :face] = lefts[n]
        bent[n, :, face:] = rights[n]


def lift_kernel(
    bent, own_lifts, first, second, received, kernel, other, order,
    lifts, lifts_left, pull, pull_left, out, *refs, groups
):
    *joined, row = refs
    subs, cases, _ = bent.shape
    column, face = own_lifts.shape[1], order.shape[1]
    wide = rounded_up(column, LANES)
    join(joined, kernel, other)
    near = table(order[0:1])
    from_after, from_before = by_parity(first[...].astype(F32), second[...].astype(F32))
    eye = equal(iota((column, first.shape[1] - face), 0), iota((column, first.shape[1] - face), 1))

    def neighbour(block):
        low = block[cases:].astype(BF16)
        return low[:, :face], nt(eye, low[:, face:]).astype(BF16)

    before = nn(from_before[:, :face].astype(BF16), near)
    _, before_spread = neighbour(from_before)
    after_coupling, after_spread = neighbour(from_after)
    lifted = outer_jump(
        [own_lifts[n, :, :face].astype(F32) for n in range(subs)],
        [own_lifts[n, :, face:].astype(F32) for n in range(subs)],
        nn(before_spread, before[cases:].astype(BF16)).astype(BF16).astype(F32),
        nn(after_spread, after_coupling).astype(BF16).astype(F32),
    )
    bent = outer_jump(
        [bent[n, :, :face] for n in range(subs)],
        [bent[n, :, face:] for n in range(subs)],
        before[:cases],
        from_after[:cases, :face],
    )
    for n in range(subs):
        lifted[n] = lifted[n].astype(BF16)
        lifts[n] = lifted[n]
        lifts_left[n] = lifted[n][:, :face]
    flat = jnp.concatenate(chain_sums(received, groups, wide), axis=1)
    values = nt2(flat, kernel[...])
    corner, norms = None, None
    for n in range(subs):
        whole = bent[n] + nn2(values, lifted[n])
        pull[n] = whole
        left = whole[:, :face]
        pull_left[n] = left
        part, norm = nt2(left, lifted[n][:, :face]), both3(nt, left, left)
        corner = part if corner is None else corner + part
        norms = norm if norms is None else norms + norm
    row[...] = jnp.zeros(row.shape, F32)
    row[:, :column] = corner
    store_halves(row, norms, slice(0, cases), column)
    copies_of(out, row[...].astype(BF16))


def join(out, low, high):
    for ref in out:
        ref[: low.shape[0]] = low[...]
        ref[low.shape[0] :] = high[...]


def store_halves(row, gram, rows, at):
    for half in halves(gram):
        row[rows, at : at + gram.shape[1]] = half.astype(F32)
        at += gram.shape[1]


def sum_halves(row, rows, at, count):
    return row[rows, at : at + count] + row[rows, at + count : at + 2 * count]


def second_kernel(matrix, pull, order, out, first, second, held, sems):
    copies = start_fetch(matrix, held, sems)
    subs = pull.shape[0]
    face = order.shape[1]
    near = back_table(order, 0)
    for n in range(subs):
        out[n] = folded(times_matrix(stacked(pull[n]), n, held, copies))
    one, two = by_parity(out[subs - 1, :, face:], nn2(out[0, :, :face], near))
    first[...] = one.astype(BF16)
    second[...] = two.astype(BF16)


def middle_kernel(matrix, displaced, received, kernel, lifts, order, *refs):
    base, norms0, ahead, row, tables, backs, ahead_sems = refs
    copies = start_ahead(matrix, ahead, ahead_sems)
    subs, cases, _ = displaced.shape
    column, face = lifts.shape[1], order.shape[1]
    wide = rounded_up(column, LANES)
    groups = kernel.shape[1] // wide
    fill_tables(tables, backs, order)
    sums = chain_sums(received, groups, received.shape[2])
    flat = jnp.concatenate([part[:, :wide] for part in sums], axis=1)
    values = nt2(flat, kernel[...])
    row[:cases] = sum(sums)
    norms0[...] = sum_halves(row, slice(0, cases), column, cases)
    lefts, rights = inner_jump([displaced[n] for n in range(subs)], tables, backs)
    for n in range(subs):
        base[n] = jnp.concatenate([lefts[n], rights[n]], axis=1) + nn2(values, lifts[n])
    for copy in copies:
        copy.wait()


def third_kernel(matrix, base, first, second, lifts, pull0, order, ahead, low, high, *refs):
    pull, bent2, after, payload, *joined, held, sems, tables, _, row = refs
    copies = start_fetch(matrix, held, sems, ahead.shape[0] // CHUNK)
    subs, cases, _ = base.shape
    face = order.shape[1]
    column = lifts.shape[1]
    for n in range(subs):
        tables[n] = table(order[n : n + 1])
    join(joined, low, high)
    from_after, from_before = by_parity(first[...].astype(F32), second[...].astype(F32))
    bent = outer_jump(
        [base[n, :, :face] for n in range(subs)],
        [base[n, :, face:] for n in range(subs)],
        nn(from_before.astype(BF16), tables[0]),
        from_after,
    )
    totals = None
    for n in range(subs):
        whole = bent[n]
        left = whole[:, :face]
        pull[n] = left
        moved = folded(times_matrix(stacked(whole), n, held, copies, ahead))
        bent2[n] = moved[:, :face]
        if n > 0:
            bent2[n] = moved[:, :face] - nn2(previous, tables[n])
        previous = moved[:, face:]
        parts = [
            nt2(left, lifts[n]),
            both3(nt, pull0[n], left),
            both3(nt, left, left),
            both3(nt, whole, moved),
        ]
        totals = parts if totals is None else [a + b for a, b in zip(totals, parts)]
    after[...] = previous.astype(BF16)
    corner, gram1, gram2, gram3 = totals
    row[...] = jnp.zeros(row.shape, F32)
    row[:cases, :column] = corner
    store_halves(row, gram1, slice(0, cases), column)
    step = cases // 2
    for j in range(2):
        for i, gram in enumerate((gram2, gram3)):
            part = gram[j * step : (j + 1) * step]
            store_halves(row, part, slice(cases, cases + step), (4 * j + 2 * i) * cases)
    copies_of(payload, row[...].astype(BF16))


def scene_kernel(
    bent, first, second, received, kernel, lifts, pull0, pull1, order, norms0,
    scene_loads, scene_weights, *refs, groups, pieces, slots
):
    blocks = refs[:pieces]
    multipliers_far, residual_far, held, row, multipliers, residual, sems = refs[pieces:]
    subs, cases, _ = bent.shape
    column = lifts.shape[1]
    wide = rounded_up(column, LANES)
    group = lax.axis_index("coarse")
    sums = chain_sums(received, groups, received.shape[2])
    for c in range(groups):
        held[c] = sums[c][:cases, :wide]
    flat = jnp.concatenate([held[c] for c in range(groups)], axis=1)
    values = nt2(flat, kernel[:column])
    if groups_whole(blocks, column, groups):
        lifted, index = None, iter(slots)
        for block in blocks:
            for i in range(block.shape[0] // column):
                sums_here = held[group ^ next(index)][:, :column]
                part = nn2(sums_here, block[i * column : (i + 1) * column])
                lifted = part if lifted is None else lifted + part
        energy = both3(nt, lifted, flat)
    else:
        energy = blocks[0][...]
    row[...] = sum(sums)
    norms1 = sum_halves(row, slice(0, cases), column, cases)
    lower = slice(cases, cases + cases // 2)
    norms2, norms3 = (
        jnp.concatenate(
            [sum_halves(row, lower, (4 * j + 2 * i) * cases, cases) for j in range(2)], axis=0
        )
        for i in range(2)
    )
    norms3 = norms3 + energy

    ids = iota((cases, scene_loads.shape[1]), 0)
    mixing = sum(
        jnp.where(ids == scene_loads[i : i + 1], scene_weights[i : i + 1], 0.0)
        for i in range(scene_loads.shape[0])
    )

    def moment(norms):
        return jnp.sum(both3(nn, norms, mixing) * mixing, axis=0, keepdims=True)

    moment0, moment1 = moment(norms0[...]), moment(norms1)
    moment2, moment3 = moment(norms2), moment(norms3)
    step0 = moment0 / moment1
    norm1 = moment0 - 2.0 * step0 * moment1 + step0 * step0 * moment2
    grow = 1.0 + norm1 / moment0
    curvature = grow * grow * moment1 - 2.0 * grow * step0 * moment2 + step0 * step0 * moment3
    step1 = norm1 / curvature
    zeros = jnp.zeros_like(mixing)

    def transposed(parts):
        weights = -jnp.concatenate(parts, axis=0)
        high = weights.astype(BF16).astype(F32)
        return jnp.concatenate([high, high, weights - high], axis=0).T.astype(BF16)

    for_multipliers = transposed(
        [(step0 + step1 * grow) * mixing, (-step0 * step1) * mixing, zeros]
    )
    for_residual = transposed(
        [mixing, (-step0 - step1 * grow) * mixing, (step0 * step1) * mixing]
    )
    _, from_before = by_parity(first[...].astype(F32), second[...].astype(F32))
    copies = []
    for n in range(subs):
        pull2 = bent[n]
        if n == 0:
            pull2 = pull2 - nn(from_before.astype(BF16), table(order[0:1]))
            pull2 = jnp.where(lax.axis_index("sub") == 0, 0.0, pull2)
        pull2 = pull2 + nn2(values, lifts[n])
        basis = jnp.concatenate([pull0[n], pull1[n], pull2], axis=0)
        high, low = halves(basis)
        basis = jnp.concatenate([high, low, high], axis=0)
        multipliers[n] = nn(for_multipliers, basis)
        copies += fetched([(multipliers.at[n], multipliers_far.at[n])], sems.at[pl.ds(2 * n, 1)])
        residual[n] = nn(for_residual, basis)
        copies += fetched([(residual.at[n], residual_far.at[n])], sems.at[pl.ds(2 * n + 1, 1)])
    for copy in copies:
        copy.wait()


def groups_whole(blocks, column, groups):
    return sum(block.shape[0] for block in blocks) == column * groups


def everywhere(x, axes):
    return lax.all_to_all(x, axes, 0, 0)


def swapped(x, axis, bit):
    return lax.ppermute(x, axis, [(i, i ^ bit) for i in range(lax.axis_size(axis))])


def pair_swaps(first, second, wrap=True):
    length = lax.axis_size("sub")

    def partner(i, j):
        return (i, j % length if wrap or 0 <= j < length else i)

    one = lax.ppermute(first, "sub", [partner(i, i ^ 1) for i in range(length)])
    two = lax.ppermute(
        second, "sub", [partner(i, i + 1 if i & 1 else i - 1) for i in range(length)]
    )
    return one, two


def call(kernel, outs, args, scratch=(), flops=0, moved=0, far=0, ends=pltpu.VMEM):
    specs = [pl.BlockSpec(memory_space=pltpu.HBM)] * far
    specs += [pl.BlockSpec(memory_space=pltpu.VMEM)] * (len(args) - far)
    pinned = [pltpu.with_memory_space_constraint(x, pltpu.HBM) for x in args[:far]]
    shapes = [jax.ShapeDtypeStruct(shape, kind) for shape, kind in outs]
    return pl.pallas_call(
        kernel,
        out_shape=shapes,
        in_specs=specs,
        out_specs=[pl.BlockSpec(memory_space=ends)] * len(outs),
        scratch_shapes=list(scratch),
        compiler_params=pltpu.CompilerParams(vmem_limit_bytes=32 << 20),
        cost_estimate=pl.CostEstimate(flops=flops, bytes_accessed=moved, transcendentals=0),
    )(*pinned, *args[far:])


def per_device(
    schur_inverse,
    corner_coupling,
    coarse_inverse,
    load_cases,
    face_order,
    corner_dofs,
    scene_loads,
    scene_weights,
):
    subs, iface = schur_inverse.shape[0], schur_inverse.shape[1]
    face = face_order.shape[1]
    corners = corner_dofs.shape[1]
    cases = load_cases.shape[1]
    scenes = scene_loads.shape[0]
    chain, groups = lax.axis_size("sub"), lax.axis_size("coarse")
    devices = chain * groups
    column = chain * corners
    wide = rounded_up(column, LANES)
    along = groups * wide
    work = dict(flops=4 * cases * schur_inverse.size, moved=2 * schur_inverse.size)

    fetch = [
        pltpu.VMEM(schur_inverse.shape, BF16),
        pltpu.SemaphoreType.DMA((subs * (iface // CHUNK),)),
    ]
    tables = [
        pltpu.VMEM((subs, face, face), BF16), pltpu.VMEM((max(subs - 1, 1), face, face), BF16)
    ]
    row = pltpu.VMEM((cases + cases // 2, rounded_up(column + 2 * cases, LANES)), F32)

    shard = coarse_inverse.reshape(column, groups * corners)
    shards = [swapped(shard, "sub", j) for j in range(1, chain)]

    lane = np.arange(along)
    inner = lane % wide
    source = (inner // corners * groups + lane // wide) * corners + inner % corners
    regroup = jnp.asarray(np.where(inner < column, source, -1)[None].astype(np.int32))

    bits = []
    if groups == 1 << 3 and (column * groups) ** 2 <= schur_inverse.size:
        bits = [1 << b for b in reversed(range(groups.bit_length() - 1))]

    small = [face_order, corner_coupling, corner_dofs, load_cases]
    sent0, *small = call(
        functools.partial(corner_kernel, chain=chain, groups=groups),
        [((devices, cases, wide), BF16)] + [(x.shape, x.dtype) for x in small],
        small,
        [pltpu.SemaphoreType.DMA((len(small),))],
        far=len(small),
    )
    face_order, corner_coupling, corner_dofs, load_cases = small
    received0 = everywhere(sent0, ("sub", "coarse"))
    packet = (cases + rounded_up(corners, 16), face + wide)
    displaced0, first, second, kernel = call(
        functools.partial(first_kernel, chain=chain, groups=groups),
        [
            ((subs, cases, iface), F32),
            (packet, BF16),
            (packet, BF16),
            ((column, along), BF16),
        ],
        [schur_inverse, shard, regroup, *small, *shards],
        fetch
        + [pltpu.VMEM(x.shape, x.dtype) for x in (shard, regroup)]
        + [pltpu.SemaphoreType.DMA((2,))],
        far=3,
        **work,
    )
    first, second = pair_swaps(first, second)
    own_lifts, bent0 = call(
        functools.partial(inner_kernel, chain=chain, groups=groups),
        [((subs, column, iface), BF16), ((subs, cases, iface), F32)],
        [displaced0, corner_coupling, corner_dofs, face_order],
        tables,
        flops=10**9,
        moved=2 * 10**6,
    )
    other = swapped(kernel, "coarse", bits[0]) if bits else kernel
    lifts, lifts_left, pull0, pull0_left, sent1, *joined = call(
        functools.partial(lift_kernel, groups=groups),
        [
            ((subs, column, iface), BF16),
            ((subs, column, face), BF16),
            ((subs, cases, iface), F32),
            ((subs, cases, face), F32),
            ((devices, cases, rounded_up(column + 2 * cases, LANES)), BF16),
        ]
        + [((2 * column, along), BF16)] * bool(bits),
        [bent0, own_lifts, first, second, received0, kernel, other, face_order],
        [pltpu.VMEM((cases, rounded_up(column + 2 * cases, LANES)), F32)],
        flops=10**9,
        moved=10**6,
    )
    received1 = everywhere(sent1, ("sub", "coarse"))
    displaced1, first, second = call(
        second_kernel,
        [((subs, cases, iface), F32), ((cases, face), BF16), ((cases, face), BF16)],
        [schur_inverse, pull0, face_order],
        fetch,
        far=1,
        **work,
    )
    first, second = pair_swaps(first, second)

    low = joined[0] if bits else kernel
    high = swapped(low, "coarse", bits[1]) if bits else kernel
    base, norms0, ahead = call(
        middle_kernel,
        [
            ((subs, cases, iface), F32),
            ((cases, cases), F32),
            ((AHEAD * CHUNK, iface), BF16),
        ],
        [schur_inverse, displaced1, received1, kernel, lifts, face_order],
        [row, *tables, pltpu.SemaphoreType.DMA((AHEAD,))],
        far=1,
        flops=10**9,
        moved=2 * 10**6,
    )
    pull1, bent2, after, sent2, *joined = call(
        third_kernel,
        [
            ((subs, cases, face), F32),
            ((subs, cases, face), F32),
            ((cases, face), BF16),
            ((devices, cases + cases // 2, rounded_up(column + 2 * cases, LANES)), BF16),
        ]
        + [((4 * column, along), BF16)] * bool(bits),
        [schur_inverse, base, first, second, lifts_left, pull0_left, face_order]
        + [ahead, low, high],
        [*fetch, *tables, row],
        far=1,
        **work,
    )
    received2 = everywhere(sent2, ("sub", "coarse"))
    first, second = pair_swaps(after, after, wrap=False)
    if bits:
        blocks = [joined[0], swapped(joined[0], "coarse", bits[2])]
        slots = [0, bits[0], bits[1], bits[0] ^ bits[1]]
        slots = slots + [slot ^ bits[2] for slot in slots]
    else:
        slots = []
        sums = received2.reshape((chain, groups) + received2.shape[1:])[..., :cases, :wide]
        sums = jnp.sum(sums.astype(F32), axis=0)
        flat = jnp.moveaxis(sums, 0, 1).reshape(cases, along)
        own = lax.dynamic_index_in_dim(sums, lax.axis_index("coarse"), 0, keepdims=False)
        values = jnp.dot(flat, kernel.astype(F32).T, precision=lax.Precision.HIGHEST)
        energy = jnp.dot(values, own[:, :column].T, precision=lax.Precision.HIGHEST)
        blocks = [lax.psum(energy, "coarse")]
    multipliers, residual = call(
        functools.partial(scene_kernel, groups=groups, pieces=len(blocks), slots=slots),
        [((subs, scenes, face), F32), ((subs, scenes, face), F32)],
        [bent2, first, second, received2, joined[0] if bits else kernel, lifts_left, pull0_left]
        + [pull1, face_order, norms0]
        + [scene_loads.T, scene_weights.T, *blocks],
        [pltpu.VMEM((groups, cases, wide), F32), row]
        + [pltpu.VMEM((subs, scenes, face), F32)] * 2
        + [pltpu.SemaphoreType.DMA((2 * subs,))],
        flops=10**9,
        moved=4 * 10**6,
        ends=pltpu.HBM,
    )
    return (multipliers, residual)


def solution(mesh):
    return jax.shard_map(
        per_device,
        mesh=mesh,
        in_specs=(
            P(("sub", "coarse"), None, None),
            P(("sub", "coarse"), None, None),
            P(None, "coarse", None, "sub"),
            P(("sub", "coarse"), None, None),
            P(("sub", "coarse"), None),
            P(("sub", "coarse"), None),
            P(),
            P(),
        ),
        out_specs=(P(("sub", "coarse"), None, None), P(("sub", "coarse"), None, None)),
        check_vma=False,
    )
```

```python
import functools

import jax
import jax.numpy as jnp
import numpy as np
from jax import lax
from jax.experimental import pallas as pl
from jax.experimental.pallas import tpu as pltpu
from jax.sharding import PartitionSpec as P

LANES = 128
CHUNK = 256
F32, BF16 = jnp.float32, jnp.bfloat16


def nn(a, b):
    return lax.dot_general(a, b, (((1,), (0,)), ((), ())), preferred_element_type=F32)


def nt(a, b):
    return lax.dot_general(a, b, (((1,), (1,)), ((), ())), preferred_element_type=F32)


def halves(x):
    high = x.astype(BF16)
    return high, (x - high.astype(F32)).astype(BF16)


def stacked(x):
    return jnp.concatenate(halves(x), axis=0)


def folded(x):
    rows = x.shape[0] // 2
    return x[:rows] + x[rows:]


def nn2(x, narrow):
    return folded(nn(stacked(x), narrow))


def nt2(x, narrow):
    return folded(nt(stacked(x), narrow))


def both3(product, x, y):
    high, low = halves(y)
    return folded(product(stacked(x), high)) + product(x.astype(BF16), low)


def equal(a, b):
    return jnp.where(a == b, 1.0, 0.0).astype(BF16)


def iota(shape, dim):
    return lax.broadcasted_iota(jnp.int32, shape, dim)


def rounded_up(value, unit):
    return (value + unit - 1) // unit * unit


def table(order_row):
    size = order_row.shape[1]
    return equal(iota((size, size), 0), order_row)


def back_table(order, n):
    subs, size = order.shape
    rows = jnp.concatenate(
        [order[...].astype(F32), jnp.zeros((rounded_up(subs, 8) - subs, size), F32)], axis=0
    )
    return equal(rows.T[:, n : n + 1].astype(jnp.int32), iota((size, size), 1))


def fill_tables(tables, backs, order):
    for n in range(1, tables.shape[0]):
        tables[n] = table(order[n : n + 1])
        backs[n - 1] = back_table(order, n)


def spread_of(dofs_row, chain, corners, groups):
    column = chain * corners
    ids = iota((column, 1), 0)
    slot = sum((ids >= t * corners).astype(jnp.int32) for t in range(1, chain))
    target = ids + slot * ((groups - 1) * corners) + lax.axis_index("coarse") * corners
    return equal(target, dofs_row)


def placed(x, width, at):
    rows = x.shape[1]
    return nn(x, equal(iota((rows, width), 0) + at, iota((rows, width), 1)))


def by_parity(to_after, to_before):
    odd = (lax.axis_index("sub") & 1) == 1
    return jnp.where(odd, to_before, to_after), jnp.where(odd, to_after, to_before)


def start_fetch(matrix, held, sems):
    subs, size = matrix.shape[0], matrix.shape[1]
    copies = []
    for n in range(subs):
        for k in range(size // CHUNK):
            part = pl.ds(k * CHUNK, CHUNK)
            copy = pltpu.make_async_copy(
                matrix.at[n, part], held.at[n, part], sems.at[n * (size // CHUNK) + k]
            )
            copy.start()
            copies.append(copy)
    return copies


def times_matrix(x, n, held, copies):
    size = held.shape[1]
    count = size // CHUNK
    total = None
    for k in range(count):
        rows = slice(k * CHUNK, (k + 1) * CHUNK)
        copies[n * count + k].wait()
        part = nn(x[:, rows], held[n, rows])
        total = part if total is None else total + part
    return total


def inner_jump(displaced, tables, backs):
    subs = len(displaced)
    face = tables.shape[1]
    lefts = [part[:, :face] for part in displaced]
    rights = [part[:, face:] for part in displaced]
    for n in range(1, subs):
        lefts[n] = lefts[n] - nn2(displaced[n - 1][:, face:], tables[n])
        rights[n - 1] = rights[n - 1] - nn2(displaced[n][:, :face], backs[n - 1])
    return lefts, rights


def outer_jump(lefts, rights, before, after):
    at_head = lax.axis_index("sub") == 0
    at_tail = lax.axis_index("sub") == lax.axis_size("sub") - 1
    lefts = [jnp.where(at_head, 0.0, lefts[0] - before), *lefts[1:]]
    rights = [*rights[:-1], jnp.where(at_tail, 0.0, rights[-1] - after)]
    return [jnp.concatenate(pair, axis=1) for pair in zip(lefts, rights)]


def chain_sums(received, groups, width):
    chain = received.shape[0] // groups
    sums = []
    for c in range(groups):
        total = None
        for z in range(chain):
            part = received[z * groups + c, :, :width].astype(F32)
            total = part if total is None else total + part
        sums.append(total)
    return sums


def copies_of(out, x):
    for i in range(out.shape[0]):
        out[i] = x


def fetched(pairs, sems):
    copies = [pltpu.make_async_copy(a, b, sems.at[i]) for i, (a, b) in enumerate(pairs)]
    for copy in copies:
        copy.start()
    return copies


def corner_kernel(*refs, chain, groups):
    far, out, (order, coupling, dofs, loads), sems = refs[:4], refs[4], refs[5:9], refs[9]
    for copy in fetched(list(zip(far, refs[5:9])), sems):
        copy.wait()
    corners = coupling.shape[1]
    total = None
    for n in range(loads.shape[0]):
        terms = nt(loads[n], coupling[n])
        part = nt2(terms, spread_of(dofs[n : n + 1], chain, corners, groups))
        total = part if total is None else total + part
    copies_of(out, placed(total.astype(BF16), out.shape[2], 0).astype(BF16))


def first_kernel(
    matrix, shard_far, regroup_far, order, coupling, dofs, loads, *refs, chain, groups
):
    shards, refs = refs[: chain - 1], refs[chain - 1 :]
    out, first, second, kernel, held, sems, shard, regroup, small = refs
    copies = start_fetch(matrix, held, sems)
    small_copies = fetched([(shard_far, shard), (regroup_far, regroup)], small)
    subs, cases, iface = loads.shape
    corners, face = coupling.shape[1], order.shape[1]
    pad = rounded_up(corners, 16) - corners

    def packet(displaced, coupled, n):
        spread = spread_of(dofs[n : n + 1], chain, corners, groups)
        eye = equal(iota((corners, corners), 0), iota((corners, corners), 1))
        hot = placed(nt(eye, spread).astype(BF16), first.shape[1] - face, 0)
        lower = jnp.concatenate([coupled, hot], axis=1)
        upper = jnp.concatenate([displaced, jnp.zeros((cases, hot.shape[1]), F32)], axis=1)
        return jnp.concatenate([upper, lower, jnp.zeros((pad, lower.shape[1]), F32)], axis=0)

    for n in range(subs):
        out[n] = times_matrix(loads[n], n, held, copies)
        if n == 0:
            near = table(order[0:1])
            to_before = packet(
                nt(out[0, :, :face].astype(BF16), near), nt(coupling[0, :, :face], near), 0
            )
            for copy in small_copies:
                copy.wait()
            position = lax.axis_index("sub")
            depth = groups * corners
            rows = None
            for j, block in enumerate([shard, *shards]):
                ids = iota((depth, regroup.shape[1]), 0) + (position ^ j) * depth
                part = nn(block[...], equal(ids, regroup[...]))
                rows = part if rows is None else rows + part
            kernel[...] = rows.astype(BF16)
    last = subs - 1
    to_after = packet(out[last, :, face:], coupling[last, :, face:].astype(F32), last)
    one, two = by_parity(to_after, to_before)
    first[...] = one.astype(BF16)
    second[...] = two.astype(BF16)


def inner_kernel(
    displaced, coupling, dofs, order, lifts, bent, tables, backs, *, chain, groups
):
    subs, cases, _ = displaced.shape
    corners, face = coupling.shape[1], order.shape[1]
    fill_tables(tables, backs, order)
    spreads = [spread_of(dofs[n : n + 1], chain, corners, groups) for n in range(subs)]
    for n in range(subs):
        left, right = nn(spreads[n], coupling[n, :, :face]), nn(spreads[n], coupling[n, :, face:])
        if n > 0:
            moved = nn(coupling[n - 1, :, face:], tables[n]).astype(BF16)
            left = left - nn(spreads[n - 1], moved)
        if n < subs - 1:
            moved = nn(coupling[n + 1, :, :face], backs[n]).astype(BF16)
            right = right - nn(spreads[n + 1], moved)
        lifts[n, :, :face] = left.astype(BF16)
        lifts[n, :, face:] = right.astype(BF16)
    lefts, rights = inner_jump([displaced[n] for n in range(subs)], tables, backs)
    for n in range(subs):
        bent[n, :, :face] = lefts[n]
        bent[n, :, face:] = rights[n]


def lift_kernel(
    bent, own_lifts, first, second, received, kernel, other, order,
    lifts, lifts_left, pull, pull_left, out, *refs, groups
):
    *joined, row = refs
    subs, cases, _ = bent.shape
    column, face = own_lifts.shape[1], order.shape[1]
    wide = rounded_up(column, LANES)
    join(joined, kernel, other)
    near = table(order[0:1])
    from_after, from_before = by_parity(first[...].astype(F32), second[...].astype(F32))
    eye = equal(iota((column, first.shape[1] - face), 0), iota((column, first.shape[1] - face), 1))

    def neighbour(block):
        low = block[cases:].astype(BF16)
        return low[:, :face], nt(eye, low[:, face:]).astype(BF16)

    before = nn(from_before[:, :face].astype(BF16), near)
    _, before_spread = neighbour(from_before)
    after_coupling, after_spread = neighbour(from_after)
    lifted = outer_jump(
        [own_lifts[n, :, :face].astype(F32) for n in range(subs)],
        [own_lifts[n, :, face:].astype(F32) for n in range(subs)],
        nn(before_spread, before[cases:].astype(BF16)).astype(BF16).astype(F32),
        nn(after_spread, after_coupling).astype(BF16).astype(F32),
    )
    bent = outer_jump(
        [bent[n, :, :face] for n in range(subs)],
        [bent[n, :, face:] for n in range(subs)],
        before[:cases],
        from_after[:cases, :face],
    )
    for n in range(subs):
        lifted[n] = lifted[n].astype(BF16)
        lifts[n] = lifted[n]
        lifts_left[n] = lifted[n][:, :face]
    flat = jnp.concatenate(chain_sums(received, groups, wide), axis=1)
    values = nt2(flat, kernel[...])
    corner, norms = None, None
    for n in range(subs):
        whole = bent[n] + nn2(values, lifted[n])
        pull[n] = whole
        left = whole[:, :face]
        pull_left[n] = left
        part, norm = nt2(left, lifted[n][:, :face]), both3(nt, left, left)
        corner = part if corner is None else corner + part
        norms = norm if norms is None else norms + norm
    row[...] = jnp.zeros(row.shape, F32)
    row[:, :column] = corner
    store_halves(row, norms, slice(0, cases), column)
    copies_of(out, row[...].astype(BF16))


def join(out, low, high):
    for ref in out:
        ref[: low.shape[0]] = low[...]
        ref[low.shape[0] :] = high[...]


def store_halves(row, gram, rows, at):
    for half in halves(gram):
        row[rows, at : at + gram.shape[1]] = half.astype(F32)
        at += gram.shape[1]


def sum_halves(row, rows, at, count):
    return row[rows, at : at + count] + row[rows, at + count : at + 2 * count]


def second_kernel(matrix, pull, order, out, first, second, held, sems):
    copies = start_fetch(matrix, held, sems)
    subs = pull.shape[0]
    face = order.shape[1]
    near = back_table(order, 0)
    for n in range(subs):
        out[n] = folded(times_matrix(stacked(pull[n]), n, held, copies))
    one, two = by_parity(out[subs - 1, :, face:], nn2(out[0, :, :face], near))
    first[...] = one.astype(BF16)
    second[...] = two.astype(BF16)


def middle_kernel(displaced, received, kernel, lifts, order, base, norms0, row, tables, backs):
    subs, cases, _ = displaced.shape
    column, face = lifts.shape[1], order.shape[1]
    wide = rounded_up(column, LANES)
    groups = kernel.shape[1] // wide
    fill_tables(tables, backs, order)
    sums = chain_sums(received, groups, received.shape[2])
    flat = jnp.concatenate([part[:, :wide] for part in sums], axis=1)
    values = nt2(flat, kernel[...])
    row[:cases] = sum(sums)
    norms0[...] = sum_halves(row, slice(0, cases), column, cases)
    lefts, rights = inner_jump([displaced[n] for n in range(subs)], tables, backs)
    for n in range(subs):
        base[n] = jnp.concatenate([lefts[n], rights[n]], axis=1) + nn2(values, lifts[n])


def third_kernel(matrix, base, first, second, lifts, pull0, order, low, high, *refs):
    pull, bent2, after, payload, *joined, held, sems, tables, _, row = refs
    copies = start_fetch(matrix, held, sems)
    subs, cases, _ = base.shape
    face = order.shape[1]
    column = lifts.shape[1]
    for n in range(subs):
        tables[n] = table(order[n : n + 1])
    join(joined, low, high)
    from_after, from_before = by_parity(first[...].astype(F32), second[...].astype(F32))
    bent = outer_jump(
        [base[n, :, :face] for n in range(subs)],
        [base[n, :, face:] for n in range(subs)],
        nn(from_before.astype(BF16), tables[0]),
        from_after,
    )
    totals = None
    for n in range(subs):
        whole = bent[n]
        left = whole[:, :face]
        pull[n] = left
        moved = folded(times_matrix(stacked(whole), n, held, copies))
        bent2[n] = moved[:, :face]
        if n > 0:
            bent2[n] = moved[:, :face] - nn2(previous, tables[n])
        previous = moved[:, face:]
        parts = [
            nt2(left, lifts[n]),
            both3(nt, pull0[n], left),
            both3(nt, left, left),
            both3(nt, whole, moved),
        ]
        totals = parts if totals is None else [a + b for a, b in zip(totals, parts)]
    after[...] = previous.astype(BF16)
    corner, gram1, gram2, gram3 = totals
    row[...] = jnp.zeros(row.shape, F32)
    row[:cases, :column] = corner
    store_halves(row, gram1, slice(0, cases), column)
    step = cases // 2
    for j in range(2):
        for i, gram in enumerate((gram2, gram3)):
            part = gram[j * step : (j + 1) * step]
            store_halves(row, part, slice(cases, cases + step), (4 * j + 2 * i) * cases)
    copies_of(payload, row[...].astype(BF16))


def scene_kernel(
    bent, first, second, received, kernel, lifts, pull0, pull1, order, norms0,
    scene_loads, scene_weights, *refs, groups, pieces, slots
):
    blocks = refs[:pieces]
    multipliers_far, residual_far, held, row, multipliers, residual, sems = refs[pieces:]
    subs, cases, _ = bent.shape
    column = lifts.shape[1]
    wide = rounded_up(column, LANES)
    group = lax.axis_index("coarse")
    sums = chain_sums(received, groups, received.shape[2])
    for c in range(groups):
        held[c] = sums[c][:cases, :wide]
    flat = jnp.concatenate([held[c] for c in range(groups)], axis=1)
    values = nt2(flat, kernel[:column])
    if groups_whole(blocks, column, groups):
        lifted, index = None, iter(slots)
        for block in blocks:
            for i in range(block.shape[0] // column):
                sums_here = held[group ^ next(index)][:, :column]
                part = nn2(sums_here, block[i * column : (i + 1) * column])
                lifted = part if lifted is None else lifted + part
        energy = both3(nt, lifted, flat)
    else:
        energy = blocks[0][...]
    row[...] = sum(sums)
    norms1 = sum_halves(row, slice(0, cases), column, cases)
    lower = slice(cases, cases + cases // 2)
    norms2, norms3 = (
        jnp.concatenate(
            [sum_halves(row, lower, (4 * j + 2 * i) * cases, cases) for j in range(2)], axis=0
        )
        for i in range(2)
    )
    norms3 = norms3 + energy

    ids = iota((cases, scene_loads.shape[1]), 0)
    mixing = sum(
        jnp.where(ids == scene_loads[i : i + 1], scene_weights[i : i + 1], 0.0)
        for i in range(scene_loads.shape[0])
    )

    def moment(norms):
        return jnp.sum(both3(nn, norms, mixing) * mixing, axis=0, keepdims=True)

    moment0, moment1 = moment(norms0[...]), moment(norms1)
    moment2, moment3 = moment(norms2), moment(norms3)
    step0 = moment0 / moment1
    norm1 = moment0 - 2.0 * step0 * moment1 + step0 * step0 * moment2
    grow = 1.0 + norm1 / moment0
    curvature = grow * grow * moment1 - 2.0 * grow * step0 * moment2 + step0 * step0 * moment3
    step1 = norm1 / curvature
    zeros = jnp.zeros_like(mixing)

    def transposed(parts):
        weights = -jnp.concatenate(parts, axis=0)
        high = weights.astype(BF16).astype(F32)
        return jnp.concatenate([high, high, weights - high], axis=0).T.astype(BF16)

    for_multipliers = transposed(
        [(step0 + step1 * grow) * mixing, (-step0 * step1) * mixing, zeros]
    )
    for_residual = transposed(
        [mixing, (-step0 - step1 * grow) * mixing, (step0 * step1) * mixing]
    )
    _, from_before = by_parity(first[...].astype(F32), second[...].astype(F32))
    copies = []
    for n in range(subs):
        pull2 = bent[n]
        if n == 0:
            pull2 = pull2 - nn(from_before.astype(BF16), table(order[0:1]))
            pull2 = jnp.where(lax.axis_index("sub") == 0, 0.0, pull2)
        pull2 = pull2 + nn2(values, lifts[n])
        basis = jnp.concatenate([pull0[n], pull1[n], pull2], axis=0)
        high, low = halves(basis)
        basis = jnp.concatenate([high, low, high], axis=0)
        multipliers[n] = nn(for_multipliers, basis)
        copies += fetched([(multipliers.at[n], multipliers_far.at[n])], sems.at[pl.ds(2 * n, 1)])
        residual[n] = nn(for_residual, basis)
        copies += fetched([(residual.at[n], residual_far.at[n])], sems.at[pl.ds(2 * n + 1, 1)])
    for copy in copies:
        copy.wait()


def groups_whole(blocks, column, groups):
    return sum(block.shape[0] for block in blocks) == column * groups


def everywhere(x, axes):
    return lax.all_to_all(x, axes, 0, 0)


def swapped(x, axis, bit):
    return lax.ppermute(x, axis, [(i, i ^ bit) for i in range(lax.axis_size(axis))])


def pair_swaps(first, second, wrap=True):
    length = lax.axis_size("sub")

    def partner(i, j):
        return (i, j % length if wrap or 0 <= j < length else i)

    one = lax.ppermute(first, "sub", [partner(i, i ^ 1) for i in range(length)])
    two = lax.ppermute(
        second, "sub", [partner(i, i + 1 if i & 1 else i - 1) for i in range(length)]
    )
    return one, two


def call(kernel, outs, args, scratch=(), flops=0, moved=0, far=0, ends=pltpu.VMEM):
    specs = [pl.BlockSpec(memory_space=pltpu.HBM)] * far
    specs += [pl.BlockSpec(memory_space=pltpu.VMEM)] * (len(args) - far)
    pinned = [pltpu.with_memory_space_constraint(x, pltpu.HBM) for x in args[:far]]
    shapes = [jax.ShapeDtypeStruct(shape, kind) for shape, kind in outs]
    return pl.pallas_call(
        kernel,
        out_shape=shapes,
        in_specs=specs,
        out_specs=[pl.BlockSpec(memory_space=ends)] * len(outs),
        scratch_shapes=list(scratch),
        compiler_params=pltpu.CompilerParams(vmem_limit_bytes=32 << 20),
        cost_estimate=pl.CostEstimate(flops=flops, bytes_accessed=moved, transcendentals=0),
    )(*pinned, *args[far:])


def per_device(
    schur_inverse,
    corner_coupling,
    coarse_inverse,
    load_cases,
    face_order,
    corner_dofs,
    scene_loads,
    scene_weights,
):
    subs, iface = schur_inverse.shape[0], schur_inverse.shape[1]
    face = face_order.shape[1]
    corners = corner_dofs.shape[1]
    cases = load_cases.shape[1]
    scenes = scene_loads.shape[0]
    chain, groups = lax.axis_size("sub"), lax.axis_size("coarse")
    devices = chain * groups
    column = chain * corners
    wide = rounded_up(column, LANES)
    along = groups * wide
    work = dict(flops=4 * cases * schur_inverse.size, moved=2 * schur_inverse.size)

    fetch = [
        pltpu.VMEM(schur_inverse.shape, BF16),
        pltpu.SemaphoreType.DMA((subs * (iface // CHUNK),)),
    ]
    tables = [
        pltpu.VMEM((subs, face, face), BF16), pltpu.VMEM((max(subs - 1, 1), face, face), BF16)
    ]
    row = pltpu.VMEM((cases + cases // 2, rounded_up(column + 2 * cases, LANES)), F32)

    shard = coarse_inverse.reshape(column, groups * corners)
    shards = [swapped(shard, "sub", j) for j in range(1, chain)]

    lane = np.arange(along)
    inner = lane % wide
    source = (inner // corners * groups + lane // wide) * corners + inner % corners
    regroup = jnp.asarray(np.where(inner < column, source, -1)[None].astype(np.int32))

    bits = []
    if groups == 1 << 3 and (column * groups) ** 2 <= schur_inverse.size:
        bits = [1 << b for b in reversed(range(groups.bit_length() - 1))]

    small = [face_order, corner_coupling, corner_dofs, load_cases]
    sent0, *small = call(
        functools.partial(corner_kernel, chain=chain, groups=groups),
        [((devices, cases, wide), BF16)] + [(x.shape, x.dtype) for x in small],
        small,
        [pltpu.SemaphoreType.DMA((len(small),))],
        far=len(small),
    )
    face_order, corner_coupling, corner_dofs, load_cases = small
    received0 = everywhere(sent0, ("sub", "coarse"))
    packet = (cases + rounded_up(corners, 16), face + wide)
    displaced0, first, second, kernel = call(
        functools.partial(first_kernel, chain=chain, groups=groups),
        [
            ((subs, cases, iface), F32),
            (packet, BF16),
            (packet, BF16),
            ((column, along), BF16),
        ],
        [schur_inverse, shard, regroup, *small, *shards],
        fetch
        + [pltpu.VMEM(x.shape, x.dtype) for x in (shard, regroup)]
        + [pltpu.SemaphoreType.DMA((2,))],
        far=3,
        **work,
    )
    first, second = pair_swaps(first, second)
    own_lifts, bent0 = call(
        functools.partial(inner_kernel, chain=chain, groups=groups),
        [((subs, column, iface), BF16), ((subs, cases, iface), F32)],
        [displaced0, corner_coupling, corner_dofs, face_order],
        tables,
        flops=10**9,
        moved=2 * 10**6,
    )
    other = swapped(kernel, "coarse", bits[0]) if bits else kernel
    lifts, lifts_left, pull0, pull0_left, sent1, *joined = call(
        functools.partial(lift_kernel, groups=groups),
        [
            ((subs, column, iface), BF16),
            ((subs, column, face), BF16),
            ((subs, cases, iface), F32),
            ((subs, cases, face), F32),
            ((devices, cases, rounded_up(column + 2 * cases, LANES)), BF16),
        ]
        + [((2 * column, along), BF16)] * bool(bits),
        [bent0, own_lifts, first, second, received0, kernel, other, face_order],
        [pltpu.VMEM((cases, rounded_up(column + 2 * cases, LANES)), F32)],
        flops=10**9,
        moved=10**6,
    )
    received1 = everywhere(sent1, ("sub", "coarse"))
    displaced1, first, second = call(
        second_kernel,
        [((subs, cases, iface), F32), ((cases, face), BF16), ((cases, face), BF16)],
        [schur_inverse, pull0, face_order],
        fetch,
        far=1,
        **work,
    )
    first, second = pair_swaps(first, second)

    low = joined[0] if bits else kernel
    high = swapped(low, "coarse", bits[1]) if bits else kernel
    base, norms0 = call(
        middle_kernel,
        [((subs, cases, iface), F32), ((cases, cases), F32)],
        [displaced1, received1, kernel, lifts, face_order],
        [row, *tables],
        flops=10**9,
        moved=2 * 10**6,
    )
    pull1, bent2, after, sent2, *joined = call(
        third_kernel,
        [
            ((subs, cases, face), F32),
            ((subs, cases, face), F32),
            ((cases, face), BF16),
            ((devices, cases + cases // 2, rounded_up(column + 2 * cases, LANES)), BF16),
        ]
        + [((4 * column, along), BF16)] * bool(bits),
        [schur_inverse, base, first, second, lifts_left, pull0_left, face_order]
        + [low, high],
        [*fetch, *tables, row],
        far=1,
        **work,
    )
    received2 = everywhere(sent2, ("sub", "coarse"))
    first, second = pair_swaps(after, after, wrap=False)
    if bits:
        blocks = [joined[0], swapped(joined[0], "coarse", bits[2])]
        slots = [0, bits[0], bits[1], bits[0] ^ bits[1]]
        slots = slots + [slot ^ bits[2] for slot in slots]
    else:
        slots = []
        sums = received2.reshape((chain, groups) + received2.shape[1:])[..., :cases, :wide]
        sums = jnp.sum(sums.astype(F32), axis=0)
        flat = jnp.moveaxis(sums, 0, 1).reshape(cases, along)
        own = lax.dynamic_index_in_dim(sums, lax.axis_index("coarse"), 0, keepdims=False)
        values = jnp.dot(flat, kernel.astype(F32).T, precision=lax.Precision.HIGHEST)
        energy = jnp.dot(values, own[:, :column].T, precision=lax.Precision.HIGHEST)
        blocks = [lax.psum(energy, "coarse")]
    multipliers, residual = call(
        functools.partial(scene_kernel, groups=groups, pieces=len(blocks), slots=slots),
        [((subs, scenes, face), F32), ((subs, scenes, face), F32)],
        [bent2, first, second, received2, joined[0] if bits else kernel, lifts_left, pull0_left]
        + [pull1, face_order, norms0]
        + [scene_loads.T, scene_weights.T, *blocks],
        [pltpu.VMEM((groups, cases, wide), F32), row]
        + [pltpu.VMEM((subs, scenes, face), F32)] * 2
        + [pltpu.SemaphoreType.DMA((2 * subs,))],
        flops=10**9,
        moved=4 * 10**6,
        ends=pltpu.HBM,
    )
    return (multipliers, residual)


def solution(mesh):
    return jax.shard_map(
        per_device,
        mesh=mesh,
        in_specs=(
            P(("sub", "coarse"), None, None),
            P(("sub", "coarse"), None, None),
            P(None, "coarse", None, "sub"),
            P(("sub", "coarse"), None, None),
            P(("sub", "coarse"), None),
            P(("sub", "coarse"), None),
            P(),
            P(),
        ),
        out_specs=(P(("sub", "coarse"), None, None), P(("sub", "coarse"), None, None)),
        check_vma=False,
    )
```
